32 devices in a mesh: sent: 32 (over z, y, x, core).
Axes of the slice: x: 2, y: 2, z: 4, core: 2. Of those that a mesh axis runs over, the one named last changes fastest.
Arguments:
- embeddings: bfloat16 [8192, 768], P('sent'), may hold values from -6 to 6
- cotangent: bfloat16 [2, 8192, 768], P(None, 'sent'), may hold values from -0.011962891 to 0.011962891
- drop_masks: int32 [2, 3, 8192, 768], P(None, None, 'sent'), may hold values 0 or 1
- lengths: int32 [256], P('sent'), may hold values from 0 to 128, as said below
- buckets: int32 [32], replicated, may hold values from 0 to 2, as said below
- attn_params: float32 [2463744], P('sent'), may hold values from -3 to 3
- attn_moment: float32 [2463744], P('sent'), may hold values from -1 to 1
- attn_second: float32 [2463744], P('sent'), may hold values from 0 to 1, as said below
- attn_ema: float32 [2463744], P('sent'), may hold values from -3 to 3
- head_params: float32 [5314560], P('sent'), may hold values from -3 to 3
- head_moment: float32 [5314560], P('sent'), may hold values from -1 to 1
- head_second: float32 [5314560], P('sent'), may hold values from 0 to 1, as said below
- head_ema: float32 [5314560], P('sent'), may hold values from -3 to 3
Outputs:
- hidden: bfloat16 [2, 8192, 768], P(None, 'sent')
- input_grad: float32 [8192, 768], P('sent')
- loss: float32 [], replicated
- grad_norm: float32 [], replicated
- attn_first: float32 [2463744], P('sent')
- attn_second_new: float32 [2463744], P('sent')
- attn_updated: float32 [2463744], P('sent')
- attn_average: float32 [2463744], P('sent')
- head_first: float32 [5314560], P('sent')
- head_second_new: float32 [5314560], P('sent')
- head_updated: float32 [5314560], P('sent')
- head_average: float32 [5314560], P('sent')
The draws below stay inside these ranges and needn't reach their ends.
Inputs may be any that keep to these rules, and one draw needn't show every extreme that they name: `buckets`: sentences of device b have 32 * 2^code rows; some device has code 2. `lengths`: slot s of a device holds a sentence of 1 to its bucket length rows when s < 256 // (bucket length), else 0; the first slot of every device is full. `attn_second`: positive. `head_second`: positive.
All inputs are finite; a program needn't handle non-finite values. No bound on the sum of `drop_masks` on one device may be relied on, other than what follows from the above.
Results may differ from the reference program's by a relative error of at most 0.017.
The reference program's roundings to bfloat16 on the way count: a program that leaves them out, or rounds other values in their place, can miss the bound.
Values may be sent and summed in bfloat16 or wider, within the bound.
No kernel may reach another device: no remote copies, remote signals or barrier semaphores. Data moves between devices by JAX's collectives and lax.ppermute only.
A program may use at most 192 MiB of HBM per device.

```python
import jax
import jax.numpy as jnp
from jax import lax

D = 768
H = 12
HD = 64
LMIN = 32
POS = 128
TOK_DEV = 256
SLOTS = 8
TOKENS = 8192
SENTS = 256
PA = 2463744
PH = 5314560
STEP = 5
N_SENT = 32


clip_bound = 0.001


def bucket_draw(key):
    sub_keys = jax.random.split(key, 2)
    device_count = SENTS // SLOTS
    code_draw = jax.random.randint(sub_keys[0], (device_count,), 0, 3)
    forced = jax.random.randint(sub_keys[1], (), 0, device_count)
    return jnp.where(jnp.arange(device_count) == forced, 2, code_draw).astype(jnp.int32)


def draw_buckets(key, part):
    return bucket_draw(key)


def draw_lengths(key, part):
    code_draw = bucket_draw(key)
    key = jax.random.fold_in(key, 7)
    slot_index = jnp.arange(SENTS)
    owner = slot_index // SLOTS
    slot_pos = slot_index % SLOTS
    bucket_len = LMIN * jnp.where(code_draw == 0, 1, jnp.where(code_draw == 1, 2, 4))
    owner_len = bucket_len[owner]
    raw_draw = jax.random.randint(key, (SENTS,), 0, 4 * LMIN)
    length = jnp.where(slot_pos == 0, owner_len, 1 + raw_draw % owner_len)
    return jnp.where(slot_pos < TOK_DEV // owner_len, length, 0).astype(jnp.int32)


def normal_draw(key, shape):
    return jax.random.truncated_normal(key, -4.0, 4.0, shape, jnp.float32)


def draw_embeddings(key, part):
    code_draw = bucket_draw(key)
    key = jax.random.fold_in(key, 31)
    sub_keys = jax.random.split(key, 2)
    row_index = jnp.arange(TOKENS)
    owner = row_index // TOK_DEV
    bucket_len = LMIN * jnp.where(code_draw == 0, 1, jnp.where(code_draw == 1, 2, 4))
    place = row_index % TOK_DEV % bucket_len[owner]
    common = normal_draw(sub_keys[0], (POS, D))
    noise = 0.1 * normal_draw(sub_keys[1], (TOKENS, D))
    return (jnp.take(common, place, axis=0) + noise).astype(jnp.bfloat16)


def rising_gain(key):
    row_pos = jnp.arange(D, dtype=jnp.float32)
    return (0.6 + 1.2 * row_pos / (D - 1)) * jax.random.uniform(key, (D,), jnp.float32, 0.85, 1.15)


def attn_layout(key):
    sub_keys = jax.random.split(key, 5)
    inv_root = D ** (-0.5)
    col_ids = jnp.arange(4 * D)
    matrix = normal_draw(sub_keys[0], (D, 4 * D)) * jnp.where(col_ids < 3 * D, inv_root, 4.0 * inv_root)
    vec_ids = jnp.arange(8)
    small_vals = 0.1 * normal_draw(sub_keys[1], (D, 8))
    vectors = jnp.where(vec_ids == 3, rising_gain(sub_keys[2])[:, None], jnp.where(vec_ids == 5, rising_gain(sub_keys[3])[:, None], small_vals))
    pos_table = 0.3 * normal_draw(sub_keys[4], (D, POS))
    return jnp.concatenate([matrix.reshape(-1), jnp.concatenate([vectors, pos_table], axis=1).reshape(-1)])


def head_layout(key):
    sub_keys = jax.random.split(key, 3)
    inv_root = D ** (-0.5)
    col_ids = jnp.arange(9 * D)
    col_scale = jnp.where((col_ids >= 4 * D) & (col_ids < 8 * D), (4 * D) ** (-0.5), inv_root)
    matrix = normal_draw(sub_keys[0], (D, 9 * D)) * col_scale
    vec_ids = jnp.arange(8)
    small_vals = 0.1 * normal_draw(sub_keys[1], (D, 8))
    vectors = jnp.where(vec_ids == 5, rising_gain(sub_keys[2])[:, None], small_vals)
    return jnp.concatenate([matrix.reshape(-1), vectors.reshape(-1)])


def kind_scale(mat_count, total_count):
    entry_size = clip_bound * (PA + PH) ** (-0.5)
    return jnp.where(jnp.arange(total_count) < mat_count, 1.0, 3.0) * entry_size


def draw_attn_params(key, part):
    key = jax.random.fold_in(key, 11)
    return attn_layout(key)


def draw_attn_ema(key, part):
    key = jax.random.fold_in(key, 12)
    return attn_layout(key)


def draw_attn_moment(key, part):
    key = jax.random.fold_in(key, 13)
    return normal_draw(key, (PA,)) * kind_scale(4 * D * D, PA)


def draw_attn_second(key, part):
    key = jax.random.fold_in(key, 14)
    scale_vals = kind_scale(4 * D * D, PA)
    return scale_vals * scale_vals * jnp.exp(jax.random.uniform(key, (PA,), jnp.float32, 0.0, 1.3862944))


def draw_head_params(key, part):
    key = jax.random.fold_in(key, 21)
    return head_layout(key)


def draw_head_ema(key, part):
    key = jax.random.fold_in(key, 22)
    return head_layout(key)


def draw_head_moment(key, part):
    key = jax.random.fold_in(key, 23)
    return normal_draw(key, (PH,)) * kind_scale(9 * D * D, PH)


def draw_head_second(key, part):
    key = jax.random.fold_in(key, 24)
    scale_vals = kind_scale(9 * D * D, PH)
    return scale_vals * scale_vals * jnp.exp(jax.random.uniform(key, (PH,), jnp.float32, 0.0, 1.3862944))


def plant(values, key, smallest, high):
    shape = values.shape
    spot = [jax.random.randint(jax.random.fold_in(key, axis), (), 0, shape[axis]) for axis in range(len(shape))]
    values = values.at[tuple(spot)].set(smallest)
    longest = shape.index(max(shape))
    spot[longest] = (spot[longest] + 1) % shape[longest]
    return values.at[tuple(spot)].set(high)


def levels(own_key, shape, cuts, least, high):
    factor_of = 1.0
    for axis_at, shards_of in cuts:
        steps = jax.random.uniform(jax.random.fold_in(jax.random.fold_in(own_key, 6), axis_at), (shards_of,), jnp.float32, least / len(cuts), high / len(cuts))
        factor_of = factor_of * jnp.repeat(jnp.exp(steps), shape[axis_at] // shards_of).reshape((-1,) + (1,) * (len(shape) - 1 - axis_at))
    return factor_of


def scatter_about(stream_key, shape, width, limit, shards=(), kind=jnp.bfloat16):
    values = jax.random.normal(stream_key, shape, jnp.float32) * width
    if len(shards) > 0:
        values = levels(stream_key, shape, shards, -0.22, 0.18) * values
    return jnp.clip(values, min=-limit, max=limit).astype(kind)


def setup_inputs(seed: int = 0) -> dict:
    arg_keys = jax.random.split(jax.random.key(seed), 14)
    return {
        "embeddings": draw_embeddings(jax.random.fold_in(arg_keys[13], 71), 0),
        "cotangent": scatter_about(arg_keys[1], (2, TOKENS, D), 0.002, 0.011962891, ((1, 32),)),
        "drop_masks": plant((jax.random.randint(arg_keys[2], (2, 3, TOKENS, D), 0, 10) < 9).astype(jnp.int32), jax.random.fold_in(arg_keys[2], 1), 0, 1),
        "lengths": draw_lengths(jax.random.fold_in(arg_keys[13], 71), 0),
        "buckets": draw_buckets(jax.random.fold_in(arg_keys[13], 71), 0),
        "attn_params": draw_attn_params(jax.random.fold_in(arg_keys[13], 71), 0),
        "attn_moment": draw_attn_moment(jax.random.fold_in(arg_keys[13], 71), 0),
        "attn_second": draw_attn_second(jax.random.fold_in(arg_keys[13], 71), 0),
        "attn_ema": draw_attn_ema(jax.random.fold_in(arg_keys[13], 71), 0),
        "head_params": draw_head_params(jax.random.fold_in(arg_keys[13], 71), 0),
        "head_moment": draw_head_moment(jax.random.fold_in(arg_keys[13], 71), 0),
        "head_second": draw_head_second(jax.random.fold_in(arg_keys[13], 71), 0),
        "head_ema": draw_head_ema(jax.random.fold_in(arg_keys[13], 71), 0),
    }


@jax.custom_vjp
def low(v):
    return lax.optimization_barrier(v.astype(jnp.bfloat16)).astype(jnp.float32)

@jax.custom_vjp
def low_back(v):
    return v

def low_keep(v):
    return (low(v), None)

def low_pass(kept, grad):
    return (grad,)

def back_keep(v):
    return (v, None)

def back_low(kept, grad):
    return (low(grad),)
low.defvjp(low_keep, low_pass)
low_back.defvjp(back_keep, back_low)
logit_divisor = 0.05
keep_prob = 0.9
norm_eps = 1e-06
clip_bound = 0.001
beta_first = 0.5
beta_second = 0.5
learn_rate = 0.05
decay_rate = 0.01
adam_eps = 1e-08
ema_rate = 0.8
masked_scores = -1e+30
highest = lax.Precision.HIGHEST

def pairwise_inner(left_op, right_op):
    return jnp.dot(left_op, right_op, precision=highest, preferred_element_type=jnp.float32)

def layer_norm(tensor, gain_vec, shift_vec):
    center = tensor - lax.optimization_barrier(jnp.mean(tensor, axis=-1, keepdims=True))
    spread = lax.optimization_barrier(jnp.mean(center * center, axis=-1, keepdims=True))
    return center * lax.rsqrt(spread + norm_eps) * gain_vec + shift_vec

def gelu_exact(tensor):
    return 0.5 * tensor * (1.0 + jax.scipy.special.erf(tensor * 0.7071067811865476))

def bucket_length(bucket_code):
    return (LMIN * jnp.where(bucket_code == 0, 1, jnp.where(bucket_code == 1, 2, 4))).astype(jnp.int32)

def device_block(attn_low, head_low, embed_rows, keep_masks, slot_lengths, bucket_code):
    attn_mats = attn_low[:4 * D * D].reshape(D, 4 * D)
    attn_vecs = attn_low[4 * D * D:].reshape(D, 8 + POS)
    head_mats = head_low[:9 * D * D].reshape(D, 9 * D)
    head_vecs = head_low[9 * D * D:].reshape(D, 8)
    bucket_len = bucket_length(bucket_code)
    sent_count = TOK_DEV // bucket_len
    row_ids = jnp.arange(TOK_DEV, dtype=jnp.int32)
    sentence = row_ids // bucket_len
    row_place = row_ids % bucket_len
    key_ok = row_place < jnp.take(slot_lengths, sentence)
    allowed = (sentence[:, None] == sentence[None, :]) & key_ok[None, :]
    pos_table = attn_vecs[:, 8:].T
    emb_rows = embed_rows + jnp.take(pos_table, row_place, axis=0) + attn_vecs[:, 7]
    normed = layer_norm(emb_rows, attn_vecs[:, 5], attn_vecs[:, 6])
    qkv_bias = jnp.concatenate([attn_vecs[:, 0], jnp.zeros((D,), jnp.float32), attn_vecs[:, 1]])
    up_bias = head_vecs[:, :4].T.reshape(4 * D)
    slot_ids = jnp.arange(SLOTS, dtype=jnp.int32)
    cls_pick = jnp.minimum(slot_ids, sent_count - 1) * bucket_len
    hidden_list = []
    unit_list = []
    for view_idx in range(2):
        attn_in = normed * keep_masks[view_idx, 0]
        qkv = low(low_back(pairwise_inner(low(attn_in), attn_mats[:, :3 * D])) + qkv_bias)
        head_split = qkv.reshape(TOK_DEV, 3, H, HD)
        raw_scores = jnp.einsum('qhd,khd->hqk', head_split[:, 0], head_split[:, 1], precision=highest)
        scores = jnp.where(allowed[None], low_back(raw_scores) * HD ** (-0.5), masked_scores)
        row_top = lax.optimization_barrier(jnp.max(scores, axis=-1, keepdims=True))
        expo_vals = jnp.exp(scores - row_top)
        attn_probs = low(expo_vals / lax.optimization_barrier(jnp.sum(expo_vals, axis=-1, keepdims=True)))
        mixed_out = jnp.einsum('hqk,khd->qhd', attn_probs, head_split[:, 2], precision=highest)
        mixed_out = low(low_back(mixed_out.reshape(TOK_DEV, D)))
        branch = low_back(pairwise_inner(mixed_out, attn_mats[:, 3 * D:])) + attn_vecs[:, 2]
        first_norm = layer_norm(attn_in + keep_masks[view_idx, 1] * branch, attn_vecs[:, 3], attn_vecs[:, 4])
        up_pre = low_back(pairwise_inner(low(first_norm), head_mats[:, :4 * D])) + up_bias
        active = low(gelu_exact(up_pre))
        down_out = low_back(pairwise_inner(active, head_mats[:, 4 * D:8 * D].T)) + head_vecs[:, 4]
        second_norm = layer_norm(first_norm + keep_masks[view_idx, 2] * down_out, head_vecs[:, 5], head_vecs[:, 6])
        cls_rows = jnp.take(second_norm, cls_pick, axis=0)
        pooled = jnp.tanh(low_back(pairwise_inner(low(cls_rows), head_mats[:, 8 * D:])) + head_vecs[:, 7])
        unit_rows = pooled * lax.rsqrt(lax.optimization_barrier(jnp.sum(pooled * pooled, axis=-1, keepdims=True)) + norm_eps)
        hidden_list.append(second_norm)
        unit_list.append(unit_rows)
    return (jnp.stack(hidden_list), jnp.stack(unit_list))

def objective(attn_weights, head_weights, embed_rows, cotangent, keep_masks, lengths, buckets):
    attn_low = low(attn_weights)
    head_low = low(head_weights)
    run_block = jax.checkpoint(device_block)
    item_set = (embed_rows.reshape(N_SENT, TOK_DEV, D), jnp.moveaxis(keep_masks.reshape(2, 3, N_SENT, TOK_DEV, D), 2, 0), lengths.reshape(N_SENT, SLOTS), buckets)
    hidden_all, unit_all = lax.map(lambda items: run_block(attn_low, head_low, items[0], items[1], items[2], items[3]), item_set)
    slot_ids = jnp.arange(SLOTS, dtype=jnp.int32)
    valid_mask = (slot_ids[None, :] < (TOK_DEV // bucket_length(buckets))[:, None]).reshape(SENTS).astype(jnp.float32)
    query_embeddings = low(unit_all[:, 0].reshape(SENTS, D))
    positive_view_set = low(unit_all[:, 1].reshape(SENTS, D))
    cosine_logit_table = low_back(pairwise_inner(query_embeddings, positive_view_set.T)) / logit_divisor
    cosine_logit_table = jnp.where(valid_mask[None, :] > 0, cosine_logit_table, masked_scores)
    sim_top = lax.optimization_barrier(jnp.max(cosine_logit_table, axis=-1, keepdims=True))
    row_lse = sim_top[:, 0] + jnp.log(lax.optimization_barrier(jnp.sum(jnp.exp(cosine_logit_table - sim_top), axis=-1)))
    loss_sum = jnp.sum(valid_mask * (row_lse - jnp.diagonal(cosine_logit_table)))
    hidden_rows = jnp.moveaxis(hidden_all, 1, 0).reshape(2, TOKENS, D)
    return (loss_sum + jnp.sum(cotangent * hidden_rows), (hidden_rows, loss_sum, valid_mask))

def adam_step(grad_flat, params, moment, second, average):
    first_new = beta_first * moment + (1.0 - beta_first) * grad_flat
    second_new = beta_second * second + (1.0 - beta_second) * grad_flat * grad_flat
    fix_first = 1.0 - beta_first ** STEP
    fix_second = 1.0 - beta_second ** STEP
    adam_dir = first_new / fix_first / (jnp.sqrt(second_new / fix_second) + adam_eps)
    updated = params - learn_rate * (adam_dir + decay_rate * params)
    average_new = ema_rate * average + (1.0 - ema_rate) * updated
    return (first_new, second_new, updated, average_new)

def reference(embeddings, cotangent, drop_masks, lengths, buckets, attn_params, attn_moment, attn_second, attn_ema, head_params, head_moment, head_second, head_ema):
    keep_masks = drop_masks.astype(jnp.float32) / keep_prob
    cotangent_f = cotangent.astype(jnp.float32)

    def wrapped(attn_weights, head_weights, embed_rows):
        return objective(attn_weights, head_weights, embed_rows, cotangent_f, keep_masks, lengths, buckets)
    total, pullback, extra = jax.vjp(wrapped, attn_params, head_params, embeddings.astype(jnp.float32), has_aux=True)
    attn_grad, head_grad, input_grad = pullback(jnp.ones_like(total))
    hidden_rows, loss_sum, valid_mask = extra
    loss = loss_sum / jnp.sum(valid_mask)
    grad_norm = jnp.sqrt(jnp.sum(attn_grad * attn_grad) + jnp.sum(head_grad * head_grad))
    clip_scale = jnp.minimum(1.0, clip_bound / grad_norm)
    attn_new = adam_step(attn_grad * clip_scale, attn_params, attn_moment, attn_second, attn_ema)
    head_new = adam_step(head_grad * clip_scale, head_params, head_moment, head_second, head_ema)
    return (hidden_rows.astype(jnp.bfloat16), input_grad, loss, grad_norm, attn_new[0], attn_new[1], attn_new[2], attn_new[3], head_new[0], head_new[1], head_new[2], head_new[3])
```

```python
import functools

import jax
import jax.numpy as jnp
from jax import lax
from jax.experimental import pallas as pl
from jax.experimental.pallas import tpu as pltpu
from jax.sharding import PartitionSpec as P

D = 768
H = 12
HD = 64
LMIN = 32
POS = 128
STEP = 5


logit_divisor = 0.05
keep_prob = 0.9
norm_eps = 1e-06
clip_bound = 0.001
beta_first = 0.5
beta_second = 0.5
learn_rate = 0.05
decay_rate = 0.01
adam_eps = 1e-08
ema_rate = 0.8
masked_scores = -1e30
highest = lax.Precision.HIGHEST


def layer_norm(tensor, gain_vec, shift_vec):
    center = tensor - jnp.mean(tensor, axis=-1, keepdims=True)
    spread = jnp.mean(center * center, axis=-1, keepdims=True)
    return center * lax.rsqrt(spread + norm_eps) * gain_vec + shift_vec


def gelu_exact(tensor):
    return 0.5 * tensor * (1.0 + jax.scipy.special.erf(tensor * 0.7071067811865476))


def unit_scale(tensor):
    return tensor * lax.rsqrt(jnp.sum(tensor * tensor, axis=-1, keepdims=True) + norm_eps)


def bucket_length(bucket_code):
    return (LMIN * jnp.where(bucket_code == 0, 1, jnp.where(bucket_code == 1, 2, 4))).astype(
        jnp.int32
    )


def plain_dot(left_op, right_op):
    return jnp.dot(left_op, right_op, preferred_element_type=jnp.float32)


def rows_dot(left_op, right_op):
    return lax.dot_general(
        left_op, right_op, (((0,), (0,)), ((), ())), preferred_element_type=jnp.float32
    )


def target_dot_terms(left_op, right_op):
    return lax.dot_general(
        left_op, right_op, (((1,), (1,)), ((), ())), preferred_element_type=jnp.float32
    )


def adam_step(grad_flat, params, moment, second, average):
    first_new = beta_first * moment + (1.0 - beta_first) * grad_flat
    second_new = beta_second * second + (1.0 - beta_second) * grad_flat * grad_flat
    fix_first = 1.0 - beta_first**STEP
    fix_second = 1.0 - beta_second**STEP
    adam_dir = first_new / fix_first / (jnp.sqrt(second_new / fix_second) + adam_eps)
    updated = params - learn_rate * (adam_dir + decay_rate * params)
    average_new = ema_rate * average + (1.0 - ema_rate) * updated
    return (first_new, second_new, updated, average_new)


LANES = 128
VMEM_CAP = 60 * 2**20
CORE, XBIT, YBIT, ZBITS = 1, 2, 4, (8, 16, 24)


def swap(value, bit):
    count = lax.axis_size("sent")
    return lax.ppermute(value, "sent", [(i, i ^ bit) for i in range(count)])


def is_grid(count, *shards):
    return count == 32 and all(2 * shard % LANES == 0 for shard in shards)


def block_rows(shard):
    return -(-(-(-shard // LANES) + 8) // 16) * 16


def first_row(device, shard):
    return (device * shard) // LANES


def pack_shard(values, device):
    shard = values.shape[0]
    rows = block_rows(shard)
    size = rows * LANES
    odd = (device * shard) % LANES != 0
    lead = jnp.where(
        odd,
        jnp.pad(values, (LANES // 2, size - shard - LANES // 2)),
        jnp.pad(values, (0, size - shard)),
    ).reshape(rows, LANES)
    offset = first_row(device, shard) % 8
    padded = jnp.pad(lead, ((8, 0), (0, 0)))
    return lax.dynamic_slice(padded, (8 - offset, 0), (rows, LANES)).astype(jnp.bfloat16)


def unpack_shard(block, device, shard):
    rows = -(-shard // LANES)
    offset = first_row(device, shard) % 8
    odd = (device * shard) % LANES != 0
    flat = lax.dynamic_slice(block, (offset, 0), (rows, LANES)).reshape(-1)
    longer = jnp.pad(flat, (0, LANES))
    return jnp.where(odd, longer[LANES // 2 : LANES // 2 + shard], flat[:shard])


def piece_slots(me):
    order = []
    for core in (0, 1):
        order += [
            (core, 0, 0, 0, 4),
            (core, 0, 1, 0, 2),
            (core, 0, 1, 2, 2),
            (core, 1, 0, 0, 2),
            (core, 1, 0, 2, 2),
            (core, 1, 1, 0, 2),
            (core, 1, 1, 2, 2),
        ]
    slots = []
    for core, y, x, z, n in order:
        slots.append([me ^ (core + 2 * x + 4 * y + 8 * (z + k)) for k in range(n)])
    return slots


def gather_pieces(block):
    zs = [block] + [swap(block, bit) for bit in ZBITS]
    low_half = jnp.stack(zs[:2])
    high_half = jnp.stack(zs[2:])
    x_low, x_high = swap(low_half, XBIT), swap(high_half, XBIT)
    y_low, y_high = swap(low_half, YBIT), swap(high_half, YBIT)
    d_low, d_high = swap(y_low, XBIT), swap(x_high, YBIT)
    own = [jnp.concatenate([low_half, high_half]), x_low, x_high, y_low, y_high, d_low, d_high]
    return own + [swap(piece, CORE) for piece in own]


def low_sum(*terms):
    total = terms[0].astype(jnp.float32)
    for term in terms[1:]:
        total = total + term.astype(jnp.float32)
    return total.astype(jnp.bfloat16)


def scatter_pieces(pieces):
    got = [swap(piece, CORE) for piece in pieces[7:]]
    own, x_low, x_high, y_low, y_high, d_low, d_high = pieces[:7]
    d_low = swap(low_sum(d_low, got[5]), XBIT)
    d_high = swap(low_sum(d_high, got[6]), YBIT)
    x_low = swap(low_sum(x_low, got[1]), XBIT)
    y_high = swap(low_sum(y_high, got[4]), YBIT)
    x_high = swap(low_sum(x_high, got[2], d_high), XBIT)
    y_low = swap(low_sum(y_low, got[3], d_low), YBIT)
    low_half = low_sum(own[:2], got[0][:2], x_low, y_low)
    high_half = low_sum(own[2:], got[0][2:], x_high, y_high)
    zs = [low_half[0], low_half[1], high_half[0], high_half[1]]
    total = zs[0].astype(jnp.float32)
    for value, bit in zip(zs[1:], ZBITS):
        total = total + swap(value, bit).astype(jnp.float32)
    return total


def unflatten_kernel(shard, cols, me_ref, *refs):
    pieces, (w_ref, v_ref), (stage, flat, sems) = refs[:14], refs[14:16], refs[16:]
    count, rows = stage.shape[0], stage.shape[1]
    me = me_ref[0]
    for piece, slots in zip(pieces, piece_slots(me)):
        for k, slot in enumerate(slots):
            pltpu.make_async_copy(piece.at[k], stage.at[slot], sems.at[slot]).start()
    flat[pl.ds(0, 8), :] = jnp.zeros((8, LANES), jnp.float32)

    def place(device, carry):
        pltpu.make_async_copy(pieces[0].at[0], stage.at[device], sems.at[device]).wait()
        at = pl.multiple_of(device * shard // LANES // 8 * 8, 8)
        before = flat[pl.ds(at, 8), :]
        flat[pl.ds(at, rows), :] = stage[device].astype(jnp.float32)
        flat[pl.ds(at, 8), :] += before
        return carry

    lax.fori_loop(0, count, place, 0)

    def gather_rows(group, carry):
        at = pl.multiple_of(group * 16, 16)
        for col in range(cols):
            rows16 = flat[pl.ds(group * 16 * cols + col, 16, stride=cols), :]
            w_ref[pl.ds(at, 16), pl.ds(col * LANES, LANES)] = rows16.astype(jnp.bfloat16)
        return carry

    lax.fori_loop(0, D // 16, gather_rows, 0)
    v_ref[...] = flat[pl.ds(D * cols, v_ref.shape[0]), :]


def unflatten(pieces, me, shard, cols):
    rows = pieces[0].shape[1]
    whole = shard * 32 // LANES
    return pl.pallas_call(
        functools.partial(unflatten_kernel, shard, cols),
        out_shape=(
            jax.ShapeDtypeStruct((D, cols * LANES), jnp.bfloat16),
            jax.ShapeDtypeStruct((whole - D * cols, LANES), jnp.float32),
        ),
        in_specs=[pl.BlockSpec(memory_space=pltpu.SMEM)] + [pl.BlockSpec(memory_space=pl.ANY)] * 14,
        out_specs=(pl.BlockSpec(memory_space=pltpu.VMEM), pl.BlockSpec(memory_space=pltpu.VMEM)),
        scratch_shapes=[
            pltpu.VMEM((32, rows, LANES), jnp.bfloat16),
            pltpu.VMEM((whole + rows, LANES), jnp.float32),
            pltpu.SemaphoreType.DMA((32,)),
        ],
        compiler_params=pltpu.CompilerParams(vmem_limit_bytes=VMEM_CAP),
    )(jnp.reshape(me, (1,)), *pieces)


def flatten_kernel(shard, widths, me_ref, *refs):
    n_in = len(widths)
    mats, v_ref = refs[:n_in], refs[n_in]
    pieces, (stage, flat, sems) = refs[n_in + 1 : n_in + 15], refs[n_in + 15 :]
    count, rows = stage.shape[0], stage.shape[1]
    cols = sum(widths)
    me = me_ref[0]

    def scatter_rows(group, carry):
        at = pl.multiple_of(group * 16, 16)
        col = 0
        for mat, width in zip(mats, widths):
            for k in range(width):
                rows16 = mat[pl.ds(at, 16), pl.ds(k * LANES, LANES)].astype(jnp.float32)
                flat[pl.ds(group * 16 * cols + col, 16, stride=cols), :] = rows16
                col += 1
        return carry

    lax.fori_loop(0, D // 16, scatter_rows, 0)
    flat[pl.ds(D * cols, v_ref.shape[0]), :] = v_ref[...]
    tail = D * cols + v_ref.shape[0]
    flat[pl.ds(tail, rows), :] = jnp.zeros((rows, LANES), jnp.float32)
    copies = []
    for piece, slots in zip(pieces, piece_slots(me)):
        for k, slot in enumerate(slots):
            at = pl.multiple_of(slot * shard // LANES // 8 * 8, 8)
            stage[slot] = flat[pl.ds(at, rows), :].astype(jnp.bfloat16)
            copy = pltpu.make_async_copy(stage.at[slot], piece.at[k], sems.at[len(copies)])
            copy.start()
            copies.append(copy)
    for copy in copies:
        copy.wait()


def flatten(mats, vec_rows, me, shard):
    rows = block_rows(shard)
    whole = shard * 32 // LANES
    widths = tuple(mat.shape[1] // LANES for mat in mats)
    counts = [len(slots) for slots in piece_slots(0)]
    return pl.pallas_call(
        functools.partial(flatten_kernel, shard, widths),
        out_shape=tuple(jax.ShapeDtypeStruct((n, rows, LANES), jnp.bfloat16) for n in counts),
        in_specs=[pl.BlockSpec(memory_space=pltpu.SMEM)]
        + [pl.BlockSpec(memory_space=pltpu.VMEM)] * (len(mats) + 1),
        out_specs=tuple(pl.BlockSpec(memory_space=pl.ANY) for _ in counts),
        scratch_shapes=[
            pltpu.VMEM((32, rows, LANES), jnp.bfloat16),
            pltpu.VMEM((whole + rows, LANES), jnp.float32),
            pltpu.SemaphoreType.DMA((32,)),
        ],
        compiler_params=pltpu.CompilerParams(vmem_limit_bytes=VMEM_CAP),
    )(jnp.reshape(me, (1,)), *mats, vec_rows)


def gather_weights(values, device, cols, vec_cols):
    shard = values.shape[0]
    count = lax.axis_size("sent")
    if is_grid(count, shard):
        pieces = gather_pieces(pack_shard(values, device))
        mats, vec_rows = unflatten(pieces, device, shard, cols)
        return mats, vec_rows.reshape(D, vec_cols)
    full = lax.all_gather(values.astype(jnp.bfloat16), "sent", axis=0, tiled=True)
    split = D * cols * LANES
    vecs = full[split:].reshape(D, vec_cols).astype(jnp.float32)
    return full[:split].reshape(D, cols * LANES), vecs


def scatter_grads(mats, vecs, device, shard):
    count = lax.axis_size("sent")
    if is_grid(count, shard):
        pieces = flatten([m.astype(jnp.bfloat16) for m in mats], vecs.reshape(-1, LANES), device, shard)
        return unpack_shard(scatter_pieces(list(pieces)), device, shard)
    flat = jnp.concatenate([jnp.concatenate(mats, axis=1).reshape(-1), vecs.reshape(-1)])
    return lax.psum_scatter(flat, "sent", scatter_dimension=0, tiled=True)


def gather_small(value, device):
    count = lax.axis_size("sent")
    if count != 32:
        return lax.all_gather(value, "sent", axis=0)
    got = jnp.stack([value, swap(value, CORE)])
    got = jnp.concatenate([got] + [swap(got, bit) for bit in (XBIT, YBIT, XBIT | YBIT)])
    got = jnp.concatenate([got] + [swap(got, bit) for bit in ZBITS])
    return jnp.take(got, jnp.arange(count) ^ device, axis=0)


def sum_small(value):
    if lax.axis_size("sent") != 32:
        return lax.psum(value, "sent")
    value = value + swap(value, CORE)
    across = [swap(value, bit) for bit in (XBIT, YBIT, XBIT | YBIT)]
    value = (value + across[0]) + (across[1] + across[2])
    along = [swap(value, bit) for bit in ZBITS]
    return (value + along[0]) + (along[1] + along[2])


def on_device(
    embeddings,
    cotangent,
    drop_masks,
    lengths,
    buckets,
    attn_params,
    attn_moment,
    attn_second,
    attn_ema,
    head_params,
    head_moment,
    head_second,
    head_ema,
):
    tok_rows = embeddings.shape[0]
    slot_count = lengths.shape[0]
    all_rows = 2 * tok_rows
    device = lax.axis_index("sent")
    attn_mats, attn_vecs = gather_weights(attn_params, device, 24, 8 + POS)
    head_mats, head_vecs = gather_weights(head_params, device, 54, 8)
    attn_vecs_low = attn_vecs.astype(jnp.bfloat16)
    w_qkv = attn_mats[:, : 3 * D]
    w_out = attn_mats[:, 3 * D :]
    w_up = head_mats[:, : 4 * D]
    w_down = head_mats[:, 4 * D : 8 * D]
    w_pool = head_mats[:, 8 * D :]
    bucket_all = bucket_length(buckets)
    slot_ids = jnp.arange(slot_count, dtype=jnp.int32)
    valid_everything = (
        (slot_ids[None, :] < (tok_rows // bucket_all)[:, None]).astype(jnp.float32).reshape(-1)
    )
    bucket_len = bucket_all[device]
    sent_count = tok_rows // bucket_len
    valid_own = (slot_ids < sent_count).astype(jnp.float32)
    row_ids = jnp.arange(tok_rows, dtype=jnp.int32)
    sentence = row_ids // bucket_len
    row_place = row_ids % bucket_len
    slot_len = jnp.sum(
        jnp.where(sentence[:, None] == slot_ids[None, :], lengths[None, :], 0), axis=1
    )
    key_ok = row_place < slot_len
    block = POS
    sent_blocks = sentence.reshape(-1, block)
    ok_blocks = key_ok.reshape(-1, block)
    allowed = (sent_blocks[:, :, None] == sent_blocks[:, None, :]) & ok_blocks[:, None, :]
    allowed = jnp.concatenate([allowed, allowed], axis=0)[:, None]
    place_hot = (row_place[:, None] == jnp.arange(POS, dtype=jnp.int32)[None, :]).astype(
        jnp.bfloat16
    )
    pos_rows = plain_dot(place_hot, attn_vecs_low[:, 8:].T)
    emb_rows = embeddings.astype(jnp.float32) + pos_rows + attn_vecs[:, 7]
    normed, emb_back = jax.vjp(layer_norm, emb_rows, attn_vecs[:, 5], attn_vecs[:, 6])
    keep_masks = drop_masks.astype(jnp.float32) / keep_prob
    keep_attn = keep_masks[:, 1].reshape(all_rows, D)
    keep_ffn = keep_masks[:, 2].reshape(all_rows, D)
    attn_in = (normed[None] * keep_masks[:, 0]).reshape(all_rows, D)
    attn_in_low = attn_in.astype(jnp.bfloat16)
    qkv_bias = jnp.concatenate([attn_vecs[:, 0], jnp.zeros((D,), jnp.float32), attn_vecs[:, 1]])
    qkv_low = (plain_dot(attn_in_low, w_qkv) + qkv_bias).astype(jnp.bfloat16)
    head_split = qkv_low.reshape(-1, block, 3, H, HD)
    queries = head_split[:, :, 0]
    keys_low = head_split[:, :, 1]
    values_low = head_split[:, :, 2]
    score_scale = HD ** (-0.5)
    raw_scores = jnp.einsum(
        "bqhd,bkhd->bhqk", queries, keys_low, preferred_element_type=jnp.float32
    )
    scores = jnp.where(allowed, raw_scores * score_scale, masked_scores)
    row_top = jnp.max(scores, axis=-1, keepdims=True)
    expo_vals = jnp.exp(scores - row_top)
    row_total = jnp.sum(expo_vals, axis=-1, keepdims=True)
    attn_probs = expo_vals / row_total
    score_lse = row_top + jnp.log(row_total)
    mixed_out = jnp.einsum(
        "bhqk,bkhd->bqhd",
        attn_probs.astype(jnp.bfloat16),
        values_low,
        preferred_element_type=jnp.float32,
    )
    mixed_low = mixed_out.reshape(all_rows, D).astype(jnp.bfloat16)
    branch = plain_dot(mixed_low, w_out) + attn_vecs[:, 2]
    first_res = attn_in + keep_attn * branch
    first_norm, first_back = jax.vjp(layer_norm, first_res, attn_vecs[:, 3], attn_vecs[:, 4])
    first_low = first_norm.astype(jnp.bfloat16)
    up_bias = head_vecs[:, :4].T.reshape(4 * D)
    up_pre = plain_dot(first_low, w_up) + up_bias
    active, gelu_back = jax.vjp(gelu_exact, up_pre)
    active_low = active.astype(jnp.bfloat16)
    down_out = target_dot_terms(active_low, w_down) + head_vecs[:, 4]
    second_res = first_norm + keep_ffn * down_out
    second_norm, second_back = jax.vjp(layer_norm, second_res, head_vecs[:, 5], head_vecs[:, 6])
    hidden_out = second_norm.astype(jnp.bfloat16).reshape(2, tok_rows, D)
    cls_pick = jnp.minimum(slot_ids, sent_count - 1) * bucket_len
    cls_rows = jnp.take(second_norm.reshape(2, tok_rows, D), cls_pick, axis=1).reshape(
        2 * slot_count, D
    )
    cls_low = cls_rows.astype(jnp.bfloat16)
    pooled = jnp.tanh(plain_dot(cls_low, w_pool) + head_vecs[:, 7])
    unit_rows, unit_back = jax.vjp(unit_scale, pooled)
    unit_low = unit_rows.astype(jnp.bfloat16)
    units = gather_small(unit_low, device)
    anchors = units[:, :slot_count].reshape(-1, D)
    partners = units[:, slot_count:].reshape(-1, D)
    slots_all = anchors.shape[0]
    cosine_logit_table = jnp.where(
        valid_everything[None, :] > 0,
        target_dot_terms(anchors, partners) / logit_divisor,
        masked_scores,
    )
    diagonal = jnp.arange(slots_all)[:, None] == jnp.arange(slots_all)[None, :]
    sim_top = jnp.max(cosine_logit_table, axis=-1, keepdims=True)
    row_lse = sim_top + jnp.log(
        jnp.sum(jnp.exp(cosine_logit_table - sim_top), axis=-1, keepdims=True)
    )
    positive = jnp.sum(jnp.where(diagonal, cosine_logit_table, 0.0), axis=-1)
    loss_sum = jnp.sum(valid_everything * (row_lse[:, 0] - positive))
    sim_low = (
        valid_everything[:, None]
        * (jnp.exp(cosine_logit_table - row_lse) - diagonal.astype(jnp.float32))
        / logit_divisor
    ).astype(jnp.bfloat16)
    d_anchor = lax.dynamic_slice(
        plain_dot(sim_low, partners), (device * slot_count, 0), (slot_count, D)
    )
    d_partner = lax.dynamic_slice(
        rows_dot(sim_low, anchors), (device * slot_count, 0), (slot_count, D)
    )
    d_unit = jnp.concatenate([d_anchor, d_partner], axis=0)
    d_pooled = unit_back(d_unit)[0]
    d_pool_pre = d_pooled * (1.0 - pooled * pooled)
    pool_low = d_pool_pre.astype(jnp.bfloat16)
    g_pool = rows_dot(cls_low, pool_low)
    g_pool_bias = jnp.sum(d_pool_pre, axis=0)
    d_cls = target_dot_terms(pool_low, w_pool).reshape(2, slot_count, D)
    pick_hot = ((row_ids[None, :] == cls_pick[:, None]) & (slot_ids[:, None] < sent_count)).astype(
        jnp.float32
    )
    d_second = cotangent.astype(jnp.float32) + jnp.einsum(
        "st,vsd->vtd", pick_hot, d_cls, precision=highest
    )
    d_second_res, g_gain_two, g_shift_two = second_back(d_second.reshape(all_rows, D))
    d_down = d_second_res * keep_ffn
    g_down_bias = jnp.sum(d_down, axis=0)
    down_low = d_down.astype(jnp.bfloat16)
    g_down = rows_dot(down_low, active_low)
    d_active = plain_dot(down_low, w_down)
    d_up = gelu_back(d_active)[0]
    g_up_bias = jnp.sum(d_up, axis=0)
    up_low = d_up.astype(jnp.bfloat16)
    g_up = rows_dot(first_low, up_low)
    d_first = d_second_res + target_dot_terms(up_low, w_up)
    head_vec_grad = jnp.concatenate(
        [
            g_up_bias.reshape(4, D).T,
            jnp.stack([g_down_bias, g_gain_two, g_shift_two, g_pool_bias], axis=1),
        ],
        axis=1,
    )
    head_share = scatter_grads([g_up, g_down, g_pool], head_vec_grad, device, head_params.shape[0])
    d_first_res, g_gain_one, g_shift_one = first_back(d_first)
    d_branch = d_first_res * keep_attn
    g_out_bias = jnp.sum(d_branch, axis=0)
    branch_low = d_branch.astype(jnp.bfloat16)
    g_out = rows_dot(mixed_low, branch_low)
    d_mixed = target_dot_terms(branch_low, w_out).astype(jnp.bfloat16).reshape(-1, block, H, HD)
    again = jnp.where(
        allowed,
        jnp.einsum("bqhd,bkhd->bhqk", queries, keys_low, preferred_element_type=jnp.float32)
        * score_scale,
        masked_scores,
    )
    probs_again = jnp.exp(again - score_lse)
    d_values = jnp.einsum(
        "bhqk,bqhd->bkhd",
        probs_again.astype(jnp.bfloat16),
        d_mixed,
        preferred_element_type=jnp.float32,
    )
    d_probs = jnp.einsum("bqhd,bkhd->bhqk", d_mixed, values_low, preferred_element_type=jnp.float32)
    row_delta = jnp.sum(probs_again * d_probs, axis=-1, keepdims=True)
    score_low = (probs_again * (d_probs - row_delta) * score_scale).astype(jnp.bfloat16)
    d_queries = jnp.einsum(
        "bhqk,bkhd->bqhd", score_low, keys_low, preferred_element_type=jnp.float32
    )
    d_keys = jnp.einsum("bhqk,bqhd->bkhd", score_low, queries, preferred_element_type=jnp.float32)
    d_qkv = jnp.stack([d_queries, d_keys, d_values], axis=2).reshape(all_rows, 3 * D)
    g_q_bias = jnp.sum(d_queries.reshape(all_rows, D), axis=0)
    g_v_bias = jnp.sum(d_values.reshape(all_rows, D), axis=0)
    qkv_grad_low = d_qkv.astype(jnp.bfloat16)
    g_qkv = rows_dot(attn_in_low, qkv_grad_low)
    d_attn_in = d_first_res + target_dot_terms(qkv_grad_low, w_qkv)
    d_normed = jnp.sum(d_attn_in.reshape(2, tok_rows, D) * keep_masks[:, 0], axis=0)
    input_grad, g_gain_emb, g_shift_emb = emb_back(d_normed)
    g_type = jnp.sum(input_grad, axis=0)
    g_table = lax.dot_general(
        place_hot.astype(jnp.float32),
        input_grad,
        (((0,), (0,)), ((), ())),
        precision=highest,
        preferred_element_type=jnp.float32,
    )
    attn_vec_grad = jnp.concatenate(
        [
            jnp.stack(
                [
                    g_q_bias,
                    g_v_bias,
                    g_out_bias,
                    g_gain_one,
                    g_shift_one,
                    g_gain_emb,
                    g_shift_emb,
                    g_type,
                ],
                axis=1,
            ),
            g_table.T,
        ],
        axis=1,
    )
    attn_share = scatter_grads([g_qkv, g_out], attn_vec_grad, device, attn_params.shape[0])
    squares = jnp.sum(attn_share * attn_share) + jnp.sum(head_share * head_share)
    total_squares = sum_small(squares)
    loss = loss_sum / jnp.sum(valid_everything)
    grad_norm = jnp.sqrt(total_squares)
    clip_scale = jnp.minimum(1.0, clip_bound / grad_norm)
    attn_new = adam_step(attn_share * clip_scale, attn_params, attn_moment, attn_second, attn_ema)
    head_new = adam_step(head_share * clip_scale, head_params, head_moment, head_second, head_ema)
    return (
        hidden_out,
        input_grad,
        loss,
        grad_norm,
        attn_new[0],
        attn_new[1],
        attn_new[2],
        attn_new[3],
        head_new[0],
        head_new[1],
        head_new[2],
        head_new[3],
    )


def solution(mesh):
    in_specs = (
        P("sent", None),
        P(None, "sent", None),
        P(None, None, "sent", None),
        P("sent"),
        P(),
        P("sent"),
        P("sent"),
        P("sent"),
        P("sent"),
        P("sent"),
        P("sent"),
        P("sent"),
        P("sent"),
    )
    out_specs = (
        P(None, "sent", None),
        P("sent", None),
        P(),
        P(),
        P("sent"),
        P("sent"),
        P("sent"),
        P("sent"),
        P("sent"),
        P("sent"),
        P("sent"),
        P("sent"),
    )
    return jax.shard_map(
        on_device, mesh=mesh, in_specs=in_specs, out_specs=out_specs, check_vma=False
    )
```

```python
import functools

import jax
import jax.numpy as jnp
from jax import lax
from jax.experimental import pallas as pl
from jax.experimental.pallas import tpu as pltpu
from jax.sharding import PartitionSpec as P

D = 768
H = 12
HD = 64
LMIN = 32
POS = 128
STEP = 5


logit_divisor = 0.05
keep_prob = 0.9
norm_eps = 1e-06
clip_bound = 0.001
beta_first = 0.5
beta_second = 0.5
learn_rate = 0.05
decay_rate = 0.01
adam_eps = 1e-08
ema_rate = 0.8
masked_scores = -1e30
highest = lax.Precision.HIGHEST


def layer_norm(tensor, gain_vec, shift_vec):
    center = tensor - jnp.mean(tensor, axis=-1, keepdims=True)
    spread = jnp.mean(center * center, axis=-1, keepdims=True)
    return center * lax.rsqrt(spread + norm_eps) * gain_vec + shift_vec


def gelu_exact(tensor):
    return 0.5 * tensor * (1.0 + jax.scipy.special.erf(tensor * 0.7071067811865476))


def unit_scale(tensor):
    return tensor * lax.rsqrt(jnp.sum(tensor * tensor, axis=-1, keepdims=True) + norm_eps)


def bucket_length(bucket_code):
    return (LMIN * jnp.where(bucket_code == 0, 1, jnp.where(bucket_code == 1, 2, 4))).astype(
        jnp.int32
    )


def plain_dot(left_op, right_op):
    return jnp.dot(left_op, right_op, preferred_element_type=jnp.float32)


def rows_dot(left_op, right_op):
    return lax.dot_general(
        left_op, right_op, (((0,), (0,)), ((), ())), preferred_element_type=jnp.float32
    )


def target_dot_terms(left_op, right_op):
    return lax.dot_general(
        left_op, right_op, (((1,), (1,)), ((), ())), preferred_element_type=jnp.float32
    )


def adam_step(grad_flat, params, moment, second, average):
    first_new = beta_first * moment + (1.0 - beta_first) * grad_flat
    second_new = beta_second * second + (1.0 - beta_second) * grad_flat * grad_flat
    fix_first = 1.0 - beta_first**STEP
    fix_second = 1.0 - beta_second**STEP
    adam_dir = first_new / fix_first / (jnp.sqrt(second_new / fix_second) + adam_eps)
    updated = params - learn_rate * (adam_dir + decay_rate * params)
    average_new = ema_rate * average + (1.0 - ema_rate) * updated
    return (first_new, second_new, updated, average_new)


LANES = 128
VMEM_CAP = 60 * 2**20
CORE, XBIT, YBIT, ZBITS = 1, 2, 4, (8, 16, 24)


def swap(value, bit):
    count = lax.axis_size("sent")
    return lax.ppermute(value, "sent", [(i, i ^ bit) for i in range(count)])


def is_grid(count, *shards):
    return count == 32 and all(2 * shard % LANES == 0 for shard in shards)


def block_rows(shard):
    return -(-(-(-shard // LANES) + 8) // 16) * 16


def first_row(device, shard):
    return (device * shard) // LANES


def pack_shard(values, device):
    shard = values.shape[0]
    rows = block_rows(shard)
    size = rows * LANES
    odd = (device * shard) % LANES != 0
    lead = jnp.where(
        odd,
        jnp.pad(values, (LANES // 2, size - shard - LANES // 2)),
        jnp.pad(values, (0, size - shard)),
    ).reshape(rows, LANES)
    offset = first_row(device, shard) % 8
    padded = jnp.pad(lead, ((8, 0), (0, 0)))
    return lax.dynamic_slice(padded, (8 - offset, 0), (rows, LANES)).astype(jnp.bfloat16)


def unpack_shard(block, device, shard):
    rows = -(-shard // LANES)
    offset = first_row(device, shard) % 8
    odd = (device * shard) % LANES != 0
    flat = lax.dynamic_slice(block, (offset, 0), (rows, LANES)).reshape(-1)
    longer = jnp.pad(flat, (0, LANES))
    return jnp.where(odd, longer[LANES // 2 : LANES // 2 + shard], flat[:shard])


def piece_slots(me):
    slots = []
    for core in (0, 1):
        for across, first, n in ((0, 0, 4), (1, 0, 4), (2, 0, 4), (3, 0, 2), (3, 2, 2)):
            slots.append([me ^ (core + 2 * across + 8 * (first + k)) for k in range(n)])
    return slots


def after(value, *others):
    return lax.optimization_barrier((value, others))[0]


def gather_along(block):
    return [block] + [swap(block, bit) for bit in ZBITS]


def gather_across(line):
    x, y = swap(line, XBIT), swap(line, YBIT)
    return line, x, y


def gather_diagonal(x, y):
    return swap(y[:2], XBIT), swap(x[2:], YBIT)


def low_sum(*terms):
    total = terms[0].astype(jnp.float32)
    for term in terms[1:]:
        total = total + term.astype(jnp.float32)
    return total.astype(jnp.bfloat16)


def scatter_core(pieces):
    half = len(pieces) // 2
    got = [swap(piece, CORE) for piece in reversed(pieces[half:])][::-1]
    return [low_sum(piece, other) for piece, other in zip(pieces[:half], got)]


def scatter_diagonal(sums):
    return swap(sums[3], XBIT), swap(sums[4], YBIT)


def scatter_across(sums, diagonal):
    line, x, y = sums[:3]
    d_low, d_high = diagonal
    x = swap(jnp.concatenate([x[:2], low_sum(x[2:], d_high)]), XBIT)
    y = swap(jnp.concatenate([low_sum(y[:2], d_low), y[2:]]), YBIT)
    return x, y


def scatter_line(sums, across):
    line = low_sum(sums[0], *across)
    return [line[k] for k in range(4)]


def scatter_along(zs):
    total = zs[0].astype(jnp.float32)
    for value, bit in zip(zs[1:], ZBITS):
        total = total + swap(value, bit).astype(jnp.float32)
    return total


def unflatten_kernel(shard, cols, me_ref, *refs):
    pieces, (w_ref, v_ref), (stage, flat, sems) = refs[:10], refs[10:12], refs[12:]
    count, rows = stage.shape[0], stage.shape[1]
    me = me_ref[0]
    for piece, slots in zip(pieces, piece_slots(me)):
        for k, slot in enumerate(slots):
            pltpu.make_async_copy(piece.at[k], stage.at[slot], sems.at[slot]).start()
    flat[pl.ds(0, 8), :] = jnp.zeros((8, LANES), jnp.float32)

    def place(device, carry):
        pltpu.make_async_copy(pieces[0].at[0], stage.at[device], sems.at[device]).wait()
        at = pl.multiple_of(device * shard // LANES // 8 * 8, 8)
        before = flat[pl.ds(at, 8), :]
        flat[pl.ds(at, rows), :] = stage[device].astype(jnp.float32)
        flat[pl.ds(at, 8), :] += before
        return carry

    lax.fori_loop(0, count, place, 0)

    def gather_rows(group, carry):
        at = pl.multiple_of(group * 16, 16)
        for col in range(cols):
            rows16 = flat[pl.ds(group * 16 * cols + col, 16, stride=cols), :]
            w_ref[pl.ds(at, 16), pl.ds(col * LANES, LANES)] = rows16.astype(jnp.bfloat16)
        return carry

    lax.fori_loop(0, D // 16, gather_rows, 0)
    v_ref[...] = flat[pl.ds(D * cols, v_ref.shape[0]), :]


def unflatten(pieces, me, shard, cols):
    rows = pieces[0].shape[1]
    whole = shard * 32 // LANES
    return pl.pallas_call(
        functools.partial(unflatten_kernel, shard, cols),
        out_shape=(
            jax.ShapeDtypeStruct((D, cols * LANES), jnp.bfloat16),
            jax.ShapeDtypeStruct((whole - D * cols, LANES), jnp.float32),
        ),
        in_specs=[pl.BlockSpec(memory_space=pltpu.SMEM)] + [pl.BlockSpec(memory_space=pl.ANY)] * len(pieces),
        out_specs=(pl.BlockSpec(memory_space=pltpu.VMEM), pl.BlockSpec(memory_space=pltpu.VMEM)),
        scratch_shapes=[
            pltpu.VMEM((32, rows, LANES), jnp.bfloat16),
            pltpu.VMEM((whole + rows, LANES), jnp.float32),
            pltpu.SemaphoreType.DMA((32,)),
        ],
        compiler_params=pltpu.CompilerParams(vmem_limit_bytes=VMEM_CAP),
    )(jnp.reshape(me, (1,)), *pieces)


def flatten_kernel(shard, widths, me_ref, *refs):
    n_in = len(widths)
    mats, v_ref = refs[:n_in], refs[n_in]
    pieces, (stage, flat, sems) = refs[n_in + 1 : n_in + 11], refs[n_in + 11 :]
    count, rows = stage.shape[0], stage.shape[1]
    cols = sum(widths)
    me = me_ref[0]

    def scatter_rows(group, carry):
        at = pl.multiple_of(group * 16, 16)
        col = 0
        for mat, width in zip(mats, widths):
            for k in range(width):
                rows16 = mat[pl.ds(at, 16), pl.ds(k * LANES, LANES)].astype(jnp.float32)
                flat[pl.ds(group * 16 * cols + col, 16, stride=cols), :] = rows16
                col += 1
        return carry

    lax.fori_loop(0, D // 16, scatter_rows, 0)
    flat[pl.ds(D * cols, v_ref.shape[0]), :] = v_ref[...]
    tail = D * cols + v_ref.shape[0]
    flat[pl.ds(tail, rows), :] = jnp.zeros((rows, LANES), jnp.float32)
    copies = []
    for piece, slots in zip(pieces, piece_slots(me)):
        for k, slot in enumerate(slots):
            at = pl.multiple_of(slot * shard // LANES // 8 * 8, 8)
            stage[slot] = flat[pl.ds(at, rows), :].astype(jnp.bfloat16)
            copy = pltpu.make_async_copy(stage.at[slot], piece.at[k], sems.at[len(copies)])
            copy.start()
            copies.append(copy)
    for copy in copies:
        copy.wait()


def flatten(mats, vec_rows, me, shard):
    rows = block_rows(shard)
    whole = shard * 32 // LANES
    widths = tuple(mat.shape[1] // LANES for mat in mats)
    counts = [len(slots) for slots in piece_slots(0)]
    return pl.pallas_call(
        functools.partial(flatten_kernel, shard, widths),
        out_shape=tuple(jax.ShapeDtypeStruct((n, rows, LANES), jnp.bfloat16) for n in counts),
        in_specs=[pl.BlockSpec(memory_space=pltpu.SMEM)]
        + [pl.BlockSpec(memory_space=pltpu.VMEM)] * (len(mats) + 1),
        out_specs=tuple(pl.BlockSpec(memory_space=pl.ANY) for _ in counts),
        scratch_shapes=[
            pltpu.VMEM((32, rows, LANES), jnp.bfloat16),
            pltpu.VMEM((whole + rows, LANES), jnp.float32),
            pltpu.SemaphoreType.DMA((32,)),
        ],
        compiler_params=pltpu.CompilerParams(vmem_limit_bytes=VMEM_CAP),
    )(jnp.reshape(me, (1,)), *mats, vec_rows)


def gather_weights(attn_values, head_values, device):
    shards = (attn_values.shape[0], head_values.shape[0])
    if is_grid(lax.axis_size("sent"), *shards):
        attn_zs = gather_along(pack_shard(attn_values, device))
        head_block = after(pack_shard(head_values, device), attn_zs[1])
        attn_line, attn_x, attn_y = gather_across(jnp.stack(attn_zs))
        head_zs = gather_along(head_block)
        attn_diagonal = gather_diagonal(attn_x, attn_y)
        attn_own = (attn_line, attn_x, attn_y) + attn_diagonal
        attn_pieces = attn_own + tuple(swap(piece, CORE) for piece in attn_own)
        head_line, _ = lax.optimization_barrier((jnp.stack(head_zs), attn_diagonal))
        head_line, head_x, head_y = gather_across(head_line)
        head_own = (head_line, head_x, head_y) + gather_diagonal(head_x, head_y)
        head_pieces = head_own + tuple(swap(piece, CORE) for piece in head_own)
        attn_mats, attn_rows = unflatten(attn_pieces, device, shards[0], 24)
        head_mats, head_rows = unflatten(head_pieces, device, shards[1], 54)
        return attn_mats, attn_rows.reshape(D, 8 + POS), head_mats, head_rows.reshape(D, 8)
    found = []
    for values, cols, vec_cols in ((attn_values, 24, 8 + POS), (head_values, 54, 8)):
        full = lax.all_gather(values.astype(jnp.bfloat16), "sent", axis=0, tiled=True)
        split = D * cols * LANES
        found.append(full[:split].reshape(D, cols * LANES))
        found.append(full[split:].reshape(D, vec_cols).astype(jnp.float32))
    return tuple(found)


def gather_small(value, device):
    count = lax.axis_size("sent")
    if count != 32:
        return lax.all_gather(value, "sent", axis=0)
    got = jnp.stack([value] + [swap(value, bit) for bit in ZBITS])
    got = jnp.stack([got] + [swap(got, bit) for bit in (XBIT, YBIT, XBIT | YBIT)])
    got = jnp.stack([got, swap(got, CORE)])
    got = jnp.transpose(got, (2, 1, 0, 3, 4)).reshape((count,) + value.shape)
    return jnp.take(got, jnp.arange(count) ^ device, axis=0)


def scatter_flat(mats, vecs):
    flat = jnp.concatenate([jnp.concatenate(mats, axis=1).reshape(-1), vecs.reshape(-1)])
    return lax.psum_scatter(flat, "sent", scatter_dimension=0, tiled=True)


def sum_small(value):
    if lax.axis_size("sent") != 32:
        return lax.psum(value, "sent")
    value = value + swap(value, CORE)
    across = [swap(value, bit) for bit in (XBIT, YBIT, XBIT | YBIT)]
    value = (value + across[0]) + (across[1] + across[2])
    along = [swap(value, bit) for bit in ZBITS]
    return (value + along[0]) + (along[1] + along[2])


def on_device(
    embeddings,
    cotangent,
    drop_masks,
    lengths,
    buckets,
    attn_params,
    attn_moment,
    attn_second,
    attn_ema,
    head_params,
    head_moment,
    head_second,
    head_ema,
):
    tok_rows = embeddings.shape[0]
    slot_count = lengths.shape[0]
    all_rows = 2 * tok_rows
    device = lax.axis_index("sent")
    attn_mats, attn_vecs, head_mats, head_vecs = gather_weights(attn_params, head_params, device)
    attn_vecs_low = attn_vecs.astype(jnp.bfloat16)
    w_qkv = attn_mats[:, : 3 * D]
    w_out = attn_mats[:, 3 * D :]
    w_up = head_mats[:, : 4 * D]
    w_down = head_mats[:, 4 * D : 8 * D]
    w_pool = head_mats[:, 8 * D :]
    bucket_all = bucket_length(buckets)
    slot_ids = jnp.arange(slot_count, dtype=jnp.int32)
    valid_everything = (
        (slot_ids[None, :] < (tok_rows // bucket_all)[:, None]).astype(jnp.float32).reshape(-1)
    )
    bucket_len = bucket_all[device]
    sent_count = tok_rows // bucket_len
    valid_own = (slot_ids < sent_count).astype(jnp.float32)
    row_ids = jnp.arange(tok_rows, dtype=jnp.int32)
    sentence = row_ids // bucket_len
    row_place = row_ids % bucket_len
    slot_len = jnp.sum(
        jnp.where(sentence[:, None] == slot_ids[None, :], lengths[None, :], 0), axis=1
    )
    key_ok = row_place < slot_len
    block = POS
    sent_blocks = sentence.reshape(-1, block)
    ok_blocks = key_ok.reshape(-1, block)
    allowed = (sent_blocks[:, :, None] == sent_blocks[:, None, :]) & ok_blocks[:, None, :]
    allowed = jnp.concatenate([allowed, allowed], axis=0)[:, None]
    place_hot = (row_place[:, None] == jnp.arange(POS, dtype=jnp.int32)[None, :]).astype(
        jnp.bfloat16
    )
    pos_rows = plain_dot(place_hot, attn_vecs_low[:, 8:].T)
    emb_rows = embeddings.astype(jnp.float32) + pos_rows + attn_vecs[:, 7]
    normed, emb_back = jax.vjp(layer_norm, emb_rows, attn_vecs[:, 5], attn_vecs[:, 6])
    keep_masks = drop_masks.astype(jnp.float32) / keep_prob
    keep_attn = keep_masks[:, 1].reshape(all_rows, D)
    keep_ffn = keep_masks[:, 2].reshape(all_rows, D)
    attn_in = (normed[None] * keep_masks[:, 0]).reshape(all_rows, D)
    attn_in_low = attn_in.astype(jnp.bfloat16)
    qkv_bias = jnp.concatenate([attn_vecs[:, 0], jnp.zeros((D,), jnp.float32), attn_vecs[:, 1]])
    qkv_low = (plain_dot(attn_in_low, w_qkv) + qkv_bias).astype(jnp.bfloat16)
    head_split = qkv_low.reshape(-1, block, 3, H, HD)
    queries = head_split[:, :, 0]
    keys_low = head_split[:, :, 1]
    values_low = head_split[:, :, 2]
    score_scale = HD ** (-0.5)
    raw_scores = jnp.einsum(
        "bqhd,bkhd->bhqk", queries, keys_low, preferred_element_type=jnp.float32
    )
    scores = jnp.where(allowed, raw_scores * score_scale, masked_scores)
    row_top = jnp.max(scores, axis=-1, keepdims=True)
    expo_vals = jnp.exp(scores - row_top)
    row_total = jnp.sum(expo_vals, axis=-1, keepdims=True)
    attn_probs = expo_vals / row_total
    score_lse = row_top + jnp.log(row_total)
    mixed_out = jnp.einsum(
        "bhqk,bkhd->bqhd",
        attn_probs.astype(jnp.bfloat16),
        values_low,
        preferred_element_type=jnp.float32,
    )
    mixed_low = mixed_out.reshape(all_rows, D).astype(jnp.bfloat16)
    branch = plain_dot(mixed_low, w_out) + attn_vecs[:, 2]
    first_res = attn_in + keep_attn * branch
    first_norm, first_back = jax.vjp(layer_norm, first_res, attn_vecs[:, 3], attn_vecs[:, 4])
    first_low = first_norm.astype(jnp.bfloat16)
    up_bias = head_vecs[:, :4].T.reshape(4 * D)
    up_pre = plain_dot(first_low, w_up) + up_bias
    active, gelu_back = jax.vjp(gelu_exact, up_pre)
    active_low = active.astype(jnp.bfloat16)
    down_out = target_dot_terms(active_low, w_down) + head_vecs[:, 4]
    second_res = first_norm + keep_ffn * down_out
    second_norm, second_back = jax.vjp(layer_norm, second_res, head_vecs[:, 5], head_vecs[:, 6])
    hidden_out = second_norm.astype(jnp.bfloat16).reshape(2, tok_rows, D)
    cls_pick = jnp.minimum(slot_ids, sent_count - 1) * bucket_len
    cls_rows = jnp.take(second_norm.reshape(2, tok_rows, D), cls_pick, axis=1).reshape(
        2 * slot_count, D
    )
    cls_low = cls_rows.astype(jnp.bfloat16)
    pooled = jnp.tanh(plain_dot(cls_low, w_pool) + head_vecs[:, 7])
    unit_rows, unit_back = jax.vjp(unit_scale, pooled)
    unit_low = unit_rows.astype(jnp.bfloat16)
    units = gather_small(unit_low, device)
    anchors = units[:, :slot_count].reshape(-1, D)
    partners = units[:, slot_count:].reshape(-1, D)
    slots_all = anchors.shape[0]
    cosine_logit_table = jnp.where(
        valid_everything[None, :] > 0,
        target_dot_terms(anchors, partners) / logit_divisor,
        masked_scores,
    )
    diagonal = jnp.arange(slots_all)[:, None] == jnp.arange(slots_all)[None, :]
    sim_top = jnp.max(cosine_logit_table, axis=-1, keepdims=True)
    row_lse = sim_top + jnp.log(
        jnp.sum(jnp.exp(cosine_logit_table - sim_top), axis=-1, keepdims=True)
    )
    positive = jnp.sum(jnp.where(diagonal, cosine_logit_table, 0.0), axis=-1)
    loss_sum = jnp.sum(valid_everything * (row_lse[:, 0] - positive))
    sim_low = (
        valid_everything[:, None]
        * (jnp.exp(cosine_logit_table - row_lse) - diagonal.astype(jnp.float32))
        / logit_divisor
    ).astype(jnp.bfloat16)
    d_anchor = lax.dynamic_slice(
        plain_dot(sim_low, partners), (device * slot_count, 0), (slot_count, D)
    )
    d_partner = lax.dynamic_slice(
        rows_dot(sim_low, anchors), (device * slot_count, 0), (slot_count, D)
    )
    d_unit = jnp.concatenate([d_anchor, d_partner], axis=0)
    d_pooled = unit_back(d_unit)[0]
    d_pool_pre = d_pooled * (1.0 - pooled * pooled)
    pool_low = d_pool_pre.astype(jnp.bfloat16)
    g_pool = rows_dot(cls_low, pool_low)
    g_pool_bias = jnp.sum(d_pool_pre, axis=0)
    d_cls = target_dot_terms(pool_low, w_pool).reshape(2, slot_count, D)
    pick_hot = ((row_ids[None, :] == cls_pick[:, None]) & (slot_ids[:, None] < sent_count)).astype(
        jnp.float32
    )
    d_second = cotangent.astype(jnp.float32) + jnp.einsum(
        "st,vsd->vtd", pick_hot, d_cls, precision=highest
    )
    d_second_res, g_gain_two, g_shift_two = second_back(d_second.reshape(all_rows, D))
    d_down = d_second_res * keep_ffn
    g_down_bias = jnp.sum(d_down, axis=0)
    down_low = d_down.astype(jnp.bfloat16)
    g_down = rows_dot(down_low, active_low)
    d_active = plain_dot(down_low, w_down)
    d_up = gelu_back(d_active)[0]
    g_up_bias = jnp.sum(d_up, axis=0)
    up_low = d_up.astype(jnp.bfloat16)
    g_up = rows_dot(first_low, up_low)
    d_first = d_second_res + target_dot_terms(up_low, w_up)
    head_vec_grad = jnp.concatenate(
        [
            g_up_bias.reshape(4, D).T,
            jnp.stack([g_down_bias, g_gain_two, g_shift_two, g_pool_bias], axis=1),
        ],
        axis=1,
    )
    shards = (attn_params.shape[0], head_params.shape[0])
    on_grid = is_grid(lax.axis_size("sent"), *shards)
    head_mat_grads = [g_up, g_down, g_pool]
    if on_grid:
        head_pieces = flatten(
            [m.astype(jnp.bfloat16) for m in head_mat_grads],
            head_vec_grad.reshape(-1, LANES),
            device,
            shards[1],
        )
        d_first, head_pieces = lax.optimization_barrier((d_first, head_pieces))
        head_sums = scatter_core(head_pieces)
    else:
        head_share = scatter_flat(head_mat_grads, head_vec_grad)
    d_first_res, g_gain_one, g_shift_one = first_back(d_first)
    d_branch = d_first_res * keep_attn
    g_out_bias = jnp.sum(d_branch, axis=0)
    branch_low = d_branch.astype(jnp.bfloat16)
    g_out = rows_dot(mixed_low, branch_low)
    d_mixed = target_dot_terms(branch_low, w_out).astype(jnp.bfloat16).reshape(-1, block, H, HD)
    if on_grid:
        d_mixed, head_sums = lax.optimization_barrier((d_mixed, head_sums))
        head_diagonal = scatter_diagonal(head_sums)
    again = jnp.where(
        allowed,
        jnp.einsum("bqhd,bkhd->bhqk", queries, keys_low, preferred_element_type=jnp.float32)
        * score_scale,
        masked_scores,
    )
    probs_again = jnp.exp(again - score_lse)
    d_values = jnp.einsum(
        "bhqk,bqhd->bkhd",
        probs_again.astype(jnp.bfloat16),
        d_mixed,
        preferred_element_type=jnp.float32,
    )
    d_probs = jnp.einsum("bqhd,bkhd->bhqk", d_mixed, values_low, preferred_element_type=jnp.float32)
    row_delta = jnp.sum(probs_again * d_probs, axis=-1, keepdims=True)
    score_low = (probs_again * (d_probs - row_delta) * score_scale).astype(jnp.bfloat16)
    d_queries = jnp.einsum(
        "bhqk,bkhd->bqhd", score_low, keys_low, preferred_element_type=jnp.float32
    )
    d_keys = jnp.einsum("bhqk,bqhd->bkhd", score_low, queries, preferred_element_type=jnp.float32)
    d_qkv = jnp.stack([d_queries, d_keys, d_values], axis=2).reshape(all_rows, 3 * D)
    g_q_bias = jnp.sum(d_queries.reshape(all_rows, D), axis=0)
    g_v_bias = jnp.sum(d_values.reshape(all_rows, D), axis=0)
    qkv_grad_low = d_qkv.astype(jnp.bfloat16)
    if on_grid:
        qkv_grad_low, head_diagonal = lax.optimization_barrier((qkv_grad_low, head_diagonal))
        head_across = scatter_across(head_sums, head_diagonal)
    g_qkv = rows_dot(attn_in_low, qkv_grad_low)
    d_attn_in = d_first_res + target_dot_terms(qkv_grad_low, w_qkv)
    d_normed = jnp.sum(d_attn_in.reshape(2, tok_rows, D) * keep_masks[:, 0], axis=0)
    input_grad, g_gain_emb, g_shift_emb = emb_back(d_normed)
    g_type = jnp.sum(input_grad, axis=0)
    g_table = lax.dot_general(
        place_hot.astype(jnp.float32),
        input_grad,
        (((0,), (0,)), ((), ())),
        precision=highest,
        preferred_element_type=jnp.float32,
    )
    attn_vec_grad = jnp.concatenate(
        [
            jnp.stack(
                [
                    g_q_bias,
                    g_v_bias,
                    g_out_bias,
                    g_gain_one,
                    g_shift_one,
                    g_gain_emb,
                    g_shift_emb,
                    g_type,
                ],
                axis=1,
            ),
            g_table.T,
        ],
        axis=1,
    )
    attn_mat_grads = [g_qkv, g_out]
    if on_grid:
        attn_pieces = flatten(
            [m.astype(jnp.bfloat16) for m in attn_mat_grads],
            attn_vec_grad.reshape(-1, LANES),
            device,
            shards[0],
        )
        attn_pieces, head_across = lax.optimization_barrier((attn_pieces, head_across))
        head_zs = scatter_line(head_sums, head_across)
        attn_sums = scatter_core(attn_pieces)
        attn_diagonal = scatter_diagonal(attn_sums)
        attn_zs = scatter_line(attn_sums, scatter_across(attn_sums, attn_diagonal))
        head_share = unpack_shard(scatter_along(head_zs), device, shards[1])
        attn_share = unpack_shard(scatter_along(attn_zs), device, shards[0])
    else:
        attn_share = scatter_flat(attn_mat_grads, attn_vec_grad)
    squares = jnp.sum(attn_share * attn_share) + jnp.sum(head_share * head_share)
    total_squares = sum_small(squares)
    loss = loss_sum / jnp.sum(valid_everything)
    grad_norm = jnp.sqrt(total_squares)
    clip_scale = jnp.minimum(1.0, clip_bound / grad_norm)
    attn_new = adam_step(attn_share * clip_scale, attn_params, attn_moment, attn_second, attn_ema)
    head_new = adam_step(head_share * clip_scale, head_params, head_moment, head_second, head_ema)
    return (
        hidden_out,
        input_grad,
        loss,
        grad_norm,
        attn_new[0],
        attn_new[1],
        attn_new[2],
        attn_new[3],
        head_new[0],
        head_new[1],
        head_new[2],
        head_new[3],
    )


def solution(mesh):
    in_specs = (
        P("sent", None),
        P(None, "sent", None),
        P(None, None, "sent", None),
        P("sent"),
        P(),
        P("sent"),
        P("sent"),
        P("sent"),
        P("sent"),
        P("sent"),
        P("sent"),
        P("sent"),
        P("sent"),
    )
    out_specs = (
        P(None, "sent", None),
        P("sent", None),
        P(),
        P(),
        P("sent"),
        P("sent"),
        P("sent"),
        P("sent"),
        P("sent"),
        P("sent"),
        P("sent"),
        P("sent"),
    )
    return jax.shard_map(
        on_device, mesh=mesh, in_specs=in_specs, out_specs=out_specs, check_vma=False
    )
```

```python
import functools

import jax
import jax.numpy as jnp
from jax import lax
from jax.experimental import pallas as pl
from jax.experimental.pallas import tpu as pltpu
from jax.sharding import PartitionSpec as P

D = 768
H = 12
HD = 64
LMIN = 32
POS = 128
STEP = 5


logit_divisor = 0.05
keep_prob = 0.9
norm_eps = 1e-06
clip_bound = 0.001
beta_first = 0.5
beta_second = 0.5
learn_rate = 0.05
decay_rate = 0.01
adam_eps = 1e-08
ema_rate = 0.8
masked_scores = -1e30
highest = lax.Precision.HIGHEST


def layer_norm(tensor, gain_vec, shift_vec):
    center = tensor - jnp.mean(tensor, axis=-1, keepdims=True)
    spread = jnp.mean(center * center, axis=-1, keepdims=True)
    return center * lax.rsqrt(spread + norm_eps) * gain_vec + shift_vec


def gelu_exact(tensor):
    return 0.5 * tensor * (1.0 + jax.scipy.special.erf(tensor * 0.7071067811865476))


def unit_scale(tensor):
    return tensor * lax.rsqrt(jnp.sum(tensor * tensor, axis=-1, keepdims=True) + norm_eps)


def bucket_length(bucket_code):
    return (LMIN * jnp.where(bucket_code == 0, 1, jnp.where(bucket_code == 1, 2, 4))).astype(
        jnp.int32
    )


def plain_dot(left_op, right_op):
    return jnp.dot(left_op, right_op, preferred_element_type=jnp.float32)


def rows_dot(left_op, right_op):
    return lax.dot_general(
        left_op, right_op, (((0,), (0,)), ((), ())), preferred_element_type=jnp.float32
    )


def target_dot_terms(left_op, right_op):
    return lax.dot_general(
        left_op, right_op, (((1,), (1,)), ((), ())), preferred_element_type=jnp.float32
    )


def adam_step(grad_flat, params, moment, second, average):
    first_new = beta_first * moment + (1.0 - beta_first) * grad_flat
    second_new = beta_second * second + (1.0 - beta_second) * grad_flat * grad_flat
    fix_first = 1.0 - beta_first**STEP
    fix_second = 1.0 - beta_second**STEP
    adam_dir = first_new / fix_first / (jnp.sqrt(second_new / fix_second) + adam_eps)
    updated = params - learn_rate * (adam_dir + decay_rate * params)
    average_new = ema_rate * average + (1.0 - ema_rate) * updated
    return (first_new, second_new, updated, average_new)


LANES = 128
VMEM_CAP = 60 * 2**20
CORE, XBIT, YBIT, ZBITS = 1, 2, 4, (8, 16, 24)


def swap(value, bit):
    count = lax.axis_size("sent")
    return lax.ppermute(value, "sent", [(i, i ^ bit) for i in range(count)])


def is_grid(count, *shards):
    return count == 32 and all(2 * shard % LANES == 0 for shard in shards)


def block_rows(shard):
    return -(-(-(-shard // LANES) + 8) // 16) * 16


def first_row(device, shard):
    return (device * shard) // LANES


def pack_shard(values, device):
    shard = values.shape[0]
    rows = block_rows(shard)
    size = rows * LANES
    odd = (device * shard) % LANES != 0
    lead = jnp.where(
        odd,
        jnp.pad(values, (LANES // 2, size - shard - LANES // 2)),
        jnp.pad(values, (0, size - shard)),
    ).reshape(rows, LANES)
    offset = first_row(device, shard) % 8
    padded = jnp.pad(lead, ((8, 0), (0, 0)))
    return lax.dynamic_slice(padded, (8 - offset, 0), (rows, LANES)).astype(jnp.bfloat16)


def unpack_shard(block, device, shard):
    rows = -(-shard // LANES)
    offset = first_row(device, shard) % 8
    odd = (device * shard) % LANES != 0
    flat = lax.dynamic_slice(block, (offset, 0), (rows, LANES)).reshape(-1)
    longer = jnp.pad(flat, (0, LANES))
    return jnp.where(odd, longer[LANES // 2 : LANES // 2 + shard], flat[:shard])


def piece_slots(me):
    slots = []
    for core in (0, 1):
        for across, first, n in ((0, 0, 4), (1, 0, 4), (2, 0, 4), (3, 0, 2), (3, 2, 2)):
            slots.append([me ^ (core + 2 * across + 8 * (first + k)) for k in range(n)])
    return slots


def after(value, *others):
    return lax.optimization_barrier((value, others))[0]


def gather_along(block):
    return [block] + [swap(block, bit) for bit in ZBITS]


def gather_across(line):
    x, y = swap(line, XBIT), swap(line, YBIT)
    return line, x, y


def gather_diagonal(x, y):
    return swap(y[:2], XBIT), swap(x[2:], YBIT)


def low_sum(*terms):
    total = terms[0].astype(jnp.float32)
    for term in terms[1:]:
        total = total + term.astype(jnp.float32)
    return total.astype(jnp.bfloat16)


def scatter_core(pieces):
    half = len(pieces) // 2
    got = [swap(piece, CORE) for piece in reversed(pieces[half:])][::-1]
    return [low_sum(piece, other) for piece, other in zip(pieces[:half], got)]


def scatter_diagonal(sums):
    return swap(sums[3], XBIT), swap(sums[4], YBIT)


def scatter_across(sums, diagonal):
    line, x, y = sums[:3]
    d_low, d_high = diagonal
    x = swap(jnp.concatenate([x[:2], low_sum(x[2:], d_high)]), XBIT)
    y = swap(jnp.concatenate([low_sum(y[:2], d_low), y[2:]]), YBIT)
    return x, y


def scatter_line(sums, across):
    line = low_sum(sums[0], *across)
    return [line[k] for k in range(4)]


def scatter_along(zs):
    total = zs[0].astype(jnp.float32)
    for value, bit in zip(zs[1:], ZBITS):
        total = total + swap(value, bit).astype(jnp.float32)
    return total


def plain_rows(left, right, dims):
    return lax.dot_general(left, right, (dims, ((), ())), preferred_element_type=jnp.float32)


NN, NT, TN = ((1,), (0,)), ((1,), (1,)), ((0,), (0,))


def one_hot(shape, left, right):
    rows = lax.broadcasted_iota(jnp.int32, shape, 0)
    cols = lax.broadcasted_iota(jnp.int32, shape, 1)
    return jnp.where(left(rows, cols) == right(rows, cols), 1.0, 0.0)


def vectors_of(flat_rows):
    spread = one_hot((D, 48), lambda r, c: r >> 4, lambda r, c: c).astype(jnp.bfloat16)
    rows = plain_rows(spread, flat_rows.astype(jnp.bfloat16), NN)
    rows = rows * one_hot((D, LANES), lambda r, c: r & 15, lambda r, c: c >> 3)
    fold = one_hot((8, LANES), lambda r, c: r, lambda r, c: c & 7).astype(jnp.bfloat16)
    return plain_rows(fold, rows.astype(jnp.bfloat16), NT)


def flat_of(vectors):
    fold = one_hot((8, LANES), lambda r, c: r, lambda r, c: c & 7).astype(jnp.bfloat16)
    rows = plain_rows(vectors.astype(jnp.bfloat16), fold, TN)
    rows = rows * one_hot((D, LANES), lambda r, c: r & 15, lambda r, c: c >> 3)
    spread = one_hot((D, 48), lambda r, c: r >> 4, lambda r, c: c).astype(jnp.bfloat16)
    return plain_rows(spread, rows.astype(jnp.bfloat16), TN)


def keep_of(mask):
    return mask.astype(jnp.float32) * (1.0 / keep_prob)


def place_blocks(shard, pieces, me, stage, flat, sems):
    count, rows = stage.shape[0], stage.shape[1]
    for piece, slots in zip(pieces, piece_slots(me)):
        for k, slot in enumerate(slots):
            pltpu.make_async_copy(piece.at[k], stage.at[slot], sems.at[slot]).start()
    flat[pl.ds(0, 8), :] = jnp.zeros((8, LANES), jnp.float32)

    def place(device, carry):
        pltpu.make_async_copy(pieces[0].at[0], stage.at[device], sems.at[device]).wait()
        at = pl.multiple_of(device * shard // LANES // 8 * 8, 8)
        before = flat[pl.ds(at, 8), :]
        flat[pl.ds(at, rows), :] = stage[device].astype(jnp.float32)
        flat[pl.ds(at, 8), :] += before
        return carry

    lax.fori_loop(0, count, place, 0)


def gather_matrix(flat, w_ref, w_out, out_sems):
    cols = w_ref.shape[1] // LANES

    def gather_rows(group, carry):
        at = pl.multiple_of(group * 16, 16)
        for col in range(cols):
            rows16 = flat[pl.ds(group * 16 * cols + col, 16, stride=cols), :]
            w_ref[pl.ds(at, 16), pl.ds(col * LANES, LANES)] = rows16.astype(jnp.bfloat16)
        return carry

    parts = 4
    span = D // parts
    copies = []
    for part in range(parts):
        lax.fori_loop(part * span // 16, (part + 1) * span // 16, gather_rows, 0)
        here = pl.ds(part * span, span)
        copies.append(pltpu.make_async_copy(w_ref.at[here], w_out.at[here], out_sems.at[part]))
        copies[-1].start()
    return copies


VEC = 8 + POS


def table_of(flat, base, body, tail):
    lane = lax.broadcasted_iota(jnp.int32, (D // 16, LANES), 1)
    for q in range(16):
        here = flat[pl.ds(base + q, D // 16, stride=17), :]
        later = flat[pl.ds(base + q + 1, D // 16, stride=17), :]
        both = jnp.where(lane >= 8 * q, here, later)
        shift = (LANES - 8 * q) % LANES
        body[pl.ds(q, D // 16, stride=16), :] = pltpu.roll(both, shift, 1) if shift else both
        tail[pl.ds(q, D // 16, stride=16), :] = pltpu.roll(later, shift, 1) if shift else later
    return body[...].T, tail[...].T[:8]


def flat_table(flat, base, first, last, body, tail):
    body[...] = first.T
    tail[...] = jnp.concatenate([last, jnp.zeros((LANES - 8, D), jnp.float32)]).T
    lane = lax.broadcasted_iota(jnp.int32, (D // 16, LANES), 1)
    carried = None
    for q in range(17):
        row = carried
        if q < 16:
            main = body[pl.ds(q, D // 16, stride=16), :]
            end = tail[pl.ds(q, D // 16, stride=16), :]
            if q:
                main, end = pltpu.roll(main, 8 * q, 1), pltpu.roll(end, 8 * q, 1)
            row = main if carried is None else jnp.where(lane >= 8 * q, main, carried)
            carried = jnp.where(lane < 8 * q, main, end)
        flat[pl.ds(base + q, D // 16, stride=17), :] = row


def repeat_places(table, length):
    twice = jnp.concatenate([table[:64]] * 2)
    four = jnp.concatenate([table[:32]] * 4)
    return jnp.where(length == 128, table, jnp.where(length == 64, twice, four))


def fold_places(rows, length):
    half = rows[:64] + rows[64:]
    quarter = half[:32] + half[32:]
    none = jnp.zeros_like(rows)
    twice = jnp.concatenate([half, none[:64]])
    four = jnp.concatenate([quarter, none[:96]])
    return jnp.where(length == 128, rows, jnp.where(length == 64, twice, four))


def stack_heads(pair):
    lane = lax.broadcasted_iota(jnp.int32, pair.shape, 1)
    none = jnp.zeros_like(pair)
    return jnp.concatenate([jnp.where(lane < HD, pair, none), jnp.where(lane < HD, none, pair)])


def unstack_heads(rows):
    half = rows.shape[0] // 2
    lane = lax.broadcasted_iota(jnp.int32, (half, rows.shape[1]), 1)
    return jnp.where(lane < HD, rows[:half], rows[half:])


ROWS = 32


def attn_kernel(shard, me_ref, length_ref, lens_ref, *refs):
    pieces, (emb_ref, mask_hbm) = refs[:10], refs[10:12]
    (w_out, vec_ref, rows_ref, in_low_ref, qkv_ref, prob_ref, mixed_ref, res_ref, norm_ref, low_ref) = refs[12:22]
    (stage, flat, w_ref, body, tail, mask, attn_in, bias_ref, sems, out_sems, mask_sems) = refs[22:]
    me = me_ref[0]
    tokens = emb_ref.shape[0]
    masks = []
    for view in range(2):
        for which in range(2):
            at = 2 * view + which
            masks.append(pltpu.make_async_copy(mask_hbm.at[view, which], mask.at[at], mask_sems.at[at]))
            masks[-1].start()
    place_blocks(shard, pieces, me, stage, flat, sems)
    copies = gather_matrix(flat, w_ref, w_out, out_sems)
    first, last = table_of(flat, D * w_ref.shape[1] // LANES, body, tail)
    vecs = first[:8]
    vec_ref[...] = vecs
    length = length_ref[0]
    places = repeat_places(jnp.concatenate([first[8:], last]), length)
    for copy in masks:
        copy.wait()
    for block in range(tokens // LANES):
        key = lax.broadcasted_iota(jnp.int32, (LANES, LANES), 1) + block * LANES
        query = lax.broadcasted_iota(jnp.int32, (LANES, LANES), 0) + block * LANES
        shift = jnp.where(length == 128, 7, jnp.where(length == 64, 6, 5))
        sent = lax.shift_right_logical(key, jnp.full_like(key, 1) * shift)
        sent_q = lax.shift_right_logical(query, jnp.full_like(key, 1) * shift)
        real = jnp.zeros_like(key)
        for slot in range(lens_ref.shape[0]):
            real = jnp.where(sent == slot, lens_ref[slot], real)
        ok = (sent == sent_q) & ((key & (length - 1)) < real)
        bias_ref[block] = jnp.where(ok, 0.0, masked_scores)
        here = pl.ds(block * LANES, LANES)
        emb = emb_ref[here, :].astype(jnp.float32) + places + vecs[7:8]
        rows_ref[here, :] = emb
        normed = layer_norm(emb, vecs[5:6], vecs[6:7])
        for view in range(2):
            at = pl.ds(view * tokens + block * LANES, LANES)
            given = normed * keep_of(mask[2 * view, here, :])
            attn_in[at, :] = given
            in_low_ref[at, :] = given.astype(jnp.bfloat16)
    for part in range(3):
        cols = pl.ds(part * D, D)
        made = plain_rows(in_low_ref[...], w_ref[:, cols], NN)
        if part != 1:
            made = made + vecs[part // 2 : part // 2 + 1]
        qkv_ref[:, cols] = made.astype(jnp.bfloat16)

    def attend(block, carry):
        here = pl.ds(pl.multiple_of(block * LANES, LANES), LANES)
        bias = bias_ref[block & 1]
        bias = jnp.concatenate([bias, bias])
        for pair in range(H // 2):
            q = stack_heads(qkv_ref[here, pl.ds(pair * LANES, LANES)])
            k = qkv_ref[here, pl.ds(D + pair * LANES, LANES)]
            v = qkv_ref[here, pl.ds(2 * D + pair * LANES, LANES)]
            scores = plain_rows(q, k, NT) * HD ** (-0.5) + bias
            expo = jnp.exp(scores - jnp.max(scores, axis=-1, keepdims=True))
            probs = expo / jnp.sum(expo, axis=-1, keepdims=True)
            prob_ref[block, pair] = probs
            mixed = unstack_heads(plain_rows(probs.astype(jnp.bfloat16), v, NN))
            mixed_ref[here, pl.ds(pair * LANES, LANES)] = mixed.astype(jnp.bfloat16)
        return carry

    lax.fori_loop(0, 2 * tokens // LANES, attend, 0)
    res_ref[...] = plain_rows(mixed_ref[...], w_ref[:, 3 * D :], NN)
    for view in range(2):
        def finish(chunk, carry, view=view):
            own = pl.ds(pl.multiple_of(chunk * ROWS, ROWS), ROWS)
            at = pl.ds(pl.multiple_of(view * tokens + chunk * ROWS, ROWS), ROWS)
            res = attn_in[at, :] + keep_of(mask[2 * view + 1, own, :]) * (res_ref[at, :] + vecs[2:3])
            res_ref[at, :] = res
            norm = layer_norm(res, vecs[3:4], vecs[4:5])
            norm_ref[at, :] = norm
            low_ref[at, :] = norm.astype(jnp.bfloat16)
            return carry

        lax.fori_loop(0, tokens // ROWS, finish, 0)
    for copy in copies:
        copy.wait()


def attn_forward(pieces, me, shard, length, lengths, embeddings, masks):
    rows = pieces[0].shape[1]
    whole = shard * 32 // LANES
    tokens = embeddings.shape[0]
    both = 2 * tokens
    any_space, vmem = pl.BlockSpec(memory_space=pl.ANY), pl.BlockSpec(memory_space=pltpu.VMEM)
    smem = pl.BlockSpec(memory_space=pltpu.SMEM)
    f32, low = jnp.float32, jnp.bfloat16
    shapes = [
        ((D, 4 * D), low),
        ((8, D), f32),
        ((tokens, D), f32),
        ((both, D), low),
        ((both, 3 * D), low),
        ((both // LANES, H // 2, 2 * LANES, LANES), f32),
        ((both, D), low),
        ((both, D), f32),
        ((both, D), f32),
        ((both, D), low),
    ]
    return pl.pallas_call(
        functools.partial(attn_kernel, shard),
        out_shape=tuple(jax.ShapeDtypeStruct(*s) for s in shapes),
        in_specs=[smem] * 3 + [any_space] * len(pieces) + [vmem, any_space],
        out_specs=(any_space,) + (vmem,) * 9,
        scratch_shapes=[
            pltpu.VMEM((32, rows, LANES), low),
            pltpu.VMEM((whole + rows, LANES), f32),
            pltpu.VMEM((D, 4 * D), low),
            pltpu.VMEM((D, LANES), f32),
            pltpu.VMEM((D, LANES), f32),
            pltpu.VMEM((4, tokens, D), jnp.int32),
            pltpu.VMEM((both, D), f32),
            pltpu.VMEM((tokens // LANES, LANES, LANES), f32),
            pltpu.SemaphoreType.DMA((32,)),
            pltpu.SemaphoreType.DMA((4,)),
            pltpu.SemaphoreType.DMA((4,)),
        ],
        compiler_params=pltpu.CompilerParams(vmem_limit_bytes=VMEM_CAP),
    )(jnp.reshape(me, (1,)), jnp.reshape(length, (1,)), lengths, *pieces, embeddings, masks)


def sum_rows(rows):
    return jnp.sum(rows, axis=0, keepdims=True)


def attn_back_kernel(pick_ref, d_first, d_cls, res_ref, vec_ref, mask_hbm, mixed_ref, w_ref, qkv_ref, prob_ref,
                     d_res_ref, g_out_ref, d_qkv_ref, part_ref, mask, given, branch, d_mixed, mask_sems):
    tokens = mask.shape[1]
    both = 2 * tokens
    masks = []
    for view in range(2):
        masks.append(pltpu.make_async_copy(mask_hbm.at[view, 1], mask.at[view], mask_sems.at[view]))
        masks[-1].start()
    given[...] = d_first[...]
    n = d_cls.shape[0] // 2
    for slot in range(n):
        real = jnp.where(slot < pick_ref[n], 1.0, 0.0)
        for view in range(2):
            at = pl.ds(view * tokens + pick_ref[slot], 1)
            given[at, :] += real * d_cls[view * n + slot : view * n + slot + 1, :]
    for copy in masks:
        copy.wait()
    gain = vec_ref[3:4, :]
    sums = tuple(jnp.zeros((1, D), jnp.float32) for _ in range(3))
    for view in range(2):
        def one_chunk(chunk, sums, view=view):
            own = pl.ds(pl.multiple_of(chunk * ROWS, ROWS), ROWS)
            at = pl.ds(pl.multiple_of(view * tokens + chunk * ROWS, ROWS), ROWS)
            grad = given[at, :]
            center, inv = norm_parts(res_ref[at, :])
            d_res, unit = norm_back(grad, center, inv, gain)
            d_branch = d_res * keep_of(mask[view, own, :])
            d_res_ref[at, :] = d_res
            branch[at, :] = d_branch.astype(jnp.bfloat16)
            return (
                sums[0] + sum_rows(d_branch),
                sums[1] + sum_rows(grad * unit),
                sums[2] + sum_rows(grad),
            )

        sums = lax.fori_loop(0, tokens // ROWS, one_chunk, sums)
    d_mixed[...] = plain_rows(branch[...], w_ref[...], NT).astype(jnp.bfloat16)
    g_out_ref[...] = plain_rows(mixed_ref[...], branch[...], TN).astype(jnp.bfloat16)
    for k in range(3):
        part_ref[2 + k : 3 + k, :] = sums[k]
    part_ref[5:8, :] = jnp.zeros((3, D), jnp.float32)
    part_ref[0:2, :] = jnp.zeros((2, D), jnp.float32)

    def one_block(block, carry):
        here = pl.ds(pl.multiple_of(block * LANES, LANES), LANES)
        for pair in range(H // 2):
            cols = pl.ds(pair * LANES, LANES)
            q = stack_heads(qkv_ref[here, cols])
            k = qkv_ref[here, pl.ds(D + pair * LANES, LANES)]
            v = qkv_ref[here, pl.ds(2 * D + pair * LANES, LANES)]
            d_out = stack_heads(d_mixed[here, cols])
            probs = prob_ref[block, pair]
            d_v = plain_rows(probs.astype(jnp.bfloat16), d_out, TN)
            d_probs = plain_rows(d_out, v, NT)
            delta = jnp.sum(probs * d_probs, axis=-1, keepdims=True)
            score = (probs * (d_probs - delta) * HD ** (-0.5)).astype(jnp.bfloat16)
            d_q = unstack_heads(plain_rows(score, k, NN))
            d_k = plain_rows(score, q, TN)
            d_qkv_ref[here, cols] = d_q.astype(jnp.bfloat16)
            d_qkv_ref[here, pl.ds(D + pair * LANES, LANES)] = d_k.astype(jnp.bfloat16)
            d_qkv_ref[here, pl.ds(2 * D + pair * LANES, LANES)] = d_v.astype(jnp.bfloat16)
            part_ref[0:1, cols] += sum_rows(d_q)
            part_ref[1:2, cols] += sum_rows(d_v)
        return carry

    lax.fori_loop(0, both // LANES, one_block, 0)


def attn_backward(picks, d_first, d_cls, res, vecs, masks, mixed, w_attn, qkv, probs):
    both = res.shape[0]
    tokens = both // 2
    any_space, vmem = pl.BlockSpec(memory_space=pl.ANY), pl.BlockSpec(memory_space=pltpu.VMEM)
    f32, low = jnp.float32, jnp.bfloat16
    shapes = [((both, D), f32), ((D, D), low), ((both, 3 * D), low), ((8, D), f32)]
    return pl.pallas_call(
        attn_back_kernel,
        out_shape=tuple(jax.ShapeDtypeStruct(*s) for s in shapes),
        grid=(1,),
        in_specs=[pl.BlockSpec(memory_space=pltpu.SMEM), vmem, vmem, vmem, vmem, any_space, vmem]
        + [pl.BlockSpec((D, D), lambda i: (0, 3)), vmem, vmem],
        out_specs=(vmem,) * 4,
        scratch_shapes=[
            pltpu.VMEM((2, tokens, D), jnp.int32),
            pltpu.VMEM((both, D), f32),
            pltpu.VMEM((both, D), low),
            pltpu.VMEM((both, D), low),
            pltpu.SemaphoreType.DMA((2,)),
        ],
        compiler_params=pltpu.CompilerParams(vmem_limit_bytes=VMEM_CAP),
    )(picks, d_first, d_cls, res, vecs, masks, mixed, w_attn, qkv, probs)


def attn_grad_kernel(shard, me_ref, length_ref, d_qkv, in_low, w_ref, d_res, rows_ref, vec_ref, mask_hbm, g_out,
                     part_ref, input_ref, *refs):
    pieces, (stage, flat, body, tail, mask, d_in, sems, mask_sems) = refs[:10], refs[10:]
    cols = 4 * D // LANES
    tokens = rows_ref.shape[0]
    masks = []
    for view in range(2):
        masks.append(pltpu.make_async_copy(mask_hbm.at[view, 0], mask.at[view], mask_sems.at[view]))
        masks[-1].start()
    d_in[...] = plain_rows(d_qkv[...], w_ref[...], NT)
    for copy in masks:
        copy.wait()
    gain = vec_ref[5:6, :]

    def one_chunk(chunk, sums):
        own = pl.ds(pl.multiple_of(chunk * ROWS, ROWS), ROWS)
        other = pl.ds(pl.multiple_of(tokens + chunk * ROWS, ROWS), ROWS)
        grad = (d_in[own, :] + d_res[own, :]) * keep_of(mask[0, own, :])
        grad = grad + (d_in[other, :] + d_res[other, :]) * keep_of(mask[1, own, :])
        center, inv = norm_parts(rows_ref[own, :])
        back, unit = norm_back(grad, center, inv, gain)
        input_ref[own, :] = back
        return (sums[0] + sum_rows(grad * unit), sums[1] + sum_rows(grad), sums[2] + sum_rows(back))

    sums = lax.fori_loop(
        0, tokens // ROWS, one_chunk, tuple(jnp.zeros((1, D), jnp.float32) for _ in range(3))
    )
    table = jnp.zeros((LANES, D), jnp.float32)
    for block in range(tokens // LANES):
        table = table + input_ref[block * LANES : (block + 1) * LANES, :]
    table = fold_places(table, length_ref[0])
    first = jnp.concatenate([part_ref[0:5, :], *sums, table[: LANES - 8]])
    base = D * cols
    flat_table(flat, base, first, table[LANES - 8 :], body, tail)
    span, width = 256, 3 * LANES

    def one_block(block, carry):
        left = in_low[:, pl.ds(pl.multiple_of(block * span, span), span)]
        for k in range(3 * D // width):
            grads = plain_rows(left, d_qkv[:, pl.ds(k * width, width)], TN)
            for col in range(width // LANES):
                for group in range(span // 16):
                    at = (block * span + group * 16) * cols + k * width // LANES + col
                    tile = grads[group * 16 : (group + 1) * 16, col * LANES : (col + 1) * LANES]
                    flat[pl.ds(at, 16, stride=cols), :] = tile
        return carry

    lax.fori_loop(0, D // span, one_block, 0)

    def one_group(group, carry):
        at = pl.multiple_of(group * 16, 16)
        for col in range(D // LANES):
            tile = g_out[pl.ds(at, 16), pl.ds(col * LANES, LANES)].astype(jnp.float32)
            flat[pl.ds(group * 16 * cols + 3 * D // LANES + col, 16, stride=cols), :] = tile
        return carry

    lax.fori_loop(0, D // 16, one_group, 0)
    rows = stage.shape[1]
    flat[pl.ds(base + D * VEC // LANES, rows), :] = jnp.zeros((rows, LANES), jnp.float32)
    store_pieces(shard, me_ref[0], pieces, stage, flat, sems)


def attn_grads(me, shard, length, d_qkv, in_low, w_attn, d_res, rows_in, vecs, masks, g_out, parts):
    rows = block_rows(shard)
    whole = shard * 32 // LANES
    tokens = rows_in.shape[0]
    counts = [len(slots) for slots in piece_slots(0)]
    any_space, vmem = pl.BlockSpec(memory_space=pl.ANY), pl.BlockSpec(memory_space=pltpu.VMEM)
    smem = pl.BlockSpec(memory_space=pltpu.SMEM)
    f32, low = jnp.float32, jnp.bfloat16
    return pl.pallas_call(
        functools.partial(attn_grad_kernel, shard),
        out_shape=(jax.ShapeDtypeStruct((tokens, D), f32),)
        + tuple(jax.ShapeDtypeStruct((n, rows, LANES), low) for n in counts),
        grid=(1,),
        in_specs=[smem, smem, vmem, vmem, pl.BlockSpec((D, 3 * D), lambda i: (0, 0)), vmem, vmem, vmem]
        + [any_space, vmem, vmem],
        out_specs=(vmem,) + (any_space,) * len(counts),
        scratch_shapes=[
            pltpu.VMEM((32, rows, LANES), low),
            pltpu.VMEM((whole + rows, LANES), f32),
            pltpu.VMEM((D, LANES), f32),
            pltpu.VMEM((D, LANES), f32),
            pltpu.VMEM((2, tokens, D), jnp.int32),
            pltpu.VMEM((2 * tokens, D), f32),
            pltpu.SemaphoreType.DMA((32,)),
            pltpu.SemaphoreType.DMA((2,)),
        ],
        compiler_params=pltpu.CompilerParams(vmem_limit_bytes=VMEM_CAP),
    )(jnp.reshape(me, (1,)), jnp.reshape(length, (1,)), d_qkv, in_low, w_attn, d_res, rows_in, vecs, masks, g_out, parts)


def head_kernel(shard, me_ref, pick_ref, *refs):
    pieces, (first_hbm, mask_hbm) = refs[:10], refs[10:12]
    w_out, vec_ref, unit_ref, pooled_ref, res_ref, up_ref, cls_ref, act_ref, keep_ref, low_ref = refs[12:22]
    stage, flat, w_ref, first_all, picked, mask, sems, out_sems, in_sems = refs[22:]
    cols = w_ref.shape[1] // LANES
    tokens = mask.shape[1]
    loads = [pltpu.make_async_copy(first_hbm, first_all, in_sems.at[2])]
    for view in range(2):
        loads.append(pltpu.make_async_copy(mask_hbm.at[view, 2], mask.at[view], in_sems.at[view]))
    for load in loads:
        load.start()
    place_blocks(shard, pieces, me_ref[0], stage, flat, sems)
    copies = gather_matrix(flat, w_ref, w_out, out_sems)
    for load in loads:
        load.wait()
    n = unit_ref.shape[0] // 2
    for view in range(2):
        for slot in range(n):
            at, to = pick_ref[slot], view * n + slot
            picked[to : to + 1, :] = first_all[pl.ds(view * tokens + at, 1), :]
            keep_ref[to : to + 1, :] = keep_of(mask[view, pl.ds(at, 1), :])
    vecs = vectors_of(flat[pl.ds(D * cols, 48), :])
    vec_ref[...] = vecs
    first = picked[...]
    low_ref[...] = first.astype(jnp.bfloat16)
    up_bias = jnp.concatenate([vecs[c : c + 1] for c in range(4)], axis=1)
    up_pre = plain_rows(first.astype(jnp.bfloat16), w_ref[:, : 4 * D], NN) + up_bias
    active = gelu_exact(up_pre).astype(jnp.bfloat16)
    down = plain_rows(active, w_ref[:, 4 * D : 8 * D], NT) + vecs[4:5]
    res = first + keep_ref[...] * down
    cls_low = layer_norm(res, vecs[5:6], vecs[6:7]).astype(jnp.bfloat16)
    pooled = jnp.tanh(plain_rows(cls_low, w_ref[:, 8 * D :], NN) + vecs[7:8])
    unit_ref[...] = unit_scale(pooled).astype(jnp.bfloat16)
    pooled_ref[...] = pooled
    res_ref[...] = res
    up_ref[...] = up_pre
    cls_ref[...] = cls_low
    act_ref[...] = active
    for copy in copies:
        copy.wait()


def make_head(pieces, me, shard, picks, first_norm, masks):
    rows = pieces[0].shape[1]
    whole = shard * 32 // LANES
    n = 2 * (picks.shape[0] - 1)
    any_space, vmem = pl.BlockSpec(memory_space=pl.ANY), pl.BlockSpec(memory_space=pltpu.VMEM)
    smem = pl.BlockSpec(memory_space=pltpu.SMEM)
    f32, low = jnp.float32, jnp.bfloat16
    shapes = [
        ((D, 9 * D), low),
        ((8, D), f32),
        ((n, D), low),
        ((n, D), f32),
        ((n, D), f32),
        ((n, 4 * D), f32),
        ((n, D), low),
        ((n, 4 * D), low),
        ((n, D), f32),
        ((n, D), low),
    ]
    return pl.pallas_call(
        functools.partial(head_kernel, shard),
        out_shape=tuple(jax.ShapeDtypeStruct(*s) for s in shapes),
        in_specs=[smem] * 2 + [any_space] * (len(pieces) + 2),
        out_specs=(any_space,) + (vmem,) * 9,
        scratch_shapes=[
            pltpu.VMEM((32, rows, LANES), low),
            pltpu.VMEM((whole + rows, LANES), f32),
            pltpu.VMEM((D, 9 * D), low),
            pltpu.VMEM(first_norm.shape, f32),
            pltpu.VMEM((n, D), f32),
            pltpu.VMEM((2,) + masks.shape[2:], jnp.int32),
            pltpu.SemaphoreType.DMA((32,)),
            pltpu.SemaphoreType.DMA((4,)),
            pltpu.SemaphoreType.DMA((3,)),
        ],
        compiler_params=pltpu.CompilerParams(vmem_limit_bytes=VMEM_CAP),
    )(jnp.reshape(me, (1,)), picks, *pieces, first_norm, masks)


def norm_back(grad, center, inv, gain):
    unit = center * inv
    scaled = grad * gain
    mean = jnp.mean(scaled, axis=-1, keepdims=True)
    along = jnp.mean(scaled * unit, axis=-1, keepdims=True)
    return inv * (scaled - mean - unit * along), unit


def norm_parts(rows):
    center = rows - jnp.mean(rows, axis=-1, keepdims=True)
    return center, lax.rsqrt(jnp.mean(center * center, axis=-1, keepdims=True) + norm_eps)


def gelu_slope(values):
    cdf = 0.5 * (1.0 + lax.erf(values * 0.7071067811865476))
    return cdf + values * (0.3989422804014327 * jnp.exp(-0.5 * values * values))


def pooled_kernel(me_ref, own_ref, sib_ref, w_hbm, vrow_ref, vcol_ref, vec_ref, pooled_ref, res_ref,
                  up_ref, keep_ref, loss_ref, pool_ref, down_ref, uplow_ref, first_ref, part_ref,
                  units, sims, back, w_ref, sems, w_sems):
    me = me_ref[0]
    w_copies = []
    for k, (start, size) in enumerate(((8 * D, D), (4 * D, 4 * D), (0, 4 * D))):
        here = pl.ds(start, size)
        w_copies.append(pltpu.make_async_copy(w_hbm.at[:, here], w_ref.at[:, here], w_sems.at[k]))
    copies = []
    for core, ref in ((0, own_ref), (1, sib_ref)):
        for across in range(4):
            for k in range(4):
                slot = me ^ (core + 2 * across + 8 * k)
                copies.append(
                    pltpu.make_async_copy(ref.at[across, k], units.at[slot], sems.at[len(copies)])
                )
    for copy in copies + w_copies:
        copy.start()
    for copy in copies:
        copy.wait()
    n = units.shape[1]
    half = n // 2
    total = units.shape[0] * n
    everyone = units[...].reshape(total, D)
    table = plain_rows(everyone, everyone, NT) * (1.0 / logit_divisor)
    row = lax.broadcasted_iota(jnp.int32, (total, total), 0)
    col = lax.broadcasted_iota(jnp.int32, (total, total), 1)
    valid_row = vrow_ref[...] > 0
    table = jnp.where(((col & (n - 1)) >= half) & (vcol_ref[...] > 0), table, masked_scores)
    top = jnp.max(table, axis=-1, keepdims=True)
    row_lse = top + jnp.log(jnp.sum(jnp.exp(table - top), axis=-1, keepdims=True))
    diagonal = col == row + half
    positive = jnp.sum(jnp.where(diagonal, table, 0.0), axis=-1, keepdims=True)
    row_one = lax.broadcasted_iota(jnp.int32, (total, 1), 0)
    anchors = ((row_one & (n - 1)) < half) & valid_row
    loss_ref[0, 0] = jnp.sum(jnp.where(anchors, row_lse - positive, 0.0))
    slope = (jnp.exp(table - row_lse) - jnp.where(diagonal, 1.0, 0.0)) * (1.0 / logit_divisor)
    sims[...] = jnp.where(anchors, slope, 0.0).astype(jnp.bfloat16)
    back[...] = plain_rows(sims[...], everyone, TN)
    mine = pl.ds(pl.multiple_of(me * n, n), n)
    d_unit = plain_rows(sims[mine, :], everyone, NN) + back[mine, :]
    pooled = pooled_ref[...]
    inv = lax.rsqrt(jnp.sum(pooled * pooled, axis=-1, keepdims=True) + norm_eps)
    along = jnp.sum(pooled * d_unit, axis=-1, keepdims=True)
    d_pooled = inv * d_unit - pooled * (inv * inv * inv * along)
    d_pre = d_pooled * (1.0 - pooled * pooled)
    pool_low = d_pre.astype(jnp.bfloat16)
    pool_ref[...] = pool_low
    w_copies[0].wait()
    d_cls = plain_rows(pool_low, w_ref[:, 8 * D :], NT)
    center, scale = norm_parts(res_ref[...])
    d_res, unit = norm_back(d_cls, center, scale, vec_ref[5:6, :])
    d_down = d_res * keep_ref[...]
    down_low = d_down.astype(jnp.bfloat16)
    down_ref[...] = down_low
    w_copies[1].wait()
    d_up = plain_rows(down_low, w_ref[:, 4 * D : 8 * D], NN) * gelu_slope(up_ref[...])
    up_low = d_up.astype(jnp.bfloat16)
    uplow_ref[...] = up_low
    w_copies[2].wait()
    first_ref[...] = d_res + plain_rows(up_low, w_ref[:, : 4 * D], NT)
    up_sum = jnp.sum(d_up, axis=0, keepdims=True)
    rows = [up_sum[:, c * D : (c + 1) * D] for c in range(4)]
    rows += [jnp.sum(part, axis=0, keepdims=True) for part in (d_down, d_cls * unit, d_cls, d_pre)]
    for k, value in enumerate(rows):
        part_ref[k : k + 1, :] = value


def pooled_backward(me, own, sib, w_head, valid, vecs, pooled, res, up_pre, keep):
    n = pooled.shape[0]
    total = valid.shape[0]
    any_space, vmem = pl.BlockSpec(memory_space=pl.ANY), pl.BlockSpec(memory_space=pltpu.VMEM)
    smem = pl.BlockSpec(memory_space=pltpu.SMEM)
    f32, low = jnp.float32, jnp.bfloat16
    shapes = [((1, 1), f32), ((n, D), low), ((n, D), low), ((n, 4 * D), low), ((n, D), f32), ((8, D), f32)]
    return pl.pallas_call(
        pooled_kernel,
        out_shape=tuple(jax.ShapeDtypeStruct(*s) for s in shapes),
        in_specs=[smem] + [any_space] * 3 + [vmem] * 7,
        out_specs=(smem,) + (vmem,) * 5,
        scratch_shapes=[
            pltpu.VMEM((32, n, D), low),
            pltpu.VMEM((total, total), low),
            pltpu.VMEM((total, D), f32),
            pltpu.VMEM((D, 9 * D), low),
            pltpu.SemaphoreType.DMA((32,)),
            pltpu.SemaphoreType.DMA((3,)),
        ],
        compiler_params=pltpu.CompilerParams(vmem_limit_bytes=VMEM_CAP),
    )(jnp.reshape(me, (1,)), own, sib, w_head, valid[:, None], valid[None, :], vecs, pooled, res, up_pre, keep)


def head_grad_kernel(shard, me_ref, *refs):
    (first, first_cls, up, up_cls, down, down_cls, act, act_cls, cls_ref, pool_ref, vec_ref) = refs[:11]
    pieces, (first_all, up_all, down_all, act_all, stage, flat, sems, in_sems) = refs[11:21], refs[21:]
    count, rows = stage.shape[0], stage.shape[1]
    cols = 9 * D // LANES
    me = me_ref[0]
    many, few = first.shape[0], first_cls.shape[0]
    loads = []
    for main, extra, whole in (
        (first, first_cls, first_all),
        (up, up_cls, up_all),
        (down, down_cls, down_all),
        (act, act_cls, act_all),
    ):
        loads.append(pltpu.make_async_copy(main, whole.at[pl.ds(0, many)], in_sems.at[len(loads)]))
        loads.append(pltpu.make_async_copy(extra, whole.at[pl.ds(many, few)], in_sems.at[len(loads)]))
    for load in loads:
        load.start()
    span = 256

    def fill(left, right, first_col, width):
        def one_block(block, carry):
            part = left[:, pl.ds(pl.multiple_of(block * span, span), span)]
            for k in range(right.shape[1] // width):
                grads = plain_rows(part, right[:, pl.ds(k * width, width)], TN)
                for col in range(width // LANES):
                    for group in range(span // 16):
                        at = (block * span + group * 16) * cols + first_col + k * width // LANES + col
                        tile = grads[group * 16 : (group + 1) * 16, col * LANES : (col + 1) * LANES]
                        flat[pl.ds(at, 16, stride=cols), :] = tile
            return carry

        lax.fori_loop(0, D // span, one_block, 0)

    fill(cls_ref, pool_ref, 8 * D // LANES, 256)
    for load in loads[:4]:
        load.wait()
    fill(first_all, up_all, 0, 512)
    for load in loads[4:]:
        load.wait()
    fill(down_all, act_all, 4 * D // LANES, 512)
    flat[pl.ds(D * cols, 48), :] = flat_of(vec_ref[...])
    flat[pl.ds(D * cols + 48, rows), :] = jnp.zeros((rows, LANES), jnp.float32)
    store_pieces(shard, me, pieces, stage, flat, sems)


def store_pieces(shard, me, pieces, stage, flat, sems):
    rows = stage.shape[1]
    copies = []
    for piece, slots in list(zip(pieces, piece_slots(me)))[::-1]:
        for k, slot in enumerate(slots):
            at = pl.multiple_of(slot * shard // LANES // 8 * 8, 8)
            stage[slot] = flat[pl.ds(at, rows), :].astype(jnp.bfloat16)
            copy = pltpu.make_async_copy(stage.at[slot], piece.at[k], sems.at[len(copies)])
            copy.start()
            copies.append(copy)
    for copy in copies:
        copy.wait()


def head_grads(me, shard, first, first_cls, up, up_cls, down, down_cls, act, act_cls, cls_low, pool_low, vecs):
    rows = block_rows(shard)
    whole = shard * 32 // LANES
    counts = [len(slots) for slots in piece_slots(0)]
    any_space, vmem = pl.BlockSpec(memory_space=pl.ANY), pl.BlockSpec(memory_space=pltpu.VMEM)
    low = jnp.bfloat16
    many = first.shape[0] + first_cls.shape[0]
    return pl.pallas_call(
        functools.partial(head_grad_kernel, shard),
        out_shape=tuple(jax.ShapeDtypeStruct((n, rows, LANES), low) for n in counts),
        in_specs=[pl.BlockSpec(memory_space=pltpu.SMEM)] + [any_space] * 8 + [vmem] * 3,
        out_specs=(any_space,) * len(counts),
        scratch_shapes=[
            pltpu.VMEM((many, D), low),
            pltpu.VMEM((many, 4 * D), low),
            pltpu.VMEM((many, D), low),
            pltpu.VMEM((many, 4 * D), low),
            pltpu.VMEM((32, rows, LANES), low),
            pltpu.VMEM((whole + rows, LANES), jnp.float32),
            pltpu.SemaphoreType.DMA((32,)),
            pltpu.SemaphoreType.DMA((8,)),
        ],
        compiler_params=pltpu.CompilerParams(vmem_limit_bytes=VMEM_CAP),
    )(jnp.reshape(me, (1,)), first, first_cls, up, up_cls, down, down_cls, act, act_cls, cls_low, pool_low, vecs)


def gather_attn(values, device):
    zs = gather_along(pack_shard(values, device))
    line, x, y = gather_across(jnp.stack(zs))
    diagonal = gather_diagonal(x, y)
    own = (line, x, y) + diagonal
    return own + tuple(swap(piece, CORE) for piece in own), zs[1], diagonal


def gather_head_line(values, device, first, last):
    zs = gather_along(after(pack_shard(values, device), first))
    return gather_across(after(jnp.stack(zs), *last))


def gather_head(line, x, y):
    own = (line, x, y) + gather_diagonal(x, y)
    return own + tuple(swap(piece, CORE) for piece in own)


def gather_small(value):
    got = jnp.stack([value] + [swap(value, bit) for bit in ZBITS])
    got = jnp.stack([got] + [swap(got, bit) for bit in (XBIT, YBIT, XBIT | YBIT)])
    return got, swap(got, CORE)


def sum_small(value):
    value = value + swap(value, CORE)
    across = [swap(value, bit) for bit in (XBIT, YBIT, XBIT | YBIT)]
    value = (value + across[0]) + (across[1] + across[2])
    along = [swap(value, bit) for bit in ZBITS]
    return (value + along[0]) + (along[1] + along[2])


def on_grid(
    embeddings,
    cotangent,
    drop_masks,
    lengths,
    buckets,
    attn_params,
    attn_moment,
    attn_second,
    attn_ema,
    head_params,
    head_moment,
    head_second,
    head_ema,
):
    tok_rows = embeddings.shape[0]
    slot_count = lengths.shape[0]
    all_rows = 2 * tok_rows
    device = lax.axis_index("sent")
    shards = (attn_params.shape[0], head_params.shape[0])
    attn_pieces, attn_first, attn_last = gather_attn(attn_params, device)
    head_line, head_x, head_y = gather_head_line(head_params, device, attn_first, attn_last)
    bucket_all = bucket_length(buckets)
    slot_ids = jnp.arange(slot_count, dtype=jnp.int32)
    valid_everything = (
        (slot_ids[None, :] < (tok_rows // bucket_all)[:, None]).astype(jnp.float32).reshape(-1)
    )
    bucket_len = bucket_all[device]
    sent_count = tok_rows // bucket_len
    picks = jnp.concatenate(
        [jnp.minimum(slot_ids, sent_count - 1) * bucket_len, sent_count[None]]
    )
    (
        attn_mats,
        attn_vecs,
        emb_rows,
        attn_in_low,
        qkv_low,
        probs,
        mixed_low,
        first_res,
        first_norm,
        first_low,
    ) = attn_forward(attn_pieces, device, shards[0], bucket_len, lengths, embeddings, drop_masks)
    (head_x, head_y), first_norm = lax.optimization_barrier(((head_x, head_y), first_norm))
    head_pieces = gather_head(head_line, head_x, head_y)
    keep_ffn = (drop_masks[:, 2].astype(jnp.float32) / keep_prob).reshape(all_rows, D)
    (
        head_mats,
        head_vecs,
        unit_low,
        pooled,
        res_cls,
        up_cls,
        cls_low,
        act_cls,
        keep_cls,
        first_cls,
    ) = make_head(head_pieces, device, shards[1], picks, first_norm, drop_masks)
    units_own, units_sib = gather_small(unit_low)
    w_up = head_mats[:, : 4 * D]
    w_down = head_mats[:, 4 * D : 8 * D]
    up_pre = plain_dot(first_low, w_up) + head_vecs[:4].reshape(4 * D)
    active, gelu_back = jax.vjp(gelu_exact, up_pre)
    active_low = active.astype(jnp.bfloat16)
    down_out = target_dot_terms(active_low, w_down) + head_vecs[4]
    second_res = first_norm + keep_ffn * down_out
    second_norm, second_back = jax.vjp(layer_norm, second_res, head_vecs[5], head_vecs[6])
    hidden_out = second_norm.astype(jnp.bfloat16).reshape(2, tok_rows, D)
    d_second = cotangent.astype(jnp.float32)
    d_second_res, g_gain_two, g_shift_two = second_back(d_second.reshape(all_rows, D))
    d_down = d_second_res * keep_ffn
    g_down_bias = jnp.sum(d_down, axis=0)
    down_low = d_down.astype(jnp.bfloat16)
    d_active = plain_dot(down_low, w_down)
    d_up = gelu_back(d_active)[0]
    g_up_bias = jnp.sum(d_up, axis=0)
    up_low = d_up.astype(jnp.bfloat16)
    d_first = d_second_res + target_dot_terms(up_low, w_up)
    valid_views = jnp.broadcast_to(
        valid_everything.reshape(-1, 1, slot_count), (bucket_all.shape[0], 2, slot_count)
    ).reshape(-1)
    loss_sum, pool_low, down_cls, uplow_cls, d_first_cls, cls_parts = pooled_backward(
        device, units_own, units_sib, head_mats, valid_views, head_vecs, pooled, res_cls, up_cls, keep_cls
    )
    loss_sum = loss_sum[0, 0]
    main_parts = jnp.concatenate(
        [
            g_up_bias.reshape(4, D),
            jnp.stack([g_down_bias, g_gain_two, g_shift_two, jnp.zeros((D,), jnp.float32)]),
        ]
    )
    head_pieces = head_grads(
        device,
        shards[1],
        first_low,
        first_cls,
        up_low,
        uplow_cls,
        down_low,
        down_cls,
        active_low,
        act_cls,
        cls_low,
        pool_low,
        main_parts + cls_parts,
    )
    d_first, head_pieces = lax.optimization_barrier((d_first, head_pieces))
    head_sums = scatter_core(head_pieces)
    d_first_res, g_out, d_qkv, attn_parts = attn_backward(
        picks, d_first, d_first_cls, first_res, attn_vecs, drop_masks, mixed_low, attn_mats, qkv_low, probs
    )
    d_qkv, head_sums = lax.optimization_barrier((d_qkv, head_sums))
    head_diagonal = scatter_diagonal(head_sums)
    input_grad, *attn_pieces = attn_grads(
        device,
        shards[0],
        bucket_len,
        d_qkv,
        attn_in_low,
        attn_mats,
        d_first_res,
        emb_rows,
        attn_vecs,
        drop_masks,
        g_out,
        attn_parts,
    )
    attn_pieces, head_diagonal = lax.optimization_barrier((attn_pieces, head_diagonal))
    head_across = scatter_across(head_sums, head_diagonal)
    attn_sums = scatter_core(attn_pieces)
    attn_sums, head_across = lax.optimization_barrier((attn_sums, head_across))
    head_zs = scatter_line(head_sums, head_across)
    attn_diagonal = scatter_diagonal(attn_sums)
    attn_zs = scatter_line(attn_sums, scatter_across(attn_sums, attn_diagonal))
    head_share = unpack_shard(scatter_along(head_zs), device, shards[1])
    attn_share = unpack_shard(scatter_along(attn_zs), device, shards[0])
    squares = jnp.sum(attn_share * attn_share) + jnp.sum(head_share * head_share)
    total_squares = sum_small(squares)
    loss = loss_sum / jnp.sum(valid_everything)
    grad_norm = jnp.sqrt(total_squares)
    clip_scale = jnp.minimum(1.0, clip_bound / grad_norm)
    attn_new = adam_step(attn_share * clip_scale, attn_params, attn_moment, attn_second, attn_ema)
    head_new = adam_step(head_share * clip_scale, head_params, head_moment, head_second, head_ema)
    return (
        hidden_out,
        input_grad,
        loss,
        grad_norm,
        attn_new[0],
        attn_new[1],
        attn_new[2],
        attn_new[3],
        head_new[0],
        head_new[1],
        head_new[2],
        head_new[3],
    )


def on_any_mesh(
    embeddings,
    cotangent,
    drop_masks,
    lengths,
    buckets,
    attn_params,
    attn_moment,
    attn_second,
    attn_ema,
    head_params,
    head_moment,
    head_second,
    head_ema,
):
    tok_rows = embeddings.shape[0]
    slot_count = lengths.shape[0]
    all_rows = 2 * tok_rows
    device = lax.axis_index("sent")
    attn_full, head_full = (
        lax.all_gather(attn_params.astype(jnp.bfloat16), "sent", axis=0, tiled=True),
        lax.all_gather(head_params.astype(jnp.bfloat16), "sent", axis=0, tiled=True),
    )
    attn_mats = attn_full[: 4 * D * D].reshape(D, 4 * D)
    attn_vecs_low = attn_full[4 * D * D :].reshape(D, 8 + POS)
    attn_vecs = attn_vecs_low.astype(jnp.float32)
    head_mats = head_full[: 9 * D * D].reshape(D, 9 * D)
    head_vecs = head_full[9 * D * D :].reshape(D, 8).astype(jnp.float32)
    w_qkv = attn_mats[:, : 3 * D]
    w_out = attn_mats[:, 3 * D :]
    w_up = head_mats[:, : 4 * D]
    w_down = head_mats[:, 4 * D : 8 * D]
    w_pool = head_mats[:, 8 * D :]
    bucket_all = bucket_length(buckets)
    slot_ids = jnp.arange(slot_count, dtype=jnp.int32)
    valid_everything = (
        (slot_ids[None, :] < (tok_rows // bucket_all)[:, None]).astype(jnp.float32).reshape(-1)
    )
    bucket_len = bucket_all[device]
    sent_count = tok_rows // bucket_len
    valid_own = (slot_ids < sent_count).astype(jnp.float32)
    row_ids = jnp.arange(tok_rows, dtype=jnp.int32)
    sentence = row_ids // bucket_len
    row_place = row_ids % bucket_len
    slot_len = jnp.sum(
        jnp.where(sentence[:, None] == slot_ids[None, :], lengths[None, :], 0), axis=1
    )
    key_ok = row_place < slot_len
    block = POS
    sent_blocks = sentence.reshape(-1, block)
    ok_blocks = key_ok.reshape(-1, block)
    allowed = (sent_blocks[:, :, None] == sent_blocks[:, None, :]) & ok_blocks[:, None, :]
    allowed = jnp.concatenate([allowed, allowed], axis=0)[:, None]
    place_hot = (row_place[:, None] == jnp.arange(POS, dtype=jnp.int32)[None, :]).astype(
        jnp.bfloat16
    )
    pos_rows = plain_dot(place_hot, attn_vecs_low[:, 8:].T)
    emb_rows = embeddings.astype(jnp.float32) + pos_rows + attn_vecs[:, 7]
    normed, emb_back = jax.vjp(layer_norm, emb_rows, attn_vecs[:, 5], attn_vecs[:, 6])
    keep_masks = drop_masks.astype(jnp.float32) / keep_prob
    keep_attn = keep_masks[:, 1].reshape(all_rows, D)
    keep_ffn = keep_masks[:, 2].reshape(all_rows, D)
    attn_in = (normed[None] * keep_masks[:, 0]).reshape(all_rows, D)
    attn_in_low = attn_in.astype(jnp.bfloat16)
    qkv_bias = jnp.concatenate([attn_vecs[:, 0], jnp.zeros((D,), jnp.float32), attn_vecs[:, 1]])
    qkv_low = (plain_dot(attn_in_low, w_qkv) + qkv_bias).astype(jnp.bfloat16)
    head_split = qkv_low.reshape(-1, block, 3, H, HD)
    queries = head_split[:, :, 0]
    keys_low = head_split[:, :, 1]
    values_low = head_split[:, :, 2]
    score_scale = HD ** (-0.5)
    raw_scores = jnp.einsum(
        "bqhd,bkhd->bhqk", queries, keys_low, preferred_element_type=jnp.float32
    )
    scores = jnp.where(allowed, raw_scores * score_scale, masked_scores)
    row_top = jnp.max(scores, axis=-1, keepdims=True)
    expo_vals = jnp.exp(scores - row_top)
    row_total = jnp.sum(expo_vals, axis=-1, keepdims=True)
    attn_probs = expo_vals / row_total
    score_lse = row_top + jnp.log(row_total)
    mixed_out = jnp.einsum(
        "bhqk,bkhd->bqhd",
        attn_probs.astype(jnp.bfloat16),
        values_low,
        preferred_element_type=jnp.float32,
    )
    mixed_low = mixed_out.reshape(all_rows, D).astype(jnp.bfloat16)
    branch = plain_dot(mixed_low, w_out) + attn_vecs[:, 2]
    first_res = attn_in + keep_attn * branch
    first_norm, first_back = jax.vjp(layer_norm, first_res, attn_vecs[:, 3], attn_vecs[:, 4])
    first_low = first_norm.astype(jnp.bfloat16)
    up_bias = head_vecs[:, :4].T.reshape(4 * D)
    up_pre = plain_dot(first_low, w_up) + up_bias
    active, gelu_back = jax.vjp(gelu_exact, up_pre)
    active_low = active.astype(jnp.bfloat16)
    down_out = target_dot_terms(active_low, w_down) + head_vecs[:, 4]
    second_res = first_norm + keep_ffn * down_out
    second_norm, second_back = jax.vjp(layer_norm, second_res, head_vecs[:, 5], head_vecs[:, 6])
    hidden_out = second_norm.astype(jnp.bfloat16).reshape(2, tok_rows, D)
    cls_pick = jnp.minimum(slot_ids, sent_count - 1) * bucket_len
    cls_rows = jnp.take(second_norm.reshape(2, tok_rows, D), cls_pick, axis=1).reshape(
        2 * slot_count, D
    )
    cls_low = cls_rows.astype(jnp.bfloat16)
    pooled = jnp.tanh(plain_dot(cls_low, w_pool) + head_vecs[:, 7])
    unit_rows, unit_back = jax.vjp(unit_scale, pooled)
    unit_low = unit_rows.astype(jnp.bfloat16)
    query_embeddings = unit_low[:slot_count]
    positive_view_set = unit_low[slot_count:]
    target_sentence_set, everyone = (
        lax.all_gather(positive_view_set, "sent", axis=0, tiled=True),
        lax.all_gather(query_embeddings, "sent", axis=0, tiled=True),
    )
    own_cols = device * slot_count + slot_ids
    col_ids = jnp.arange(target_sentence_set.shape[0], dtype=jnp.int32)
    pos_hot = col_ids[None, :] == own_cols[:, None]
    cosine_logit_table = jnp.where(
        valid_everything[None, :] > 0,
        target_dot_terms(query_embeddings, target_sentence_set) / logit_divisor,
        masked_scores,
    )
    sim_top = jnp.max(cosine_logit_table, axis=-1, keepdims=True)
    row_lse = sim_top[:, 0] + jnp.log(jnp.sum(jnp.exp(cosine_logit_table - sim_top), axis=-1))
    positive = jnp.sum(jnp.where(pos_hot, cosine_logit_table, 0.0), axis=-1)
    local_loss = jnp.sum(valid_own * (row_lse - positive))
    loss_sum = lax.psum(local_loss, "sent")
    cosine_logit_cotangent = valid_own[:, None] * (
        jnp.exp(cosine_logit_table - row_lse[:, None]) - pos_hot.astype(jnp.float32)
    )
    cosine_logit_summed = (cosine_logit_cotangent / logit_divisor).astype(jnp.bfloat16)
    d_anchor = plain_dot(cosine_logit_summed, target_sentence_set)
    all_lse = lax.all_gather(row_lse, "sent", axis=0, tiled=True)
    back_sim = target_dot_terms(everyone, positive_view_set) / logit_divisor
    back_hot = (col_ids[:, None] == own_cols[None, :]).astype(jnp.float32)
    back_grad = valid_everything[:, None] * (
        jnp.exp(back_sim - all_lse[:, None]) * valid_own[None, :] - back_hot
    )
    d_partner = rows_dot((back_grad / logit_divisor).astype(jnp.bfloat16), everyone)
    d_unit = jnp.concatenate([d_anchor, d_partner], axis=0)
    d_pooled = unit_back(d_unit)[0]
    d_pool_pre = d_pooled * (1.0 - pooled * pooled)
    pool_low = d_pool_pre.astype(jnp.bfloat16)
    g_pool = rows_dot(cls_low, pool_low)
    g_pool_bias = jnp.sum(d_pool_pre, axis=0)
    d_cls = target_dot_terms(pool_low, w_pool).reshape(2, slot_count, D)
    pick_hot = ((row_ids[None, :] == cls_pick[:, None]) & (slot_ids[:, None] < sent_count)).astype(
        jnp.float32
    )
    d_second = cotangent.astype(jnp.float32) + jnp.einsum(
        "st,vsd->vtd", pick_hot, d_cls, precision=highest
    )
    d_second_res, g_gain_two, g_shift_two = second_back(d_second.reshape(all_rows, D))
    d_down = d_second_res * keep_ffn
    g_down_bias = jnp.sum(d_down, axis=0)
    down_low = d_down.astype(jnp.bfloat16)
    g_down = rows_dot(down_low, active_low)
    d_active = plain_dot(down_low, w_down)
    d_up = gelu_back(d_active)[0]
    g_up_bias = jnp.sum(d_up, axis=0)
    up_low = d_up.astype(jnp.bfloat16)
    g_up = rows_dot(first_low, up_low)
    d_first = d_second_res + target_dot_terms(up_low, w_up)
    head_vec_grad = jnp.concatenate(
        [
            g_up_bias.reshape(4, D).T,
            jnp.stack([g_down_bias, g_gain_two, g_shift_two, g_pool_bias], axis=1),
        ],
        axis=1,
    )
    head_grad = jnp.concatenate(
        [jnp.concatenate([g_up, g_down, g_pool], axis=1).reshape(-1), head_vec_grad.reshape(-1)]
    )
    d_first_res, g_gain_one, g_shift_one = first_back(d_first)
    d_branch = d_first_res * keep_attn
    g_out_bias = jnp.sum(d_branch, axis=0)
    branch_low = d_branch.astype(jnp.bfloat16)
    g_out = rows_dot(mixed_low, branch_low)
    d_mixed = target_dot_terms(branch_low, w_out).astype(jnp.bfloat16).reshape(-1, block, H, HD)
    again = jnp.where(
        allowed,
        jnp.einsum("bqhd,bkhd->bhqk", queries, keys_low, preferred_element_type=jnp.float32)
        * score_scale,
        masked_scores,
    )
    probs_again = jnp.exp(again - score_lse)
    d_values = jnp.einsum(
        "bhqk,bqhd->bkhd",
        probs_again.astype(jnp.bfloat16),
        d_mixed,
        preferred_element_type=jnp.float32,
    )
    d_probs = jnp.einsum("bqhd,bkhd->bhqk", d_mixed, values_low, preferred_element_type=jnp.float32)
    row_delta = jnp.sum(probs_again * d_probs, axis=-1, keepdims=True)
    score_low = (probs_again * (d_probs - row_delta) * score_scale).astype(jnp.bfloat16)
    d_queries = jnp.einsum(
        "bhqk,bkhd->bqhd", score_low, keys_low, preferred_element_type=jnp.float32
    )
    d_keys = jnp.einsum("bhqk,bqhd->bkhd", score_low, queries, preferred_element_type=jnp.float32)
    d_qkv = jnp.stack([d_queries, d_keys, d_values], axis=2).reshape(all_rows, 3 * D)
    g_q_bias = jnp.sum(d_queries.reshape(all_rows, D), axis=0)
    g_v_bias = jnp.sum(d_values.reshape(all_rows, D), axis=0)
    qkv_grad_low = d_qkv.astype(jnp.bfloat16)
    g_qkv = rows_dot(attn_in_low, qkv_grad_low)
    d_attn_in = d_first_res + target_dot_terms(qkv_grad_low, w_qkv)
    d_normed = jnp.sum(d_attn_in.reshape(2, tok_rows, D) * keep_masks[:, 0], axis=0)
    input_grad, g_gain_emb, g_shift_emb = emb_back(d_normed)
    g_type = jnp.sum(input_grad, axis=0)
    g_table = lax.dot_general(
        place_hot.astype(jnp.float32),
        input_grad,
        (((0,), (0,)), ((), ())),
        precision=highest,
        preferred_element_type=jnp.float32,
    )
    attn_vec_grad = jnp.concatenate(
        [
            jnp.stack(
                [
                    g_q_bias,
                    g_v_bias,
                    g_out_bias,
                    g_gain_one,
                    g_shift_one,
                    g_gain_emb,
                    g_shift_emb,
                    g_type,
                ],
                axis=1,
            ),
            g_table.T,
        ],
        axis=1,
    )
    attn_grad = jnp.concatenate(
        [jnp.concatenate([g_qkv, g_out], axis=1).reshape(-1), attn_vec_grad.reshape(-1)]
    )
    attn_share, head_share = (
        lax.psum_scatter(attn_grad, "sent", scatter_dimension=0, tiled=True),
        lax.psum_scatter(head_grad, "sent", scatter_dimension=0, tiled=True),
    )
    squares = jnp.sum(attn_share * attn_share) + jnp.sum(head_share * head_share)
    total_squares = lax.psum(squares, "sent")
    loss = loss_sum / jnp.sum(valid_everything)
    grad_norm = jnp.sqrt(total_squares)
    clip_scale = jnp.minimum(1.0, clip_bound / grad_norm)
    attn_new = adam_step(attn_share * clip_scale, attn_params, attn_moment, attn_second, attn_ema)
    head_new = adam_step(head_share * clip_scale, head_params, head_moment, head_second, head_ema)
    return (
        hidden_out,
        input_grad,
        loss,
        grad_norm,
        attn_new[0],
        attn_new[1],
        attn_new[2],
        attn_new[3],
        head_new[0],
        head_new[1],
        head_new[2],
        head_new[3],
    )


def on_device(*arrays):
    shards = (arrays[5].shape[0], arrays[9].shape[0])
    local = on_grid if is_grid(lax.axis_size("sent"), *shards) else on_any_mesh
    return local(*arrays)


def solution(mesh):
    in_specs = (
        P("sent", None),
        P(None, "sent", None),
        P(None, None, "sent", None),
        P("sent"),
        P(),
        P("sent"),
        P("sent"),
        P("sent"),
        P("sent"),
        P("sent"),
        P("sent"),
        P("sent"),
        P("sent"),
    )
    out_specs = (
        P(None, "sent", None),
        P("sent", None),
        P(),
        P(),
        P("sent"),
        P("sent"),
        P("sent"),
        P("sent"),
        P("sent"),
        P("sent"),
        P("sent"),
        P("sent"),
    )
    return jax.shard_map(
        on_device, mesh=mesh, in_specs=in_specs, out_specs=out_specs, check_vma=False
    )
```

```python
import functools

import jax
import jax.numpy as jnp
from jax import lax
from jax.experimental import pallas as pl
from jax.experimental.pallas import tpu as pltpu
from jax.sharding import PartitionSpec as P

D = 768
H = 12
HD = 64
LMIN = 32
POS = 128
STEP = 5


logit_divisor = 0.05
keep_prob = 0.9
norm_eps = 1e-06
clip_bound = 0.001
beta_first = 0.5
beta_second = 0.5
learn_rate = 0.05
decay_rate = 0.01
adam_eps = 1e-08
ema_rate = 0.8
masked_scores = -1e30
highest = lax.Precision.HIGHEST


def layer_norm(tensor, gain_vec, shift_vec):
    center = tensor - jnp.mean(tensor, axis=-1, keepdims=True)
    spread = jnp.mean(center * center, axis=-1, keepdims=True)
    return center * lax.rsqrt(spread + norm_eps) * gain_vec + shift_vec


def gelu_exact(tensor):
    return 0.5 * tensor * (1.0 + jax.scipy.special.erf(tensor * 0.7071067811865476))


def unit_scale(tensor):
    return tensor * lax.rsqrt(jnp.sum(tensor * tensor, axis=-1, keepdims=True) + norm_eps)


def bucket_length(bucket_code):
    return (LMIN * jnp.where(bucket_code == 0, 1, jnp.where(bucket_code == 1, 2, 4))).astype(
        jnp.int32
    )


def plain_dot(left_op, right_op):
    return jnp.dot(left_op, right_op, preferred_element_type=jnp.float32)


def rows_dot(left_op, right_op):
    return lax.dot_general(
        left_op, right_op, (((0,), (0,)), ((), ())), preferred_element_type=jnp.float32
    )


def target_dot_terms(left_op, right_op):
    return lax.dot_general(
        left_op, right_op, (((1,), (1,)), ((), ())), preferred_element_type=jnp.float32
    )


def adam_step(grad_flat, params, moment, second, average):
    first_new = beta_first * moment + (1.0 - beta_first) * grad_flat
    second_new = beta_second * second + (1.0 - beta_second) * grad_flat * grad_flat
    fix_first = 1.0 - beta_first**STEP
    fix_second = 1.0 - beta_second**STEP
    adam_dir = first_new / fix_first / (jnp.sqrt(second_new / fix_second) + adam_eps)
    updated = params - learn_rate * (adam_dir + decay_rate * params)
    average_new = ema_rate * average + (1.0 - ema_rate) * updated
    return (first_new, second_new, updated, average_new)


LANES = 128
VMEM_CAP = 60 * 2**20
CORE, XBIT, YBIT, ZBITS = 1, 2, 4, (8, 16, 24)


def swap(value, bit):
    count = lax.axis_size("sent")
    return lax.ppermute(value, "sent", [(i, i ^ bit) for i in range(count)])


def is_grid(count, *shards):
    return count == 32 and all(2 * shard % LANES == 0 for shard in shards)


def block_rows(shard):
    return -(-(-(-shard // LANES) + 8) // 16) * 16


def first_row(device, shard):
    return (device * shard) // LANES


def pack_shard(values, device):
    shard = values.shape[0]
    rows = block_rows(shard)
    size = rows * LANES
    odd = (device * shard) % LANES != 0
    lead = jnp.where(
        odd,
        jnp.pad(values, (LANES // 2, size - shard - LANES // 2)),
        jnp.pad(values, (0, size - shard)),
    ).reshape(rows, LANES)
    offset = first_row(device, shard) % 8
    padded = jnp.pad(lead, ((8, 0), (0, 0)))
    return lax.dynamic_slice(padded, (8 - offset, 0), (rows, LANES)).astype(jnp.bfloat16)


def unpack_shard(block, device, shard):
    rows = -(-shard // LANES)
    offset = first_row(device, shard) % 8
    odd = (device * shard) % LANES != 0
    flat = lax.dynamic_slice(block, (offset, 0), (rows, LANES)).reshape(-1)
    longer = jnp.pad(flat, (0, LANES))
    return jnp.where(odd, longer[LANES // 2 : LANES // 2 + shard], flat[:shard])


WHOLE = ((0, 0, 4), (1, 0, 4), (2, 0, 4), (3, 0, 2), (3, 2, 2))
HALVES = tuple((across, first, 2) for across in range(4) for first in (0, 2))


def piece_slots(me, layout):
    slots = []
    for core in (0, 1):
        for across, first, n in layout:
            slots.append([me ^ (core + 2 * across + 8 * (first + k)) for k in range(n)])
    return slots


def after(value, *others):
    return lax.optimization_barrier((value, others))[0]


def with_sibling(own):
    return tuple(own) + tuple(swap(piece, CORE) for piece in own)


def gather_attn(values, device):
    block = pack_shard(values, device)
    zs = [swap(block, bit) for bit in ZBITS]
    line = jnp.stack([block] + zs)
    x, y = swap(line, XBIT), swap(line, YBIT)
    diagonal = (swap(y[:2], XBIT), swap(x[2:], YBIT))
    return with_sibling((line, x, y) + diagonal), zs[0], diagonal


def gather_head_line(values, device, first):
    block = after(pack_shard(values, device), first)
    return [block] + [swap(block, bit) for bit in ZBITS]


def gather_head(line, x, y):
    return with_sibling((line, x, y, swap(y[:2], XBIT), swap(x[2:], YBIT)))


def low_sum(*terms):
    total = terms[0].astype(jnp.float32)
    for term in terms[1:]:
        total = total + term.astype(jnp.float32)
    return total.astype(jnp.bfloat16)


def scatter_core(pieces):
    half = len(pieces) // 2
    got = [swap(piece, CORE) for piece in reversed(pieces[half:])][::-1]
    return [low_sum(piece, other) for piece, other in zip(pieces[:half], got)]


def scatter_attn(sums):
    line, x, y, d_low, d_high = sums
    d_low, d_high = swap(d_low, XBIT), swap(d_high, YBIT)
    x = swap(jnp.concatenate([x[:2], low_sum(x[2:], d_high)]), XBIT)
    y = swap(jnp.concatenate([low_sum(y[:2], d_low), y[2:]]), YBIT)
    line = low_sum(line, x, y)
    return scatter_along(line[0], [line[k] for k in (1, 2, 3)])


def scatter_along(own, others):
    total = own.astype(jnp.float32)
    for value, bit in zip(others, ZBITS):
        total = total + swap(value, bit).astype(jnp.float32)
    return total


def plain_rows(left, right, dims):
    return lax.dot_general(left, right, (dims, ((), ())), preferred_element_type=jnp.float32)


NN, NT, TN = ((1,), (0,)), ((1,), (1,)), ((0,), (0,))


def one_hot(shape, left, right):
    rows = lax.broadcasted_iota(jnp.int32, shape, 0)
    cols = lax.broadcasted_iota(jnp.int32, shape, 1)
    return jnp.where(left(rows, cols) == right(rows, cols), 1.0, 0.0)


def vectors_of(flat_rows):
    spread = one_hot((D, 48), lambda r, c: r >> 4, lambda r, c: c).astype(jnp.bfloat16)
    rows = plain_rows(spread, flat_rows.astype(jnp.bfloat16), NN)
    rows = rows * one_hot((D, LANES), lambda r, c: r & 15, lambda r, c: c >> 3)
    fold = one_hot((8, LANES), lambda r, c: r, lambda r, c: c & 7).astype(jnp.bfloat16)
    return plain_rows(fold, rows.astype(jnp.bfloat16), NT)


def flat_of(vectors):
    fold = one_hot((8, LANES), lambda r, c: r, lambda r, c: c & 7).astype(jnp.bfloat16)
    rows = plain_rows(vectors.astype(jnp.bfloat16), fold, TN)
    rows = rows * one_hot((D, LANES), lambda r, c: r & 15, lambda r, c: c >> 3)
    spread = one_hot((D, 48), lambda r, c: r >> 4, lambda r, c: c).astype(jnp.bfloat16)
    return plain_rows(spread, rows.astype(jnp.bfloat16), TN)


def keep_of(mask):
    return mask.astype(jnp.float32) * (1.0 / keep_prob)


def place_blocks(shard, layout, pieces, me, stage, flat, sems):
    count, rows = stage.shape[0], stage.shape[1]
    for piece, slots in zip(pieces, piece_slots(me, layout)):
        for k, slot in enumerate(slots):
            pltpu.make_async_copy(piece.at[k], stage.at[slot], sems.at[slot]).start()
    flat[pl.ds(0, 8), :] = jnp.zeros((8, LANES), jnp.float32)

    def place(device, carry):
        pltpu.make_async_copy(pieces[0].at[0], stage.at[device], sems.at[device]).wait()
        at = pl.multiple_of(device * shard // LANES // 8 * 8, 8)
        before = flat[pl.ds(at, 8), :]
        flat[pl.ds(at, rows), :] = stage[device].astype(jnp.float32)
        flat[pl.ds(at, 8), :] += before
        return carry

    lax.fori_loop(0, count, place, 0)


def gather_matrix(flat, w_ref, w_out, out_sems):
    cols = w_ref.shape[1] // LANES

    def gather_rows(group, carry):
        at = pl.multiple_of(group * 16, 16)
        for col in range(cols):
            rows16 = flat[pl.ds(group * 16 * cols + col, 16, stride=cols), :]
            w_ref[pl.ds(at, 16), pl.ds(col * LANES, LANES)] = rows16.astype(jnp.bfloat16)
        return carry

    parts = 4
    span = D // parts
    copies = []
    for part in range(parts):
        lax.fori_loop(part * span // 16, (part + 1) * span // 16, gather_rows, 0)
        here = pl.ds(part * span, span)
        copies.append(pltpu.make_async_copy(w_ref.at[here], w_out.at[here], out_sems.at[part]))
        copies[-1].start()
    return copies


VEC = 8 + POS


def table_of(flat, base, body, tail):
    lane = lax.broadcasted_iota(jnp.int32, (D // 16, LANES), 1)
    for q in range(16):
        here = flat[pl.ds(base + q, D // 16, stride=17), :]
        later = flat[pl.ds(base + q + 1, D // 16, stride=17), :]
        both = jnp.where(lane >= 8 * q, here, later)
        shift = (LANES - 8 * q) % LANES
        body[pl.ds(q, D // 16, stride=16), :] = pltpu.roll(both, shift, 1) if shift else both
        tail[pl.ds(q, D // 16, stride=16), :] = pltpu.roll(later, shift, 1) if shift else later
    return body[...].T, tail[...].T[:8]


def flat_table(flat, base, first, last, body, tail):
    body[...] = first.T
    tail[...] = jnp.concatenate([last, jnp.zeros((LANES - 8, D), jnp.float32)]).T
    lane = lax.broadcasted_iota(jnp.int32, (D // 16, LANES), 1)
    carried = None
    for q in range(17):
        row = carried
        if q < 16:
            main = body[pl.ds(q, D // 16, stride=16), :]
            end = tail[pl.ds(q, D // 16, stride=16), :]
            if q:
                main, end = pltpu.roll(main, 8 * q, 1), pltpu.roll(end, 8 * q, 1)
            row = main if carried is None else jnp.where(lane >= 8 * q, main, carried)
            carried = jnp.where(lane < 8 * q, main, end)
        flat[pl.ds(base + q, D // 16, stride=17), :] = row


def repeat_places(table, length):
    twice = jnp.concatenate([table[:64]] * 2)
    four = jnp.concatenate([table[:32]] * 4)
    return jnp.where(length == 128, table, jnp.where(length == 64, twice, four))


def fold_places(rows, length):
    half = rows[:64] + rows[64:]
    quarter = half[:32] + half[32:]
    none = jnp.zeros_like(rows)
    twice = jnp.concatenate([half, none[:64]])
    four = jnp.concatenate([quarter, none[:96]])
    return jnp.where(length == 128, rows, jnp.where(length == 64, twice, four))


def stack_heads(pair):
    lane = lax.broadcasted_iota(jnp.int32, pair.shape, 1)
    none = jnp.zeros_like(pair)
    return jnp.concatenate([jnp.where(lane < HD, pair, none), jnp.where(lane < HD, none, pair)])


def unstack_heads(rows):
    half = rows.shape[0] // 2
    lane = lax.broadcasted_iota(jnp.int32, (half, rows.shape[1]), 1)
    return jnp.where(lane < HD, rows[:half], rows[half:])


ROWS = 32


def attn_kernel(shard, me_ref, length_ref, lens_ref, *refs):
    pieces, (emb_ref, mask_hbm) = refs[:10], refs[10:12]
    (w_out, vec_ref, rows_ref, in_low_ref, qkv_ref, prob_ref, mixed_ref, res_ref, norm_ref, low_ref) = refs[12:22]
    (stage, flat, w_ref, body, tail, mask, attn_in, bias_ref, sems, out_sems, mask_sems) = refs[22:]
    me = me_ref[0]
    tokens = emb_ref.shape[0]
    masks = []
    for view in range(2):
        for which in range(2):
            at = 2 * view + which
            masks.append(pltpu.make_async_copy(mask_hbm.at[view, which], mask.at[at], mask_sems.at[at]))
            masks[-1].start()
    place_blocks(shard, WHOLE, pieces, me, stage, flat, sems)
    copies = gather_matrix(flat, w_ref, w_out, out_sems)
    first, last = table_of(flat, D * w_ref.shape[1] // LANES, body, tail)
    vecs = first[:8]
    vec_ref[...] = vecs
    length = length_ref[0]
    places = repeat_places(jnp.concatenate([first[8:], last]), length)
    for copy in masks:
        copy.wait()
    for block in range(tokens // LANES):
        key = lax.broadcasted_iota(jnp.int32, (LANES, LANES), 1) + block * LANES
        query = lax.broadcasted_iota(jnp.int32, (LANES, LANES), 0) + block * LANES
        shift = jnp.where(length == 128, 7, jnp.where(length == 64, 6, 5))
        sent = lax.shift_right_logical(key, jnp.full_like(key, 1) * shift)
        sent_q = lax.shift_right_logical(query, jnp.full_like(key, 1) * shift)
        real = jnp.zeros_like(key)
        for slot in range(lens_ref.shape[0]):
            real = jnp.where(sent == slot, lens_ref[slot], real)
        ok = (sent == sent_q) & ((key & (length - 1)) < real)
        bias_ref[block] = jnp.where(ok, 0.0, masked_scores)
        here = pl.ds(block * LANES, LANES)
        emb = emb_ref[here, :].astype(jnp.float32) + places + vecs[7:8]
        rows_ref[here, :] = emb
        normed = layer_norm(emb, vecs[5:6], vecs[6:7])
        for view in range(2):
            at = pl.ds(view * tokens + block * LANES, LANES)
            given = normed * keep_of(mask[2 * view, here, :])
            attn_in[at, :] = given
            in_low_ref[at, :] = given.astype(jnp.bfloat16)
    for part in range(3):
        cols = pl.ds(part * D, D)
        made = plain_rows(in_low_ref[...], w_ref[:, cols], NN)
        if part != 1:
            made = made + vecs[part // 2 : part // 2 + 1]
        qkv_ref[:, cols] = made.astype(jnp.bfloat16)

    def attend(block, carry):
        here = pl.ds(pl.multiple_of(block * LANES, LANES), LANES)
        bias = bias_ref[block & 1]
        bias = jnp.concatenate([bias, bias])
        for pair in range(H // 2):
            q = stack_heads(qkv_ref[here, pl.ds(pair * LANES, LANES)])
            k = qkv_ref[here, pl.ds(D + pair * LANES, LANES)]
            v = qkv_ref[here, pl.ds(2 * D + pair * LANES, LANES)]
            scores = plain_rows(q, k, NT) * HD ** (-0.5) + bias
            expo = jnp.exp(scores - jnp.max(scores, axis=-1, keepdims=True))
            probs = expo / jnp.sum(expo, axis=-1, keepdims=True)
            prob_ref[block, pair] = probs
            mixed = unstack_heads(plain_rows(probs.astype(jnp.bfloat16), v, NN))
            mixed_ref[here, pl.ds(pair * LANES, LANES)] = mixed.astype(jnp.bfloat16)
        return carry

    lax.fori_loop(0, 2 * tokens // LANES, attend, 0)
    res_ref[...] = plain_rows(mixed_ref[...], w_ref[:, 3 * D :], NN)
    for view in range(2):
        def finish(chunk, carry, view=view):
            own = pl.ds(pl.multiple_of(chunk * ROWS, ROWS), ROWS)
            at = pl.ds(pl.multiple_of(view * tokens + chunk * ROWS, ROWS), ROWS)
            res = attn_in[at, :] + keep_of(mask[2 * view + 1, own, :]) * (res_ref[at, :] + vecs[2:3])
            res_ref[at, :] = res
            norm = layer_norm(res, vecs[3:4], vecs[4:5])
            norm_ref[at, :] = norm
            low_ref[at, :] = norm.astype(jnp.bfloat16)
            return carry

        lax.fori_loop(0, tokens // ROWS, finish, 0)
    for copy in copies:
        copy.wait()


def attn_forward(pieces, me, shard, length, lengths, embeddings, masks):
    rows = pieces[0].shape[1]
    whole = shard * 32 // LANES
    tokens = embeddings.shape[0]
    both = 2 * tokens
    any_space, vmem = pl.BlockSpec(memory_space=pl.ANY), pl.BlockSpec(memory_space=pltpu.VMEM)
    smem = pl.BlockSpec(memory_space=pltpu.SMEM)
    f32, low = jnp.float32, jnp.bfloat16
    shapes = [
        ((D, 4 * D), low),
        ((8, D), f32),
        ((tokens, D), f32),
        ((both, D), low),
        ((both, 3 * D), low),
        ((both // LANES, H // 2, 2 * LANES, LANES), f32),
        ((both, D), low),
        ((both, D), f32),
        ((both, D), f32),
        ((both, D), low),
    ]
    return pl.pallas_call(
        functools.partial(attn_kernel, shard),
        out_shape=tuple(jax.ShapeDtypeStruct(*s) for s in shapes),
        in_specs=[smem] * 3 + [any_space] * len(pieces) + [vmem, any_space],
        out_specs=(any_space,) + (vmem,) * 9,
        scratch_shapes=[
            pltpu.VMEM((32, rows, LANES), low),
            pltpu.VMEM((whole + rows, LANES), f32),
            pltpu.VMEM((D, 4 * D), low),
            pltpu.VMEM((D, LANES), f32),
            pltpu.VMEM((D, LANES), f32),
            pltpu.VMEM((4, tokens, D), jnp.int32),
            pltpu.VMEM((both, D), f32),
            pltpu.VMEM((tokens // LANES, LANES, LANES), f32),
            pltpu.SemaphoreType.DMA((32,)),
            pltpu.SemaphoreType.DMA((4,)),
            pltpu.SemaphoreType.DMA((4,)),
        ],
        compiler_params=pltpu.CompilerParams(vmem_limit_bytes=VMEM_CAP),
    )(jnp.reshape(me, (1,)), jnp.reshape(length, (1,)), lengths, *pieces, embeddings, masks)


def sum_rows(rows):
    return jnp.sum(rows, axis=0, keepdims=True)


def norm_back_kernel(pick_ref, d_first, d_cls, res_ref, vec_ref, mask_hbm, mixed_ref, w_ref,
                     d_res_ref, g_out_ref, d_mixed, part_ref, mask, given, branch, mask_sems):
    tokens = mask.shape[1]
    both = 2 * tokens
    masks = []
    for view in range(2):
        masks.append(pltpu.make_async_copy(mask_hbm.at[view, 1], mask.at[view], mask_sems.at[view]))
        masks[-1].start()
    given[...] = d_first[...]
    n = d_cls.shape[0] // 2
    for slot in range(n):
        real = jnp.where(slot < pick_ref[n], 1.0, 0.0)
        for view in range(2):
            at = pl.ds(view * tokens + pick_ref[slot], 1)
            given[at, :] += real * d_cls[view * n + slot : view * n + slot + 1, :]
    for copy in masks:
        copy.wait()
    gain = vec_ref[3:4, :]
    sums = tuple(jnp.zeros((1, D), jnp.float32) for _ in range(3))
    for view in range(2):
        def one_chunk(chunk, sums, view=view):
            own = pl.ds(pl.multiple_of(chunk * ROWS, ROWS), ROWS)
            at = pl.ds(pl.multiple_of(view * tokens + chunk * ROWS, ROWS), ROWS)
            grad = given[at, :]
            center, inv = norm_parts(res_ref[at, :])
            d_res, unit = norm_back(grad, center, inv, gain)
            d_branch = d_res * keep_of(mask[view, own, :])
            d_res_ref[at, :] = d_res
            branch[at, :] = d_branch.astype(jnp.bfloat16)
            return (
                sums[0] + sum_rows(d_branch),
                sums[1] + sum_rows(grad * unit),
                sums[2] + sum_rows(grad),
            )

        sums = lax.fori_loop(0, tokens // ROWS, one_chunk, sums)
    d_mixed[...] = plain_rows(branch[...], w_ref[...], NT).astype(jnp.bfloat16)
    g_out_ref[...] = plain_rows(mixed_ref[...], branch[...], TN).astype(jnp.bfloat16)
    for k in range(3):
        part_ref[k : k + 1, :] = sums[k]
    part_ref[3:8, :] = jnp.zeros((5, D), jnp.float32)


def norm_backward(picks, d_first, d_cls, res, vecs, masks, mixed, w_attn):
    both = res.shape[0]
    any_space, vmem = pl.BlockSpec(memory_space=pl.ANY), pl.BlockSpec(memory_space=pltpu.VMEM)
    f32, low = jnp.float32, jnp.bfloat16
    shapes = [((both, D), f32), ((D, D), low), ((both, D), low), ((8, D), f32)]
    return pl.pallas_call(
        norm_back_kernel,
        out_shape=tuple(jax.ShapeDtypeStruct(*s) for s in shapes),
        grid=(1,),
        in_specs=[pl.BlockSpec(memory_space=pltpu.SMEM), vmem, vmem, vmem, vmem, any_space, vmem]
        + [pl.BlockSpec((D, D), lambda i: (0, 3))],
        out_specs=(vmem,) * 4,
        scratch_shapes=[
            pltpu.VMEM((2, both // 2, D), jnp.int32),
            pltpu.VMEM((both, D), f32),
            pltpu.VMEM((both, D), low),
            pltpu.SemaphoreType.DMA((2,)),
        ],
        compiler_params=pltpu.CompilerParams(vmem_limit_bytes=VMEM_CAP),
    )(picks, d_first, d_cls, res, vecs, masks, mixed, w_attn)


def attn_back_kernel(d_mixed, qkv_ref, prob_ref, d_qkv_ref, part_ref):
    part_ref[...] = jnp.zeros_like(part_ref)

    def one_block(block, carry):
        here = pl.ds(pl.multiple_of(block * LANES, LANES), LANES)
        for pair in range(H // 2):
            cols = pl.ds(pair * LANES, LANES)
            q = stack_heads(qkv_ref[here, cols])
            k = qkv_ref[here, pl.ds(D + pair * LANES, LANES)]
            v = qkv_ref[here, pl.ds(2 * D + pair * LANES, LANES)]
            d_out = stack_heads(d_mixed[here, cols])
            probs = prob_ref[block, pair]
            d_v = plain_rows(probs.astype(jnp.bfloat16), d_out, TN)
            d_probs = plain_rows(d_out, v, NT)
            delta = jnp.sum(probs * d_probs, axis=-1, keepdims=True)
            score = (probs * (d_probs - delta) * HD ** (-0.5)).astype(jnp.bfloat16)
            d_q = unstack_heads(plain_rows(score, k, NN))
            d_k = plain_rows(score, q, TN)
            d_qkv_ref[here, cols] = d_q.astype(jnp.bfloat16)
            d_qkv_ref[here, pl.ds(D + pair * LANES, LANES)] = d_k.astype(jnp.bfloat16)
            d_qkv_ref[here, pl.ds(2 * D + pair * LANES, LANES)] = d_v.astype(jnp.bfloat16)
            part_ref[0:1, cols] += sum_rows(d_q)
            part_ref[1:2, cols] += sum_rows(d_v)
        return carry

    lax.fori_loop(0, qkv_ref.shape[0] // LANES, one_block, 0)


def attn_backward(d_mixed, qkv, probs):
    vmem = pl.BlockSpec(memory_space=pltpu.VMEM)
    shapes = [(qkv.shape, jnp.bfloat16), ((8, D), jnp.float32)]
    return pl.pallas_call(
        attn_back_kernel,
        out_shape=tuple(jax.ShapeDtypeStruct(*s) for s in shapes),
        in_specs=[vmem] * 3,
        out_specs=(vmem,) * 2,
        compiler_params=pltpu.CompilerParams(vmem_limit_bytes=VMEM_CAP),
    )(d_mixed, qkv, probs)


def attn_grad_kernel(shard, me_ref, length_ref, d_qkv, in_low, w_ref, d_res, rows_ref, vec_ref, mask_hbm, g_out,
                     part_ref, norm_part_ref, input_ref, *refs):
    pieces, (stage, flat, body, tail, mask, d_in, sems, mask_sems) = refs[:10], refs[10:]
    cols = 4 * D // LANES
    tokens = rows_ref.shape[0]
    masks = []
    for view in range(2):
        masks.append(pltpu.make_async_copy(mask_hbm.at[view, 0], mask.at[view], mask_sems.at[view]))
        masks[-1].start()
    d_in[...] = plain_rows(d_qkv[...], w_ref[...], NT)
    for copy in masks:
        copy.wait()
    gain = vec_ref[5:6, :]

    def one_chunk(chunk, sums):
        own = pl.ds(pl.multiple_of(chunk * ROWS, ROWS), ROWS)
        other = pl.ds(pl.multiple_of(tokens + chunk * ROWS, ROWS), ROWS)
        grad = (d_in[own, :] + d_res[own, :]) * keep_of(mask[0, own, :])
        grad = grad + (d_in[other, :] + d_res[other, :]) * keep_of(mask[1, own, :])
        center, inv = norm_parts(rows_ref[own, :])
        back, unit = norm_back(grad, center, inv, gain)
        input_ref[own, :] = back
        return (sums[0] + sum_rows(grad * unit), sums[1] + sum_rows(grad), sums[2] + sum_rows(back))

    sums = lax.fori_loop(
        0, tokens // ROWS, one_chunk, tuple(jnp.zeros((1, D), jnp.float32) for _ in range(3))
    )
    table = jnp.zeros((LANES, D), jnp.float32)
    for block in range(tokens // LANES):
        table = table + input_ref[block * LANES : (block + 1) * LANES, :]
    table = fold_places(table, length_ref[0])
    first = jnp.concatenate([part_ref[0:2, :], norm_part_ref[0:3, :], *sums, table[: LANES - 8]])
    base = D * cols
    flat_table(flat, base, first, table[LANES - 8 :], body, tail)
    span, width = 256, 3 * LANES

    def one_block(block, carry):
        left = in_low[:, pl.ds(pl.multiple_of(block * span, span), span)]
        for k in range(3 * D // width):
            grads = plain_rows(left, d_qkv[:, pl.ds(k * width, width)], TN)
            for col in range(width // LANES):
                for group in range(span // 16):
                    at = (block * span + group * 16) * cols + k * width // LANES + col
                    tile = grads[group * 16 : (group + 1) * 16, col * LANES : (col + 1) * LANES]
                    flat[pl.ds(at, 16, stride=cols), :] = tile
        return carry

    lax.fori_loop(0, D // span, one_block, 0)

    def one_group(group, carry):
        at = pl.multiple_of(group * 16, 16)
        for col in range(D // LANES):
            tile = g_out[pl.ds(at, 16), pl.ds(col * LANES, LANES)].astype(jnp.float32)
            flat[pl.ds(group * 16 * cols + 3 * D // LANES + col, 16, stride=cols), :] = tile
        return carry

    lax.fori_loop(0, D // 16, one_group, 0)
    rows = stage.shape[1]
    flat[pl.ds(base + D * VEC // LANES, rows), :] = jnp.zeros((rows, LANES), jnp.float32)
    store_pieces(shard, WHOLE, me_ref[0], pieces, stage, flat, sems)


def attn_grads(me, shard, length, d_qkv, in_low, w_attn, d_res, rows_in, vecs, masks, g_out, parts, norm_parts_in):
    rows = block_rows(shard)
    whole = shard * 32 // LANES
    tokens = rows_in.shape[0]
    counts = [len(slots) for slots in piece_slots(0, WHOLE)]
    any_space, vmem = pl.BlockSpec(memory_space=pl.ANY), pl.BlockSpec(memory_space=pltpu.VMEM)
    smem = pl.BlockSpec(memory_space=pltpu.SMEM)
    f32, low = jnp.float32, jnp.bfloat16
    return pl.pallas_call(
        functools.partial(attn_grad_kernel, shard),
        out_shape=(jax.ShapeDtypeStruct((tokens, D), f32),)
        + tuple(jax.ShapeDtypeStruct((n, rows, LANES), low) for n in counts),
        grid=(1,),
        in_specs=[smem, smem, vmem, vmem, pl.BlockSpec((D, 3 * D), lambda i: (0, 0)), vmem, vmem, vmem]
        + [any_space, vmem, vmem, vmem],
        out_specs=(vmem,) + (any_space,) * len(counts),
        scratch_shapes=[
            pltpu.VMEM((32, rows, LANES), low),
            pltpu.VMEM((whole + rows, LANES), f32),
            pltpu.VMEM((D, LANES), f32),
            pltpu.VMEM((D, LANES), f32),
            pltpu.VMEM((2, tokens, D), jnp.int32),
            pltpu.VMEM((2 * tokens, D), f32),
            pltpu.SemaphoreType.DMA((32,)),
            pltpu.SemaphoreType.DMA((2,)),
        ],
        compiler_params=pltpu.CompilerParams(vmem_limit_bytes=VMEM_CAP),
    )(jnp.reshape(me, (1,)), jnp.reshape(length, (1,)), d_qkv, in_low, w_attn, d_res, rows_in, vecs, masks, g_out, parts, norm_parts_in)


def head_kernel(shard, me_ref, pick_ref, *refs):
    pieces, (first_hbm, mask_hbm) = refs[:10], refs[10:12]
    w_out, vec_ref, unit_ref, pooled_ref, res_ref, up_ref, cls_ref, act_ref, keep_ref, low_ref = refs[12:22]
    stage, flat, w_ref, first_all, picked, mask, sems, out_sems, in_sems = refs[22:]
    cols = w_ref.shape[1] // LANES
    tokens = mask.shape[1]
    loads = [pltpu.make_async_copy(first_hbm, first_all, in_sems.at[2])]
    for view in range(2):
        loads.append(pltpu.make_async_copy(mask_hbm.at[view, 2], mask.at[view], in_sems.at[view]))
    for load in loads:
        load.start()
    place_blocks(shard, WHOLE, pieces, me_ref[0], stage, flat, sems)
    copies = gather_matrix(flat, w_ref, w_out, out_sems)
    for load in loads:
        load.wait()
    n = unit_ref.shape[0] // 2
    for view in range(2):
        for slot in range(n):
            at, to = pick_ref[slot], view * n + slot
            picked[to : to + 1, :] = first_all[pl.ds(view * tokens + at, 1), :]
            keep_ref[to : to + 1, :] = keep_of(mask[view, pl.ds(at, 1), :])
    vecs = vectors_of(flat[pl.ds(D * cols, 48), :])
    vec_ref[...] = vecs
    first = picked[...]
    low_ref[...] = first.astype(jnp.bfloat16)
    up_bias = jnp.concatenate([vecs[c : c + 1] for c in range(4)], axis=1)
    up_pre = plain_rows(first.astype(jnp.bfloat16), w_ref[:, : 4 * D], NN) + up_bias
    active = gelu_exact(up_pre).astype(jnp.bfloat16)
    down = plain_rows(active, w_ref[:, 4 * D : 8 * D], NT) + vecs[4:5]
    res = first + keep_ref[...] * down
    cls_low = layer_norm(res, vecs[5:6], vecs[6:7]).astype(jnp.bfloat16)
    pooled = jnp.tanh(plain_rows(cls_low, w_ref[:, 8 * D :], NN) + vecs[7:8])
    unit_ref[...] = unit_scale(pooled).astype(jnp.bfloat16)
    pooled_ref[...] = pooled
    res_ref[...] = res
    up_ref[...] = up_pre
    cls_ref[...] = cls_low
    act_ref[...] = active
    for copy in copies:
        copy.wait()


def make_head(pieces, me, shard, picks, first_norm, masks):
    rows = pieces[0].shape[1]
    whole = shard * 32 // LANES
    n = 2 * (picks.shape[0] - 1)
    any_space, vmem = pl.BlockSpec(memory_space=pl.ANY), pl.BlockSpec(memory_space=pltpu.VMEM)
    smem = pl.BlockSpec(memory_space=pltpu.SMEM)
    f32, low = jnp.float32, jnp.bfloat16
    shapes = [
        ((D, 9 * D), low),
        ((8, D), f32),
        ((n, D), low),
        ((n, D), f32),
        ((n, D), f32),
        ((n, 4 * D), f32),
        ((n, D), low),
        ((n, 4 * D), low),
        ((n, D), f32),
        ((n, D), low),
    ]
    return pl.pallas_call(
        functools.partial(head_kernel, shard),
        out_shape=tuple(jax.ShapeDtypeStruct(*s) for s in shapes),
        in_specs=[smem] * 2 + [any_space] * (len(pieces) + 2),
        out_specs=(any_space,) + (vmem,) * 9,
        scratch_shapes=[
            pltpu.VMEM((32, rows, LANES), low),
            pltpu.VMEM((whole + rows, LANES), f32),
            pltpu.VMEM((D, 9 * D), low),
            pltpu.VMEM(first_norm.shape, f32),
            pltpu.VMEM((n, D), f32),
            pltpu.VMEM((2,) + masks.shape[2:], jnp.int32),
            pltpu.SemaphoreType.DMA((32,)),
            pltpu.SemaphoreType.DMA((4,)),
            pltpu.SemaphoreType.DMA((3,)),
        ],
        compiler_params=pltpu.CompilerParams(vmem_limit_bytes=VMEM_CAP),
    )(jnp.reshape(me, (1,)), picks, *pieces, first_norm, masks)


def norm_back(grad, center, inv, gain):
    unit = center * inv
    scaled = grad * gain
    mean = jnp.mean(scaled, axis=-1, keepdims=True)
    along = jnp.mean(scaled * unit, axis=-1, keepdims=True)
    return inv * (scaled - mean - unit * along), unit


def norm_parts(rows):
    center = rows - jnp.mean(rows, axis=-1, keepdims=True)
    return center, lax.rsqrt(jnp.mean(center * center, axis=-1, keepdims=True) + norm_eps)


def gelu_slope(values):
    cdf = 0.5 * (1.0 + lax.erf(values * 0.7071067811865476))
    return cdf + values * (0.3989422804014327 * jnp.exp(-0.5 * values * values))


def pooled_kernel(me_ref, own_ref, sib_ref, w_hbm, vrow_ref, vcol_ref, vec_ref, pooled_ref, res_ref,
                  up_ref, keep_ref, loss_ref, pool_ref, down_ref, uplow_ref, first_ref, part_ref,
                  units, sims, back, w_ref, sems, w_sems):
    me = me_ref[0]
    w_copies = []
    for k, (start, size) in enumerate(((8 * D, D), (4 * D, 4 * D), (0, 4 * D))):
        here = pl.ds(start, size)
        w_copies.append(pltpu.make_async_copy(w_hbm.at[:, here], w_ref.at[:, here], w_sems.at[k]))
    copies = []
    for core, ref in ((0, own_ref), (1, sib_ref)):
        for across in range(4):
            for k in range(4):
                slot = me ^ (core + 2 * across + 8 * k)
                copies.append(
                    pltpu.make_async_copy(ref.at[across, k], units.at[slot], sems.at[len(copies)])
                )
    for copy in copies + w_copies:
        copy.start()
    for copy in copies:
        copy.wait()
    n = units.shape[1]
    half = n // 2
    total = units.shape[0] * n
    everyone = units[...].reshape(total, D)
    table = plain_rows(everyone, everyone, NT) * (1.0 / logit_divisor)
    row = lax.broadcasted_iota(jnp.int32, (total, total), 0)
    col = lax.broadcasted_iota(jnp.int32, (total, total), 1)
    valid_row = vrow_ref[...] > 0
    table = jnp.where(((col & (n - 1)) >= half) & (vcol_ref[...] > 0), table, masked_scores)
    top = jnp.max(table, axis=-1, keepdims=True)
    row_lse = top + jnp.log(jnp.sum(jnp.exp(table - top), axis=-1, keepdims=True))
    diagonal = col == row + half
    positive = jnp.sum(jnp.where(diagonal, table, 0.0), axis=-1, keepdims=True)
    row_one = lax.broadcasted_iota(jnp.int32, (total, 1), 0)
    anchors = ((row_one & (n - 1)) < half) & valid_row
    loss_ref[0, 0] = jnp.sum(jnp.where(anchors, row_lse - positive, 0.0))
    slope = (jnp.exp(table - row_lse) - jnp.where(diagonal, 1.0, 0.0)) * (1.0 / logit_divisor)
    sims[...] = jnp.where(anchors, slope, 0.0).astype(jnp.bfloat16)
    back[...] = plain_rows(sims[...], everyone, TN)
    mine = pl.ds(pl.multiple_of(me * n, n), n)
    d_unit = plain_rows(sims[mine, :], everyone, NN) + back[mine, :]
    pooled = pooled_ref[...]
    inv = lax.rsqrt(jnp.sum(pooled * pooled, axis=-1, keepdims=True) + norm_eps)
    along = jnp.sum(pooled * d_unit, axis=-1, keepdims=True)
    d_pooled = inv * d_unit - pooled * (inv * inv * inv * along)
    d_pre = d_pooled * (1.0 - pooled * pooled)
    pool_low = d_pre.astype(jnp.bfloat16)
    pool_ref[...] = pool_low
    w_copies[0].wait()
    d_cls = plain_rows(pool_low, w_ref[:, 8 * D :], NT)
    center, scale = norm_parts(res_ref[...])
    d_res, unit = norm_back(d_cls, center, scale, vec_ref[5:6, :])
    d_down = d_res * keep_ref[...]
    down_low = d_down.astype(jnp.bfloat16)
    down_ref[...] = down_low
    w_copies[1].wait()
    d_up = plain_rows(down_low, w_ref[:, 4 * D : 8 * D], NN) * gelu_slope(up_ref[...])
    up_low = d_up.astype(jnp.bfloat16)
    uplow_ref[...] = up_low
    w_copies[2].wait()
    first_ref[...] = d_res + plain_rows(up_low, w_ref[:, : 4 * D], NT)
    up_sum = jnp.sum(d_up, axis=0, keepdims=True)
    rows = [up_sum[:, c * D : (c + 1) * D] for c in range(4)]
    rows += [jnp.sum(part, axis=0, keepdims=True) for part in (d_down, d_cls * unit, d_cls, d_pre)]
    for k, value in enumerate(rows):
        part_ref[k : k + 1, :] = value


def pooled_backward(me, own, sib, w_head, valid, vecs, pooled, res, up_pre, keep):
    n = pooled.shape[0]
    total = valid.shape[0]
    any_space, vmem = pl.BlockSpec(memory_space=pl.ANY), pl.BlockSpec(memory_space=pltpu.VMEM)
    smem = pl.BlockSpec(memory_space=pltpu.SMEM)
    f32, low = jnp.float32, jnp.bfloat16
    shapes = [((1, 1), f32), ((n, D), low), ((n, D), low), ((n, 4 * D), low), ((n, D), f32), ((8, D), f32)]
    return pl.pallas_call(
        pooled_kernel,
        out_shape=tuple(jax.ShapeDtypeStruct(*s) for s in shapes),
        in_specs=[smem] + [any_space] * 3 + [vmem] * 7,
        out_specs=(smem,) + (vmem,) * 5,
        scratch_shapes=[
            pltpu.VMEM((32, n, D), low),
            pltpu.VMEM((total, total), low),
            pltpu.VMEM((total, D), f32),
            pltpu.VMEM((D, 9 * D), low),
            pltpu.SemaphoreType.DMA((32,)),
            pltpu.SemaphoreType.DMA((3,)),
        ],
        compiler_params=pltpu.CompilerParams(vmem_limit_bytes=VMEM_CAP),
    )(jnp.reshape(me, (1,)), own, sib, w_head, valid[:, None], valid[None, :], vecs, pooled, res, up_pre, keep)


def head_grad_kernel(shard, me_ref, *refs):
    (first, first_cls, up, up_cls, down, down_cls, act, act_cls, cls_ref, pool_ref, vec_ref) = refs[:11]
    pieces, (first_all, up_all, down_all, act_all, stage, flat, sems, in_sems) = refs[11:27], refs[27:]
    count, rows = stage.shape[0], stage.shape[1]
    cols = 9 * D // LANES
    me = me_ref[0]
    many, few = first.shape[0], first_cls.shape[0]
    loads = []
    for main, extra, whole in (
        (first, first_cls, first_all),
        (up, up_cls, up_all),
        (down, down_cls, down_all),
        (act, act_cls, act_all),
    ):
        loads.append(pltpu.make_async_copy(main, whole.at[pl.ds(0, many)], in_sems.at[len(loads)]))
        loads.append(pltpu.make_async_copy(extra, whole.at[pl.ds(many, few)], in_sems.at[len(loads)]))
    for load in loads:
        load.start()
    span = 256

    def fill(left, right, first_col, width):
        def one_block(block, carry):
            part = left[:, pl.ds(pl.multiple_of(block * span, span), span)]
            for k in range(right.shape[1] // width):
                grads = plain_rows(part, right[:, pl.ds(k * width, width)], TN)
                for col in range(width // LANES):
                    for group in range(span // 16):
                        at = (block * span + group * 16) * cols + first_col + k * width // LANES + col
                        tile = grads[group * 16 : (group + 1) * 16, col * LANES : (col + 1) * LANES]
                        flat[pl.ds(at, 16, stride=cols), :] = tile
            return carry

        lax.fori_loop(0, D // span, one_block, 0)

    fill(cls_ref, pool_ref, 8 * D // LANES, 256)
    for load in loads[:4]:
        load.wait()
    fill(first_all, up_all, 0, 512)
    for load in loads[4:]:
        load.wait()
    fill(down_all, act_all, 4 * D // LANES, 512)
    flat[pl.ds(D * cols, 48), :] = flat_of(vec_ref[...])
    flat[pl.ds(D * cols + 48, rows), :] = jnp.zeros((rows, LANES), jnp.float32)
    store_pieces(shard, HALVES, me, pieces, stage, flat, sems)


def store_pieces(shard, layout, me, pieces, stage, flat, sems):
    rows = stage.shape[1]
    copies = []
    for piece, slots in list(zip(pieces, piece_slots(me, layout)))[::-1]:
        for k, slot in enumerate(slots):
            at = pl.multiple_of(slot * shard // LANES // 8 * 8, 8)
            stage[slot] = flat[pl.ds(at, rows), :].astype(jnp.bfloat16)
            copy = pltpu.make_async_copy(stage.at[slot], piece.at[k], sems.at[len(copies)])
            copy.start()
            copies.append(copy)
    for copy in copies:
        copy.wait()


def head_grads(me, shard, first, first_cls, up, up_cls, down, down_cls, act, act_cls, cls_low, pool_low, vecs):
    rows = block_rows(shard)
    whole = shard * 32 // LANES
    counts = [len(slots) for slots in piece_slots(0, HALVES)]
    any_space, vmem = pl.BlockSpec(memory_space=pl.ANY), pl.BlockSpec(memory_space=pltpu.VMEM)
    low = jnp.bfloat16
    many = first.shape[0] + first_cls.shape[0]
    return pl.pallas_call(
        functools.partial(head_grad_kernel, shard),
        out_shape=tuple(jax.ShapeDtypeStruct((n, rows, LANES), low) for n in counts),
        in_specs=[pl.BlockSpec(memory_space=pltpu.SMEM)] + [any_space] * 8 + [vmem] * 3,
        out_specs=(any_space,) * len(counts),
        scratch_shapes=[
            pltpu.VMEM((many, D), low),
            pltpu.VMEM((many, 4 * D), low),
            pltpu.VMEM((many, D), low),
            pltpu.VMEM((many, 4 * D), low),
            pltpu.VMEM((32, rows, LANES), low),
            pltpu.VMEM((whole + rows, LANES), jnp.float32),
            pltpu.SemaphoreType.DMA((32,)),
            pltpu.SemaphoreType.DMA((8,)),
        ],
        compiler_params=pltpu.CompilerParams(vmem_limit_bytes=VMEM_CAP),
    )(jnp.reshape(me, (1,)), first, first_cls, up, up_cls, down, down_cls, act, act_cls, cls_low, pool_low, vecs)


def gather_small(value):
    got = jnp.stack([value] + [swap(value, bit) for bit in ZBITS])
    got = jnp.stack([got] + [swap(got, bit) for bit in (XBIT, YBIT, XBIT | YBIT)])
    return got, swap(got, CORE)


def sum_small(value):
    for bit in (CORE, XBIT, YBIT, 8, 16):
        value = value + swap(value, bit)
    return value


def on_grid(
    embeddings,
    cotangent,
    drop_masks,
    lengths,
    buckets,
    attn_params,
    attn_moment,
    attn_second,
    attn_ema,
    head_params,
    head_moment,
    head_second,
    head_ema,
):
    tok_rows = embeddings.shape[0]
    slot_count = lengths.shape[0]
    all_rows = 2 * tok_rows
    device = lax.axis_index("sent")
    shards = (attn_params.shape[0], head_params.shape[0])
    attn_pieces, attn_first, attn_last = gather_attn(attn_params, device)
    head_zs = gather_head_line(head_params, device, attn_first)
    bucket_all = bucket_length(buckets)
    slot_ids = jnp.arange(slot_count, dtype=jnp.int32)
    valid_everything = (
        (slot_ids[None, :] < (tok_rows // bucket_all)[:, None]).astype(jnp.float32).reshape(-1)
    )
    bucket_len = bucket_all[device]
    sent_count = tok_rows // bucket_len
    picks = jnp.concatenate(
        [jnp.minimum(slot_ids, sent_count - 1) * bucket_len, sent_count[None]]
    )
    head_line = after(jnp.stack(head_zs), *attn_last)
    head_x, head_y = swap(head_line, XBIT), swap(head_line, YBIT)
    (
        attn_mats,
        attn_vecs,
        emb_rows,
        attn_in_low,
        qkv_low,
        probs,
        mixed_low,
        first_res,
        first_norm,
        first_low,
    ) = attn_forward(attn_pieces, device, shards[0], bucket_len, lengths, embeddings, drop_masks)
    head_x, head_y, first_norm = lax.optimization_barrier((head_x, head_y, first_norm))
    head_pieces = gather_head(head_line, head_x, head_y)
    keep_ffn = (drop_masks[:, 2].astype(jnp.float32) / keep_prob).reshape(all_rows, D)
    (
        head_mats,
        head_vecs,
        unit_low,
        pooled,
        res_cls,
        up_cls,
        cls_low,
        act_cls,
        keep_cls,
        first_cls,
    ) = make_head(head_pieces, device, shards[1], picks, first_norm, drop_masks)
    units_own, units_sib = gather_small(unit_low)
    w_up = head_mats[:, : 4 * D]
    w_down = head_mats[:, 4 * D : 8 * D]
    up_pre = plain_dot(first_low, w_up) + head_vecs[:4].reshape(4 * D)
    active, gelu_back = jax.vjp(gelu_exact, up_pre)
    active_low = active.astype(jnp.bfloat16)
    down_out = target_dot_terms(active_low, w_down) + head_vecs[4]
    second_res = first_norm + keep_ffn * down_out
    second_norm, second_back = jax.vjp(layer_norm, second_res, head_vecs[5], head_vecs[6])
    hidden_out = second_norm.astype(jnp.bfloat16).reshape(2, tok_rows, D)
    d_second = cotangent.astype(jnp.float32)
    d_second_res, g_gain_two, g_shift_two = second_back(d_second.reshape(all_rows, D))
    d_down = d_second_res * keep_ffn
    g_down_bias = jnp.sum(d_down, axis=0)
    down_low = d_down.astype(jnp.bfloat16)
    d_active = plain_dot(down_low, w_down)
    d_up = gelu_back(d_active)[0]
    g_up_bias = jnp.sum(d_up, axis=0)
    up_low = d_up.astype(jnp.bfloat16)
    d_first = d_second_res + target_dot_terms(up_low, w_up)
    valid_views = jnp.broadcast_to(
        valid_everything.reshape(-1, 1, slot_count), (bucket_all.shape[0], 2, slot_count)
    ).reshape(-1)
    loss_sum, pool_low, down_cls, uplow_cls, d_first_cls, cls_parts = pooled_backward(
        device, units_own, units_sib, head_mats, valid_views, head_vecs, pooled, res_cls, up_cls, keep_cls
    )
    loss_sum = loss_sum[0, 0]
    main_parts = jnp.concatenate(
        [
            g_up_bias.reshape(4, D),
            jnp.stack([g_down_bias, g_gain_two, g_shift_two, jnp.zeros((D,), jnp.float32)]),
        ]
    )
    head_pieces = head_grads(
        device,
        shards[1],
        first_low,
        first_cls,
        up_low,
        uplow_cls,
        down_low,
        down_cls,
        active_low,
        act_cls,
        cls_low,
        pool_low,
        main_parts + cls_parts,
    )
    d_first, head_pieces = lax.optimization_barrier((d_first, head_pieces))
    line_low, line_high, x_low, x_high, y_low, y_high, d_low, d_high = scatter_core(head_pieces)
    d_first_res, g_out, d_mixed, norm_parts_in = norm_backward(
        picks, d_first, d_first_cls, first_res, attn_vecs, drop_masks, mixed_low, attn_mats
    )
    d_mixed, d_low, d_high = lax.optimization_barrier((d_mixed, d_low, d_high))
    d_low, d_high = swap(d_low, XBIT), swap(d_high, YBIT)
    d_qkv, attn_parts = attn_backward(d_mixed, qkv_low, probs)
    d_qkv, d_low, d_high = lax.optimization_barrier((d_qkv, d_low, d_high))
    x_high, y_high = swap(low_sum(x_high, d_high), XBIT), swap(y_high, YBIT)
    input_grad, *attn_pieces = attn_grads(
        device,
        shards[0],
        bucket_len,
        d_qkv,
        attn_in_low,
        attn_mats,
        d_first_res,
        emb_rows,
        attn_vecs,
        drop_masks,
        g_out,
        attn_parts,
        norm_parts_in,
    )
    attn_pieces, d_low, x_low, x_high, y_high = lax.optimization_barrier(
        (attn_pieces, d_low, x_low, x_high, y_high)
    )
    line_high = low_sum(line_high, x_high, y_high)
    x_low, y_low = swap(x_low, XBIT), swap(low_sum(y_low, d_low), YBIT)
    attn_sums = scatter_core(attn_pieces)
    attn_sums, x_low, y_low = lax.optimization_barrier((attn_sums, x_low, y_low))
    line_low = low_sum(line_low, x_low, y_low)
    head_sum = scatter_along(line_low[0], [line_low[1], line_high[0], line_high[1]])
    head_share = unpack_shard(head_sum, device, shards[1])
    attn_share = unpack_shard(scatter_attn(attn_sums), device, shards[0])
    squares = jnp.sum(attn_share * attn_share) + jnp.sum(head_share * head_share)
    total_squares = sum_small(squares)
    loss = loss_sum / jnp.sum(valid_everything)
    grad_norm = jnp.sqrt(total_squares)
    clip_scale = jnp.minimum(1.0, clip_bound / grad_norm)
    attn_new = adam_step(attn_share * clip_scale, attn_params, attn_moment, attn_second, attn_ema)
    head_new = adam_step(head_share * clip_scale, head_params, head_moment, head_second, head_ema)
    return (
        hidden_out,
        input_grad,
        loss,
        grad_norm,
        attn_new[0],
        attn_new[1],
        attn_new[2],
        attn_new[3],
        head_new[0],
        head_new[1],
        head_new[2],
        head_new[3],
    )


def on_any_mesh(
    embeddings,
    cotangent,
    drop_masks,
    lengths,
    buckets,
    attn_params,
    attn_moment,
    attn_second,
    attn_ema,
    head_params,
    head_moment,
    head_second,
    head_ema,
):
    tok_rows = embeddings.shape[0]
    slot_count = lengths.shape[0]
    all_rows = 2 * tok_rows
    device = lax.axis_index("sent")
    attn_full, head_full = (
        lax.all_gather(attn_params.astype(jnp.bfloat16), "sent", axis=0, tiled=True),
        lax.all_gather(head_params.astype(jnp.bfloat16), "sent", axis=0, tiled=True),
    )
    attn_mats = attn_full[: 4 * D * D].reshape(D, 4 * D)
    attn_vecs_low = attn_full[4 * D * D :].reshape(D, 8 + POS)
    attn_vecs = attn_vecs_low.astype(jnp.float32)
    head_mats = head_full[: 9 * D * D].reshape(D, 9 * D)
    head_vecs = head_full[9 * D * D :].reshape(D, 8).astype(jnp.float32)
    w_qkv = attn_mats[:, : 3 * D]
    w_out = attn_mats[:, 3 * D :]
    w_up = head_mats[:, : 4 * D]
    w_down = head_mats[:, 4 * D : 8 * D]
    w_pool = head_mats[:, 8 * D :]
    bucket_all = bucket_length(buckets)
    slot_ids = jnp.arange(slot_count, dtype=jnp.int32)
    valid_everything = (
        (slot_ids[None, :] < (tok_rows // bucket_all)[:, None]).astype(jnp.float32).reshape(-1)
    )
    bucket_len = bucket_all[device]
    sent_count = tok_rows // bucket_len
    valid_own = (slot_ids < sent_count).astype(jnp.float32)
    row_ids = jnp.arange(tok_rows, dtype=jnp.int32)
    sentence = row_ids // bucket_len
    row_place = row_ids % bucket_len
    slot_len = jnp.sum(
        jnp.where(sentence[:, None] == slot_ids[None, :], lengths[None, :], 0), axis=1
    )
    key_ok = row_place < slot_len
    block = POS
    sent_blocks = sentence.reshape(-1, block)
    ok_blocks = key_ok.reshape(-1, block)
    allowed = (sent_blocks[:, :, None] == sent_blocks[:, None, :]) & ok_blocks[:, None, :]
    allowed = jnp.concatenate([allowed, allowed], axis=0)[:, None]
    place_hot = (row_place[:, None] == jnp.arange(POS, dtype=jnp.int32)[None, :]).astype(
        jnp.bfloat16
    )
    pos_rows = plain_dot(place_hot, attn_vecs_low[:, 8:].T)
    emb_rows = embeddings.astype(jnp.float32) + pos_rows + attn_vecs[:, 7]
    normed, emb_back = jax.vjp(layer_norm, emb_rows, attn_vecs[:, 5], attn_vecs[:, 6])
    keep_masks = drop_masks.astype(jnp.float32) / keep_prob
    keep_attn = keep_masks[:, 1].reshape(all_rows, D)
    keep_ffn = keep_masks[:, 2].reshape(all_rows, D)
    attn_in = (normed[None] * keep_masks[:, 0]).reshape(all_rows, D)
    attn_in_low = attn_in.astype(jnp.bfloat16)
    qkv_bias = jnp.concatenate([attn_vecs[:, 0], jnp.zeros((D,), jnp.float32), attn_vecs[:, 1]])
    qkv_low = (plain_dot(attn_in_low, w_qkv) + qkv_bias).astype(jnp.bfloat16)
    head_split = qkv_low.reshape(-1, block, 3, H, HD)
    queries = head_split[:, :, 0]
    keys_low = head_split[:, :, 1]
    values_low = head_split[:, :, 2]
    score_scale = HD ** (-0.5)
    raw_scores = jnp.einsum(
        "bqhd,bkhd->bhqk", queries, keys_low, preferred_element_type=jnp.float32
    )
    scores = jnp.where(allowed, raw_scores * score_scale, masked_scores)
    row_top = jnp.max(scores, axis=-1, keepdims=True)
    expo_vals = jnp.exp(scores - row_top)
    row_total = jnp.sum(expo_vals, axis=-1, keepdims=True)
    attn_probs = expo_vals / row_total
    score_lse = row_top + jnp.log(row_total)
    mixed_out = jnp.einsum(
        "bhqk,bkhd->bqhd",
        attn_probs.astype(jnp.bfloat16),
        values_low,
        preferred_element_type=jnp.float32,
    )
    mixed_low = mixed_out.reshape(all_rows, D).astype(jnp.bfloat16)
    branch = plain_dot(mixed_low, w_out) + attn_vecs[:, 2]
    first_res = attn_in + keep_attn * branch
    first_norm, first_back = jax.vjp(layer_norm, first_res, attn_vecs[:, 3], attn_vecs[:, 4])
    first_low = first_norm.astype(jnp.bfloat16)
    up_bias = head_vecs[:, :4].T.reshape(4 * D)
    up_pre = plain_dot(first_low, w_up) + up_bias
    active, gelu_back = jax.vjp(gelu_exact, up_pre)
    active_low = active.astype(jnp.bfloat16)
    down_out = target_dot_terms(active_low, w_down) + head_vecs[:, 4]
    second_res = first_norm + keep_ffn * down_out
    second_norm, second_back = jax.vjp(layer_norm, second_res, head_vecs[:, 5], head_vecs[:, 6])
    hidden_out = second_norm.astype(jnp.bfloat16).reshape(2, tok_rows, D)
    cls_pick = jnp.minimum(slot_ids, sent_count - 1) * bucket_len
    cls_rows = jnp.take(second_norm.reshape(2, tok_rows, D), cls_pick, axis=1).reshape(
        2 * slot_count, D
    )
    cls_low = cls_rows.astype(jnp.bfloat16)
    pooled = jnp.tanh(plain_dot(cls_low, w_pool) + head_vecs[:, 7])
    unit_rows, unit_back = jax.vjp(unit_scale, pooled)
    unit_low = unit_rows.astype(jnp.bfloat16)
    query_embeddings = unit_low[:slot_count]
    positive_view_set = unit_low[slot_count:]
    target_sentence_set, everyone = (
        lax.all_gather(positive_view_set, "sent", axis=0, tiled=True),
        lax.all_gather(query_embeddings, "sent", axis=0, tiled=True),
    )
    own_cols = device * slot_count + slot_ids
    col_ids = jnp.arange(target_sentence_set.shape[0], dtype=jnp.int32)
    pos_hot = col_ids[None, :] == own_cols[:, None]
    cosine_logit_table = jnp.where(
        valid_everything[None, :] > 0,
        target_dot_terms(query_embeddings, target_sentence_set) / logit_divisor,
        masked_scores,
    )
    sim_top = jnp.max(cosine_logit_table, axis=-1, keepdims=True)
    row_lse = sim_top[:, 0] + jnp.log(jnp.sum(jnp.exp(cosine_logit_table - sim_top), axis=-1))
    positive = jnp.sum(jnp.where(pos_hot, cosine_logit_table, 0.0), axis=-1)
    local_loss = jnp.sum(valid_own * (row_lse - positive))
    loss_sum = lax.psum(local_loss, "sent")
    cosine_logit_cotangent = valid_own[:, None] * (
        jnp.exp(cosine_logit_table - row_lse[:, None]) - pos_hot.astype(jnp.float32)
    )
    cosine_logit_summed = (cosine_logit_cotangent / logit_divisor).astype(jnp.bfloat16)
    d_anchor = plain_dot(cosine_logit_summed, target_sentence_set)
    all_lse = lax.all_gather(row_lse, "sent", axis=0, tiled=True)
    back_sim = target_dot_terms(everyone, positive_view_set) / logit_divisor
    back_hot = (col_ids[:, None] == own_cols[None, :]).astype(jnp.float32)
    back_grad = valid_everything[:, None] * (
        jnp.exp(back_sim - all_lse[:, None]) * valid_own[None, :] - back_hot
    )
    d_partner = rows_dot((back_grad / logit_divisor).astype(jnp.bfloat16), everyone)
    d_unit = jnp.concatenate([d_anchor, d_partner], axis=0)
    d_pooled = unit_back(d_unit)[0]
    d_pool_pre = d_pooled * (1.0 - pooled * pooled)
    pool_low = d_pool_pre.astype(jnp.bfloat16)
    g_pool = rows_dot(cls_low, pool_low)
    g_pool_bias = jnp.sum(d_pool_pre, axis=0)
    d_cls = target_dot_terms(pool_low, w_pool).reshape(2, slot_count, D)
    pick_hot = ((row_ids[None, :] == cls_pick[:, None]) & (slot_ids[:, None] < sent_count)).astype(
        jnp.float32
    )
    d_second = cotangent.astype(jnp.float32) + jnp.einsum(
        "st,vsd->vtd", pick_hot, d_cls, precision=highest
    )
    d_second_res, g_gain_two, g_shift_two = second_back(d_second.reshape(all_rows, D))
    d_down = d_second_res * keep_ffn
    g_down_bias = jnp.sum(d_down, axis=0)
    down_low = d_down.astype(jnp.bfloat16)
    g_down = rows_dot(down_low, active_low)
    d_active = plain_dot(down_low, w_down)
    d_up = gelu_back(d_active)[0]
    g_up_bias = jnp.sum(d_up, axis=0)
    up_low = d_up.astype(jnp.bfloat16)
    g_up = rows_dot(first_low, up_low)
    d_first = d_second_res + target_dot_terms(up_low, w_up)
    head_vec_grad = jnp.concatenate(
        [
            g_up_bias.reshape(4, D).T,
            jnp.stack([g_down_bias, g_gain_two, g_shift_two, g_pool_bias], axis=1),
        ],
        axis=1,
    )
    head_grad = jnp.concatenate(
        [jnp.concatenate([g_up, g_down, g_pool], axis=1).reshape(-1), head_vec_grad.reshape(-1)]
    )
    d_first_res, g_gain_one, g_shift_one = first_back(d_first)
    d_branch = d_first_res * keep_attn
    g_out_bias = jnp.sum(d_branch, axis=0)
    branch_low = d_branch.astype(jnp.bfloat16)
    g_out = rows_dot(mixed_low, branch_low)
    d_mixed = target_dot_terms(branch_low, w_out).astype(jnp.bfloat16).reshape(-1, block, H, HD)
    again = jnp.where(
        allowed,
        jnp.einsum("bqhd,bkhd->bhqk", queries, keys_low, preferred_element_type=jnp.float32)
        * score_scale,
        masked_scores,
    )
    probs_again = jnp.exp(again - score_lse)
    d_values = jnp.einsum(
        "bhqk,bqhd->bkhd",
        probs_again.astype(jnp.bfloat16),
        d_mixed,
        preferred_element_type=jnp.float32,
    )
    d_probs = jnp.einsum("bqhd,bkhd->bhqk", d_mixed, values_low, preferred_element_type=jnp.float32)
    row_delta = jnp.sum(probs_again * d_probs, axis=-1, keepdims=True)
    score_low = (probs_again * (d_probs - row_delta) * score_scale).astype(jnp.bfloat16)
    d_queries = jnp.einsum(
        "bhqk,bkhd->bqhd", score_low, keys_low, preferred_element_type=jnp.float32
    )
    d_keys = jnp.einsum("bhqk,bqhd->bkhd", score_low, queries, preferred_element_type=jnp.float32)
    d_qkv = jnp.stack([d_queries, d_keys, d_values], axis=2).reshape(all_rows, 3 * D)
    g_q_bias = jnp.sum(d_queries.reshape(all_rows, D), axis=0)
    g_v_bias = jnp.sum(d_values.reshape(all_rows, D), axis=0)
    qkv_grad_low = d_qkv.astype(jnp.bfloat16)
    g_qkv = rows_dot(attn_in_low, qkv_grad_low)
    d_attn_in = d_first_res + target_dot_terms(qkv_grad_low, w_qkv)
    d_normed = jnp.sum(d_attn_in.reshape(2, tok_rows, D) * keep_masks[:, 0], axis=0)
    input_grad, g_gain_emb, g_shift_emb = emb_back(d_normed)
    g_type = jnp.sum(input_grad, axis=0)
    g_table = lax.dot_general(
        place_hot.astype(jnp.float32),
        input_grad,
        (((0,), (0,)), ((), ())),
        precision=highest,
        preferred_element_type=jnp.float32,
    )
    attn_vec_grad = jnp.concatenate(
        [
            jnp.stack(
                [
                    g_q_bias,
                    g_v_bias,
                    g_out_bias,
                    g_gain_one,
                    g_shift_one,
                    g_gain_emb,
                    g_shift_emb,
                    g_type,
                ],
                axis=1,
            ),
            g_table.T,
        ],
        axis=1,
    )
    attn_grad = jnp.concatenate(
        [jnp.concatenate([g_qkv, g_out], axis=1).reshape(-1), attn_vec_grad.reshape(-1)]
    )
    attn_share, head_share = (
        lax.psum_scatter(attn_grad, "sent", scatter_dimension=0, tiled=True),
        lax.psum_scatter(head_grad, "sent", scatter_dimension=0, tiled=True),
    )
    squares = jnp.sum(attn_share * attn_share) + jnp.sum(head_share * head_share)
    total_squares = lax.psum(squares, "sent")
    loss = loss_sum / jnp.sum(valid_everything)
    grad_norm = jnp.sqrt(total_squares)
    clip_scale = jnp.minimum(1.0, clip_bound / grad_norm)
    attn_new = adam_step(attn_share * clip_scale, attn_params, attn_moment, attn_second, attn_ema)
    head_new = adam_step(head_share * clip_scale, head_params, head_moment, head_second, head_ema)
    return (
        hidden_out,
        input_grad,
        loss,
        grad_norm,
        attn_new[0],
        attn_new[1],
        attn_new[2],
        attn_new[3],
        head_new[0],
        head_new[1],
        head_new[2],
        head_new[3],
    )


def on_device(*arrays):
    shards = (arrays[5].shape[0], arrays[9].shape[0])
    local = on_grid if is_grid(lax.axis_size("sent"), *shards) else on_any_mesh
    return local(*arrays)


def solution(mesh):
    in_specs = (
        P("sent", None),
        P(None, "sent", None),
        P(None, None, "sent", None),
        P("sent"),
        P(),
        P("sent"),
        P("sent"),
        P("sent"),
        P("sent"),
        P("sent"),
        P("sent"),
        P("sent"),
        P("sent"),
    )
    out_specs = (
        P(None, "sent", None),
        P("sent", None),
        P(),
        P(),
        P("sent"),
        P("sent"),
        P("sent"),
        P("sent"),
        P("sent"),
        P("sent"),
        P("sent"),
        P("sent"),
    )
    return jax.shard_map(
        on_device, mesh=mesh, in_specs=in_specs, out_specs=out_specs, check_vma=False
    )
```

```python
import functools

import jax
import jax.numpy as jnp
from jax import lax
from jax.experimental import pallas as pl
from jax.experimental.pallas import tpu as pltpu
from jax.sharding import PartitionSpec as P

D = 768
H = 12
HD = 64
LMIN = 32
POS = 128
STEP = 5


logit_divisor = 0.05
keep_prob = 0.9
norm_eps = 1e-06
clip_bound = 0.001
beta_first = 0.5
beta_second = 0.5
learn_rate = 0.05
decay_rate = 0.01
adam_eps = 1e-08
ema_rate = 0.8
masked_scores = -1e30
highest = lax.Precision.HIGHEST


def layer_norm(tensor, gain_vec, shift_vec):
    center = tensor - jnp.mean(tensor, axis=-1, keepdims=True)
    spread = jnp.mean(center * center, axis=-1, keepdims=True)
    return center * lax.rsqrt(spread + norm_eps) * gain_vec + shift_vec


def gelu_exact(tensor):
    return 0.5 * tensor * (1.0 + jax.scipy.special.erf(tensor * 0.7071067811865476))


def unit_scale(tensor):
    return tensor * lax.rsqrt(jnp.sum(tensor * tensor, axis=-1, keepdims=True) + norm_eps)


def bucket_length(bucket_code):
    return (LMIN * jnp.where(bucket_code == 0, 1, jnp.where(bucket_code == 1, 2, 4))).astype(
        jnp.int32
    )


def plain_dot(left_op, right_op):
    return jnp.dot(left_op, right_op, preferred_element_type=jnp.float32)


def rows_dot(left_op, right_op):
    return lax.dot_general(
        left_op, right_op, (((0,), (0,)), ((), ())), preferred_element_type=jnp.float32
    )


def target_dot_terms(left_op, right_op):
    return lax.dot_general(
        left_op, right_op, (((1,), (1,)), ((), ())), preferred_element_type=jnp.float32
    )


def adam_step(grad_flat, params, moment, second, average):
    first_new = beta_first * moment + (1.0 - beta_first) * grad_flat
    second_new = beta_second * second + (1.0 - beta_second) * grad_flat * grad_flat
    fix_first = 1.0 - beta_first**STEP
    fix_second = 1.0 - beta_second**STEP
    adam_dir = first_new / fix_first / (jnp.sqrt(second_new / fix_second) + adam_eps)
    updated = params - learn_rate * (adam_dir + decay_rate * params)
    average_new = ema_rate * average + (1.0 - ema_rate) * updated
    return (first_new, second_new, updated, average_new)


LANES = 128
VMEM_CAP = 60 * 2**20


def room(mib):
    return pltpu.CompilerParams(vmem_limit_bytes=mib * 2**20)


def far(*arrays):
    return [pltpu.with_memory_space_constraint(array, pltpu.HBM) for array in arrays]


def bring(pairs, sems, first=0):
    copies = []
    for source, target in pairs:
        copies.append(pltpu.make_async_copy(source, target, sems.at[first + len(copies)]))
        copies[-1].start()
    return copies


def await_all(copies):
    for copy in copies:
        copy.wait()


def result(shape, dtype, stays=False):
    return pltpu.VMEM(shape, dtype) if stays else jax.ShapeDtypeStruct(shape, dtype)
CORE, XBIT, YBIT, ZBITS = 1, 2, 4, (8, 16, 24)


def swap(value, bit):
    count = lax.axis_size("sent")
    return lax.ppermute(value, "sent", [(i, i ^ bit) for i in range(count)])


def is_grid(count, *shards):
    return count == 32 and all(2 * shard % LANES == 0 for shard in shards)


def block_rows(shard):
    return -(-(-(-shard // LANES) + 8) // 16) * 16


def first_row(device, shard):
    return (device * shard) // LANES


def pack_shard(values, device):
    shard = values.shape[0]
    rows = block_rows(shard)
    size = rows * LANES
    odd = (device * shard) % LANES != 0
    lead = jnp.where(
        odd,
        jnp.pad(values, (LANES // 2, size - shard - LANES // 2)),
        jnp.pad(values, (0, size - shard)),
    ).reshape(rows, LANES)
    offset = first_row(device, shard) % 8
    padded = jnp.pad(lead, ((8, 0), (0, 0)))
    return lax.dynamic_slice(padded, (8 - offset, 0), (rows, LANES)).astype(jnp.bfloat16)


def unpack_shard(block, device, shard):
    rows = -(-shard // LANES)
    offset = first_row(device, shard) % 8
    odd = (device * shard) % LANES != 0
    flat = lax.dynamic_slice(block, (offset, 0), (rows, LANES)).reshape(-1)
    longer = jnp.pad(flat, (0, LANES))
    return jnp.where(odd, longer[LANES // 2 : LANES // 2 + shard], flat[:shard])


WHOLE = ((0, 0, 4), (1, 0, 4), (2, 0, 4), (3, 0, 2), (3, 2, 2))
HALVES = tuple((across, first, 2) for across in range(4) for first in (0, 2))


def piece_slots(me, layout):
    slots = []
    for core in (0, 1):
        for across, first, n in layout:
            slots.append([me ^ (core + 2 * across + 8 * (first + k)) for k in range(n)])
    return slots


def after(value, *others):
    return lax.optimization_barrier((value, others))[0]


def with_sibling(own):
    return tuple(own) + tuple(swap(piece, CORE) for piece in own)


def gather_attn(values, device):
    block = pack_shard(values, device)
    zs = [swap(block, bit) for bit in ZBITS]
    line = jnp.stack([block] + zs)
    x, y = swap(line, XBIT), swap(line, YBIT)
    diagonal = (swap(y[:2], XBIT), swap(x[2:], YBIT))
    return with_sibling((line, x, y) + diagonal), zs[0], diagonal


def gather_head_line(values, device, first):
    block = after(pack_shard(values, device), first)
    return [block] + [swap(block, bit) for bit in ZBITS]


def gather_head(line, x, y):
    return with_sibling((line, x, y, swap(y[:2], XBIT), swap(x[2:], YBIT)))


def low_sum(*terms):
    total = terms[0].astype(jnp.float32)
    for term in terms[1:]:
        total = total + term.astype(jnp.float32)
    return total.astype(jnp.bfloat16)


def scatter_core(pieces):
    half = len(pieces) // 2
    got = [swap(piece, CORE) for piece in reversed(pieces[half:])][::-1]
    return [low_sum(piece, other) for piece, other in zip(pieces[:half], got)]


def scatter_attn(sums):
    line, x, y, d_low, d_high = sums
    d_low, d_high = swap(d_low, XBIT), swap(d_high, YBIT)
    x = swap(jnp.concatenate([x[:2], low_sum(x[2:], d_high)]), XBIT)
    y = swap(jnp.concatenate([low_sum(y[:2], d_low), y[2:]]), YBIT)
    line = low_sum(line, x, y)
    return scatter_along(line[0], [line[k] for k in (1, 2, 3)])


def scatter_along(own, others):
    total = own.astype(jnp.float32)
    for value, bit in zip(others, ZBITS):
        total = total + swap(value, bit).astype(jnp.float32)
    return total


def plain_rows(left, right, dims):
    return lax.dot_general(left, right, (dims, ((), ())), preferred_element_type=jnp.float32)


NN, NT, TN = ((1,), (0,)), ((1,), (1,)), ((0,), (0,))


def one_hot(shape, left, right):
    rows = lax.broadcasted_iota(jnp.int32, shape, 0)
    cols = lax.broadcasted_iota(jnp.int32, shape, 1)
    return jnp.where(left(rows, cols) == right(rows, cols), 1.0, 0.0)


def vectors_of(flat_rows):
    spread = one_hot((D, 48), lambda r, c: r >> 4, lambda r, c: c).astype(jnp.bfloat16)
    rows = plain_rows(spread, flat_rows.astype(jnp.bfloat16), NN)
    rows = rows * one_hot((D, LANES), lambda r, c: r & 15, lambda r, c: c >> 3)
    fold = one_hot((8, LANES), lambda r, c: r, lambda r, c: c & 7).astype(jnp.bfloat16)
    return plain_rows(fold, rows.astype(jnp.bfloat16), NT)


def flat_of(vectors):
    fold = one_hot((8, LANES), lambda r, c: r, lambda r, c: c & 7).astype(jnp.bfloat16)
    rows = plain_rows(vectors.astype(jnp.bfloat16), fold, TN)
    rows = rows * one_hot((D, LANES), lambda r, c: r & 15, lambda r, c: c >> 3)
    spread = one_hot((D, 48), lambda r, c: r >> 4, lambda r, c: c).astype(jnp.bfloat16)
    return plain_rows(spread, rows.astype(jnp.bfloat16), TN)


def keep_of(mask):
    return mask.astype(jnp.float32) * (1.0 / keep_prob)


def place_blocks(shard, layout, pieces, me, stage, flat, sems):
    count, rows = stage.shape[0], stage.shape[1]
    for piece, slots in zip(pieces, piece_slots(me, layout)):
        for k, slot in enumerate(slots):
            pltpu.make_async_copy(piece.at[k], stage.at[slot], sems.at[slot]).start()
    flat[pl.ds(0, 8), :] = jnp.zeros((8, LANES), jnp.float32)

    def place(device, carry):
        pltpu.make_async_copy(pieces[0].at[0], stage.at[device], sems.at[device]).wait()
        at = pl.multiple_of(device * shard // LANES // 8 * 8, 8)
        before = flat[pl.ds(at, 8), :]
        flat[pl.ds(at, rows), :] = stage[device].astype(jnp.float32)
        flat[pl.ds(at, 8), :] += before
        return carry

    lax.fori_loop(0, count, place, 0)


def gather_matrix(flat, w_ref, w_out=None, out_sems=None):
    cols = w_ref.shape[1] // LANES

    def gather_rows(group, carry):
        at = pl.multiple_of(group * 16, 16)
        for col in range(cols):
            rows16 = flat[pl.ds(group * 16 * cols + col, 16, stride=cols), :]
            w_ref[pl.ds(at, 16), pl.ds(col * LANES, LANES)] = rows16.astype(jnp.bfloat16)
        return carry

    parts = 4
    span = D // parts
    copies = []
    for part in range(parts):
        lax.fori_loop(part * span // 16, (part + 1) * span // 16, gather_rows, 0)
        here = pl.ds(part * span, span)
        if w_out is not None:
            copies.append(pltpu.make_async_copy(w_ref.at[here], w_out.at[here], out_sems.at[part]))
            copies[-1].start()
    return copies


VEC = 8 + POS


def table_of(flat, base, body, tail):
    lane = lax.broadcasted_iota(jnp.int32, (D // 16, LANES), 1)
    for q in range(16):
        here = flat[pl.ds(base + q, D // 16, stride=17), :]
        later = flat[pl.ds(base + q + 1, D // 16, stride=17), :]
        both = jnp.where(lane >= 8 * q, here, later)
        shift = (LANES - 8 * q) % LANES
        body[pl.ds(q, D // 16, stride=16), :] = pltpu.roll(both, shift, 1) if shift else both
        tail[pl.ds(q, D // 16, stride=16), :] = pltpu.roll(later, shift, 1) if shift else later
    return body[...].T, tail[...].T[:8]


def flat_table(flat, base, first, last, body, tail):
    body[...] = first.T
    tail[...] = jnp.concatenate([last, jnp.zeros((LANES - 8, D), jnp.float32)]).T
    lane = lax.broadcasted_iota(jnp.int32, (D // 16, LANES), 1)
    carried = None
    for q in range(17):
        row = carried
        if q < 16:
            main = body[pl.ds(q, D // 16, stride=16), :]
            end = tail[pl.ds(q, D // 16, stride=16), :]
            if q:
                main, end = pltpu.roll(main, 8 * q, 1), pltpu.roll(end, 8 * q, 1)
            row = main if carried is None else jnp.where(lane >= 8 * q, main, carried)
            carried = jnp.where(lane < 8 * q, main, end)
        flat[pl.ds(base + q, D // 16, stride=17), :] = row


def repeat_places(table, length):
    twice = jnp.concatenate([table[:64]] * 2)
    four = jnp.concatenate([table[:32]] * 4)
    return jnp.where(length == 128, table, jnp.where(length == 64, twice, four))


def fold_places(rows, length):
    half = rows[:64] + rows[64:]
    quarter = half[:32] + half[32:]
    none = jnp.zeros_like(rows)
    twice = jnp.concatenate([half, none[:64]])
    four = jnp.concatenate([quarter, none[:96]])
    return jnp.where(length == 128, rows, jnp.where(length == 64, twice, four))


def stack_heads(pair):
    lane = lax.broadcasted_iota(jnp.int32, pair.shape, 1)
    none = jnp.zeros_like(pair)
    return jnp.concatenate([jnp.where(lane < HD, pair, none), jnp.where(lane < HD, none, pair)])


def unstack_heads(rows):
    half = rows.shape[0] // 2
    lane = lax.broadcasted_iota(jnp.int32, (half, rows.shape[1]), 1)
    return jnp.where(lane < HD, rows[:half], rows[half:])


ROWS = 64


def attn_kernel(shard, me_ref, length_ref, lens_ref, *refs):
    pieces, (emb_ref, mask_hbm) = refs[:10], refs[10:12]
    (w_out, vec_ref, rows_ref, in_low_ref, qkv_ref, prob_ref, mixed_ref, res_ref, norm_ref, low_ref) = refs[12:22]
    (stage, flat, w_ref, body, tail, mask, attn_in, bias_ref, sems, out_sems, mask_sems) = refs[22:]
    me = me_ref[0]
    tokens = emb_ref.shape[0]
    masks = []
    for view in range(2):
        for which in range(2):
            at = 2 * view + which
            masks.append(pltpu.make_async_copy(mask_hbm.at[view, which], mask.at[at], mask_sems.at[at]))
            masks[-1].start()
    place_blocks(shard, WHOLE, pieces, me, stage, flat, sems)
    copies = gather_matrix(flat, w_ref, w_out, out_sems)
    first, last = table_of(flat, D * w_ref.shape[1] // LANES, body, tail)
    vecs = first[:8]
    vec_ref[...] = vecs
    length = length_ref[0]
    places = repeat_places(jnp.concatenate([first[8:], last]), length)
    for copy in masks:
        copy.wait()
    for block in range(tokens // LANES):
        key = lax.broadcasted_iota(jnp.int32, (LANES, LANES), 1) + block * LANES
        query = lax.broadcasted_iota(jnp.int32, (LANES, LANES), 0) + block * LANES
        shift = jnp.where(length == 128, 7, jnp.where(length == 64, 6, 5))
        sent = lax.shift_right_logical(key, jnp.full_like(key, 1) * shift)
        sent_q = lax.shift_right_logical(query, jnp.full_like(key, 1) * shift)
        real = jnp.zeros_like(key)
        for slot in range(lens_ref.shape[0]):
            real = jnp.where(sent == slot, lens_ref[slot], real)
        ok = (sent == sent_q) & ((key & (length - 1)) < real)
        bias_ref[block] = jnp.where(ok, 0.0, masked_scores)
        here = pl.ds(block * LANES, LANES)
        emb = emb_ref[here, :].astype(jnp.float32) + places + vecs[7:8]
        rows_ref[here, :] = emb
        normed = layer_norm(emb, vecs[5:6], vecs[6:7])
        for view in range(2):
            at = pl.ds(view * tokens + block * LANES, LANES)
            given = normed * keep_of(mask[2 * view, here, :])
            attn_in[at, :] = given
            in_low_ref[at, :] = given.astype(jnp.bfloat16)
    for part in range(3):
        cols = pl.ds(part * D, D)
        made = plain_rows(in_low_ref[...], w_ref[:, cols], NN)
        if part != 1:
            made = made + vecs[part // 2 : part // 2 + 1]
        qkv_ref[:, cols] = made.astype(jnp.bfloat16)

    def attend(block, carry):
        here = pl.ds(pl.multiple_of(block * LANES, LANES), LANES)
        bias = bias_ref[block & 1]
        bias = jnp.concatenate([bias, bias])
        for pair in range(H // 2):
            q = stack_heads(qkv_ref[here, pl.ds(pair * LANES, LANES)])
            k = qkv_ref[here, pl.ds(D + pair * LANES, LANES)]
            v = qkv_ref[here, pl.ds(2 * D + pair * LANES, LANES)]
            scores = plain_rows(q, k, NT) * HD ** (-0.5) + bias
            expo = jnp.exp(scores - jnp.max(scores, axis=-1, keepdims=True))
            probs = expo / jnp.sum(expo, axis=-1, keepdims=True)
            prob_ref[block, pair] = probs
            mixed = unstack_heads(plain_rows(probs.astype(jnp.bfloat16), v, NN))
            mixed_ref[here, pl.ds(pair * LANES, LANES)] = mixed.astype(jnp.bfloat16)
        return carry

    lax.fori_loop(0, 2 * tokens // LANES, attend, 0)
    res_ref[...] = plain_rows(mixed_ref[...], w_ref[:, 3 * D :], NN)
    for view in range(2):
        def finish(chunk, carry, view=view):
            own = pl.ds(pl.multiple_of(chunk * ROWS, ROWS), ROWS)
            at = pl.ds(pl.multiple_of(view * tokens + chunk * ROWS, ROWS), ROWS)
            res = attn_in[at, :] + keep_of(mask[2 * view + 1, own, :]) * (res_ref[at, :] + vecs[2:3])
            res_ref[at, :] = res
            norm = layer_norm(res, vecs[3:4], vecs[4:5])
            norm_ref[at, :] = norm
            low_ref[at, :] = norm.astype(jnp.bfloat16)
            return carry

        lax.fori_loop(0, tokens // ROWS, finish, 0, unroll=True)
    for copy in copies:
        copy.wait()


def attn_forward(pieces, me, shard, length, lengths, embeddings, masks):
    rows = pieces[0].shape[1]
    whole = shard * 32 // LANES
    tokens = embeddings.shape[0]
    both = 2 * tokens
    any_space, vmem = pl.BlockSpec(memory_space=pltpu.HBM), pl.BlockSpec(memory_space=pltpu.VMEM)
    smem = pl.BlockSpec(memory_space=pltpu.SMEM)
    f32, low = jnp.float32, jnp.bfloat16
    shapes = [
        ((D, 4 * D), low),
        ((8, D), f32),
        ((tokens, D), f32),
        ((both, D), low),
        ((both, 3 * D), low),
        ((both // LANES, H // 2, 2 * LANES, LANES), f32),
        ((both, D), low),
        ((both, D), f32),
        ((both, D), f32),
        ((both, D), low),
    ]
    return pl.pallas_call(
        functools.partial(attn_kernel, shard),
        out_shape=tuple(jax.ShapeDtypeStruct(*s) for s in shapes),
        in_specs=[smem] * 3 + [any_space] * len(pieces) + [vmem, any_space],
        out_specs=(any_space,) + (vmem,) * 9,
        scratch_shapes=[
            pltpu.VMEM((32, rows, LANES), low),
            pltpu.VMEM((whole + rows, LANES), f32),
            pltpu.VMEM((D, 4 * D), low),
            pltpu.VMEM((D, LANES), f32),
            pltpu.VMEM((D, LANES), f32),
            pltpu.VMEM((4, tokens, D), jnp.int32),
            pltpu.VMEM((both, D), f32),
            pltpu.VMEM((tokens // LANES, LANES, LANES), f32),
            pltpu.SemaphoreType.DMA((32,)),
            pltpu.SemaphoreType.DMA((4,)),
            pltpu.SemaphoreType.DMA((4,)),
        ],
        compiler_params=pltpu.CompilerParams(vmem_limit_bytes=VMEM_CAP),
    )(jnp.reshape(me, (1,)), jnp.reshape(length, (1,)), lengths, *far(*pieces), embeddings, *far(masks))


def sum_rows(rows):
    return jnp.sum(rows, axis=0, keepdims=True)


def norm_back_kernel(pick_ref, d_first, d_cls_in, res_in, vec_in, mask_hbm, mixed_in, w_in,
                     d_res_ref, g_out_ref, d_mixed, part_ref,
                     mask, given, branch, d_cls, res_ref, vec_ref, mixed_ref, w_ref, sems):
    tokens = mask.shape[1]
    both = 2 * tokens
    copies = bring(
        [(d_first, given), (d_cls_in, d_cls), (res_in, res_ref), (vec_in, vec_ref)]
        + [(mask_hbm.at[view, 1], mask.at[view]) for view in range(2)]
        + [(w_in.at[:, pl.ds(3 * D, D)], w_ref), (mixed_in, mixed_ref)],
        sems,
    )
    await_all(copies[:6])
    n = d_cls.shape[0] // 2
    for slot in range(n):
        real = jnp.where(slot < pick_ref[n], 1.0, 0.0)
        for view in range(2):
            at = pl.ds(view * tokens + pick_ref[slot], 1)
            given[at, :] += real * d_cls[view * n + slot : view * n + slot + 1, :]
    gain = vec_ref[3:4, :]
    sums = tuple(jnp.zeros((1, D), jnp.float32) for _ in range(3))
    for view in range(2):
        def one_chunk(chunk, sums, view=view):
            own = pl.ds(pl.multiple_of(chunk * ROWS, ROWS), ROWS)
            at = pl.ds(pl.multiple_of(view * tokens + chunk * ROWS, ROWS), ROWS)
            grad = given[at, :]
            center, inv = norm_parts(res_ref[at, :])
            d_res, unit = norm_back(grad, center, inv, gain)
            d_branch = d_res * keep_of(mask[view, own, :])
            d_res_ref[at, :] = d_res
            branch[at, :] = d_branch.astype(jnp.bfloat16)
            return (
                sums[0] + sum_rows(d_branch),
                sums[1] + sum_rows(grad * unit),
                sums[2] + sum_rows(grad),
            )

        sums = lax.fori_loop(0, tokens // ROWS, one_chunk, sums, unroll=True)
    await_all(copies[6:])
    d_mixed[...] = plain_rows(branch[...], w_ref[...], NT).astype(jnp.bfloat16)
    g_out_ref[...] = plain_rows(mixed_ref[...], branch[...], TN).astype(jnp.bfloat16)
    for k in range(3):
        part_ref[k : k + 1, :] = sums[k]
    part_ref[3:8, :] = jnp.zeros((5, D), jnp.float32)


def norm_backward(picks, d_first, d_cls, res, vecs, masks, mixed, w_attn):
    both = res.shape[0]
    any_space, vmem = pl.BlockSpec(memory_space=pltpu.HBM), pl.BlockSpec(memory_space=pltpu.VMEM)
    f32, low = jnp.float32, jnp.bfloat16
    return pl.pallas_call(
        norm_back_kernel,
        out_shape=(
            result((both, D), f32),
            result((D, D), low),
            result((both, D), low, True),
            result((8, D), f32),
        ),
        in_specs=[pl.BlockSpec(memory_space=pltpu.SMEM)] + [any_space] * 7,
        out_specs=(vmem,) * 4,
        scratch_shapes=[
            pltpu.VMEM((2, both // 2, D), jnp.int32),
            pltpu.VMEM((both, D), f32),
            pltpu.VMEM((both, D), low),
            pltpu.VMEM(d_cls.shape, f32),
            pltpu.VMEM((both, D), f32),
            pltpu.VMEM((8, D), f32),
            pltpu.VMEM((both, D), low),
            pltpu.VMEM((D, D), low),
            pltpu.SemaphoreType.DMA((8,)),
        ],
        compiler_params=room(16),
    )(picks, *far(d_first, d_cls, res, vecs, masks, mixed, w_attn))


def attn_back_kernel(d_mixed, qkv_ref, prob_ref, d_qkv_ref, part_ref):
    part_ref[...] = jnp.zeros_like(part_ref)

    def one_block(block, carry):
        here = pl.ds(pl.multiple_of(block * LANES, LANES), LANES)
        for pair in range(H // 2):
            cols = pl.ds(pair * LANES, LANES)
            q = stack_heads(qkv_ref[here, cols])
            k = qkv_ref[here, pl.ds(D + pair * LANES, LANES)]
            v = qkv_ref[here, pl.ds(2 * D + pair * LANES, LANES)]
            d_out = stack_heads(d_mixed[here, cols])
            probs = prob_ref[block, pair]
            d_v = plain_rows(probs.astype(jnp.bfloat16), d_out, TN)
            d_probs = plain_rows(d_out, v, NT)
            delta = jnp.sum(probs * d_probs, axis=-1, keepdims=True)
            score = (probs * (d_probs - delta) * HD ** (-0.5)).astype(jnp.bfloat16)
            d_q = unstack_heads(plain_rows(score, k, NN))
            d_k = plain_rows(score, q, TN)
            d_qkv_ref[here, cols] = d_q.astype(jnp.bfloat16)
            d_qkv_ref[here, pl.ds(D + pair * LANES, LANES)] = d_k.astype(jnp.bfloat16)
            d_qkv_ref[here, pl.ds(2 * D + pair * LANES, LANES)] = d_v.astype(jnp.bfloat16)
            part_ref[0:1, cols] += sum_rows(d_q)
            part_ref[1:2, cols] += sum_rows(d_v)
        return carry

    lax.fori_loop(0, qkv_ref.shape[0] // LANES, one_block, 0)


def attn_backward(d_mixed, qkv, probs):
    vmem = pl.BlockSpec(memory_space=pltpu.VMEM)
    return pl.pallas_call(
        attn_back_kernel,
        out_shape=(result(qkv.shape, jnp.bfloat16, True), result((8, D), jnp.float32)),
        in_specs=[vmem] * 3,
        out_specs=(vmem,) * 2,
        compiler_params=room(16),
    )(d_mixed, qkv, probs)


def attn_grad_kernel(shard, me_ref, length_ref, d_qkv, *refs):
    sources, input_ref, pieces, scratch = refs[:9], refs[9], refs[10:20], refs[20:]
    stage, flat, body, tail, d_in, sems, in_sems, mask = scratch[:8]
    in_low, w_ref, d_res, rows_ref, vec_ref, g_out, part_ref, norm_part_ref = scratch[8:]
    in_hbm, w_hbm, d_res_hbm, rows_hbm, vec_hbm, mask_hbm, g_hbm, part_hbm, norm_part_hbm = sources
    cols = 4 * D // LANES
    tokens = rows_ref.shape[0]
    copies = bring(
        [(in_hbm, in_low), (g_hbm, g_out), (w_hbm.at[:, pl.ds(0, 3 * D)], w_ref), (d_res_hbm, d_res)]
        + [(mask_hbm.at[view, 0], mask.at[view]) for view in range(2)]
        + [(rows_hbm, rows_ref), (vec_hbm, vec_ref), (part_hbm, part_ref), (norm_part_hbm, norm_part_ref)],
        in_sems,
    )
    await_all(copies[:2])
    span, width = 256, 3 * LANES

    def one_block(block, carry):
        left = in_low[:, pl.ds(pl.multiple_of(block * span, span), span)]
        for k in range(3 * D // width):
            grads = plain_rows(left, d_qkv[:, pl.ds(k * width, width)], TN)
            for col in range(width // LANES):
                for group in range(span // 16):
                    at = (block * span + group * 16) * cols + k * width // LANES + col
                    tile = grads[group * 16 : (group + 1) * 16, col * LANES : (col + 1) * LANES]
                    flat[pl.ds(at, 16, stride=cols), :] = tile
        return carry

    lax.fori_loop(0, D // span, one_block, 0)

    def one_group(group, carry):
        at = pl.multiple_of(group * 16, 16)
        for col in range(D // LANES):
            tile = g_out[pl.ds(at, 16), pl.ds(col * LANES, LANES)].astype(jnp.float32)
            flat[pl.ds(group * 16 * cols + 3 * D // LANES + col, 16, stride=cols), :] = tile
        return carry

    lax.fori_loop(0, D // 16, one_group, 0)
    copies[2].wait()
    d_in[...] = plain_rows(d_qkv[...], w_ref[...], NT)
    await_all(copies[3:])
    gain = vec_ref[5:6, :]

    def one_chunk(chunk, sums):
        own = pl.ds(pl.multiple_of(chunk * ROWS, ROWS), ROWS)
        other = pl.ds(pl.multiple_of(tokens + chunk * ROWS, ROWS), ROWS)
        grad = (d_in[own, :] + d_res[own, :]) * keep_of(mask[0, own, :])
        grad = grad + (d_in[other, :] + d_res[other, :]) * keep_of(mask[1, own, :])
        center, inv = norm_parts(rows_ref[own, :])
        back, unit = norm_back(grad, center, inv, gain)
        input_ref[own, :] = back
        return (sums[0] + sum_rows(grad * unit), sums[1] + sum_rows(grad), sums[2] + sum_rows(back))

    none = tuple(jnp.zeros((1, D), jnp.float32) for _ in range(3))
    sums = lax.fori_loop(0, tokens // ROWS, one_chunk, none, unroll=True)
    table = jnp.zeros((LANES, D), jnp.float32)
    for block in range(tokens // LANES):
        table = table + input_ref[block * LANES : (block + 1) * LANES, :]
    table = fold_places(table, length_ref[0])
    first = jnp.concatenate([part_ref[0:2, :], norm_part_ref[0:3, :], *sums, table[: LANES - 8]])
    base = D * cols
    flat_table(flat, base, first, table[LANES - 8 :], body, tail)
    rows = stage.shape[1]
    flat[pl.ds(base + D * VEC // LANES, rows), :] = jnp.zeros((rows, LANES), jnp.float32)
    store_pieces(shard, WHOLE, me_ref[0], pieces, stage, flat, sems)


def attn_grads(me, shard, length, d_qkv, in_low, w_attn, d_res, rows_in, vecs, masks, g_out, parts, norm_parts_in):
    rows = block_rows(shard)
    whole = shard * 32 // LANES
    tokens = rows_in.shape[0]
    counts = [len(slots) for slots in piece_slots(0, WHOLE)]
    any_space, vmem = pl.BlockSpec(memory_space=pltpu.HBM), pl.BlockSpec(memory_space=pltpu.VMEM)
    smem = pl.BlockSpec(memory_space=pltpu.SMEM)
    f32, low = jnp.float32, jnp.bfloat16
    return pl.pallas_call(
        functools.partial(attn_grad_kernel, shard),
        out_shape=(jax.ShapeDtypeStruct((tokens, D), f32),)
        + tuple(jax.ShapeDtypeStruct((n, rows, LANES), low) for n in counts),
        in_specs=[smem, smem, vmem] + [any_space] * 9,
        out_specs=(vmem,) + (any_space,) * len(counts),
        scratch_shapes=[
            pltpu.VMEM((32, rows, LANES), low),
            pltpu.VMEM((whole + rows, LANES), f32),
            pltpu.VMEM((D, LANES), f32),
            pltpu.VMEM((D, LANES), f32),
            pltpu.VMEM((2 * tokens, D), f32),
            pltpu.SemaphoreType.DMA((32,)),
            pltpu.SemaphoreType.DMA((10,)),
            pltpu.VMEM((2, tokens, D), jnp.int32),
            pltpu.VMEM((2 * tokens, D), low),
            pltpu.VMEM((D, 3 * D), low),
            pltpu.VMEM((2 * tokens, D), f32),
            pltpu.VMEM((tokens, D), f32),
            pltpu.VMEM((8, D), f32),
            pltpu.VMEM((D, D), low),
            pltpu.VMEM((8, D), f32),
            pltpu.VMEM((8, D), f32),
        ],
        compiler_params=room(40),
    )(
        jnp.reshape(me, (1,)),
        jnp.reshape(length, (1,)),
        d_qkv,
        *far(in_low, w_attn, d_res, rows_in, vecs, masks, g_out, parts, norm_parts_in),
    )


def head_kernel(shard, me_ref, pick_ref, *refs):
    pieces, (first_hbm, mask_hbm) = refs[:10], refs[10:12]
    w_ref, vec_ref, unit_ref, cls_ref = refs[12:16]
    stage, flat, first_all, picked, mask, sems, in_sems = refs[16:]
    cols = w_ref.shape[1] // LANES
    tokens = mask.shape[1]
    loads = [pltpu.make_async_copy(first_hbm, first_all, in_sems.at[2])]
    for view in range(2):
        loads.append(pltpu.make_async_copy(mask_hbm.at[view, 2], mask.at[view], in_sems.at[view]))
    for load in loads:
        load.start()
    place_blocks(shard, WHOLE, pieces, me_ref[0], stage, flat, sems)
    gather_matrix(flat, w_ref)
    for load in loads:
        load.wait()
    n = unit_ref.shape[0] // 2
    for view in range(2):
        for slot in range(n):
            at, to = pick_ref[slot], view * n + slot
            picked[to : to + 1, :] = first_all[pl.ds(view * tokens + at, 1), :]
            cls_ref[to : to + 1, 2 * D : 3 * D] = keep_of(mask[view, pl.ds(at, 1), :])
    vecs = vectors_of(flat[pl.ds(D * cols, 48), :])
    vec_ref[...] = vecs
    first = picked[...]
    up_bias = jnp.concatenate([vecs[c : c + 1] for c in range(4)], axis=1)
    up_pre = plain_rows(first.astype(jnp.bfloat16), w_ref[:, : 4 * D], NN) + up_bias
    active = gelu_exact(up_pre).astype(jnp.bfloat16)
    down = plain_rows(active, w_ref[:, 4 * D : 8 * D], NT) + vecs[4:5]
    res = first + cls_ref[:, 2 * D : 3 * D] * down
    cls_low = layer_norm(res, vecs[5:6], vecs[6:7]).astype(jnp.bfloat16)
    pooled = jnp.tanh(plain_rows(cls_low, w_ref[:, 8 * D :], NN) + vecs[7:8])
    unit_ref[...] = unit_scale(pooled).astype(jnp.bfloat16)
    cls_ref[:, :D] = pooled
    cls_ref[:, D : 2 * D] = res
    cls_ref[:, 3 * D :] = up_pre


def make_head(pieces, me, shard, picks, first_norm, masks):
    rows = pieces[0].shape[1]
    whole = shard * 32 // LANES
    n = 2 * (picks.shape[0] - 1)
    any_space, vmem = pl.BlockSpec(memory_space=pltpu.HBM), pl.BlockSpec(memory_space=pltpu.VMEM)
    smem = pl.BlockSpec(memory_space=pltpu.SMEM)
    f32, low = jnp.float32, jnp.bfloat16
    return pl.pallas_call(
        functools.partial(head_kernel, shard),
        out_shape=(
            result((D, 9 * D), low, True),
            result((8, D), f32, True),
            result((n, D), low),
            result((n, 7 * D), f32),
        ),
        in_specs=[smem] * 2 + [any_space] * (len(pieces) + 2),
        out_specs=(vmem,) * 4,
        scratch_shapes=[
            pltpu.VMEM((32, rows, LANES), low),
            pltpu.VMEM((whole + rows, LANES), f32),
            pltpu.VMEM(first_norm.shape, f32),
            pltpu.VMEM((n, D), f32),
            pltpu.VMEM((2,) + masks.shape[2:], jnp.int32),
            pltpu.SemaphoreType.DMA((32,)),
            pltpu.SemaphoreType.DMA((3,)),
        ],
        compiler_params=room(42),
    )(jnp.reshape(me, (1,)), picks, *far(*pieces, first_norm, masks))


def norm_back(grad, center, inv, gain):
    unit = center * inv
    scaled = grad * gain
    mean = jnp.mean(scaled, axis=-1, keepdims=True)
    along = jnp.mean(scaled * unit, axis=-1, keepdims=True)
    return inv * (scaled - mean - unit * along), unit


def norm_parts(rows):
    center = rows - jnp.mean(rows, axis=-1, keepdims=True)
    return center, lax.rsqrt(jnp.mean(center * center, axis=-1, keepdims=True) + norm_eps)


def gelu_slope(values):
    cdf = 0.5 * (1.0 + lax.erf(values * 0.7071067811865476))
    return cdf + values * (0.3989422804014327 * jnp.exp(-0.5 * values * values))


CHUNK = 1024


def forward_kernel(first_low, first_ref, w_ref, vec_ref, mask_hbm, cot_ref,
                   act_ref, slope_ref, hidden_ref, d_res_ref, down_ref, part_ref,
                   mask, acc, made, sems):
    tokens = mask.shape[1]
    both = 2 * tokens
    copies = []
    for view in range(2):
        copies.append(pltpu.make_async_copy(mask_hbm.at[view, 2], mask.at[view], sems.at[view]))
    for copy in copies:
        copy.start()
    vecs = vec_ref[...]
    for k in range(4 * D // CHUNK):
        cols = pl.ds(k * CHUNK, CHUNK)
        bias = jnp.concatenate([vecs[c : c + 1] for c in range(4)], axis=1)[:, k * CHUNK : (k + 1) * CHUNK]
        made[...] = plain_rows(first_low[...], w_ref[:, cols], NN)

        def one_group(group, carry, bias=bias, cols=cols):
            at = pl.ds(pl.multiple_of(group * ROWS, ROWS), ROWS)
            up = made[at, :] + bias
            cdf = 0.5 * (1.0 + lax.erf(up * 0.7071067811865476))
            act_ref[at, cols] = (up * cdf).astype(jnp.bfloat16)
            slope = cdf + up * (0.3989422804014327 * jnp.exp(-0.5 * up * up))
            slope_ref[at, cols] = slope.astype(jnp.bfloat16)
            return carry

        lax.fori_loop(0, both // ROWS, one_group, 0, unroll=4)
    for copy in copies:
        copy.wait()
    acc[...] = plain_rows(act_ref[...], w_ref[:, 4 * D : 8 * D], NT)
    sums = tuple(jnp.zeros((1, D), jnp.float32) for _ in range(3))
    for view in range(2):
        def one_chunk(chunk, sums, view=view):
            own = pl.ds(pl.multiple_of(chunk * ROWS, ROWS), ROWS)
            at = pl.ds(pl.multiple_of(view * tokens + chunk * ROWS, ROWS), ROWS)
            keep = keep_of(mask[view, own, :])
            center, inv = norm_parts(first_ref[at, :] + keep * (acc[at, :] + vecs[4:5]))
            grad = cot_ref[view, own, :].astype(jnp.float32)
            hidden_ref[view, own, :] = (center * inv * vecs[5:6] + vecs[6:7]).astype(jnp.bfloat16)
            d_res, unit = norm_back(grad, center, inv, vecs[5:6])
            d_down = d_res * keep
            d_res_ref[at, :] = d_res
            down_ref[at, :] = d_down.astype(jnp.bfloat16)
            return (sums[0] + sum_rows(d_down), sums[1] + sum_rows(grad * unit), sums[2] + sum_rows(grad))

        sums = lax.fori_loop(0, tokens // ROWS, one_chunk, sums, unroll=True)
    part_ref[...] = jnp.zeros_like(part_ref)
    for k in range(3):
        part_ref[4 + k : 5 + k, :] = sums[k]


def head_forward(first_low, first_norm, w_head, vecs, masks, cotangent):
    both = first_low.shape[0]
    tokens = both // 2
    any_space, vmem = pl.BlockSpec(memory_space=pltpu.HBM), pl.BlockSpec(memory_space=pltpu.VMEM)
    f32, low = jnp.float32, jnp.bfloat16
    return pl.pallas_call(
        forward_kernel,
        out_shape=(
            result((both, 4 * D), low, True),
            result((both, 4 * D), low, True),
            result((2, tokens, D), low),
            result((both, D), f32, True),
            result((both, D), low, True),
            result((8, D), f32, True),
        ),
        in_specs=[vmem, vmem, vmem, vmem, any_space, vmem],
        out_specs=(vmem,) * 6,
        scratch_shapes=[
            pltpu.VMEM((2, tokens, D), jnp.int32),
            pltpu.VMEM((both, D), f32),
            pltpu.VMEM((both, CHUNK), f32),
            pltpu.SemaphoreType.DMA((2,)),
        ],
        compiler_params=room(14),
    )(first_low, first_norm, w_head, vecs, masks, cotangent)


def backward_kernel(down_ref, slope_ref, d_res_ref, part_in, w_ref, up_ref, first_ref, part_ref, made):
    part_ref[...] = part_in[...]
    both = down_ref.shape[0]
    sums = []
    for k in range(4 * D // CHUNK):
        cols = pl.ds(k * CHUNK, CHUNK)
        made[...] = plain_rows(down_ref[...], w_ref[:, pl.ds(4 * D + k * CHUNK, CHUNK)], NN)

        def one_group(group, total, cols=cols):
            at = pl.ds(pl.multiple_of(group * ROWS, ROWS), ROWS)
            d_up = made[at, :] * slope_ref[at, cols].astype(jnp.float32)
            up_ref[at, cols] = d_up.astype(jnp.bfloat16)
            return total + sum_rows(d_up)

        sums.append(lax.fori_loop(0, both // ROWS, one_group, jnp.zeros((1, CHUNK), jnp.float32), unroll=4))
    sums = jnp.concatenate(sums, axis=1)
    for c in range(4):
        part_ref[c : c + 1, :] = sums[:, c * D : (c + 1) * D]
    first_ref[...] = d_res_ref[...] + plain_rows(up_ref[...], w_ref[:, : 4 * D], NT)


def head_backward(down_low, slope, d_res, parts, w_head):
    both = down_low.shape[0]
    vmem = pl.BlockSpec(memory_space=pltpu.VMEM)
    f32, low = jnp.float32, jnp.bfloat16
    return pl.pallas_call(
        backward_kernel,
        out_shape=(
            result((both, 4 * D), low, True),
            result((both, D), f32),
            result((8, D), f32, True),
        ),
        in_specs=[vmem] * 5,
        out_specs=(vmem,) * 3,
        scratch_shapes=[
            pltpu.VMEM((both, CHUNK), f32),
        ],
        compiler_params=room(10),
    )(down_low, slope, d_res, parts, w_head)


def pick_columns(core, blocks):
    shape = (blocks * 32, D)
    index = lax.broadcasted_iota(jnp.int32, shape, 0)
    wanted = (index >> 5) * 48 + 24 * core + (index & 31)
    return (wanted == lax.broadcasted_iota(jnp.int32, shape, 1)).astype(jnp.bfloat16)


def pooled_kernel(me_ref, own_ref, sib_ref, w_hbm, cls_own, cls_sib, vrow_in, vcol_in, vec_in,
                  loss_ref, first_ref, out_ref, low_ref, part_ref,
                  units, sims, back, cls, vrow_ref, vcol_ref, vec_ref, w_ref, sems, w_sems):
    me = me_ref[0]
    core = me & 1
    n = units.shape[1]
    pairs = []
    for side, ref in ((0, own_ref), (1, sib_ref)):
        for across in range(4):
            for k in range(4):
                pairs.append((ref.at[across, k], units.at[me ^ (side + 2 * across + 8 * k)]))
    place = pl.multiple_of(core * n, n)
    pairs += [(cls_own, cls.at[pl.ds(place, n)]), (cls_sib, cls.at[pl.ds(n - place, n)])]
    pairs += [(vrow_in, vrow_ref), (vcol_in, vcol_ref), (vec_in, vec_ref)]
    copies = bring(pairs, sems)
    w_copies = bring(
        [
            (w_hbm.at[:, pl.ds(start, size)], w_ref.at[:, pl.ds(start, size)])
            for start, size in ((8 * D, D), (4 * D, 4 * D), (0, 4 * D))
        ],
        w_sems,
    )
    await_all(copies)
    half = n // 2
    total = units.shape[0] * n
    everyone = units[...].reshape(total, D)
    table = plain_rows(everyone, everyone, NT) * (1.0 / logit_divisor)
    row = lax.broadcasted_iota(jnp.int32, (total, total), 0)
    col = lax.broadcasted_iota(jnp.int32, (total, total), 1)
    valid_row = vrow_ref[...] > 0
    table = jnp.where(((col & (n - 1)) >= half) & (vcol_ref[...] > 0), table, masked_scores)
    top = jnp.max(table, axis=-1, keepdims=True)
    row_lse = top + jnp.log(jnp.sum(jnp.exp(table - top), axis=-1, keepdims=True))
    diagonal = col == row + half
    positive = jnp.sum(jnp.where(diagonal, table, 0.0), axis=-1, keepdims=True)
    row_one = lax.broadcasted_iota(jnp.int32, (total, 1), 0)
    anchors = ((row_one & (n - 1)) < half) & valid_row
    loss_ref[0, 0] = jnp.sum(jnp.where(anchors, row_lse - positive, 0.0))
    slope = (jnp.exp(table - row_lse) - jnp.where(diagonal, 1.0, 0.0)) * (1.0 / logit_divisor)
    sims[...] = jnp.where(anchors, slope, 0.0).astype(jnp.bfloat16)
    back[...] = plain_rows(sims[...], everyone, TN)
    chip = pl.ds(pl.multiple_of((me >> 1) * 2 * n, 2 * n), 2 * n)
    d_unit = plain_rows(sims[chip, :], everyone, NN) + back[chip, :]
    pooled = cls[:, :D]
    inv = lax.rsqrt(jnp.sum(pooled * pooled, axis=-1, keepdims=True) + norm_eps)
    along = jnp.sum(pooled * d_unit, axis=-1, keepdims=True)
    d_pooled = inv * d_unit - pooled * (inv * inv * inv * along)
    d_pre = d_pooled * (1.0 - pooled * pooled)
    pool_low = d_pre.astype(jnp.bfloat16)
    await_all(w_copies)
    d_cls = plain_rows(pool_low, w_ref[:, 8 * D :], NT)
    center, scale = norm_parts(cls[:, D : 2 * D])
    cls_low = (center * scale * vec_ref[5:6, :] + vec_ref[6:7, :]).astype(jnp.bfloat16)
    d_res, unit = norm_back(d_cls, center, scale, vec_ref[5:6, :])
    d_down = d_res * cls[:, 2 * D : 3 * D]
    down_low = d_down.astype(jnp.bfloat16)
    d_up = plain_rows(down_low, w_ref[:, 4 * D : 8 * D], NN) * gelu_slope(cls[:, 3 * D :])
    up_low = d_up.astype(jnp.bfloat16)
    cls[:, :D] = d_res + plain_rows(up_low, w_ref[:, : 4 * D], NT)
    first_ref[...] = cls[pl.ds(place, n), :D]
    out_ref[:, :D] = d_down
    out_ref[:, D:] = d_up
    low_ref[:, :D] = cls_low
    low_ref[:, D:] = pool_low
    up_sum = jnp.sum(d_up, axis=0, keepdims=True)
    rows = [up_sum[:, c * D : (c + 1) * D] for c in range(4)]
    rows += [jnp.sum(each, axis=0, keepdims=True) for each in (d_down, d_cls * unit, d_cls, d_pre)]
    for k, value in enumerate(rows):
        part_ref[k : k + 1, :] = value


def pooled_backward(me, units, w_head, cls, valid, vecs):
    n = cls[0].shape[0]
    total = valid.shape[0]
    hbm, vmem = pl.BlockSpec(memory_space=pltpu.HBM), pl.BlockSpec(memory_space=pltpu.VMEM)
    smem = pl.BlockSpec(memory_space=pltpu.SMEM)
    f32, low = jnp.float32, jnp.bfloat16
    return pl.pallas_call(
        pooled_kernel,
        out_shape=(
            result((1, 1), f32),
            result((n, D), f32),
            result((2 * n, 5 * D), f32, True),
            result((2 * n, 2 * D), low, True),
            result((8, D), f32, True),
        ),
        in_specs=[smem] + [hbm] * 8,
        out_specs=(smem,) + (vmem,) * 4,
        scratch_shapes=[
            pltpu.VMEM((32, n, D), low),
            pltpu.VMEM((total, total), low),
            pltpu.VMEM((total, D), f32),
            pltpu.VMEM((2 * n, 7 * D), f32),
            pltpu.VMEM((total, 1), f32),
            pltpu.VMEM((1, total), f32),
            pltpu.VMEM((8, D), f32),
            pltpu.VMEM((D, 9 * D), low),
            pltpu.SemaphoreType.DMA((37,)),
            pltpu.SemaphoreType.DMA((3,)),
        ],
        compiler_params=room(25),
    )(jnp.reshape(me, (1,)), *units, *far(w_head), *cls, valid[:, None], valid[None, :], vecs)


def head_grad_kernel(shard, me_ref, pick_ref, *refs):
    mains, (cls, cls_low, cls_part, part_in, part_sib_in) = refs[:8], refs[8:13]
    pieces, scratch = refs[13:21], refs[21:]
    first, up, down, act, part, part_sib, stage, flat, sems, in_sems = scratch
    me = me_ref[0]
    core = me & 1
    many = mains[0].shape[0]
    n = cls.shape[0] // 2
    half = n // 2
    place = pl.multiple_of(core * n, n)
    pairs = []
    for k, whole in enumerate((first, up, down, act)):
        for side in range(2):
            pairs.append((mains[2 * k + side], whole.at[pl.ds(side * many, many)]))
    loads = bring(pairs + [(part_in, part), (part_sib_in, part_sib)], in_sems)
    for load in loads[:6]:
        load.wait()
    top_row = lax.broadcasted_iota(jnp.int32, (16, 1), 0) == 0
    for side in range(2):
        first_at = place if side == 0 else n - place
        for view in range(2):
            for slot in range(half):
                at = pl.multiple_of(side * many + view * (many // 2) + pick_ref[side, slot], 16)
                source = pl.ds(first_at + view * half + slot, 1)
                for whole, cols in ((up, pl.ds(D, 4 * D)), (down, pl.ds(0, D))):
                    more = jnp.where(top_row, cls[source, cols], 0.0)
                    whole[pl.ds(at, 16), :] = (whole[pl.ds(at, 16), :] + more).astype(jnp.bfloat16)
    blocks, rows = stage.shape[0], stage.shape[1]
    cols = 9 * D // LANES
    pick = pick_columns(core, blocks)

    def spread(grads, first_col):
        for block in range(blocks):
            for group in range(4):
                for k in range(grads.shape[1] // LANES):
                    at = group * 8 * cols + first_col + k
                    size = 8 if group < 3 else 2
                    tile = grads[block * 32 + group * 8 : block * 32 + group * 8 + size]
                    flat[block, pl.ds(at, size, stride=cols), :] = tile[:, k * LANES : (k + 1) * LANES]

    def fill(left, right, first_col):
        chunk = 4 * LANES
        for k in range(right.shape[1] // chunk):
            spread(plain_rows(left, right[:, pl.ds(k * chunk, chunk)], NN), first_col + k * chunk // LANES)

    fill(plain_rows(pick, first[...], NT).astype(jnp.bfloat16), up, 0)
    few = plain_rows(pick, cls_low[:, :D], NT).astype(jnp.bfloat16)
    spread(plain_rows(few, cls_low[:, D:], NN), 8 * D // LANES)
    for load in loads[6:]:
        load.wait()
    fill(plain_rows(pick, down[...], NT).astype(jnp.bfloat16), act, 4 * D // LANES)

    @pl.when(core == 1)
    def _():
        flat[blocks - 1, pl.ds(24 * cols, 48), :] = flat_of(part[...] + part_sib[...] + cls_part[...])

    outs = []
    for piece, slots in list(zip(pieces, piece_slots(me, HALVES)))[::-1]:
        for k, slot in enumerate(slots):
            chip_at = slot >> 1
            at = pl.multiple_of(slot * shard // LANES // 8 * 8 - slot * 24 * cols, 8)
            stage[chip_at] = flat[chip_at, pl.ds(at, rows), :].astype(jnp.bfloat16)
            copy = pltpu.make_async_copy(stage.at[chip_at], piece.at[k], sems.at[len(outs)])
            copy.start()
            outs.append(copy)
    for copy in outs:
        copy.wait()


def head_grads(me, shard, picks, mains, cls, cls_low, cls_part, parts):
    many = mains[0].shape[0]
    rows = block_rows(shard)
    hbm, vmem = pl.BlockSpec(memory_space=pltpu.HBM), pl.BlockSpec(memory_space=pltpu.VMEM)
    smem = pl.BlockSpec(memory_space=pltpu.SMEM)
    f32, low = jnp.float32, jnp.bfloat16
    return pl.pallas_call(
        functools.partial(head_grad_kernel, shard),
        out_shape=tuple(result((2, rows, LANES), low) for _ in HALVES),
        in_specs=[smem] * 2 + [hbm] * 8 + [vmem] * 3 + [hbm] * 2,
        out_specs=(hbm,) * len(HALVES),
        scratch_shapes=[
            pltpu.VMEM((2 * many, D), low),
            pltpu.VMEM((2 * many, 4 * D), low),
            pltpu.VMEM((2 * many, D), low),
            pltpu.VMEM((2 * many, 4 * D), low),
            pltpu.VMEM((8, D), f32),
            pltpu.VMEM((8, D), f32),
            pltpu.VMEM((16, rows, LANES), low),
            pltpu.VMEM((16, 26 * 9 * D // LANES + 4, LANES), f32),
            pltpu.SemaphoreType.DMA((16,)),
            pltpu.SemaphoreType.DMA((10,)),
        ],
        compiler_params=room(44),
    )(jnp.reshape(me, (1,)), picks, *mains, cls, cls_low, cls_part, *parts)


def store_pieces(shard, layout, me, pieces, stage, flat, sems):
    rows = stage.shape[1]
    copies = []
    for piece, slots in list(zip(pieces, piece_slots(me, layout)))[::-1]:
        for k, slot in enumerate(slots):
            at = pl.multiple_of(slot * shard // LANES // 8 * 8, 8)
            stage[slot] = flat[pl.ds(at, rows), :].astype(jnp.bfloat16)
            copy = pltpu.make_async_copy(stage.at[slot], piece.at[k], sems.at[len(copies)])
            copy.start()
            copies.append(copy)
    for copy in copies:
        copy.wait()


def sum_small(value):
    for bit in (CORE, XBIT, YBIT, 8, 16):
        value = value + swap(value, bit)
    return value


def on_grid(
    embeddings,
    cotangent,
    drop_masks,
    lengths,
    buckets,
    attn_params,
    attn_moment,
    attn_second,
    attn_ema,
    head_params,
    head_moment,
    head_second,
    head_ema,
):
    tok_rows = embeddings.shape[0]
    slot_count = lengths.shape[0]
    all_rows = 2 * tok_rows
    device = lax.axis_index("sent")
    shards = (attn_params.shape[0], head_params.shape[0])
    attn_pieces, attn_first, attn_last = gather_attn(attn_params, device)
    head_zs = gather_head_line(head_params, device, attn_first)
    bucket_all = bucket_length(buckets)
    slot_ids = jnp.arange(slot_count, dtype=jnp.int32)
    valid_everything = (
        (slot_ids[None, :] < (tok_rows // bucket_all)[:, None]).astype(jnp.float32).reshape(-1)
    )
    bucket_len = bucket_all[device]

    def picks_of(length):
        count = tok_rows // length
        return jnp.concatenate([jnp.minimum(slot_ids, count - 1) * length, count[None]])

    picks = picks_of(bucket_len)
    both_picks = jnp.stack([picks, picks_of(bucket_all[device ^ CORE])])
    head_line = after(jnp.stack(head_zs), *attn_last)
    head_x, head_y = swap(head_line, XBIT), swap(head_line, YBIT)
    (
        attn_mats,
        attn_vecs,
        emb_rows,
        attn_in_low,
        qkv_low,
        probs,
        mixed_low,
        first_res,
        first_norm,
        first_low,
    ) = attn_forward(attn_pieces, device, shards[0], bucket_len, lengths, embeddings, drop_masks)
    head_x, head_y, first_norm = lax.optimization_barrier((head_x, head_y, first_norm))
    head_pieces = gather_head(head_line, head_x, head_y)
    first_sib = swap(first_low, CORE)
    head_mats, head_vecs, unit_low, cls = make_head(
        head_pieces, device, shards[1], picks, first_norm, drop_masks
    )
    unit_zs = [unit_low] + [swap(unit_low, bit) for bit in ZBITS]
    cls_sib = swap(cls, CORE)
    active_low, slope, hidden_out, d_second_res, down_low, parts = head_forward(
        first_low, first_norm, head_mats, head_vecs, drop_masks, cotangent
    )
    active_low, down_low, unit_zs, cls_sib = lax.optimization_barrier(
        (active_low, down_low, unit_zs, cls_sib)
    )
    unit_line = jnp.stack(unit_zs)
    unit_lines = [unit_line] + [swap(unit_line, bit) for bit in (XBIT, YBIT, XBIT | YBIT)]
    active_sib, down_sib = swap(active_low, CORE), swap(down_low, CORE)
    up_low, d_first, parts = head_backward(down_low, slope, d_second_res, parts, head_mats)
    up_low, unit_lines, active_sib, down_sib = lax.optimization_barrier(
        (up_low, unit_lines, active_sib, down_sib)
    )
    units = jnp.stack(unit_lines)
    units_sib = swap(units, CORE)
    up_sib, parts_sib = swap(after(up_low, units_sib), CORE), swap(parts, CORE)
    valid_views = jnp.broadcast_to(
        valid_everything.reshape(-1, 1, slot_count), (bucket_all.shape[0], 2, slot_count)
    ).reshape(-1)
    loss_sum, d_first_cls, cls_grads, cls_low, cls_part = pooled_backward(
        device, (units, units_sib), head_mats, (cls, cls_sib), valid_views, head_vecs
    )
    head_pieces = head_grads(
        device,
        shards[1],
        both_picks,
        (first_low, first_sib, up_low, up_sib, down_low, down_sib, active_low, active_sib),
        cls_grads,
        cls_low,
        cls_part,
        (parts, parts_sib),
    )
    loss_sum = loss_sum[0, 0]
    d_first, head_pieces = lax.optimization_barrier((d_first, head_pieces))
    line_low, line_high, x_low, x_high, y_low, y_high, d_low, d_high = head_pieces
    d_low, d_high = swap(d_low, XBIT), swap(d_high, YBIT)
    d_first_res, g_out, d_mixed, norm_parts_in = norm_backward(
        picks, d_first, d_first_cls, first_res, attn_vecs, drop_masks, mixed_low, attn_mats
    )
    d_qkv, attn_parts = attn_backward(d_mixed, qkv_low, probs)
    d_qkv, d_low, d_high = lax.optimization_barrier((d_qkv, d_low, d_high))
    x_high, y_high = swap(low_sum(x_high, d_high), XBIT), swap(y_high, YBIT)
    input_grad, *attn_pieces = attn_grads(
        device,
        shards[0],
        bucket_len,
        d_qkv,
        attn_in_low,
        attn_mats,
        d_first_res,
        emb_rows,
        attn_vecs,
        drop_masks,
        g_out,
        attn_parts,
        norm_parts_in,
    )
    attn_pieces, d_low, x_low, x_high, y_high = lax.optimization_barrier(
        (attn_pieces, d_low, x_low, x_high, y_high)
    )
    line_high = low_sum(line_high, x_high, y_high)
    x_low, y_low = swap(x_low, XBIT), swap(low_sum(y_low, d_low), YBIT)
    attn_sums = scatter_core(attn_pieces)
    attn_sums, x_low, y_low = lax.optimization_barrier((attn_sums, x_low, y_low))
    line_low = low_sum(line_low, x_low, y_low)
    head_sum = scatter_along(line_low[0], [line_low[1], line_high[0], line_high[1]])
    head_share = unpack_shard(head_sum, device, shards[1])
    attn_share = unpack_shard(scatter_attn(attn_sums), device, shards[0])
    squares = jnp.sum(attn_share * attn_share) + jnp.sum(head_share * head_share)
    total_squares = sum_small(squares)
    loss = loss_sum / jnp.sum(valid_everything)
    grad_norm = jnp.sqrt(total_squares)
    clip_scale = jnp.minimum(1.0, clip_bound / grad_norm)
    attn_new = adam_step(attn_share * clip_scale, attn_params, attn_moment, attn_second, attn_ema)
    head_new = adam_step(head_share * clip_scale, head_params, head_moment, head_second, head_ema)
    return (
        hidden_out,
        input_grad,
        loss,
        grad_norm,
        attn_new[0],
        attn_new[1],
        attn_new[2],
        attn_new[3],
        head_new[0],
        head_new[1],
        head_new[2],
        head_new[3],
    )


def on_any_mesh(
    embeddings,
    cotangent,
    drop_masks,
    lengths,
    buckets,
    attn_params,
    attn_moment,
    attn_second,
    attn_ema,
    head_params,
    head_moment,
    head_second,
    head_ema,
):
    tok_rows = embeddings.shape[0]
    slot_count = lengths.shape[0]
    all_rows = 2 * tok_rows
    device = lax.axis_index("sent")
    attn_full, head_full = (
        lax.all_gather(attn_params.astype(jnp.bfloat16), "sent", axis=0, tiled=True),
        lax.all_gather(head_params.astype(jnp.bfloat16), "sent", axis=0, tiled=True),
    )
    attn_mats = attn_full[: 4 * D * D].reshape(D, 4 * D)
    attn_vecs_low = attn_full[4 * D * D :].reshape(D, 8 + POS)
    attn_vecs = attn_vecs_low.astype(jnp.float32)
    head_mats = head_full[: 9 * D * D].reshape(D, 9 * D)
    head_vecs = head_full[9 * D * D :].reshape(D, 8).astype(jnp.float32)
    w_qkv = attn_mats[:, : 3 * D]
    w_out = attn_mats[:, 3 * D :]
    w_up = head_mats[:, : 4 * D]
    w_down = head_mats[:, 4 * D : 8 * D]
    w_pool = head_mats[:, 8 * D :]
    bucket_all = bucket_length(buckets)
    slot_ids = jnp.arange(slot_count, dtype=jnp.int32)
    valid_everything = (
        (slot_ids[None, :] < (tok_rows // bucket_all)[:, None]).astype(jnp.float32).reshape(-1)
    )
    bucket_len = bucket_all[device]
    sent_count = tok_rows // bucket_len
    valid_own = (slot_ids < sent_count).astype(jnp.float32)
    row_ids = jnp.arange(tok_rows, dtype=jnp.int32)
    sentence = row_ids // bucket_len
    row_place = row_ids % bucket_len
    slot_len = jnp.sum(
        jnp.where(sentence[:, None] == slot_ids[None, :], lengths[None, :], 0), axis=1
    )
    key_ok = row_place < slot_len
    block = POS
    sent_blocks = sentence.reshape(-1, block)
    ok_blocks = key_ok.reshape(-1, block)
    allowed = (sent_blocks[:, :, None] == sent_blocks[:, None, :]) & ok_blocks[:, None, :]
    allowed = jnp.concatenate([allowed, allowed], axis=0)[:, None]
    place_hot = (row_place[:, None] == jnp.arange(POS, dtype=jnp.int32)[None, :]).astype(
        jnp.bfloat16
    )
    pos_rows = plain_dot(place_hot, attn_vecs_low[:, 8:].T)
    emb_rows = embeddings.astype(jnp.float32) + pos_rows + attn_vecs[:, 7]
    normed, emb_back = jax.vjp(layer_norm, emb_rows, attn_vecs[:, 5], attn_vecs[:, 6])
    keep_masks = drop_masks.astype(jnp.float32) / keep_prob
    keep_attn = keep_masks[:, 1].reshape(all_rows, D)
    keep_ffn = keep_masks[:, 2].reshape(all_rows, D)
    attn_in = (normed[None] * keep_masks[:, 0]).reshape(all_rows, D)
    attn_in_low = attn_in.astype(jnp.bfloat16)
    qkv_bias = jnp.concatenate([attn_vecs[:, 0], jnp.zeros((D,), jnp.float32), attn_vecs[:, 1]])
    qkv_low = (plain_dot(attn_in_low, w_qkv) + qkv_bias).astype(jnp.bfloat16)
    head_split = qkv_low.reshape(-1, block, 3, H, HD)
    queries = head_split[:, :, 0]
    keys_low = head_split[:, :, 1]
    values_low = head_split[:, :, 2]
    score_scale = HD ** (-0.5)
    raw_scores = jnp.einsum(
        "bqhd,bkhd->bhqk", queries, keys_low, preferred_element_type=jnp.float32
    )
    scores = jnp.where(allowed, raw_scores * score_scale, masked_scores)
    row_top = jnp.max(scores, axis=-1, keepdims=True)
    expo_vals = jnp.exp(scores - row_top)
    row_total = jnp.sum(expo_vals, axis=-1, keepdims=True)
    attn_probs = expo_vals / row_total
    score_lse = row_top + jnp.log(row_total)
    mixed_out = jnp.einsum(
        "bhqk,bkhd->bqhd",
        attn_probs.astype(jnp.bfloat16),
        values_low,
        preferred_element_type=jnp.float32,
    )
    mixed_low = mixed_out.reshape(all_rows, D).astype(jnp.bfloat16)
    branch = plain_dot(mixed_low, w_out) + attn_vecs[:, 2]
    first_res = attn_in + keep_attn * branch
    first_norm, first_back = jax.vjp(layer_norm, first_res, attn_vecs[:, 3], attn_vecs[:, 4])
    first_low = first_norm.astype(jnp.bfloat16)
    up_bias = head_vecs[:, :4].T.reshape(4 * D)
    up_pre = plain_dot(first_low, w_up) + up_bias
    active, gelu_back = jax.vjp(gelu_exact, up_pre)
    active_low = active.astype(jnp.bfloat16)
    down_out = target_dot_terms(active_low, w_down) + head_vecs[:, 4]
    second_res = first_norm + keep_ffn * down_out
    second_norm, second_back = jax.vjp(layer_norm, second_res, head_vecs[:, 5], head_vecs[:, 6])
    hidden_out = second_norm.astype(jnp.bfloat16).reshape(2, tok_rows, D)
    cls_pick = jnp.minimum(slot_ids, sent_count - 1) * bucket_len
    cls_rows = jnp.take(second_norm.reshape(2, tok_rows, D), cls_pick, axis=1).reshape(
        2 * slot_count, D
    )
    cls_low = cls_rows.astype(jnp.bfloat16)
    pooled = jnp.tanh(plain_dot(cls_low, w_pool) + head_vecs[:, 7])
    unit_rows, unit_back = jax.vjp(unit_scale, pooled)
    unit_low = unit_rows.astype(jnp.bfloat16)
    query_embeddings = unit_low[:slot_count]
    positive_view_set = unit_low[slot_count:]
    target_sentence_set, everyone = (
        lax.all_gather(positive_view_set, "sent", axis=0, tiled=True),
        lax.all_gather(query_embeddings, "sent", axis=0, tiled=True),
    )
    own_cols = device * slot_count + slot_ids
    col_ids = jnp.arange(target_sentence_set.shape[0], dtype=jnp.int32)
    pos_hot = col_ids[None, :] == own_cols[:, None]
    cosine_logit_table = jnp.where(
        valid_everything[None, :] > 0,
        target_dot_terms(query_embeddings, target_sentence_set) / logit_divisor,
        masked_scores,
    )
    sim_top = jnp.max(cosine_logit_table, axis=-1, keepdims=True)
    row_lse = sim_top[:, 0] + jnp.log(jnp.sum(jnp.exp(cosine_logit_table - sim_top), axis=-1))
    positive = jnp.sum(jnp.where(pos_hot, cosine_logit_table, 0.0), axis=-1)
    local_loss = jnp.sum(valid_own * (row_lse - positive))
    loss_sum = lax.psum(local_loss, "sent")
    cosine_logit_cotangent = valid_own[:, None] * (
        jnp.exp(cosine_logit_table - row_lse[:, None]) - pos_hot.astype(jnp.float32)
    )
    cosine_logit_summed = (cosine_logit_cotangent / logit_divisor).astype(jnp.bfloat16)
    d_anchor = plain_dot(cosine_logit_summed, target_sentence_set)
    all_lse = lax.all_gather(row_lse, "sent", axis=0, tiled=True)
    back_sim = target_dot_terms(everyone, positive_view_set) / logit_divisor
    back_hot = (col_ids[:, None] == own_cols[None, :]).astype(jnp.float32)
    back_grad = valid_everything[:, None] * (
        jnp.exp(back_sim - all_lse[:, None]) * valid_own[None, :] - back_hot
    )
    d_partner = rows_dot((back_grad / logit_divisor).astype(jnp.bfloat16), everyone)
    d_unit = jnp.concatenate([d_anchor, d_partner], axis=0)
    d_pooled = unit_back(d_unit)[0]
    d_pool_pre = d_pooled * (1.0 - pooled * pooled)
    pool_low = d_pool_pre.astype(jnp.bfloat16)
    g_pool = rows_dot(cls_low, pool_low)
    g_pool_bias = jnp.sum(d_pool_pre, axis=0)
    d_cls = target_dot_terms(pool_low, w_pool).reshape(2, slot_count, D)
    pick_hot = ((row_ids[None, :] == cls_pick[:, None]) & (slot_ids[:, None] < sent_count)).astype(
        jnp.float32
    )
    d_second = cotangent.astype(jnp.float32) + jnp.einsum(
        "st,vsd->vtd", pick_hot, d_cls, precision=highest
    )
    d_second_res, g_gain_two, g_shift_two = second_back(d_second.reshape(all_rows, D))
    d_down = d_second_res * keep_ffn
    g_down_bias = jnp.sum(d_down, axis=0)
    down_low = d_down.astype(jnp.bfloat16)
    g_down = rows_dot(down_low, active_low)
    d_active = plain_dot(down_low, w_down)
    d_up = gelu_back(d_active)[0]
    g_up_bias = jnp.sum(d_up, axis=0)
    up_low = d_up.astype(jnp.bfloat16)
    g_up = rows_dot(first_low, up_low)
    d_first = d_second_res + target_dot_terms(up_low, w_up)
    head_vec_grad = jnp.concatenate(
        [
            g_up_bias.reshape(4, D).T,
            jnp.stack([g_down_bias, g_gain_two, g_shift_two, g_pool_bias], axis=1),
        ],
        axis=1,
    )
    head_grad = jnp.concatenate(
        [jnp.concatenate([g_up, g_down, g_pool], axis=1).reshape(-1), head_vec_grad.reshape(-1)]
    )
    d_first_res, g_gain_one, g_shift_one = first_back(d_first)
    d_branch = d_first_res * keep_attn
    g_out_bias = jnp.sum(d_branch, axis=0)
    branch_low = d_branch.astype(jnp.bfloat16)
    g_out = rows_dot(mixed_low, branch_low)
    d_mixed = target_dot_terms(branch_low, w_out).astype(jnp.bfloat16).reshape(-1, block, H, HD)
    again = jnp.where(
        allowed,
        jnp.einsum("bqhd,bkhd->bhqk", queries, keys_low, preferred_element_type=jnp.float32)
        * score_scale,
        masked_scores,
    )
    probs_again = jnp.exp(again - score_lse)
    d_values = jnp.einsum(
        "bhqk,bqhd->bkhd",
        probs_again.astype(jnp.bfloat16),
        d_mixed,
        preferred_element_type=jnp.float32,
    )
    d_probs = jnp.einsum("bqhd,bkhd->bhqk", d_mixed, values_low, preferred_element_type=jnp.float32)
    row_delta = jnp.sum(probs_again * d_probs, axis=-1, keepdims=True)
    score_low = (probs_again * (d_probs - row_delta) * score_scale).astype(jnp.bfloat16)
    d_queries = jnp.einsum(
        "bhqk,bkhd->bqhd", score_low, keys_low, preferred_element_type=jnp.float32
    )
    d_keys = jnp.einsum("bhqk,bqhd->bkhd", score_low, queries, preferred_element_type=jnp.float32)
    d_qkv = jnp.stack([d_queries, d_keys, d_values], axis=2).reshape(all_rows, 3 * D)
    g_q_bias = jnp.sum(d_queries.reshape(all_rows, D), axis=0)
    g_v_bias = jnp.sum(d_values.reshape(all_rows, D), axis=0)
    qkv_grad_low = d_qkv.astype(jnp.bfloat16)
    g_qkv = rows_dot(attn_in_low, qkv_grad_low)
    d_attn_in = d_first_res + target_dot_terms(qkv_grad_low, w_qkv)
    d_normed = jnp.sum(d_attn_in.reshape(2, tok_rows, D) * keep_masks[:, 0], axis=0)
    input_grad, g_gain_emb, g_shift_emb = emb_back(d_normed)
    g_type = jnp.sum(input_grad, axis=0)
    g_table = lax.dot_general(
        place_hot.astype(jnp.float32),
        input_grad,
        (((0,), (0,)), ((), ())),
        precision=highest,
        preferred_element_type=jnp.float32,
    )
    attn_vec_grad = jnp.concatenate(
        [
            jnp.stack(
                [
                    g_q_bias,
                    g_v_bias,
                    g_out_bias,
                    g_gain_one,
                    g_shift_one,
                    g_gain_emb,
                    g_shift_emb,
                    g_type,
                ],
                axis=1,
            ),
            g_table.T,
        ],
        axis=1,
    )
    attn_grad = jnp.concatenate(
        [jnp.concatenate([g_qkv, g_out], axis=1).reshape(-1), attn_vec_grad.reshape(-1)]
    )
    attn_share, head_share = (
        lax.psum_scatter(attn_grad, "sent", scatter_dimension=0, tiled=True),
        lax.psum_scatter(head_grad, "sent", scatter_dimension=0, tiled=True),
    )
    squares = jnp.sum(attn_share * attn_share) + jnp.sum(head_share * head_share)
    total_squares = lax.psum(squares, "sent")
    loss = loss_sum / jnp.sum(valid_everything)
    grad_norm = jnp.sqrt(total_squares)
    clip_scale = jnp.minimum(1.0, clip_bound / grad_norm)
    attn_new = adam_step(attn_share * clip_scale, attn_params, attn_moment, attn_second, attn_ema)
    head_new = adam_step(head_share * clip_scale, head_params, head_moment, head_second, head_ema)
    return (
        hidden_out,
        input_grad,
        loss,
        grad_norm,
        attn_new[0],
        attn_new[1],
        attn_new[2],
        attn_new[3],
        head_new[0],
        head_new[1],
        head_new[2],
        head_new[3],
    )


def on_device(*arrays):
    shards = (arrays[5].shape[0], arrays[9].shape[0])
    local = on_grid if is_grid(lax.axis_size("sent"), *shards) else on_any_mesh
    return local(*arrays)


def solution(mesh):
    in_specs = (
        P("sent", None),
        P(None, "sent", None),
        P(None, None, "sent", None),
        P("sent"),
        P(),
        P("sent"),
        P("sent"),
        P("sent"),
        P("sent"),
        P("sent"),
        P("sent"),
        P("sent"),
        P("sent"),
    )
    out_specs = (
        P(None, "sent", None),
        P("sent", None),
        P(),
        P(),
        P("sent"),
        P("sent"),
        P("sent"),
        P("sent"),
        P("sent"),
        P("sent"),
        P("sent"),
        P("sent"),
    )
    return jax.shard_map(
        on_device, mesh=mesh, in_specs=in_specs, out_specs=out_specs, check_vma=False
    )
```

```python
import functools

import jax
import jax.numpy as jnp
from jax import lax
from jax.experimental import pallas as pl
from jax.experimental.pallas import tpu as pltpu
from jax.sharding import PartitionSpec as P

D = 768
H = 12
HD = 64
LMIN = 32
POS = 128
STEP = 5


logit_divisor = 0.05
keep_prob = 0.9
norm_eps = 1e-06
clip_bound = 0.001
beta_first = 0.5
beta_second = 0.5
learn_rate = 0.05
decay_rate = 0.01
adam_eps = 1e-08
ema_rate = 0.8
masked_scores = -1e30
highest = lax.Precision.HIGHEST


def layer_norm(tensor, gain_vec, shift_vec):
    center = tensor - jnp.mean(tensor, axis=-1, keepdims=True)
    spread = jnp.mean(center * center, axis=-1, keepdims=True)
    return center * lax.rsqrt(spread + norm_eps) * gain_vec + shift_vec


def gelu_exact(tensor):
    return 0.5 * tensor * (1.0 + jax.scipy.special.erf(tensor * 0.7071067811865476))


def unit_scale(tensor):
    return tensor * lax.rsqrt(jnp.sum(tensor * tensor, axis=-1, keepdims=True) + norm_eps)


def bucket_length(bucket_code):
    return (LMIN * jnp.where(bucket_code == 0, 1, jnp.where(bucket_code == 1, 2, 4))).astype(
        jnp.int32
    )


def plain_dot(left_op, right_op):
    return jnp.dot(left_op, right_op, preferred_element_type=jnp.float32)


def rows_dot(left_op, right_op):
    return lax.dot_general(
        left_op, right_op, (((0,), (0,)), ((), ())), preferred_element_type=jnp.float32
    )


def target_dot_terms(left_op, right_op):
    return lax.dot_general(
        left_op, right_op, (((1,), (1,)), ((), ())), preferred_element_type=jnp.float32
    )


def adam_step(grad_flat, params, moment, second, average):
    first_new = beta_first * moment + (1.0 - beta_first) * grad_flat
    second_new = beta_second * second + (1.0 - beta_second) * grad_flat * grad_flat
    fix_first = 1.0 - beta_first**STEP
    fix_second = 1.0 - beta_second**STEP
    adam_dir = first_new / fix_first / (jnp.sqrt(second_new / fix_second) + adam_eps)
    updated = params - learn_rate * (adam_dir + decay_rate * params)
    average_new = ema_rate * average + (1.0 - ema_rate) * updated
    return (first_new, second_new, updated, average_new)


LANES = 128
VMEM_CAP = 60 * 2**20


def room(mib):
    return pltpu.CompilerParams(vmem_limit_bytes=mib * 2**20)


def far(*arrays):
    return [pltpu.with_memory_space_constraint(array, pltpu.HBM) for array in arrays]


def bring(pairs, sems, first=0):
    copies = []
    for source, target in pairs:
        copies.append(pltpu.make_async_copy(source, target, sems.at[first + len(copies)]))
        copies[-1].start()
    return copies


def await_all(copies):
    for copy in copies:
        copy.wait()


def result(shape, dtype, stays=False):
    return pltpu.VMEM(shape, dtype) if stays else jax.ShapeDtypeStruct(shape, dtype)
CORE, XBIT, YBIT, ZBITS = 1, 2, 4, (8, 16, 24)


def swap(value, bit):
    count = lax.axis_size("sent")
    return lax.ppermute(value, "sent", [(i, i ^ bit) for i in range(count)])


def is_grid(count, *shards):
    return count == 32 and all(2 * shard % LANES == 0 for shard in shards)


def block_rows(shard):
    return -(-(-(-shard // LANES) + 8) // 16) * 16


def first_row(device, shard):
    return (device * shard) // LANES


def pack_shard(values, device):
    shard = values.shape[0]
    rows = block_rows(shard)
    size = rows * LANES
    odd = (device * shard) % LANES != 0
    lead = jnp.where(
        odd,
        jnp.pad(values, (LANES // 2, size - shard - LANES // 2)),
        jnp.pad(values, (0, size - shard)),
    ).reshape(rows, LANES)
    offset = first_row(device, shard) % 8
    padded = jnp.pad(lead, ((8, 0), (0, 0)))
    return lax.dynamic_slice(padded, (8 - offset, 0), (rows, LANES)).astype(jnp.bfloat16)


def unpack_shard(block, device, shard):
    rows = -(-shard // LANES)
    offset = first_row(device, shard) % 8
    odd = (device * shard) % LANES != 0
    flat = lax.dynamic_slice(block, (offset, 0), (rows, LANES)).reshape(-1)
    longer = jnp.pad(flat, (0, LANES))
    return jnp.where(odd, longer[LANES // 2 : LANES // 2 + shard], flat[:shard])


WHOLE = ((0, 0, 4), (1, 0, 4), (2, 0, 4), (3, 0, 2), (3, 2, 2))
HALVES = tuple((across, first, 2) for across in range(4) for first in (0, 2))


def piece_slots(me, layout):
    slots = []
    for core in (0, 1):
        for across, first, n in layout:
            slots.append([me ^ (core + 2 * across + 8 * (first + k)) for k in range(n)])
    return slots


def after(value, *others):
    return lax.optimization_barrier((value, others))[0]


def with_sibling(own):
    return tuple(own) + tuple(swap(piece, CORE) for piece in own)


def gather_attn(values, device):
    block = pack_shard(values, device)
    zs = [swap(block, bit) for bit in ZBITS]
    line = jnp.stack([block] + zs)
    x, y = swap(line, XBIT), swap(line, YBIT)
    diagonal = (swap(y[:2], XBIT), swap(x[2:], YBIT))
    return with_sibling((line, x, y) + diagonal), zs[0], diagonal


def gather_head_line(values, device, first):
    block = after(pack_shard(values, device), first)
    return [block] + [swap(block, bit) for bit in ZBITS]


def gather_head(low, high, x_low, x_high, y_low, y_high):
    return with_sibling((low, high, x_low, x_high, y_low, y_high, swap(y_low, XBIT), swap(x_high, YBIT)))


def low_sum(*terms):
    total = terms[0].astype(jnp.float32)
    for term in terms[1:]:
        total = total + term.astype(jnp.float32)
    return total.astype(jnp.bfloat16)


def scatter_core(pieces):
    half = len(pieces) // 2
    got = [swap(piece, CORE) for piece in reversed(pieces[half:])][::-1]
    return [low_sum(piece, other) for piece, other in zip(pieces[:half], got)]


def scatter_attn(sums):
    line, x, y, d_low, d_high = sums
    d_low, d_high = swap(d_low, XBIT), swap(d_high, YBIT)
    x = swap(jnp.concatenate([x[:2], low_sum(x[2:], d_high)]), XBIT)
    y = swap(jnp.concatenate([low_sum(y[:2], d_low), y[2:]]), YBIT)
    line = low_sum(line, x, y)
    return scatter_along(line[0], [line[k] for k in (1, 2, 3)])


def scatter_along(own, others):
    total = own.astype(jnp.float32)
    for value, bit in zip(others, ZBITS):
        total = total + swap(value, bit).astype(jnp.float32)
    return total


def plain_rows(left, right, dims):
    return lax.dot_general(left, right, (dims, ((), ())), preferred_element_type=jnp.float32)


NN, NT, TN = ((1,), (0,)), ((1,), (1,)), ((0,), (0,))


def one_hot(shape, left, right):
    rows = lax.broadcasted_iota(jnp.int32, shape, 0)
    cols = lax.broadcasted_iota(jnp.int32, shape, 1)
    return jnp.where(left(rows, cols) == right(rows, cols), 1.0, 0.0)


def vectors_of(flat_rows):
    spread = one_hot((D, 48), lambda r, c: r >> 4, lambda r, c: c).astype(jnp.bfloat16)
    rows = plain_rows(spread, flat_rows.astype(jnp.bfloat16), NN)
    rows = rows * one_hot((D, LANES), lambda r, c: r & 15, lambda r, c: c >> 3)
    fold = one_hot((8, LANES), lambda r, c: r, lambda r, c: c & 7).astype(jnp.bfloat16)
    return plain_rows(fold, rows.astype(jnp.bfloat16), NT)


def flat_of(vectors):
    fold = one_hot((8, LANES), lambda r, c: r, lambda r, c: c & 7).astype(jnp.bfloat16)
    rows = plain_rows(vectors.astype(jnp.bfloat16), fold, TN)
    rows = rows * one_hot((D, LANES), lambda r, c: r & 15, lambda r, c: c >> 3)
    spread = one_hot((D, 48), lambda r, c: r >> 4, lambda r, c: c).astype(jnp.bfloat16)
    return plain_rows(spread, rows.astype(jnp.bfloat16), TN)


def keep_of(mask):
    return mask.astype(jnp.float32) * (1.0 / keep_prob)


def place_blocks(shard, layout, pieces, me, stage, flat, sems):
    count, rows = stage.shape[0], stage.shape[1]
    for piece, slots in zip(pieces, piece_slots(me, layout)):
        for k, slot in enumerate(slots):
            pltpu.make_async_copy(piece.at[k], stage.at[slot], sems.at[slot]).start()
    flat[pl.ds(0, 8), :] = jnp.zeros((8, LANES), jnp.float32)

    def place(device, carry):
        pltpu.make_async_copy(pieces[0].at[0], stage.at[device], sems.at[device]).wait()
        at = pl.multiple_of(device * shard // LANES // 8 * 8, 8)
        before = flat[pl.ds(at, 8), :]
        flat[pl.ds(at, rows), :] = stage[device].astype(jnp.float32)
        flat[pl.ds(at, 8), :] += before
        return carry

    lax.fori_loop(0, count, place, 0)


def gather_matrix(flat, w_ref, w_out=None, out_sems=None):
    cols = w_ref.shape[1] // LANES

    def gather_rows(group, carry):
        at = pl.multiple_of(group * 16, 16)
        for col in range(cols):
            rows16 = flat[pl.ds(group * 16 * cols + col, 16, stride=cols), :]
            w_ref[pl.ds(at, 16), pl.ds(col * LANES, LANES)] = rows16.astype(jnp.bfloat16)
        return carry

    parts = 4
    span = D // parts
    copies = []
    for part in range(parts):
        lax.fori_loop(part * span // 16, (part + 1) * span // 16, gather_rows, 0)
        here = pl.ds(part * span, span)
        if w_out is not None:
            copies.append(pltpu.make_async_copy(w_ref.at[here], w_out.at[here], out_sems.at[part]))
            copies[-1].start()
    return copies


VEC = 8 + POS


def table_of(flat, base, body, tail):
    lane = lax.broadcasted_iota(jnp.int32, (D // 16, LANES), 1)
    for q in range(16):
        here = flat[pl.ds(base + q, D // 16, stride=17), :]
        later = flat[pl.ds(base + q + 1, D // 16, stride=17), :]
        both = jnp.where(lane >= 8 * q, here, later)
        shift = (LANES - 8 * q) % LANES
        body[pl.ds(q, D // 16, stride=16), :] = pltpu.roll(both, shift, 1) if shift else both
        tail[pl.ds(q, D // 16, stride=16), :] = pltpu.roll(later, shift, 1) if shift else later
    return body[...].T, tail[...].T[:8]


def flat_table(flat, base, first, last, body, tail):
    body[...] = first.T
    tail[...] = jnp.concatenate([last, jnp.zeros((LANES - 8, D), jnp.float32)]).T
    lane = lax.broadcasted_iota(jnp.int32, (D // 16, LANES), 1)
    carried = None
    for q in range(17):
        row = carried
        if q < 16:
            main = body[pl.ds(q, D // 16, stride=16), :]
            end = tail[pl.ds(q, D // 16, stride=16), :]
            if q:
                main, end = pltpu.roll(main, 8 * q, 1), pltpu.roll(end, 8 * q, 1)
            row = main if carried is None else jnp.where(lane >= 8 * q, main, carried)
            carried = jnp.where(lane < 8 * q, main, end)
        flat[pl.ds(base + q, D // 16, stride=17), :] = row


def repeat_places(table, length):
    twice = jnp.concatenate([table[:64]] * 2)
    four = jnp.concatenate([table[:32]] * 4)
    return jnp.where(length == 128, table, jnp.where(length == 64, twice, four))


def fold_places(rows, length):
    half = rows[:64] + rows[64:]
    quarter = half[:32] + half[32:]
    none = jnp.zeros_like(rows)
    twice = jnp.concatenate([half, none[:64]])
    four = jnp.concatenate([quarter, none[:96]])
    return jnp.where(length == 128, rows, jnp.where(length == 64, twice, four))


def stack_heads(pair):
    lane = lax.broadcasted_iota(jnp.int32, pair.shape, 1)
    none = jnp.zeros_like(pair)
    return jnp.concatenate([jnp.where(lane < HD, pair, none), jnp.where(lane < HD, none, pair)])


def unstack_heads(rows):
    half = rows.shape[0] // 2
    lane = lax.broadcasted_iota(jnp.int32, (half, rows.shape[1]), 1)
    return jnp.where(lane < HD, rows[:half], rows[half:])


ROWS = 64


def attn_kernel(shard, me_ref, length_ref, lens_ref, *refs):
    pieces, (emb_ref, mask_hbm) = refs[:10], refs[10:12]
    (w_out, vec_ref, rows_ref, in_low_ref, qkv_ref, prob_ref, mixed_ref, res_ref, norm_ref, low_ref) = refs[12:22]
    (stage, flat, w_ref, body, tail, mask, attn_in, bias_ref, sems, out_sems, mask_sems) = refs[22:]
    me = me_ref[0]
    tokens = emb_ref.shape[0]
    masks = []
    for view in range(2):
        for which in range(2):
            at = 2 * view + which
            masks.append(pltpu.make_async_copy(mask_hbm.at[view, which], mask.at[at], mask_sems.at[at]))
            masks[-1].start()
    place_blocks(shard, WHOLE, pieces, me, stage, flat, sems)
    copies = gather_matrix(flat, w_ref, w_out, out_sems)
    first, last = table_of(flat, D * w_ref.shape[1] // LANES, body, tail)
    vecs = first[:8]
    vec_ref[...] = vecs
    length = length_ref[0]
    places = repeat_places(jnp.concatenate([first[8:], last]), length)
    for copy in masks:
        copy.wait()
    for block in range(tokens // LANES):
        key = lax.broadcasted_iota(jnp.int32, (LANES, LANES), 1) + block * LANES
        query = lax.broadcasted_iota(jnp.int32, (LANES, LANES), 0) + block * LANES
        shift = jnp.where(length == 128, 7, jnp.where(length == 64, 6, 5))
        sent = lax.shift_right_logical(key, jnp.full_like(key, 1) * shift)
        sent_q = lax.shift_right_logical(query, jnp.full_like(key, 1) * shift)
        real = jnp.zeros_like(key)
        for slot in range(lens_ref.shape[0]):
            real = jnp.where(sent == slot, lens_ref[slot], real)
        ok = (sent == sent_q) & ((key & (length - 1)) < real)
        bias_ref[block] = jnp.where(ok, 0.0, masked_scores)
        here = pl.ds(block * LANES, LANES)
        emb = emb_ref[here, :].astype(jnp.float32) + places + vecs[7:8]
        rows_ref[here, :] = emb
        normed = layer_norm(emb, vecs[5:6], vecs[6:7])
        for view in range(2):
            at = pl.ds(view * tokens + block * LANES, LANES)
            given = normed * keep_of(mask[2 * view, here, :])
            attn_in[at, :] = given
            in_low_ref[at, :] = given.astype(jnp.bfloat16)
    for part in range(3):
        cols = pl.ds(part * D, D)
        made = plain_rows(in_low_ref[...], w_ref[:, cols], NN)
        if part != 1:
            made = made + vecs[part // 2 : part // 2 + 1]
        qkv_ref[:, cols] = made.astype(jnp.bfloat16)

    def attend(block, carry):
        here = pl.ds(pl.multiple_of(block * LANES, LANES), LANES)
        bias = bias_ref[block & 1]
        bias = jnp.concatenate([bias, bias])
        for pair in range(H // 2):
            q = stack_heads(qkv_ref[here, pl.ds(pair * LANES, LANES)])
            k = qkv_ref[here, pl.ds(D + pair * LANES, LANES)]
            v = qkv_ref[here, pl.ds(2 * D + pair * LANES, LANES)]
            scores = plain_rows(q, k, NT) * HD ** (-0.5) + bias
            expo = jnp.exp(scores - jnp.max(scores, axis=-1, keepdims=True))
            probs = expo / jnp.sum(expo, axis=-1, keepdims=True)
            prob_ref[block, pair] = probs
            mixed = unstack_heads(plain_rows(probs.astype(jnp.bfloat16), v, NN))
            mixed_ref[here, pl.ds(pair * LANES, LANES)] = mixed.astype(jnp.bfloat16)
        return carry

    lax.fori_loop(0, 2 * tokens // LANES, attend, 0)
    res_ref[...] = plain_rows(mixed_ref[...], w_ref[:, 3 * D :], NN)
    for view in range(2):
        def finish(chunk, carry, view=view):
            own = pl.ds(pl.multiple_of(chunk * ROWS, ROWS), ROWS)
            at = pl.ds(pl.multiple_of(view * tokens + chunk * ROWS, ROWS), ROWS)
            res = attn_in[at, :] + keep_of(mask[2 * view + 1, own, :]) * (res_ref[at, :] + vecs[2:3])
            res_ref[at, :] = res
            norm = layer_norm(res, vecs[3:4], vecs[4:5])
            norm_ref[at, :] = norm
            low_ref[at, :] = norm.astype(jnp.bfloat16)
            return carry

        lax.fori_loop(0, tokens // ROWS, finish, 0, unroll=True)
    for copy in copies:
        copy.wait()


def attn_forward(pieces, me, shard, length, lengths, embeddings, masks):
    rows = pieces[0].shape[1]
    whole = shard * 32 // LANES
    tokens = embeddings.shape[0]
    both = 2 * tokens
    any_space, vmem = pl.BlockSpec(memory_space=pltpu.HBM), pl.BlockSpec(memory_space=pltpu.VMEM)
    smem = pl.BlockSpec(memory_space=pltpu.SMEM)
    f32, low = jnp.float32, jnp.bfloat16
    shapes = [
        ((D, 4 * D), low),
        ((8, D), f32),
        ((tokens, D), f32),
        ((both, D), low),
        ((both, 3 * D), low),
        ((both // LANES, H // 2, 2 * LANES, LANES), f32),
        ((both, D), low),
        ((both, D), f32),
        ((both, D), f32),
        ((both, D), low),
    ]
    return pl.pallas_call(
        functools.partial(attn_kernel, shard),
        out_shape=tuple(jax.ShapeDtypeStruct(*s) for s in shapes),
        in_specs=[smem] * 3 + [any_space] * len(pieces) + [vmem, any_space],
        out_specs=(any_space,) + (vmem,) * 9,
        scratch_shapes=[
            pltpu.VMEM((32, rows, LANES), low),
            pltpu.VMEM((whole + rows, LANES), f32),
            pltpu.VMEM((D, 4 * D), low),
            pltpu.VMEM((D, LANES), f32),
            pltpu.VMEM((D, LANES), f32),
            pltpu.VMEM((4, tokens, D), jnp.int32),
            pltpu.VMEM((both, D), f32),
            pltpu.VMEM((tokens // LANES, LANES, LANES), f32),
            pltpu.SemaphoreType.DMA((32,)),
            pltpu.SemaphoreType.DMA((4,)),
            pltpu.SemaphoreType.DMA((4,)),
        ],
        compiler_params=pltpu.CompilerParams(vmem_limit_bytes=VMEM_CAP),
    )(jnp.reshape(me, (1,)), jnp.reshape(length, (1,)), lengths, *far(*pieces), embeddings, *far(masks))


def sum_rows(rows):
    return jnp.sum(rows, axis=0, keepdims=True)


def norm_back_kernel(pick_ref, d_first, d_cls_in, res_in, vec_in, mask_hbm, mixed_in, w_in,
                     d_res_ref, g_out_ref, d_mixed, part_ref,
                     mask, given, branch, d_cls, res_ref, vec_ref, mixed_ref, w_ref, sems):
    tokens = mask.shape[1]
    both = 2 * tokens
    copies = bring(
        [(d_first, given), (d_cls_in, d_cls), (res_in, res_ref), (vec_in, vec_ref)]
        + [(mask_hbm.at[view, 1], mask.at[view]) for view in range(2)]
        + [(w_in.at[:, pl.ds(3 * D, D)], w_ref), (mixed_in, mixed_ref)],
        sems,
    )
    await_all(copies[:6])
    n = d_cls.shape[0] // 2
    for slot in range(n):
        real = jnp.where(slot < pick_ref[n], 1.0, 0.0)
        for view in range(2):
            at = pl.ds(view * tokens + pick_ref[slot], 1)
            given[at, :] += real * d_cls[view * n + slot : view * n + slot + 1, :]
    gain = vec_ref[3:4, :]
    sums = tuple(jnp.zeros((1, D), jnp.float32) for _ in range(3))
    for view in range(2):
        def one_chunk(chunk, sums, view=view):
            own = pl.ds(pl.multiple_of(chunk * ROWS, ROWS), ROWS)
            at = pl.ds(pl.multiple_of(view * tokens + chunk * ROWS, ROWS), ROWS)
            grad = given[at, :]
            center, inv = norm_parts(res_ref[at, :])
            d_res, unit = norm_back(grad, center, inv, gain)
            d_branch = d_res * keep_of(mask[view, own, :])
            d_res_ref[at, :] = d_res
            branch[at, :] = d_branch.astype(jnp.bfloat16)
            return (
                sums[0] + sum_rows(d_branch),
                sums[1] + sum_rows(grad * unit),
                sums[2] + sum_rows(grad),
            )

        sums = lax.fori_loop(0, tokens // ROWS, one_chunk, sums, unroll=True)
    await_all(copies[6:])
    d_mixed[...] = plain_rows(branch[...], w_ref[...], NT).astype(jnp.bfloat16)
    g_out_ref[...] = plain_rows(mixed_ref[...], branch[...], TN).astype(jnp.bfloat16)
    for k in range(3):
        part_ref[k : k + 1, :] = sums[k]
    part_ref[3:8, :] = jnp.zeros((5, D), jnp.float32)


def norm_backward(picks, d_first, d_cls, res, vecs, masks, mixed, w_attn):
    both = res.shape[0]
    any_space, vmem = pl.BlockSpec(memory_space=pltpu.HBM), pl.BlockSpec(memory_space=pltpu.VMEM)
    f32, low = jnp.float32, jnp.bfloat16
    return pl.pallas_call(
        norm_back_kernel,
        out_shape=(
            result((both, D), f32),
            result((D, D), low),
            result((both, D), low, True),
            result((8, D), f32),
        ),
        in_specs=[pl.BlockSpec(memory_space=pltpu.SMEM)] + [any_space] * 7,
        out_specs=(vmem,) * 4,
        scratch_shapes=[
            pltpu.VMEM((2, both // 2, D), jnp.int32),
            pltpu.VMEM((both, D), f32),
            pltpu.VMEM((both, D), low),
            pltpu.VMEM(d_cls.shape, f32),
            pltpu.VMEM((both, D), f32),
            pltpu.VMEM((8, D), f32),
            pltpu.VMEM((both, D), low),
            pltpu.VMEM((D, D), low),
            pltpu.SemaphoreType.DMA((8,)),
        ],
        compiler_params=room(16),
    )(picks, *far(d_first, d_cls, res, vecs, masks, mixed, w_attn))


def attn_back_kernel(d_mixed, qkv_ref, prob_ref, d_qkv_ref, part_ref):
    part_ref[...] = jnp.zeros_like(part_ref)

    def one_block(block, carry):
        here = pl.ds(pl.multiple_of(block * LANES, LANES), LANES)
        for pair in range(H // 2):
            cols = pl.ds(pair * LANES, LANES)
            q = stack_heads(qkv_ref[here, cols])
            k = qkv_ref[here, pl.ds(D + pair * LANES, LANES)]
            v = qkv_ref[here, pl.ds(2 * D + pair * LANES, LANES)]
            d_out = stack_heads(d_mixed[here, cols])
            probs = prob_ref[block, pair]
            d_v = plain_rows(probs.astype(jnp.bfloat16), d_out, TN)
            d_probs = plain_rows(d_out, v, NT)
            delta = jnp.sum(probs * d_probs, axis=-1, keepdims=True)
            score = (probs * (d_probs - delta) * HD ** (-0.5)).astype(jnp.bfloat16)
            d_q = unstack_heads(plain_rows(score, k, NN))
            d_k = plain_rows(score, q, TN)
            d_qkv_ref[here, cols] = d_q.astype(jnp.bfloat16)
            d_qkv_ref[here, pl.ds(D + pair * LANES, LANES)] = d_k.astype(jnp.bfloat16)
            d_qkv_ref[here, pl.ds(2 * D + pair * LANES, LANES)] = d_v.astype(jnp.bfloat16)
            part_ref[0:1, cols] += sum_rows(d_q)
            part_ref[1:2, cols] += sum_rows(d_v)
        return carry

    lax.fori_loop(0, qkv_ref.shape[0] // LANES, one_block, 0)


def attn_backward(d_mixed, qkv, probs):
    vmem = pl.BlockSpec(memory_space=pltpu.VMEM)
    return pl.pallas_call(
        attn_back_kernel,
        out_shape=(result(qkv.shape, jnp.bfloat16, True), pltpu.HBM((8, D), jnp.float32)),
        in_specs=[vmem] * 3,
        out_specs=(vmem,) * 2,
        compiler_params=room(16),
    )(d_mixed, qkv, probs)


def attn_grad_kernel(shard, me_ref, length_ref, d_qkv, *refs):
    sources, input_ref, pieces, scratch = refs[:9], refs[9], refs[10:20], refs[20:]
    stage, flat, body, tail, d_in, sems, in_sems, mask = scratch[:8]
    in_low, w_ref, d_res, rows_ref, vec_ref, g_out, part_ref, norm_part_ref = scratch[8:]
    in_hbm, w_hbm, d_res_hbm, rows_hbm, vec_hbm, mask_hbm, g_hbm, part_hbm, norm_part_hbm = sources
    cols = 4 * D // LANES
    tokens = rows_ref.shape[0]
    copies = bring(
        [(in_hbm, in_low), (g_hbm, g_out), (w_hbm.at[:, pl.ds(0, 3 * D)], w_ref), (d_res_hbm, d_res)]
        + [(mask_hbm.at[view, 0], mask.at[view]) for view in range(2)]
        + [(rows_hbm, rows_ref), (vec_hbm, vec_ref), (part_hbm, part_ref), (norm_part_hbm, norm_part_ref)],
        in_sems,
    )
    await_all(copies[:2])
    span, width = 256, 3 * LANES

    def one_block(block, carry):
        left = in_low[:, pl.ds(pl.multiple_of(block * span, span), span)]
        for k in range(3 * D // width):
            grads = plain_rows(left, d_qkv[:, pl.ds(k * width, width)], TN)
            for col in range(width // LANES):
                for group in range(span // 16):
                    at = (block * span + group * 16) * cols + k * width // LANES + col
                    tile = grads[group * 16 : (group + 1) * 16, col * LANES : (col + 1) * LANES]
                    flat[pl.ds(at, 16, stride=cols), :] = tile
        return carry

    lax.fori_loop(0, D // span, one_block, 0)

    def one_group(group, carry):
        at = pl.multiple_of(group * 16, 16)
        for col in range(D // LANES):
            tile = g_out[pl.ds(at, 16), pl.ds(col * LANES, LANES)].astype(jnp.float32)
            flat[pl.ds(group * 16 * cols + 3 * D // LANES + col, 16, stride=cols), :] = tile
        return carry

    lax.fori_loop(0, D // 16, one_group, 0)
    copies[2].wait()
    d_in[...] = plain_rows(d_qkv[...], w_ref[...], NT)
    await_all(copies[3:])
    gain = vec_ref[5:6, :]

    def one_chunk(chunk, sums):
        own = pl.ds(pl.multiple_of(chunk * ROWS, ROWS), ROWS)
        other = pl.ds(pl.multiple_of(tokens + chunk * ROWS, ROWS), ROWS)
        grad = (d_in[own, :] + d_res[own, :]) * keep_of(mask[0, own, :])
        grad = grad + (d_in[other, :] + d_res[other, :]) * keep_of(mask[1, own, :])
        center, inv = norm_parts(rows_ref[own, :])
        back, unit = norm_back(grad, center, inv, gain)
        input_ref[own, :] = back
        return (sums[0] + sum_rows(grad * unit), sums[1] + sum_rows(grad), sums[2] + sum_rows(back))

    none = tuple(jnp.zeros((1, D), jnp.float32) for _ in range(3))
    sums = lax.fori_loop(0, tokens // ROWS, one_chunk, none, unroll=True)
    table = jnp.zeros((LANES, D), jnp.float32)
    for block in range(tokens // LANES):
        table = table + input_ref[block * LANES : (block + 1) * LANES, :]
    table = fold_places(table, length_ref[0])
    first = jnp.concatenate([part_ref[0:2, :], norm_part_ref[0:3, :], *sums, table[: LANES - 8]])
    base = D * cols
    flat_table(flat, base, first, table[LANES - 8 :], body, tail)
    rows = stage.shape[1]
    flat[pl.ds(base + D * VEC // LANES, rows), :] = jnp.zeros((rows, LANES), jnp.float32)
    store_pieces(shard, WHOLE, me_ref[0], pieces, stage, flat, sems)


def attn_grads(me, shard, length, d_qkv, in_low, w_attn, d_res, rows_in, vecs, masks, g_out, parts, norm_parts_in):
    rows = block_rows(shard)
    whole = shard * 32 // LANES
    tokens = rows_in.shape[0]
    counts = [len(slots) for slots in piece_slots(0, WHOLE)]
    any_space, vmem = pl.BlockSpec(memory_space=pltpu.HBM), pl.BlockSpec(memory_space=pltpu.VMEM)
    smem = pl.BlockSpec(memory_space=pltpu.SMEM)
    f32, low = jnp.float32, jnp.bfloat16
    return pl.pallas_call(
        functools.partial(attn_grad_kernel, shard),
        out_shape=(jax.ShapeDtypeStruct((tokens, D), f32),)
        + tuple(pltpu.HBM((n, rows, LANES), low) for n in counts),
        in_specs=[smem, smem, vmem] + [any_space] * 9,
        out_specs=(vmem,) + (any_space,) * len(counts),
        scratch_shapes=[
            pltpu.VMEM((32, rows, LANES), low),
            pltpu.VMEM((whole + rows, LANES), f32),
            pltpu.VMEM((D, LANES), f32),
            pltpu.VMEM((D, LANES), f32),
            pltpu.VMEM((2 * tokens, D), f32),
            pltpu.SemaphoreType.DMA((32,)),
            pltpu.SemaphoreType.DMA((10,)),
            pltpu.VMEM((2, tokens, D), jnp.int32),
            pltpu.VMEM((2 * tokens, D), low),
            pltpu.VMEM((D, 3 * D), low),
            pltpu.VMEM((2 * tokens, D), f32),
            pltpu.VMEM((tokens, D), f32),
            pltpu.VMEM((8, D), f32),
            pltpu.VMEM((D, D), low),
            pltpu.VMEM((8, D), f32),
            pltpu.VMEM((8, D), f32),
        ],
        compiler_params=room(40),
    )(
        jnp.reshape(me, (1,)),
        jnp.reshape(length, (1,)),
        d_qkv,
        *far(in_low, w_attn, d_res, rows_in, vecs, masks, g_out, parts, norm_parts_in),
    )


def head_kernel(shard, me_ref, pick_ref, *refs):
    pieces, (first_hbm, mask_hbm) = refs[:16], refs[16:18]
    w_ref, vec_ref, unit_ref, cls_ref = refs[18:22]
    stage, flat, first_all, picked, mask, sems, in_sems = refs[22:]
    cols = w_ref.shape[1] // LANES
    tokens = mask.shape[1]
    loads = [pltpu.make_async_copy(first_hbm, first_all, in_sems.at[2])]
    for view in range(2):
        loads.append(pltpu.make_async_copy(mask_hbm.at[view, 2], mask.at[view], in_sems.at[view]))
    for load in loads:
        load.start()
    place_blocks(shard, HALVES, pieces, me_ref[0], stage, flat, sems)
    gather_matrix(flat, w_ref)
    for load in loads:
        load.wait()
    n = unit_ref.shape[0] // 2
    for view in range(2):
        for slot in range(n):
            at, to = pick_ref[slot], view * n + slot
            picked[to : to + 1, :] = first_all[pl.ds(view * tokens + at, 1), :]
            cls_ref[to : to + 1, 2 * D : 3 * D] = keep_of(mask[view, pl.ds(at, 1), :])
    vecs = vectors_of(flat[pl.ds(D * cols, 48), :])
    vec_ref[...] = vecs
    first = picked[...]
    up_bias = jnp.concatenate([vecs[c : c + 1] for c in range(4)], axis=1)
    up_pre = plain_rows(first.astype(jnp.bfloat16), w_ref[:, : 4 * D], NN) + up_bias
    active = gelu_exact(up_pre).astype(jnp.bfloat16)
    down = plain_rows(active, w_ref[:, 4 * D : 8 * D], NT) + vecs[4:5]
    res = first + cls_ref[:, 2 * D : 3 * D] * down
    cls_low = layer_norm(res, vecs[5:6], vecs[6:7]).astype(jnp.bfloat16)
    pooled = jnp.tanh(plain_rows(cls_low, w_ref[:, 8 * D :], NN) + vecs[7:8])
    unit_ref[...] = unit_scale(pooled).astype(jnp.bfloat16)
    cls_ref[:, :D] = pooled
    cls_ref[:, D : 2 * D] = res
    cls_ref[:, 3 * D :] = up_pre


def make_head(pieces, me, shard, picks, first_norm, masks):
    rows = pieces[0].shape[1]
    whole = shard * 32 // LANES
    n = 2 * (picks.shape[0] - 1)
    any_space, vmem = pl.BlockSpec(memory_space=pltpu.HBM), pl.BlockSpec(memory_space=pltpu.VMEM)
    smem = pl.BlockSpec(memory_space=pltpu.SMEM)
    f32, low = jnp.float32, jnp.bfloat16
    return pl.pallas_call(
        functools.partial(head_kernel, shard),
        out_shape=(
            result((D, 9 * D), low, True),
            result((8, D), f32, True),
            result((n, D), low),
            result((n, 7 * D), f32),
        ),
        in_specs=[smem] * 2 + [any_space] * (len(pieces) + 2),
        out_specs=(vmem,) * 4,
        scratch_shapes=[
            pltpu.VMEM((32, rows, LANES), low),
            pltpu.VMEM((whole + rows, LANES), f32),
            pltpu.VMEM(first_norm.shape, f32),
            pltpu.VMEM((n, D), f32),
            pltpu.VMEM((2,) + masks.shape[2:], jnp.int32),
            pltpu.SemaphoreType.DMA((32,)),
            pltpu.SemaphoreType.DMA((3,)),
        ],
        compiler_params=room(42),
    )(jnp.reshape(me, (1,)), picks, *far(*pieces, first_norm, masks))


def norm_back(grad, center, inv, gain):
    unit = center * inv
    scaled = grad * gain
    mean = jnp.mean(scaled, axis=-1, keepdims=True)
    along = jnp.mean(scaled * unit, axis=-1, keepdims=True)
    return inv * (scaled - mean - unit * along), unit


def norm_parts(rows):
    center = rows - jnp.mean(rows, axis=-1, keepdims=True)
    return center, lax.rsqrt(jnp.mean(center * center, axis=-1, keepdims=True) + norm_eps)


def gelu_slope(values):
    cdf = 0.5 * (1.0 + lax.erf(values * 0.7071067811865476))
    return cdf + values * (0.3989422804014327 * jnp.exp(-0.5 * values * values))


CHUNK = 1024


def forward_kernel(first_low, first_ref, w_ref, vec_ref, mask_hbm, cot_ref,
                   act_ref, slope_ref, hidden_ref, d_res_ref, down_ref, part_ref,
                   mask, acc, made, sems):
    tokens = mask.shape[1]
    both = 2 * tokens
    copies = []
    for view in range(2):
        copies.append(pltpu.make_async_copy(mask_hbm.at[view, 2], mask.at[view], sems.at[view]))
    for copy in copies:
        copy.start()
    vecs = vec_ref[...]
    for k in range(4 * D // CHUNK):
        cols = pl.ds(k * CHUNK, CHUNK)
        bias = jnp.concatenate([vecs[c : c + 1] for c in range(4)], axis=1)[:, k * CHUNK : (k + 1) * CHUNK]
        made[...] = plain_rows(first_low[...], w_ref[:, cols], NN)

        def one_group(group, carry, bias=bias, cols=cols):
            at = pl.ds(pl.multiple_of(group * ROWS, ROWS), ROWS)
            up = made[at, :] + bias
            cdf = 0.5 * (1.0 + lax.erf(up * 0.7071067811865476))
            act_ref[at, cols] = (up * cdf).astype(jnp.bfloat16)
            slope = cdf + up * (0.3989422804014327 * jnp.exp(-0.5 * up * up))
            slope_ref[at, cols] = slope.astype(jnp.bfloat16)
            return carry

        lax.fori_loop(0, both // ROWS, one_group, 0, unroll=4)
    for copy in copies:
        copy.wait()
    acc[...] = plain_rows(act_ref[...], w_ref[:, 4 * D : 8 * D], NT)
    sums = tuple(jnp.zeros((1, D), jnp.float32) for _ in range(3))
    for view in range(2):
        def one_chunk(chunk, sums, view=view):
            own = pl.ds(pl.multiple_of(chunk * ROWS, ROWS), ROWS)
            at = pl.ds(pl.multiple_of(view * tokens + chunk * ROWS, ROWS), ROWS)
            keep = keep_of(mask[view, own, :])
            center, inv = norm_parts(first_ref[at, :] + keep * (acc[at, :] + vecs[4:5]))
            grad = cot_ref[view, own, :].astype(jnp.float32)
            hidden_ref[view, own, :] = (center * inv * vecs[5:6] + vecs[6:7]).astype(jnp.bfloat16)
            d_res, unit = norm_back(grad, center, inv, vecs[5:6])
            d_down = d_res * keep
            d_res_ref[at, :] = d_res
            down_ref[at, :] = d_down.astype(jnp.bfloat16)
            return (sums[0] + sum_rows(d_down), sums[1] + sum_rows(grad * unit), sums[2] + sum_rows(grad))

        sums = lax.fori_loop(0, tokens // ROWS, one_chunk, sums, unroll=True)
    part_ref[...] = jnp.zeros_like(part_ref)
    for k in range(3):
        part_ref[4 + k : 5 + k, :] = sums[k]


def head_forward(first_low, first_norm, w_head, vecs, masks, cotangent):
    both = first_low.shape[0]
    tokens = both // 2
    any_space, vmem = pl.BlockSpec(memory_space=pltpu.HBM), pl.BlockSpec(memory_space=pltpu.VMEM)
    f32, low = jnp.float32, jnp.bfloat16
    return pl.pallas_call(
        forward_kernel,
        out_shape=(
            result((both, 4 * D), low, True),
            result((both, 4 * D), low, True),
            result((2, tokens, D), low),
            result((both, D), f32, True),
            result((both, D), low, True),
            result((8, D), f32, True),
        ),
        in_specs=[vmem, vmem, vmem, vmem, any_space, vmem],
        out_specs=(vmem,) * 6,
        scratch_shapes=[
            pltpu.VMEM((2, tokens, D), jnp.int32),
            pltpu.VMEM((both, D), f32),
            pltpu.VMEM((both, CHUNK), f32),
            pltpu.SemaphoreType.DMA((2,)),
        ],
        compiler_params=room(14),
    )(first_low, first_norm, w_head, vecs, masks, cotangent)


def backward_kernel(down_ref, slope_ref, d_res_ref, part_in, w_ref, up_ref, first_ref, part_ref, made):
    part_ref[...] = part_in[...]
    both = down_ref.shape[0]
    sums = []
    for k in range(4 * D // CHUNK):
        cols = pl.ds(k * CHUNK, CHUNK)
        made[...] = plain_rows(down_ref[...], w_ref[:, pl.ds(4 * D + k * CHUNK, CHUNK)], NN)

        def one_group(group, total, cols=cols):
            at = pl.ds(pl.multiple_of(group * ROWS, ROWS), ROWS)
            d_up = made[at, :] * slope_ref[at, cols].astype(jnp.float32)
            up_ref[at, cols] = d_up.astype(jnp.bfloat16)
            return total + sum_rows(d_up)

        sums.append(lax.fori_loop(0, both // ROWS, one_group, jnp.zeros((1, CHUNK), jnp.float32), unroll=4))
    sums = jnp.concatenate(sums, axis=1)
    for c in range(4):
        part_ref[c : c + 1, :] = sums[:, c * D : (c + 1) * D]
    first_ref[...] = d_res_ref[...] + plain_rows(up_ref[...], w_ref[:, : 4 * D], NT)


def head_backward(down_low, slope, d_res, parts, w_head):
    both = down_low.shape[0]
    vmem = pl.BlockSpec(memory_space=pltpu.VMEM)
    f32, low = jnp.float32, jnp.bfloat16
    return pl.pallas_call(
        backward_kernel,
        out_shape=(
            result((both, 4 * D), low, True),
            pltpu.HBM((both, D), f32),
            result((8, D), f32, True),
        ),
        in_specs=[vmem] * 5,
        out_specs=(vmem,) * 3,
        scratch_shapes=[
            pltpu.VMEM((both, CHUNK), f32),
        ],
        compiler_params=room(10),
    )(down_low, slope, d_res, parts, w_head)


def pick_columns(core, blocks):
    shape = (blocks * 32, D)
    index = lax.broadcasted_iota(jnp.int32, shape, 0)
    wanted = (index >> 5) * 48 + 24 * core + (index & 31)
    return (wanted == lax.broadcasted_iota(jnp.int32, shape, 1)).astype(jnp.bfloat16)


def pooled_kernel(me_ref, own_ref, sib_ref, w_hbm, cls_own, cls_sib, valid_in, vec_in,
                  loss_ref, first_ref, out_ref, low_ref, part_ref,
                  units, sims, back, cls, valid_ref, vec_ref, w_ref, sems, w_sems):
    me = me_ref[0]
    core = me & 1
    n = units.shape[1]
    pairs = []
    for side, ref in ((0, own_ref), (1, sib_ref)):
        for across in range(4):
            for k in range(4):
                pairs.append((ref.at[across, k], units.at[me ^ (side + 2 * across + 8 * k)]))
    place = pl.multiple_of(core * n, n)
    pairs += [(cls_own, cls.at[pl.ds(place, n)]), (cls_sib, cls.at[pl.ds(n - place, n)])]
    pairs += [(valid_in, valid_ref), (vec_in, vec_ref)]
    copies = bring(pairs, sems)
    w_copies = bring(
        [
            (w_hbm.at[:, pl.ds(start, size)], w_ref.at[:, pl.ds(start, size)])
            for start, size in ((8 * D, D), (4 * D, 4 * D), (0, 4 * D))
        ],
        w_sems,
    )
    await_all(copies)
    half = n // 2
    total = units.shape[0] * n
    everyone = units[...].reshape(total, D)
    table = plain_rows(everyone, everyone, NT) * (1.0 / logit_divisor)
    row = lax.broadcasted_iota(jnp.int32, (total, total), 0)
    col = lax.broadcasted_iota(jnp.int32, (total, total), 1)
    table = jnp.where(((col & (n - 1)) >= half) & (valid_ref[...] > 0), table, masked_scores)
    top = jnp.max(table, axis=-1, keepdims=True)
    row_lse = top + jnp.log(jnp.sum(jnp.exp(table - top), axis=-1, keepdims=True))
    diagonal = col == row + half
    positive = jnp.sum(jnp.where(diagonal, table, 0.0), axis=-1, keepdims=True)
    row_one = lax.broadcasted_iota(jnp.int32, (total, 1), 0)
    anchors = ((row_one & (n - 1)) < half) & (positive > 0.5 * masked_scores)
    loss_ref[0, 0] = jnp.sum(jnp.where(anchors, row_lse - positive, 0.0))
    slope = (jnp.exp(table - row_lse) - jnp.where(diagonal, 1.0, 0.0)) * (1.0 / logit_divisor)
    sims[...] = jnp.where(anchors, slope, 0.0).astype(jnp.bfloat16)
    back[...] = plain_rows(sims[...], everyone, TN)
    chip = pl.ds(pl.multiple_of((me >> 1) * 2 * n, 2 * n), 2 * n)
    d_unit = plain_rows(sims[chip, :], everyone, NN) + back[chip, :]
    pooled = cls[:, :D]
    inv = lax.rsqrt(jnp.sum(pooled * pooled, axis=-1, keepdims=True) + norm_eps)
    along = jnp.sum(pooled * d_unit, axis=-1, keepdims=True)
    d_pooled = inv * d_unit - pooled * (inv * inv * inv * along)
    d_pre = d_pooled * (1.0 - pooled * pooled)
    pool_low = d_pre.astype(jnp.bfloat16)
    await_all(w_copies)
    d_cls = plain_rows(pool_low, w_ref[:, 8 * D :], NT)
    center, scale = norm_parts(cls[:, D : 2 * D])
    cls_low = (center * scale * vec_ref[5:6, :] + vec_ref[6:7, :]).astype(jnp.bfloat16)
    d_res, unit = norm_back(d_cls, center, scale, vec_ref[5:6, :])
    d_down = d_res * cls[:, 2 * D : 3 * D]
    down_low = d_down.astype(jnp.bfloat16)
    d_up = plain_rows(down_low, w_ref[:, 4 * D : 8 * D], NN) * gelu_slope(cls[:, 3 * D :])
    up_low = d_up.astype(jnp.bfloat16)
    cls[:, :D] = d_res + plain_rows(up_low, w_ref[:, : 4 * D], NT)
    first_ref[...] = cls[pl.ds(place, n), :D]
    out_ref[:, :D] = d_down
    out_ref[:, D:] = d_up
    low_ref[:, :D] = cls_low
    low_ref[:, D:] = pool_low
    up_sum = jnp.sum(d_up, axis=0, keepdims=True)
    rows = [up_sum[:, c * D : (c + 1) * D] for c in range(4)]
    rows += [jnp.sum(each, axis=0, keepdims=True) for each in (d_down, d_cls * unit, d_cls, d_pre)]
    for k, value in enumerate(rows):
        part_ref[k : k + 1, :] = value


def pooled_backward(me, units, w_head, cls, valid, vecs):
    n = cls[0].shape[0]
    total = valid.shape[1]
    hbm, vmem = pl.BlockSpec(memory_space=pltpu.HBM), pl.BlockSpec(memory_space=pltpu.VMEM)
    smem = pl.BlockSpec(memory_space=pltpu.SMEM)
    f32, low = jnp.float32, jnp.bfloat16
    return pl.pallas_call(
        pooled_kernel,
        out_shape=(
            result((1, 1), f32),
            pltpu.HBM((n, D), f32),
            result((2 * n, 5 * D), f32, True),
            result((2 * n, 2 * D), low, True),
            result((8, D), f32, True),
        ),
        in_specs=[smem] + [hbm] * 7,
        out_specs=(smem,) + (vmem,) * 4,
        scratch_shapes=[
            pltpu.VMEM((32, n, D), low),
            pltpu.VMEM((total, total), low),
            pltpu.VMEM((total, D), f32),
            pltpu.VMEM((2 * n, 7 * D), f32),
            pltpu.VMEM((1, total), f32),
            pltpu.VMEM((8, D), f32),
            pltpu.VMEM((D, 9 * D), low),
            pltpu.SemaphoreType.DMA((36,)),
            pltpu.SemaphoreType.DMA((3,)),
        ],
        compiler_params=room(25),
    )(jnp.reshape(me, (1,)), *far(*units, w_head, *cls, valid, vecs))


def head_grad_kernel(shard, me_ref, pick_ref, *refs):
    mains, (cls, cls_low, cls_part, part_in, part_sib_in) = refs[:8], refs[8:13]
    pieces, scratch = refs[13:21], refs[21:]
    first, up, down, act, part, part_sib, stage, flat, sems, in_sems = scratch
    me = me_ref[0]
    core = me & 1
    many = mains[0].shape[0]
    n = cls.shape[0] // 2
    half = n // 2
    place = pl.multiple_of(core * n, n)
    pairs = []
    for k, whole in enumerate((first, up, down, act)):
        for side in range(2):
            pairs.append((mains[2 * k + side], whole.at[pl.ds(side * many, many)]))
    loads = bring(pairs + [(part_in, part), (part_sib_in, part_sib)], in_sems)
    for load in loads[:6]:
        load.wait()
    top_row = lax.broadcasted_iota(jnp.int32, (16, 1), 0) == 0
    for side in range(2):
        first_at = place if side == 0 else n - place
        for view in range(2):
            for slot in range(half):
                at = pl.multiple_of(side * many + view * (many // 2) + pick_ref[side, slot], 16)
                source = pl.ds(first_at + view * half + slot, 1)
                for whole, cols in ((up, pl.ds(D, 4 * D)), (down, pl.ds(0, D))):
                    more = jnp.where(top_row, cls[source, cols], 0.0)
                    whole[pl.ds(at, 16), :] = (whole[pl.ds(at, 16), :] + more).astype(jnp.bfloat16)
    blocks, rows = stage.shape[0], stage.shape[1]
    cols = 9 * D // LANES
    pick = pick_columns(core, blocks)

    def spread(grads, first_col):
        for block in range(blocks):
            for group in range(4):
                for k in range(grads.shape[1] // LANES):
                    at = group * 8 * cols + first_col + k
                    size = 8 if group < 3 else 2
                    tile = grads[block * 32 + group * 8 : block * 32 + group * 8 + size]
                    flat[block, pl.ds(at, size, stride=cols), :] = tile[:, k * LANES : (k + 1) * LANES]

    def fill(left, right, first_col):
        chunk = 4 * LANES
        for k in range(right.shape[1] // chunk):
            spread(plain_rows(left, right[:, pl.ds(k * chunk, chunk)], NN), first_col + k * chunk // LANES)

    fill(plain_rows(pick, first[...], NT).astype(jnp.bfloat16), up, 0)
    few = plain_rows(pick, cls_low[:, :D], NT).astype(jnp.bfloat16)
    spread(plain_rows(few, cls_low[:, D:], NN), 8 * D // LANES)
    for load in loads[6:]:
        load.wait()
    fill(plain_rows(pick, down[...], NT).astype(jnp.bfloat16), act, 4 * D // LANES)

    @pl.when(core == 1)
    def _():
        flat[blocks - 1, pl.ds(24 * cols, 48), :] = flat_of(part[...] + part_sib[...] + cls_part[...])

    outs = []
    for piece, slots in list(zip(pieces, piece_slots(me, HALVES)))[::-1]:
        for k, slot in enumerate(slots):
            chip_at = slot >> 1
            at = pl.multiple_of(slot * shard // LANES // 8 * 8 - slot * 24 * cols, 8)
            stage[chip_at] = flat[chip_at, pl.ds(at, rows), :].astype(jnp.bfloat16)
            copy = pltpu.make_async_copy(stage.at[chip_at], piece.at[k], sems.at[len(outs)])
            copy.start()
            outs.append(copy)
    for copy in outs:
        copy.wait()


def head_grads(me, shard, picks, mains, cls, cls_low, cls_part, parts):
    many = mains[0].shape[0]
    rows = block_rows(shard)
    hbm, vmem = pl.BlockSpec(memory_space=pltpu.HBM), pl.BlockSpec(memory_space=pltpu.VMEM)
    smem = pl.BlockSpec(memory_space=pltpu.SMEM)
    f32, low = jnp.float32, jnp.bfloat16
    return pl.pallas_call(
        functools.partial(head_grad_kernel, shard),
        out_shape=tuple(pltpu.HBM((2, rows, LANES), low) for _ in HALVES),
        in_specs=[smem] * 2 + [hbm] * 8 + [vmem] * 3 + [hbm] * 2,
        out_specs=(hbm,) * len(HALVES),
        scratch_shapes=[
            pltpu.VMEM((2 * many, D), low),
            pltpu.VMEM((2 * many, 4 * D), low),
            pltpu.VMEM((2 * many, D), low),
            pltpu.VMEM((2 * many, 4 * D), low),
            pltpu.VMEM((8, D), f32),
            pltpu.VMEM((8, D), f32),
            pltpu.VMEM((16, rows, LANES), low),
            pltpu.VMEM((16, 26 * 9 * D // LANES + 4, LANES), f32),
            pltpu.SemaphoreType.DMA((16,)),
            pltpu.SemaphoreType.DMA((10,)),
        ],
        compiler_params=room(44),
    )(jnp.reshape(me, (1,)), picks, *mains, cls, cls_low, cls_part, *parts)


def store_pieces(shard, layout, me, pieces, stage, flat, sems):
    rows = stage.shape[1]
    copies = []
    for piece, slots in list(zip(pieces, piece_slots(me, layout)))[::-1]:
        for k, slot in enumerate(slots):
            at = pl.multiple_of(slot * shard // LANES // 8 * 8, 8)
            stage[slot] = flat[pl.ds(at, rows), :].astype(jnp.bfloat16)
            copy = pltpu.make_async_copy(stage.at[slot], piece.at[k], sems.at[len(copies)])
            copy.start()
            copies.append(copy)
    for copy in copies:
        copy.wait()


def sum_small(value):
    for bit in (CORE, XBIT, YBIT, 8, 16):
        value = value + swap(value, bit)
    return value


def on_grid(
    embeddings,
    cotangent,
    drop_masks,
    lengths,
    buckets,
    attn_params,
    attn_moment,
    attn_second,
    attn_ema,
    head_params,
    head_moment,
    head_second,
    head_ema,
):
    tok_rows = embeddings.shape[0]
    slot_count = lengths.shape[0]
    all_rows = 2 * tok_rows
    device = lax.axis_index("sent")
    shards = (attn_params.shape[0], head_params.shape[0])
    attn_pieces, attn_first, attn_last = gather_attn(attn_params, device)
    head_zs = gather_head_line(head_params, device, attn_first)
    bucket_all = bucket_length(buckets)
    slot_ids = jnp.arange(slot_count, dtype=jnp.int32)
    valid_everything = (
        (slot_ids[None, :] < (tok_rows // bucket_all)[:, None]).astype(jnp.float32).reshape(-1)
    )
    bucket_len = bucket_all[device]

    def picks_of(length):
        count = tok_rows // length
        return jnp.concatenate([jnp.minimum(slot_ids, count - 1) * length, count[None]])

    picks = picks_of(bucket_len)
    both_picks = jnp.stack([picks, picks_of(bucket_all[device ^ CORE])])
    head_zs = after(head_zs, *attn_last)
    z_low, z_high = jnp.stack(head_zs[:2]), jnp.stack(head_zs[2:])
    y_low, x_high = swap(z_low, YBIT), swap(z_high, XBIT)
    x_low, y_high = swap(z_low, XBIT), swap(z_high, YBIT)
    head_xy = (x_low, x_high, y_low, y_high)
    (
        attn_mats,
        attn_vecs,
        emb_rows,
        attn_in_low,
        qkv_low,
        probs,
        mixed_low,
        first_res,
        first_norm,
        first_low,
    ) = attn_forward(attn_pieces, device, shards[0], bucket_len, lengths, embeddings, drop_masks)
    valid_views = jnp.broadcast_to(
        valid_everything.reshape(-1, 1, slot_count), (bucket_all.shape[0], 2, slot_count)
    ).reshape(-1)
    valid_row = valid_views[None, :]
    head_xy, first_norm, valid_row, picks, both_picks = lax.optimization_barrier(
        (head_xy, first_norm, valid_row, picks, both_picks)
    )
    head_pieces = gather_head(z_low, z_high, *head_xy)
    first_sib = swap(first_low, CORE)
    head_mats, head_vecs, unit_low, cls = make_head(
        head_pieces, device, shards[1], picks, first_norm, drop_masks
    )
    unit_zs = [unit_low] + [swap(unit_low, bit) for bit in ZBITS]
    cls_sib = swap(cls, CORE)
    active_low, slope, hidden_out, d_second_res, down_low, parts = head_forward(
        first_low, first_norm, head_mats, head_vecs, drop_masks, cotangent
    )
    active_low, down_low, unit_zs, cls_sib = lax.optimization_barrier(
        (active_low, down_low, unit_zs, cls_sib)
    )
    unit_line = jnp.stack(unit_zs)
    unit_lines = [unit_line] + [swap(unit_line, bit) for bit in (XBIT, YBIT, XBIT | YBIT)]
    active_sib, down_sib = swap(active_low, CORE), swap(down_low, CORE)
    up_low, d_first, parts = head_backward(down_low, slope, d_second_res, parts, head_mats)
    up_low, unit_lines, active_sib, down_sib = lax.optimization_barrier(
        (up_low, unit_lines, active_sib, down_sib)
    )
    units = jnp.stack(unit_lines)
    units_sib = swap(units, CORE)
    up_sib, parts_sib = swap(after(up_low, units_sib), CORE), swap(parts, CORE)
    loss_sum, d_first_cls, cls_grads, cls_low, cls_part = pooled_backward(
        device, (units, units_sib), head_mats, (cls, cls_sib), valid_row, head_vecs
    )
    head_pieces = head_grads(
        device,
        shards[1],
        both_picks,
        (first_low, first_sib, up_low, up_sib, down_low, down_sib, active_low, active_sib),
        cls_grads,
        cls_low,
        cls_part,
        (parts, parts_sib),
    )
    loss_sum = loss_sum[0, 0]
    d_first, head_pieces = lax.optimization_barrier((d_first, head_pieces))
    line_low, line_high, x_low, x_high, y_low, y_high, d_low, d_high = head_pieces
    d_low, d_high = swap(d_low, XBIT), swap(d_high, YBIT)
    d_first_res, g_out, d_mixed, norm_parts_in = norm_backward(
        picks, d_first, d_first_cls, first_res, attn_vecs, drop_masks, mixed_low, attn_mats
    )
    d_qkv, attn_parts = attn_backward(d_mixed, qkv_low, probs)
    d_qkv, d_low, d_high = lax.optimization_barrier((d_qkv, d_low, d_high))
    x_high, y_high = swap(low_sum(x_high, d_high), XBIT), swap(y_high, YBIT)
    y_low = low_sum(y_low, d_low)
    d_qkv, y_low = lax.optimization_barrier((d_qkv, y_low))
    input_grad, *attn_pieces = attn_grads(
        device,
        shards[0],
        bucket_len,
        d_qkv,
        attn_in_low,
        attn_mats,
        d_first_res,
        emb_rows,
        attn_vecs,
        drop_masks,
        g_out,
        attn_parts,
        norm_parts_in,
    )
    attn_pieces, x_low, y_low, x_high, y_high = lax.optimization_barrier(
        (attn_pieces, x_low, y_low, x_high, y_high)
    )
    line_high = low_sum(line_high, x_high, y_high)
    x_low, y_low = swap(x_low, XBIT), swap(y_low, YBIT)
    attn_sums = scatter_core(attn_pieces)
    attn_sums, x_low, y_low = lax.optimization_barrier((attn_sums, x_low, y_low))
    line_low = low_sum(line_low, x_low, y_low)
    head_sum = scatter_along(line_low[0], [line_low[1], line_high[0], line_high[1]])
    head_share = unpack_shard(head_sum, device, shards[1])
    attn_share = unpack_shard(scatter_attn(attn_sums), device, shards[0])
    squares = jnp.sum(attn_share * attn_share) + jnp.sum(head_share * head_share)
    total_squares = sum_small(squares)
    loss = loss_sum / jnp.sum(valid_everything)
    grad_norm = jnp.sqrt(total_squares)
    clip_scale = jnp.minimum(1.0, clip_bound / grad_norm)
    attn_new = adam_step(attn_share * clip_scale, attn_params, attn_moment, attn_second, attn_ema)
    head_new = adam_step(head_share * clip_scale, head_params, head_moment, head_second, head_ema)
    return (
        hidden_out,
        input_grad,
        loss,
        grad_norm,
        attn_new[0],
        attn_new[1],
        attn_new[2],
        attn_new[3],
        head_new[0],
        head_new[1],
        head_new[2],
        head_new[3],
    )


def on_any_mesh(
    embeddings,
    cotangent,
    drop_masks,
    lengths,
    buckets,
    attn_params,
    attn_moment,
    attn_second,
    attn_ema,
    head_params,
    head_moment,
    head_second,
    head_ema,
):
    tok_rows = embeddings.shape[0]
    slot_count = lengths.shape[0]
    all_rows = 2 * tok_rows
    device = lax.axis_index("sent")
    attn_full, head_full = (
        lax.all_gather(attn_params.astype(jnp.bfloat16), "sent", axis=0, tiled=True),
        lax.all_gather(head_params.astype(jnp.bfloat16), "sent", axis=0, tiled=True),
    )
    attn_mats = attn_full[: 4 * D * D].reshape(D, 4 * D)
    attn_vecs_low = attn_full[4 * D * D :].reshape(D, 8 + POS)
    attn_vecs = attn_vecs_low.astype(jnp.float32)
    head_mats = head_full[: 9 * D * D].reshape(D, 9 * D)
    head_vecs = head_full[9 * D * D :].reshape(D, 8).astype(jnp.float32)
    w_qkv = attn_mats[:, : 3 * D]
    w_out = attn_mats[:, 3 * D :]
    w_up = head_mats[:, : 4 * D]
    w_down = head_mats[:, 4 * D : 8 * D]
    w_pool = head_mats[:, 8 * D :]
    bucket_all = bucket_length(buckets)
    slot_ids = jnp.arange(slot_count, dtype=jnp.int32)
    valid_everything = (
        (slot_ids[None, :] < (tok_rows // bucket_all)[:, None]).astype(jnp.float32).reshape(-1)
    )
    bucket_len = bucket_all[device]
    sent_count = tok_rows // bucket_len
    valid_own = (slot_ids < sent_count).astype(jnp.float32)
    row_ids = jnp.arange(tok_rows, dtype=jnp.int32)
    sentence = row_ids // bucket_len
    row_place = row_ids % bucket_len
    slot_len = jnp.sum(
        jnp.where(sentence[:, None] == slot_ids[None, :], lengths[None, :], 0), axis=1
    )
    key_ok = row_place < slot_len
    block = POS
    sent_blocks = sentence.reshape(-1, block)
    ok_blocks = key_ok.reshape(-1, block)
    allowed = (sent_blocks[:, :, None] == sent_blocks[:, None, :]) & ok_blocks[:, None, :]
    allowed = jnp.concatenate([allowed, allowed], axis=0)[:, None]
    place_hot = (row_place[:, None] == jnp.arange(POS, dtype=jnp.int32)[None, :]).astype(
        jnp.bfloat16
    )
    pos_rows = plain_dot(place_hot, attn_vecs_low[:, 8:].T)
    emb_rows = embeddings.astype(jnp.float32) + pos_rows + attn_vecs[:, 7]
    normed, emb_back = jax.vjp(layer_norm, emb_rows, attn_vecs[:, 5], attn_vecs[:, 6])
    keep_masks = drop_masks.astype(jnp.float32) / keep_prob
    keep_attn = keep_masks[:, 1].reshape(all_rows, D)
    keep_ffn = keep_masks[:, 2].reshape(all_rows, D)
    attn_in = (normed[None] * keep_masks[:, 0]).reshape(all_rows, D)
    attn_in_low = attn_in.astype(jnp.bfloat16)
    qkv_bias = jnp.concatenate([attn_vecs[:, 0], jnp.zeros((D,), jnp.float32), attn_vecs[:, 1]])
    qkv_low = (plain_dot(attn_in_low, w_qkv) + qkv_bias).astype(jnp.bfloat16)
    head_split = qkv_low.reshape(-1, block, 3, H, HD)
    queries = head_split[:, :, 0]
    keys_low = head_split[:, :, 1]
    values_low = head_split[:, :, 2]
    score_scale = HD ** (-0.5)
    raw_scores = jnp.einsum(
        "bqhd,bkhd->bhqk", queries, keys_low, preferred_element_type=jnp.float32
    )
    scores = jnp.where(allowed, raw_scores * score_scale, masked_scores)
    row_top = jnp.max(scores, axis=-1, keepdims=True)
    expo_vals = jnp.exp(scores - row_top)
    row_total = jnp.sum(expo_vals, axis=-1, keepdims=True)
    attn_probs = expo_vals / row_total
    score_lse = row_top + jnp.log(row_total)
    mixed_out = jnp.einsum(
        "bhqk,bkhd->bqhd",
        attn_probs.astype(jnp.bfloat16),
        values_low,
        preferred_element_type=jnp.float32,
    )
    mixed_low = mixed_out.reshape(all_rows, D).astype(jnp.bfloat16)
    branch = plain_dot(mixed_low, w_out) + attn_vecs[:, 2]
    first_res = attn_in + keep_attn * branch
    first_norm, first_back = jax.vjp(layer_norm, first_res, attn_vecs[:, 3], attn_vecs[:, 4])
    first_low = first_norm.astype(jnp.bfloat16)
    up_bias = head_vecs[:, :4].T.reshape(4 * D)
    up_pre = plain_dot(first_low, w_up) + up_bias
    active, gelu_back = jax.vjp(gelu_exact, up_pre)
    active_low = active.astype(jnp.bfloat16)
    down_out = target_dot_terms(active_low, w_down) + head_vecs[:, 4]
    second_res = first_norm + keep_ffn * down_out
    second_norm, second_back = jax.vjp(layer_norm, second_res, head_vecs[:, 5], head_vecs[:, 6])
    hidden_out = second_norm.astype(jnp.bfloat16).reshape(2, tok_rows, D)
    cls_pick = jnp.minimum(slot_ids, sent_count - 1) * bucket_len
    cls_rows = jnp.take(second_norm.reshape(2, tok_rows, D), cls_pick, axis=1).reshape(
        2 * slot_count, D
    )
    cls_low = cls_rows.astype(jnp.bfloat16)
    pooled = jnp.tanh(plain_dot(cls_low, w_pool) + head_vecs[:, 7])
    unit_rows, unit_back = jax.vjp(unit_scale, pooled)
    unit_low = unit_rows.astype(jnp.bfloat16)
    query_embeddings = unit_low[:slot_count]
    positive_view_set = unit_low[slot_count:]
    target_sentence_set, everyone = (
        lax.all_gather(positive_view_set, "sent", axis=0, tiled=True),
        lax.all_gather(query_embeddings, "sent", axis=0, tiled=True),
    )
    own_cols = device * slot_count + slot_ids
    col_ids = jnp.arange(target_sentence_set.shape[0], dtype=jnp.int32)
    pos_hot = col_ids[None, :] == own_cols[:, None]
    cosine_logit_table = jnp.where(
        valid_everything[None, :] > 0,
        target_dot_terms(query_embeddings, target_sentence_set) / logit_divisor,
        masked_scores,
    )
    sim_top = jnp.max(cosine_logit_table, axis=-1, keepdims=True)
    row_lse = sim_top[:, 0] + jnp.log(jnp.sum(jnp.exp(cosine_logit_table - sim_top), axis=-1))
    positive = jnp.sum(jnp.where(pos_hot, cosine_logit_table, 0.0), axis=-1)
    local_loss = jnp.sum(valid_own * (row_lse - positive))
    loss_sum = lax.psum(local_loss, "sent")
    cosine_logit_cotangent = valid_own[:, None] * (
        jnp.exp(cosine_logit_table - row_lse[:, None]) - pos_hot.astype(jnp.float32)
    )
    cosine_logit_summed = (cosine_logit_cotangent / logit_divisor).astype(jnp.bfloat16)
    d_anchor = plain_dot(cosine_logit_summed, target_sentence_set)
    all_lse = lax.all_gather(row_lse, "sent", axis=0, tiled=True)
    back_sim = target_dot_terms(everyone, positive_view_set) / logit_divisor
    back_hot = (col_ids[:, None] == own_cols[None, :]).astype(jnp.float32)
    back_grad = valid_everything[:, None] * (
        jnp.exp(back_sim - all_lse[:, None]) * valid_own[None, :] - back_hot
    )
    d_partner = rows_dot((back_grad / logit_divisor).astype(jnp.bfloat16), everyone)
    d_unit = jnp.concatenate([d_anchor, d_partner], axis=0)
    d_pooled = unit_back(d_unit)[0]
    d_pool_pre = d_pooled * (1.0 - pooled * pooled)
    pool_low = d_pool_pre.astype(jnp.bfloat16)
    g_pool = rows_dot(cls_low, pool_low)
    g_pool_bias = jnp.sum(d_pool_pre, axis=0)
    d_cls = target_dot_terms(pool_low, w_pool).reshape(2, slot_count, D)
    pick_hot = ((row_ids[None, :] == cls_pick[:, None]) & (slot_ids[:, None] < sent_count)).astype(
        jnp.float32
    )
    d_second = cotangent.astype(jnp.float32) + jnp.einsum(
        "st,vsd->vtd", pick_hot, d_cls, precision=highest
    )
    d_second_res, g_gain_two, g_shift_two = second_back(d_second.reshape(all_rows, D))
    d_down = d_second_res * keep_ffn
    g_down_bias = jnp.sum(d_down, axis=0)
    down_low = d_down.astype(jnp.bfloat16)
    g_down = rows_dot(down_low, active_low)
    d_active = plain_dot(down_low, w_down)
    d_up = gelu_back(d_active)[0]
    g_up_bias = jnp.sum(d_up, axis=0)
    up_low = d_up.astype(jnp.bfloat16)
    g_up = rows_dot(first_low, up_low)
    d_first = d_second_res + target_dot_terms(up_low, w_up)
    head_vec_grad = jnp.concatenate(
        [
            g_up_bias.reshape(4, D).T,
            jnp.stack([g_down_bias, g_gain_two, g_shift_two, g_pool_bias], axis=1),
        ],
        axis=1,
    )
    head_grad = jnp.concatenate(
        [jnp.concatenate([g_up, g_down, g_pool], axis=1).reshape(-1), head_vec_grad.reshape(-1)]
    )
    d_first_res, g_gain_one, g_shift_one = first_back(d_first)
    d_branch = d_first_res * keep_attn
    g_out_bias = jnp.sum(d_branch, axis=0)
    branch_low = d_branch.astype(jnp.bfloat16)
    g_out = rows_dot(mixed_low, branch_low)
    d_mixed = target_dot_terms(branch_low, w_out).astype(jnp.bfloat16).reshape(-1, block, H, HD)
    again = jnp.where(
        allowed,
        jnp.einsum("bqhd,bkhd->bhqk", queries, keys_low, preferred_element_type=jnp.float32)
        * score_scale,
        masked_scores,
    )
    probs_again = jnp.exp(again - score_lse)
    d_values = jnp.einsum(
        "bhqk,bqhd->bkhd",
        probs_again.astype(jnp.bfloat16),
        d_mixed,
        preferred_element_type=jnp.float32,
    )
    d_probs = jnp.einsum("bqhd,bkhd->bhqk", d_mixed, values_low, preferred_element_type=jnp.float32)
    row_delta = jnp.sum(probs_again * d_probs, axis=-1, keepdims=True)
    score_low = (probs_again * (d_probs - row_delta) * score_scale).astype(jnp.bfloat16)
    d_queries = jnp.einsum(
        "bhqk,bkhd->bqhd", score_low, keys_low, preferred_element_type=jnp.float32
    )
    d_keys = jnp.einsum("bhqk,bqhd->bkhd", score_low, queries, preferred_element_type=jnp.float32)
    d_qkv = jnp.stack([d_queries, d_keys, d_values], axis=2).reshape(all_rows, 3 * D)
    g_q_bias = jnp.sum(d_queries.reshape(all_rows, D), axis=0)
    g_v_bias = jnp.sum(d_values.reshape(all_rows, D), axis=0)
    qkv_grad_low = d_qkv.astype(jnp.bfloat16)
    g_qkv = rows_dot(attn_in_low, qkv_grad_low)
    d_attn_in = d_first_res + target_dot_terms(qkv_grad_low, w_qkv)
    d_normed = jnp.sum(d_attn_in.reshape(2, tok_rows, D) * keep_masks[:, 0], axis=0)
    input_grad, g_gain_emb, g_shift_emb = emb_back(d_normed)
    g_type = jnp.sum(input_grad, axis=0)
    g_table = lax.dot_general(
        place_hot.astype(jnp.float32),
        input_grad,
        (((0,), (0,)), ((), ())),
        precision=highest,
        preferred_element_type=jnp.float32,
    )
    attn_vec_grad = jnp.concatenate(
        [
            jnp.stack(
                [
                    g_q_bias,
                    g_v_bias,
                    g_out_bias,
                    g_gain_one,
                    g_shift_one,
                    g_gain_emb,
                    g_shift_emb,
                    g_type,
                ],
                axis=1,
            ),
            g_table.T,
        ],
        axis=1,
    )
    attn_grad = jnp.concatenate(
        [jnp.concatenate([g_qkv, g_out], axis=1).reshape(-1), attn_vec_grad.reshape(-1)]
    )
    attn_share, head_share = (
        lax.psum_scatter(attn_grad, "sent", scatter_dimension=0, tiled=True),
        lax.psum_scatter(head_grad, "sent", scatter_dimension=0, tiled=True),
    )
    squares = jnp.sum(attn_share * attn_share) + jnp.sum(head_share * head_share)
    total_squares = lax.psum(squares, "sent")
    loss = loss_sum / jnp.sum(valid_everything)
    grad_norm = jnp.sqrt(total_squares)
    clip_scale = jnp.minimum(1.0, clip_bound / grad_norm)
    attn_new = adam_step(attn_share * clip_scale, attn_params, attn_moment, attn_second, attn_ema)
    head_new = adam_step(head_share * clip_scale, head_params, head_moment, head_second, head_ema)
    return (
        hidden_out,
        input_grad,
        loss,
        grad_norm,
        attn_new[0],
        attn_new[1],
        attn_new[2],
        attn_new[3],
        head_new[0],
        head_new[1],
        head_new[2],
        head_new[3],
    )


def on_device(*arrays):
    shards = (arrays[5].shape[0], arrays[9].shape[0])
    local = on_grid if is_grid(lax.axis_size("sent"), *shards) else on_any_mesh
    return local(*arrays)


def solution(mesh):
    in_specs = (
        P("sent", None),
        P(None, "sent", None),
        P(None, None, "sent", None),
        P("sent"),
        P(),
        P("sent"),
        P("sent"),
        P("sent"),
        P("sent"),
        P("sent"),
        P("sent"),
        P("sent"),
        P("sent"),
    )
    out_specs = (
        P(None, "sent", None),
        P("sent", None),
        P(),
        P(),
        P("sent"),
        P("sent"),
        P("sent"),
        P("sent"),
        P("sent"),
        P("sent"),
        P("sent"),
        P("sent"),
    )
    return jax.shard_map(
        on_device, mesh=mesh, in_specs=in_specs, out_specs=out_specs, check_vma=False
    )
```

```python
import functools

import jax
import jax.numpy as jnp
from jax import lax
from jax.experimental import pallas as pl
from jax.experimental.pallas import tpu as pltpu
from jax.sharding import PartitionSpec as P

D = 768
H = 12
HD = 64
LMIN = 32
POS = 128
STEP = 5


logit_divisor = 0.05
keep_prob = 0.9
norm_eps = 1e-06
clip_bound = 0.001
beta_first = 0.5
beta_second = 0.5
learn_rate = 0.05
decay_rate = 0.01
adam_eps = 1e-08
ema_rate = 0.8
masked_scores = -1e30
highest = lax.Precision.HIGHEST


def layer_norm(tensor, gain_vec, shift_vec):
    center = tensor - jnp.mean(tensor, axis=-1, keepdims=True)
    spread = jnp.mean(center * center, axis=-1, keepdims=True)
    return center * lax.rsqrt(spread + norm_eps) * gain_vec + shift_vec


def gelu_exact(tensor):
    return 0.5 * tensor * (1.0 + jax.scipy.special.erf(tensor * 0.7071067811865476))


def unit_scale(tensor):
    return tensor * lax.rsqrt(jnp.sum(tensor * tensor, axis=-1, keepdims=True) + norm_eps)


def bucket_length(bucket_code):
    return (LMIN * jnp.where(bucket_code == 0, 1, jnp.where(bucket_code == 1, 2, 4))).astype(
        jnp.int32
    )


def plain_dot(left_op, right_op):
    return jnp.dot(left_op, right_op, preferred_element_type=jnp.float32)


def rows_dot(left_op, right_op):
    return lax.dot_general(
        left_op, right_op, (((0,), (0,)), ((), ())), preferred_element_type=jnp.float32
    )


def target_dot_terms(left_op, right_op):
    return lax.dot_general(
        left_op, right_op, (((1,), (1,)), ((), ())), preferred_element_type=jnp.float32
    )


def adam_step(grad_flat, params, moment, second, average):
    first_new = beta_first * moment + (1.0 - beta_first) * grad_flat
    second_new = beta_second * second + (1.0 - beta_second) * grad_flat * grad_flat
    fix_first = 1.0 - beta_first**STEP
    fix_second = 1.0 - beta_second**STEP
    adam_dir = first_new / fix_first / (jnp.sqrt(second_new / fix_second) + adam_eps)
    updated = params - learn_rate * (adam_dir + decay_rate * params)
    average_new = ema_rate * average + (1.0 - ema_rate) * updated
    return (first_new, second_new, updated, average_new)


LANES = 128
VMEM_CAP = 60 * 2**20


def room(mib):
    return pltpu.CompilerParams(vmem_limit_bytes=mib * 2**20)


def far(*arrays):
    return [pltpu.with_memory_space_constraint(array, pltpu.HBM) for array in arrays]


def bring(pairs, sems, first=0):
    copies = []
    for source, target in pairs:
        copies.append(pltpu.make_async_copy(source, target, sems.at[first + len(copies)]))
        copies[-1].start()
    return copies


def await_all(copies):
    for copy in copies:
        copy.wait()


def result(shape, dtype, stays=False):
    return pltpu.VMEM(shape, dtype) if stays else jax.ShapeDtypeStruct(shape, dtype)
CORE, XBIT, YBIT, ZBITS = 1, 2, 4, (8, 16, 24)


def swap(value, bit):
    count = lax.axis_size("sent")
    return lax.ppermute(value, "sent", [(i, i ^ bit) for i in range(count)])


def is_grid(count, *shards):
    return count == 32 and all(2 * shard % LANES == 0 for shard in shards)


def block_rows(shard):
    return -(-(-(-shard // LANES) + 8) // 16) * 16


def first_row(device, shard):
    return (device * shard) // LANES


def pack_shard(values, device):
    shard = values.shape[0]
    rows = block_rows(shard)
    size = rows * LANES
    odd = (device * shard) % LANES != 0
    lead = jnp.where(
        odd,
        jnp.pad(values, (LANES // 2, size - shard - LANES // 2)),
        jnp.pad(values, (0, size - shard)),
    ).reshape(rows, LANES)
    offset = first_row(device, shard) % 8
    padded = jnp.pad(lead, ((8, 0), (0, 0)))
    return lax.dynamic_slice(padded, (8 - offset, 0), (rows, LANES)).astype(jnp.bfloat16)


def unpack_shard(block, device, shard):
    rows = -(-shard // LANES)
    offset = first_row(device, shard) % 8
    odd = (device * shard) % LANES != 0
    flat = lax.dynamic_slice(block, (offset, 0), (rows, LANES)).reshape(-1)
    longer = jnp.pad(flat, (0, LANES))
    return jnp.where(odd, longer[LANES // 2 : LANES // 2 + shard], flat[:shard])


WHOLE = ((0, 0, 4), (1, 0, 4), (2, 0, 4), (3, 0, 2), (3, 2, 2))
HALVES = tuple((across, first, 2) for across in range(4) for first in (0, 2))


def piece_slots(me, layout):
    slots = []
    for core in (0, 1):
        for across, first, n in layout:
            slots.append([me ^ (core + 2 * across + 8 * (first + k)) for k in range(n)])
    return slots


def after(value, *others):
    return lax.optimization_barrier((value, others))[0]


def with_sibling(own):
    return tuple(own) + tuple(swap(piece, CORE) for piece in own)


def gather_attn(values, device):
    block = pack_shard(values, device)
    zs = [swap(block, bit) for bit in ZBITS]
    line = jnp.stack([block] + zs)
    x, y = swap(line, XBIT), swap(line, YBIT)
    diagonal = (swap(y[:2], XBIT), swap(x[2:], YBIT))
    return with_sibling((line, x, y) + diagonal), zs[0], diagonal


def gather_head_line(values, device, first):
    block = after(pack_shard(values, device), first)
    return [block] + [swap(block, bit) for bit in ZBITS]


def gather_head(low, high, x_low, x_high, y_low, y_high):
    return with_sibling((low, high, x_low, x_high, y_low, y_high, swap(y_low, XBIT), swap(x_high, YBIT)))


def low_sum(*terms):
    total = terms[0].astype(jnp.float32)
    for term in terms[1:]:
        total = total + term.astype(jnp.float32)
    return total.astype(jnp.bfloat16)


def scatter_core(pieces):
    half = len(pieces) // 2
    got = [swap(piece, CORE) for piece in reversed(pieces[half:])][::-1]
    return [low_sum(piece, other) for piece, other in zip(pieces[:half], got)]


def scatter_attn(sums):
    line, x, y, d_low, d_high = sums
    d_low, d_high = swap(d_low, XBIT), swap(d_high, YBIT)
    x = swap(jnp.concatenate([x[:2], low_sum(x[2:], d_high)]), XBIT)
    y = swap(jnp.concatenate([low_sum(y[:2], d_low), y[2:]]), YBIT)
    line = low_sum(line, x, y)
    return scatter_along(line[0], [line[k] for k in (1, 2, 3)])


def scatter_along(own, others):
    total = own.astype(jnp.float32)
    for value, bit in zip(others, ZBITS):
        total = total + swap(value, bit).astype(jnp.float32)
    return total


def plain_rows(left, right, dims):
    return lax.dot_general(left, right, (dims, ((), ())), preferred_element_type=jnp.float32)


NN, NT, TN = ((1,), (0,)), ((1,), (1,)), ((0,), (0,))


def one_hot(shape, left, right):
    rows = lax.broadcasted_iota(jnp.int32, shape, 0)
    cols = lax.broadcasted_iota(jnp.int32, shape, 1)
    return jnp.where(left(rows, cols) == right(rows, cols), 1.0, 0.0)


def vectors_of(flat_rows):
    spread = one_hot((D, 48), lambda r, c: r >> 4, lambda r, c: c).astype(jnp.bfloat16)
    rows = plain_rows(spread, flat_rows.astype(jnp.bfloat16), NN)
    rows = rows * one_hot((D, LANES), lambda r, c: r & 15, lambda r, c: c >> 3)
    fold = one_hot((8, LANES), lambda r, c: r, lambda r, c: c & 7).astype(jnp.bfloat16)
    return plain_rows(fold, rows.astype(jnp.bfloat16), NT)


def flat_of(vectors):
    fold = one_hot((8, LANES), lambda r, c: r, lambda r, c: c & 7).astype(jnp.bfloat16)
    rows = plain_rows(vectors.astype(jnp.bfloat16), fold, TN)
    rows = rows * one_hot((D, LANES), lambda r, c: r & 15, lambda r, c: c >> 3)
    spread = one_hot((D, 48), lambda r, c: r >> 4, lambda r, c: c).astype(jnp.bfloat16)
    return plain_rows(spread, rows.astype(jnp.bfloat16), TN)


def keep_of(mask):
    return mask.astype(jnp.float32) * (1.0 / keep_prob)


def place_blocks(shard, layout, pieces, me, stage, flat, sems):
    count, rows = stage.shape[0], stage.shape[1]
    inner = shard // (8 * LANES) * 8
    for piece, slots in zip(pieces, piece_slots(me, layout)):
        for k, slot in enumerate(slots):
            pltpu.make_async_copy(piece.at[k], stage.at[slot], sems.at[slot]).start()

    def start_of(device):
        return pl.multiple_of(device * shard // LANES // 8 * 8, 8)

    def clear(device, carry):
        at = start_of(device)
        flat[pl.ds(at, 8), :] = jnp.zeros((8, LANES), jnp.float32)
        flat[pl.ds(at + inner, 16), :] = jnp.zeros((16, LANES), jnp.float32)
        return carry

    lax.fori_loop(0, count, clear, 0)

    def place(index, carry):
        device = me ^ ((index >> 4) + 2 * ((index >> 2) & 3) + 8 * (index & 3))
        pltpu.make_async_copy(pieces[0].at[0], stage.at[device], sems.at[device]).wait()
        at = start_of(device)
        flat[pl.ds(at, 8), :] += stage[device, :16].astype(jnp.float32)[:8]
        flat[pl.ds(at + 8, inner - 8), :] = stage[device].astype(jnp.float32)[8:inner]
        flat[pl.ds(at + inner, 16), :] += stage[device].astype(jnp.float32)[inner : inner + 16]
        return carry

    lax.fori_loop(0, count, place, 0)


def gather_matrix(flat, w_ref, w_out=None, out_sems=None):
    cols = w_ref.shape[1] // LANES

    def gather_rows(group, carry):
        at = pl.multiple_of(group * 16, 16)
        for col in range(cols):
            rows16 = flat[pl.ds(group * 16 * cols + col, 16, stride=cols), :]
            w_ref[pl.ds(at, 16), pl.ds(col * LANES, LANES)] = rows16.astype(jnp.bfloat16)
        return carry

    parts = 4
    span = D // parts
    copies = []
    for part in range(parts):
        lax.fori_loop(part * span // 16, (part + 1) * span // 16, gather_rows, 0)
        here = pl.ds(part * span, span)
        if w_out is not None:
            copies.append(pltpu.make_async_copy(w_ref.at[here], w_out.at[here], out_sems.at[part]))
            copies[-1].start()
    return copies


VEC = 8 + POS


def table_of(flat, base, body, tail):
    lane = lax.broadcasted_iota(jnp.int32, (D // 16, LANES), 1)
    for q in range(16):
        here = flat[pl.ds(base + q, D // 16, stride=17), :]
        later = flat[pl.ds(base + q + 1, D // 16, stride=17), :]
        both = jnp.where(lane >= 8 * q, here, later)
        shift = (LANES - 8 * q) % LANES
        body[pl.ds(q, D // 16, stride=16), :] = pltpu.roll(both, shift, 1) if shift else both
        tail[pl.ds(q, D // 16, stride=16), :] = pltpu.roll(later, shift, 1) if shift else later
    return body[...].T, tail[...].T[:8]


def flat_table(flat, base, first, last, body, tail):
    body[...] = first.T
    tail[...] = jnp.concatenate([last, jnp.zeros((LANES - 8, D), jnp.float32)]).T
    lane = lax.broadcasted_iota(jnp.int32, (D // 16, LANES), 1)
    carried = None
    for q in range(17):
        row = carried
        if q < 16:
            main = body[pl.ds(q, D // 16, stride=16), :]
            end = tail[pl.ds(q, D // 16, stride=16), :]
            if q:
                main, end = pltpu.roll(main, 8 * q, 1), pltpu.roll(end, 8 * q, 1)
            row = main if carried is None else jnp.where(lane >= 8 * q, main, carried)
            carried = jnp.where(lane < 8 * q, main, end)
        flat[pl.ds(base + q, D // 16, stride=17), :] = row


def repeat_places(table, length):
    twice = jnp.concatenate([table[:64]] * 2)
    four = jnp.concatenate([table[:32]] * 4)
    return jnp.where(length == 128, table, jnp.where(length == 64, twice, four))


def fold_places(rows, length):
    half = rows[:64] + rows[64:]
    quarter = half[:32] + half[32:]
    none = jnp.zeros_like(rows)
    twice = jnp.concatenate([half, none[:64]])
    four = jnp.concatenate([quarter, none[:96]])
    return jnp.where(length == 128, rows, jnp.where(length == 64, twice, four))


def stack_heads(pair):
    lane = lax.broadcasted_iota(jnp.int32, pair.shape, 1)
    none = jnp.zeros_like(pair)
    return jnp.concatenate([jnp.where(lane < HD, pair, none), jnp.where(lane < HD, none, pair)])


def unstack_heads(rows):
    half = rows.shape[0] // 2
    lane = lax.broadcasted_iota(jnp.int32, (half, rows.shape[1]), 1)
    return jnp.where(lane < HD, rows[:half], rows[half:])


ROWS = 64


def attn_kernel(shard, me_ref, length_ref, lens_ref, *refs):
    pieces, (emb_ref, mask_hbm) = refs[:10], refs[10:12]
    (w_out, vec_ref, rows_ref, in_low_ref, qkv_ref, prob_ref, mixed_ref, res_ref, norm_ref, low_ref) = refs[12:22]
    (stage, flat, w_ref, body, tail, mask, attn_in, bias_ref, sems, out_sems, mask_sems) = refs[22:]
    me = me_ref[0]
    tokens = emb_ref.shape[0]
    masks = []
    for view in range(2):
        for which in range(2):
            at = 2 * view + which
            masks.append(pltpu.make_async_copy(mask_hbm.at[view, which], mask.at[at], mask_sems.at[at]))
            masks[-1].start()
    place_blocks(shard, WHOLE, pieces, me, stage, flat, sems)
    copies = gather_matrix(flat, w_ref, w_out, out_sems)
    first, last = table_of(flat, D * w_ref.shape[1] // LANES, body, tail)
    vecs = first[:8]
    vec_ref[...] = vecs
    length = length_ref[0]
    places = repeat_places(jnp.concatenate([first[8:], last]), length)
    for copy in masks:
        copy.wait()
    for block in range(tokens // LANES):
        key = lax.broadcasted_iota(jnp.int32, (LANES, LANES), 1) + block * LANES
        query = lax.broadcasted_iota(jnp.int32, (LANES, LANES), 0) + block * LANES
        shift = jnp.where(length == 128, 7, jnp.where(length == 64, 6, 5))
        sent = lax.shift_right_logical(key, jnp.full_like(key, 1) * shift)
        sent_q = lax.shift_right_logical(query, jnp.full_like(key, 1) * shift)
        real = jnp.zeros_like(key)
        for slot in range(lens_ref.shape[0]):
            real = jnp.where(sent == slot, lens_ref[slot], real)
        ok = (sent == sent_q) & ((key & (length - 1)) < real)
        bias_ref[block] = jnp.where(ok, 0.0, masked_scores)
        here = pl.ds(block * LANES, LANES)
        emb = emb_ref[here, :].astype(jnp.float32) + places + vecs[7:8]
        rows_ref[here, :] = emb
        normed = layer_norm(emb, vecs[5:6], vecs[6:7])
        for view in range(2):
            at = pl.ds(view * tokens + block * LANES, LANES)
            given = normed * keep_of(mask[2 * view, here, :])
            attn_in[at, :] = given
            in_low_ref[at, :] = given.astype(jnp.bfloat16)
    for part in range(3):
        cols = pl.ds(part * D, D)
        made = plain_rows(in_low_ref[...], w_ref[:, cols], NN)
        if part != 1:
            made = made + vecs[part // 2 : part // 2 + 1]
        qkv_ref[:, cols] = made.astype(jnp.bfloat16)

    def attend(block, carry):
        here = pl.ds(pl.multiple_of(block * LANES, LANES), LANES)
        bias = bias_ref[block & 1]
        bias = jnp.concatenate([bias, bias])
        for pair in range(H // 2):
            q = stack_heads(qkv_ref[here, pl.ds(pair * LANES, LANES)])
            k = qkv_ref[here, pl.ds(D + pair * LANES, LANES)]
            v = qkv_ref[here, pl.ds(2 * D + pair * LANES, LANES)]
            scores = plain_rows(q, k, NT) * HD ** (-0.5) + bias
            expo = jnp.exp(scores - jnp.max(scores, axis=-1, keepdims=True))
            probs = expo / jnp.sum(expo, axis=-1, keepdims=True)
            prob_ref[block, pair] = probs
            mixed = unstack_heads(plain_rows(probs.astype(jnp.bfloat16), v, NN))
            mixed_ref[here, pl.ds(pair * LANES, LANES)] = mixed.astype(jnp.bfloat16)
        return carry

    lax.fori_loop(0, 2 * tokens // LANES, attend, 0)
    res_ref[...] = plain_rows(mixed_ref[...], w_ref[:, 3 * D :], NN)
    for view in range(2):
        def finish(chunk, carry, view=view):
            own = pl.ds(pl.multiple_of(chunk * ROWS, ROWS), ROWS)
            at = pl.ds(pl.multiple_of(view * tokens + chunk * ROWS, ROWS), ROWS)
            res = attn_in[at, :] + keep_of(mask[2 * view + 1, own, :]) * (res_ref[at, :] + vecs[2:3])
            res_ref[at, :] = res
            norm = layer_norm(res, vecs[3:4], vecs[4:5])
            norm_ref[at, :] = norm
            low_ref[at, :] = norm.astype(jnp.bfloat16)
            return carry

        lax.fori_loop(0, tokens // ROWS, finish, 0, unroll=True)
    for copy in copies:
        copy.wait()


def attn_forward(pieces, me, shard, length, lengths, embeddings, masks):
    rows = pieces[0].shape[1]
    whole = shard * 32 // LANES
    tokens = embeddings.shape[0]
    both = 2 * tokens
    any_space, vmem = pl.BlockSpec(memory_space=pltpu.HBM), pl.BlockSpec(memory_space=pltpu.VMEM)
    smem = pl.BlockSpec(memory_space=pltpu.SMEM)
    f32, low = jnp.float32, jnp.bfloat16
    shapes = [
        ((D, 4 * D), low),
        ((8, D), f32),
        ((tokens, D), f32),
        ((both, D), low),
        ((both, 3 * D), low),
        ((both // LANES, H // 2, 2 * LANES, LANES), f32),
        ((both, D), low),
        ((both, D), f32),
        ((both, D), f32),
        ((both, D), low),
    ]
    return pl.pallas_call(
        functools.partial(attn_kernel, shard),
        out_shape=tuple(jax.ShapeDtypeStruct(*s) for s in shapes),
        in_specs=[smem] * 3 + [any_space] * len(pieces) + [vmem, any_space],
        out_specs=(any_space,) + (vmem,) * 9,
        scratch_shapes=[
            pltpu.VMEM((32, rows, LANES), low),
            pltpu.VMEM((whole + rows, LANES), f32),
            pltpu.VMEM((D, 4 * D), low),
            pltpu.VMEM((D, LANES), f32),
            pltpu.VMEM((D, LANES), f32),
            pltpu.VMEM((4, tokens, D), jnp.int32),
            pltpu.VMEM((both, D), f32),
            pltpu.VMEM((tokens // LANES, LANES, LANES), f32),
            pltpu.SemaphoreType.DMA((32,)),
            pltpu.SemaphoreType.DMA((4,)),
            pltpu.SemaphoreType.DMA((4,)),
        ],
        compiler_params=pltpu.CompilerParams(vmem_limit_bytes=VMEM_CAP),
    )(jnp.reshape(me, (1,)), jnp.reshape(length, (1,)), lengths, *far(*pieces), embeddings, *far(masks))


def sum_rows(rows):
    return jnp.sum(rows, axis=0, keepdims=True)


def norm_back_kernel(pick_ref, d_first, d_cls_in, res_in, vec_in, mask_hbm, mixed_in, w_in,
                     d_res_ref, g_out_ref, d_mixed, part_ref,
                     mask, given, branch, d_cls, res_ref, vec_ref, mixed_ref, w_ref, sems):
    tokens = mask.shape[1]
    both = 2 * tokens
    copies = bring(
        [(d_first, given), (d_cls_in, d_cls), (res_in, res_ref), (vec_in, vec_ref)]
        + [(mask_hbm.at[view, 1], mask.at[view]) for view in range(2)]
        + [(w_in.at[:, pl.ds(3 * D, D)], w_ref), (mixed_in, mixed_ref)],
        sems,
    )
    await_all(copies[:6])
    n = d_cls.shape[0] // 2
    for slot in range(n):
        real = jnp.where(slot < pick_ref[n], 1.0, 0.0)
        for view in range(2):
            at = pl.ds(view * tokens + pick_ref[slot], 1)
            given[at, :] += real * d_cls[view * n + slot : view * n + slot + 1, :]
    gain = vec_ref[3:4, :]
    sums = tuple(jnp.zeros((1, D), jnp.float32) for _ in range(3))
    for view in range(2):
        def one_chunk(chunk, sums, view=view):
            own = pl.ds(pl.multiple_of(chunk * ROWS, ROWS), ROWS)
            at = pl.ds(pl.multiple_of(view * tokens + chunk * ROWS, ROWS), ROWS)
            grad = given[at, :]
            center, inv = norm_parts(res_ref[at, :])
            d_res, unit = norm_back(grad, center, inv, gain)
            d_branch = d_res * keep_of(mask[view, own, :])
            d_res_ref[at, :] = d_res
            branch[at, :] = d_branch.astype(jnp.bfloat16)
            return (
                sums[0] + sum_rows(d_branch),
                sums[1] + sum_rows(grad * unit),
                sums[2] + sum_rows(grad),
            )

        sums = lax.fori_loop(0, tokens // ROWS, one_chunk, sums, unroll=True)
    await_all(copies[6:])
    d_mixed[...] = plain_rows(branch[...], w_ref[...], NT).astype(jnp.bfloat16)
    g_out_ref[...] = plain_rows(mixed_ref[...], branch[...], TN).astype(jnp.bfloat16)
    for k in range(3):
        part_ref[k : k + 1, :] = sums[k]
    part_ref[3:8, :] = jnp.zeros((5, D), jnp.float32)


def norm_backward(picks, d_first, d_cls, res, vecs, masks, mixed, w_attn):
    both = res.shape[0]
    any_space, vmem = pl.BlockSpec(memory_space=pltpu.HBM), pl.BlockSpec(memory_space=pltpu.VMEM)
    f32, low = jnp.float32, jnp.bfloat16
    return pl.pallas_call(
        norm_back_kernel,
        out_shape=(
            result((both, D), f32),
            result((D, D), low),
            result((both, D), low, True),
            result((8, D), f32),
        ),
        in_specs=[pl.BlockSpec(memory_space=pltpu.SMEM)] + [any_space] * 7,
        out_specs=(vmem,) * 4,
        scratch_shapes=[
            pltpu.VMEM((2, both // 2, D), jnp.int32),
            pltpu.VMEM((both, D), f32),
            pltpu.VMEM((both, D), low),
            pltpu.VMEM(d_cls.shape, f32),
            pltpu.VMEM((both, D), f32),
            pltpu.VMEM((8, D), f32),
            pltpu.VMEM((both, D), low),
            pltpu.VMEM((D, D), low),
            pltpu.SemaphoreType.DMA((8,)),
        ],
        compiler_params=room(16),
    )(picks, *far(d_first, d_cls, res, vecs, masks, mixed, w_attn))


def attn_back_kernel(d_mixed, qkv_ref, prob_ref, d_qkv_ref, part_ref):
    part_ref[...] = jnp.zeros_like(part_ref)

    def one_block(block, carry):
        here = pl.ds(pl.multiple_of(block * LANES, LANES), LANES)
        for pair in range(H // 2):
            cols = pl.ds(pair * LANES, LANES)
            q = stack_heads(qkv_ref[here, cols])
            k = qkv_ref[here, pl.ds(D + pair * LANES, LANES)]
            v = qkv_ref[here, pl.ds(2 * D + pair * LANES, LANES)]
            d_out = stack_heads(d_mixed[here, cols])
            probs = prob_ref[block, pair]
            d_v = plain_rows(probs.astype(jnp.bfloat16), d_out, TN)
            d_probs = plain_rows(d_out, v, NT)
            delta = jnp.sum(probs * d_probs, axis=-1, keepdims=True)
            score = (probs * (d_probs - delta) * HD ** (-0.5)).astype(jnp.bfloat16)
            d_q = unstack_heads(plain_rows(score, k, NN))
            d_k = plain_rows(score, q, TN)
            d_qkv_ref[here, cols] = d_q.astype(jnp.bfloat16)
            d_qkv_ref[here, pl.ds(D + pair * LANES, LANES)] = d_k.astype(jnp.bfloat16)
            d_qkv_ref[here, pl.ds(2 * D + pair * LANES, LANES)] = d_v.astype(jnp.bfloat16)
            part_ref[0:1, cols] += sum_rows(d_q)
            part_ref[1:2, cols] += sum_rows(d_v)
        return carry

    lax.fori_loop(0, qkv_ref.shape[0] // LANES, one_block, 0)


def attn_backward(d_mixed, qkv, probs):
    vmem = pl.BlockSpec(memory_space=pltpu.VMEM)
    return pl.pallas_call(
        attn_back_kernel,
        out_shape=(result(qkv.shape, jnp.bfloat16, True), pltpu.HBM((8, D), jnp.float32)),
        in_specs=[vmem] * 3,
        out_specs=(vmem,) * 2,
        compiler_params=room(16),
    )(d_mixed, qkv, probs)


def attn_grad_kernel(shard, me_ref, length_ref, d_qkv, *refs):
    sources, input_ref, pieces, scratch = refs[:9], refs[9], refs[10:20], refs[20:]
    stage, flat, body, tail, d_in, sems, in_sems, mask = scratch[:8]
    in_low, w_ref, d_res, rows_ref, vec_ref, g_out, part_ref, norm_part_ref = scratch[8:]
    in_hbm, w_hbm, d_res_hbm, rows_hbm, vec_hbm, mask_hbm, g_hbm, part_hbm, norm_part_hbm = sources
    cols = 4 * D // LANES
    tokens = rows_ref.shape[0]
    copies = bring(
        [(in_hbm, in_low), (g_hbm, g_out), (w_hbm.at[:, pl.ds(0, 3 * D)], w_ref), (d_res_hbm, d_res)]
        + [(mask_hbm.at[view, 0], mask.at[view]) for view in range(2)]
        + [(rows_hbm, rows_ref), (vec_hbm, vec_ref), (part_hbm, part_ref), (norm_part_hbm, norm_part_ref)],
        in_sems,
    )
    await_all(copies[:2])
    span, width = 256, 3 * LANES

    def one_block(block, carry):
        left = in_low[:, pl.ds(pl.multiple_of(block * span, span), span)]
        for k in range(3 * D // width):
            grads = plain_rows(left, d_qkv[:, pl.ds(k * width, width)], TN)
            for col in range(width // LANES):
                for group in range(span // 16):
                    at = (block * span + group * 16) * cols + k * width // LANES + col
                    tile = grads[group * 16 : (group + 1) * 16, col * LANES : (col + 1) * LANES]
                    flat[pl.ds(at, 16, stride=cols), :] = tile
        return carry

    lax.fori_loop(0, D // span, one_block, 0)

    def one_group(group, carry):
        at = pl.multiple_of(group * 16, 16)
        for col in range(D // LANES):
            tile = g_out[pl.ds(at, 16), pl.ds(col * LANES, LANES)].astype(jnp.float32)
            flat[pl.ds(group * 16 * cols + 3 * D // LANES + col, 16, stride=cols), :] = tile
        return carry

    lax.fori_loop(0, D // 16, one_group, 0)
    copies[2].wait()
    d_in[...] = plain_rows(d_qkv[...], w_ref[...], NT)
    await_all(copies[3:])
    gain = vec_ref[5:6, :]

    def one_chunk(chunk, sums):
        own = pl.ds(pl.multiple_of(chunk * ROWS, ROWS), ROWS)
        other = pl.ds(pl.multiple_of(tokens + chunk * ROWS, ROWS), ROWS)
        grad = (d_in[own, :] + d_res[own, :]) * keep_of(mask[0, own, :])
        grad = grad + (d_in[other, :] + d_res[other, :]) * keep_of(mask[1, own, :])
        center, inv = norm_parts(rows_ref[own, :])
        back, unit = norm_back(grad, center, inv, gain)
        input_ref[own, :] = back
        return (sums[0] + sum_rows(grad * unit), sums[1] + sum_rows(grad), sums[2] + sum_rows(back))

    none = tuple(jnp.zeros((1, D), jnp.float32) for _ in range(3))
    sums = lax.fori_loop(0, tokens // ROWS, one_chunk, none, unroll=True)
    table = jnp.zeros((LANES, D), jnp.float32)
    for block in range(tokens // LANES):
        table = table + input_ref[block * LANES : (block + 1) * LANES, :]
    table = fold_places(table, length_ref[0])
    first = jnp.concatenate([part_ref[0:2, :], norm_part_ref[0:3, :], *sums, table[: LANES - 8]])
    base = D * cols
    flat_table(flat, base, first, table[LANES - 8 :], body, tail)
    rows = stage.shape[1]
    flat[pl.ds(base + D * VEC // LANES, rows), :] = jnp.zeros((rows, LANES), jnp.float32)
    store_pieces(shard, WHOLE, me_ref[0], pieces, stage, flat, sems)


def attn_grads(me, shard, length, d_qkv, in_low, w_attn, d_res, rows_in, vecs, masks, g_out, parts, norm_parts_in):
    rows = block_rows(shard)
    whole = shard * 32 // LANES
    tokens = rows_in.shape[0]
    counts = [len(slots) for slots in piece_slots(0, WHOLE)]
    any_space, vmem = pl.BlockSpec(memory_space=pltpu.HBM), pl.BlockSpec(memory_space=pltpu.VMEM)
    smem = pl.BlockSpec(memory_space=pltpu.SMEM)
    f32, low = jnp.float32, jnp.bfloat16
    return pl.pallas_call(
        functools.partial(attn_grad_kernel, shard),
        out_shape=(jax.ShapeDtypeStruct((tokens, D), f32),)
        + tuple(pltpu.HBM((n, rows, LANES), low) for n in counts),
        in_specs=[smem, smem, vmem] + [any_space] * 9,
        out_specs=(vmem,) + (any_space,) * len(counts),
        scratch_shapes=[
            pltpu.VMEM((32, rows, LANES), low),
            pltpu.VMEM((whole + rows, LANES), f32),
            pltpu.VMEM((D, LANES), f32),
            pltpu.VMEM((D, LANES), f32),
            pltpu.VMEM((2 * tokens, D), f32),
            pltpu.SemaphoreType.DMA((32,)),
            pltpu.SemaphoreType.DMA((10,)),
            pltpu.VMEM((2, tokens, D), jnp.int32),
            pltpu.VMEM((2 * tokens, D), low),
            pltpu.VMEM((D, 3 * D), low),
            pltpu.VMEM((2 * tokens, D), f32),
            pltpu.VMEM((tokens, D), f32),
            pltpu.VMEM((8, D), f32),
            pltpu.VMEM((D, D), low),
            pltpu.VMEM((8, D), f32),
            pltpu.VMEM((8, D), f32),
        ],
        compiler_params=room(40),
    )(
        jnp.reshape(me, (1,)),
        jnp.reshape(length, (1,)),
        d_qkv,
        *far(in_low, w_attn, d_res, rows_in, vecs, masks, g_out, parts, norm_parts_in),
    )


def head_kernel(shard, me_ref, pick_ref, *refs):
    pieces, (first_hbm, mask_hbm) = refs[:16], refs[16:18]
    w_ref, vec_ref, unit_ref, cls_ref = refs[18:22]
    stage, flat, first_all, picked, mask, sems, in_sems = refs[22:]
    cols = w_ref.shape[1] // LANES
    tokens = mask.shape[1]
    place_blocks(shard, HALVES, pieces, me_ref[0], stage, flat, sems)
    loads = [(first_hbm, first_all)] + [(mask_hbm.at[view, 2], mask.at[view]) for view in range(2)]
    loads = bring(loads, in_sems)
    gather_matrix(flat, w_ref)
    await_all(loads)
    n = unit_ref.shape[0] // 2
    for view in range(2):
        for slot in range(n):
            at, to = pick_ref[slot], view * n + slot
            picked[to : to + 1, :] = first_all[pl.ds(view * tokens + at, 1), :]
            cls_ref[to : to + 1, 2 * D : 3 * D] = keep_of(mask[view, pl.ds(at, 1), :])
    vecs = vectors_of(flat[pl.ds(D * cols, 48), :])
    vec_ref[...] = vecs
    first = picked[...]
    up_bias = jnp.concatenate([vecs[c : c + 1] for c in range(4)], axis=1)
    up_pre = plain_rows(first.astype(jnp.bfloat16), w_ref[:, : 4 * D], NN) + up_bias
    active = gelu_exact(up_pre).astype(jnp.bfloat16)
    down = plain_rows(active, w_ref[:, 4 * D : 8 * D], NT) + vecs[4:5]
    res = first + cls_ref[:, 2 * D : 3 * D] * down
    cls_low = layer_norm(res, vecs[5:6], vecs[6:7]).astype(jnp.bfloat16)
    pooled = jnp.tanh(plain_rows(cls_low, w_ref[:, 8 * D :], NN) + vecs[7:8])
    unit_ref[...] = unit_scale(pooled).astype(jnp.bfloat16)
    cls_ref[:, :D] = pooled
    cls_ref[:, D : 2 * D] = res
    cls_ref[:, 3 * D :] = up_pre


def make_head(pieces, me, shard, picks, first_norm, masks):
    rows = pieces[0].shape[1]
    whole = shard * 32 // LANES
    n = 2 * (picks.shape[0] - 1)
    any_space, vmem = pl.BlockSpec(memory_space=pltpu.HBM), pl.BlockSpec(memory_space=pltpu.VMEM)
    smem = pl.BlockSpec(memory_space=pltpu.SMEM)
    f32, low = jnp.float32, jnp.bfloat16
    return pl.pallas_call(
        functools.partial(head_kernel, shard),
        out_shape=(
            result((D, 9 * D), low, True),
            result((8, D), f32, True),
            result((n, D), low),
            result((n, 7 * D), f32),
        ),
        in_specs=[smem] * 2 + [any_space] * (len(pieces) + 2),
        out_specs=(vmem,) * 4,
        scratch_shapes=[
            pltpu.VMEM((32, rows, LANES), low),
            pltpu.VMEM((whole + rows, LANES), f32),
            pltpu.VMEM(first_norm.shape, f32),
            pltpu.VMEM((n, D), f32),
            pltpu.VMEM((2,) + masks.shape[2:], jnp.int32),
            pltpu.SemaphoreType.DMA((32,)),
            pltpu.SemaphoreType.DMA((3,)),
        ],
        compiler_params=room(42),
    )(jnp.reshape(me, (1,)), picks, *far(*pieces, first_norm, masks))


def norm_back(grad, center, inv, gain):
    unit = center * inv
    scaled = grad * gain
    mean = jnp.mean(scaled, axis=-1, keepdims=True)
    along = jnp.mean(scaled * unit, axis=-1, keepdims=True)
    return inv * (scaled - mean - unit * along), unit


def norm_parts(rows):
    center = rows - jnp.mean(rows, axis=-1, keepdims=True)
    return center, lax.rsqrt(jnp.mean(center * center, axis=-1, keepdims=True) + norm_eps)


def gelu_slope(values):
    cdf = 0.5 * (1.0 + lax.erf(values * 0.7071067811865476))
    return cdf + values * (0.3989422804014327 * jnp.exp(-0.5 * values * values))


CHUNK = 1024


def forward_kernel(first_low, first_ref, w_ref, vec_ref, mask_hbm, cot_ref,
                   act_ref, slope_ref, hidden_ref, d_res_ref, down_ref, part_ref,
                   mask, acc, made, sems):
    tokens = mask.shape[1]
    both = 2 * tokens
    copies = []
    for view in range(2):
        copies.append(pltpu.make_async_copy(mask_hbm.at[view, 2], mask.at[view], sems.at[view]))
    for copy in copies:
        copy.start()
    vecs = vec_ref[...]
    for k in range(4 * D // CHUNK):
        cols = pl.ds(k * CHUNK, CHUNK)
        bias = jnp.concatenate([vecs[c : c + 1] for c in range(4)], axis=1)[:, k * CHUNK : (k + 1) * CHUNK]
        made[...] = plain_rows(first_low[...], w_ref[:, cols], NN)

        def one_group(group, carry, bias=bias, cols=cols):
            at = pl.ds(pl.multiple_of(group * ROWS, ROWS), ROWS)
            up = made[at, :] + bias
            cdf = 0.5 * (1.0 + lax.erf(up * 0.7071067811865476))
            act_ref[at, cols] = (up * cdf).astype(jnp.bfloat16)
            slope = cdf + up * (0.3989422804014327 * jnp.exp(-0.5 * up * up))
            slope_ref[at, cols] = slope.astype(jnp.bfloat16)
            return carry

        lax.fori_loop(0, both // ROWS, one_group, 0, unroll=4)
    for copy in copies:
        copy.wait()
    acc[...] = plain_rows(act_ref[...], w_ref[:, 4 * D : 8 * D], NT)
    sums = tuple(jnp.zeros((1, D), jnp.float32) for _ in range(3))
    for view in range(2):
        def one_chunk(chunk, sums, view=view):
            own = pl.ds(pl.multiple_of(chunk * ROWS, ROWS), ROWS)
            at = pl.ds(pl.multiple_of(view * tokens + chunk * ROWS, ROWS), ROWS)
            keep = keep_of(mask[view, own, :])
            center, inv = norm_parts(first_ref[at, :] + keep * (acc[at, :] + vecs[4:5]))
            grad = cot_ref[view, own, :].astype(jnp.float32)
            hidden_ref[view, own, :] = (center * inv * vecs[5:6] + vecs[6:7]).astype(jnp.bfloat16)
            d_res, unit = norm_back(grad, center, inv, vecs[5:6])
            d_down = d_res * keep
            d_res_ref[at, :] = d_res
            down_ref[at, :] = d_down.astype(jnp.bfloat16)
            return (sums[0] + sum_rows(d_down), sums[1] + sum_rows(grad * unit), sums[2] + sum_rows(grad))

        sums = lax.fori_loop(0, tokens // ROWS, one_chunk, sums, unroll=True)
    part_ref[...] = jnp.zeros_like(part_ref)
    for k in range(3):
        part_ref[4 + k : 5 + k, :] = sums[k]


def head_forward(first_low, first_norm, w_head, vecs, masks, cotangent):
    both = first_low.shape[0]
    tokens = both // 2
    any_space, vmem = pl.BlockSpec(memory_space=pltpu.HBM), pl.BlockSpec(memory_space=pltpu.VMEM)
    f32, low = jnp.float32, jnp.bfloat16
    return pl.pallas_call(
        forward_kernel,
        out_shape=(
            result((both, 4 * D), low, True),
            result((both, 4 * D), low, True),
            result((2, tokens, D), low),
            result((both, D), f32, True),
            result((both, D), low, True),
            result((8, D), f32, True),
        ),
        in_specs=[vmem, vmem, vmem, vmem, any_space, vmem],
        out_specs=(vmem,) * 6,
        scratch_shapes=[
            pltpu.VMEM((2, tokens, D), jnp.int32),
            pltpu.VMEM((both, D), f32),
            pltpu.VMEM((both, CHUNK), f32),
            pltpu.SemaphoreType.DMA((2,)),
        ],
        compiler_params=room(14),
    )(first_low, first_norm, w_head, vecs, masks, cotangent)


def backward_kernel(down_ref, slope_ref, d_res_ref, part_in, w_ref, up_ref, first_ref, part_ref, made):
    part_ref[...] = part_in[...]
    both = down_ref.shape[0]
    sums = []
    for k in range(4 * D // CHUNK):
        cols = pl.ds(k * CHUNK, CHUNK)
        made[...] = plain_rows(down_ref[...], w_ref[:, pl.ds(4 * D + k * CHUNK, CHUNK)], NN)

        def one_group(group, total, cols=cols):
            at = pl.ds(pl.multiple_of(group * ROWS, ROWS), ROWS)
            d_up = made[at, :] * slope_ref[at, cols].astype(jnp.float32)
            up_ref[at, cols] = d_up.astype(jnp.bfloat16)
            return total + sum_rows(d_up)

        sums.append(lax.fori_loop(0, both // ROWS, one_group, jnp.zeros((1, CHUNK), jnp.float32), unroll=4))
    sums = jnp.concatenate(sums, axis=1)
    for c in range(4):
        part_ref[c : c + 1, :] = sums[:, c * D : (c + 1) * D]
    first_ref[...] = d_res_ref[...] + plain_rows(up_ref[...], w_ref[:, : 4 * D], NT)


def head_backward(down_low, slope, d_res, parts, w_head):
    both = down_low.shape[0]
    vmem = pl.BlockSpec(memory_space=pltpu.VMEM)
    f32, low = jnp.float32, jnp.bfloat16
    return pl.pallas_call(
        backward_kernel,
        out_shape=(
            result((both, 4 * D), low, True),
            pltpu.HBM((both, D), f32),
            result((8, D), f32, True),
        ),
        in_specs=[vmem] * 5,
        out_specs=(vmem,) * 3,
        scratch_shapes=[
            pltpu.VMEM((both, CHUNK), f32),
        ],
        compiler_params=room(10),
    )(down_low, slope, d_res, parts, w_head)


def pick_columns(core, blocks):
    shape = (blocks * 32, D)
    index = lax.broadcasted_iota(jnp.int32, shape, 0)
    wanted = (index >> 5) * 48 + 24 * core + (index & 31)
    return (wanted == lax.broadcasted_iota(jnp.int32, shape, 1)).astype(jnp.bfloat16)


def pooled_kernel(me_ref, own_ref, sib_ref, w_hbm, cls_own, cls_sib, valid_in, vec_in,
                  loss_ref, first_ref, out_ref, low_ref, part_ref,
                  units, sims, back, cls, valid_ref, vec_ref, w_ref, sems, w_sems):
    me = me_ref[0]
    core = me & 1
    n = units.shape[1]
    pairs = []
    for side, ref in ((0, own_ref), (1, sib_ref)):
        for across in range(4):
            for k in range(4):
                pairs.append((ref.at[across, k], units.at[me ^ (side + 2 * across + 8 * k)]))
    place = pl.multiple_of(core * n, n)
    pairs += [(cls_own, cls.at[pl.ds(place, n)]), (cls_sib, cls.at[pl.ds(n - place, n)])]
    pairs += [(valid_in, valid_ref), (vec_in, vec_ref)]
    copies = bring(pairs, sems)
    w_copies = bring(
        [
            (w_hbm.at[:, pl.ds(start, size)], w_ref.at[:, pl.ds(start, size)])
            for start, size in ((8 * D, D), (4 * D, 4 * D), (0, 4 * D))
        ],
        w_sems,
    )
    await_all(copies)
    half = n // 2
    total = units.shape[0] * n
    everyone = units[...].reshape(total, D)
    table = plain_rows(everyone, everyone, NT) * (1.0 / logit_divisor)
    row = lax.broadcasted_iota(jnp.int32, (total, total), 0)
    col = lax.broadcasted_iota(jnp.int32, (total, total), 1)
    table = jnp.where(((col & (n - 1)) >= half) & (valid_ref[...] > 0), table, masked_scores)
    top = jnp.max(table, axis=-1, keepdims=True)
    row_lse = top + jnp.log(jnp.sum(jnp.exp(table - top), axis=-1, keepdims=True))
    diagonal = col == row + half
    positive = jnp.sum(jnp.where(diagonal, table, 0.0), axis=-1, keepdims=True)
    row_one = lax.broadcasted_iota(jnp.int32, (total, 1), 0)
    anchors = ((row_one & (n - 1)) < half) & (positive > 0.5 * masked_scores)
    loss_ref[0, 0] = jnp.sum(jnp.where(anchors, row_lse - positive, 0.0))
    slope = (jnp.exp(table - row_lse) - jnp.where(diagonal, 1.0, 0.0)) * (1.0 / logit_divisor)
    sims[...] = jnp.where(anchors, slope, 0.0).astype(jnp.bfloat16)
    back[...] = plain_rows(sims[...], everyone, TN)
    chip = pl.ds(pl.multiple_of((me >> 1) * 2 * n, 2 * n), 2 * n)
    d_unit = plain_rows(sims[chip, :], everyone, NN) + back[chip, :]
    pooled = cls[:, :D]
    inv = lax.rsqrt(jnp.sum(pooled * pooled, axis=-1, keepdims=True) + norm_eps)
    along = jnp.sum(pooled * d_unit, axis=-1, keepdims=True)
    d_pooled = inv * d_unit - pooled * (inv * inv * inv * along)
    d_pre = d_pooled * (1.0 - pooled * pooled)
    pool_low = d_pre.astype(jnp.bfloat16)
    await_all(w_copies)
    d_cls = plain_rows(pool_low, w_ref[:, 8 * D :], NT)
    center, scale = norm_parts(cls[:, D : 2 * D])
    cls_low = (center * scale * vec_ref[5:6, :] + vec_ref[6:7, :]).astype(jnp.bfloat16)
    d_res, unit = norm_back(d_cls, center, scale, vec_ref[5:6, :])
    d_down = d_res * cls[:, 2 * D : 3 * D]
    down_low = d_down.astype(jnp.bfloat16)
    d_up = plain_rows(down_low, w_ref[:, 4 * D : 8 * D], NN) * gelu_slope(cls[:, 3 * D :])
    up_low = d_up.astype(jnp.bfloat16)
    cls[:, :D] = d_res + plain_rows(up_low, w_ref[:, : 4 * D], NT)
    first_ref[...] = cls[pl.ds(place, n), :D]
    out_ref[:, :D] = d_down
    out_ref[:, D:] = d_up
    low_ref[:, :D] = cls_low
    low_ref[:, D:] = pool_low
    up_sum = jnp.sum(d_up, axis=0, keepdims=True)
    rows = [up_sum[:, c * D : (c + 1) * D] for c in range(4)]
    rows += [jnp.sum(each, axis=0, keepdims=True) for each in (d_down, d_cls * unit, d_cls, d_pre)]
    for k, value in enumerate(rows):
        part_ref[k : k + 1, :] = value


def pooled_backward(me, units, w_head, cls, valid, vecs):
    n = cls[0].shape[0]
    total = valid.shape[1]
    hbm, vmem = pl.BlockSpec(memory_space=pltpu.HBM), pl.BlockSpec(memory_space=pltpu.VMEM)
    smem = pl.BlockSpec(memory_space=pltpu.SMEM)
    f32, low = jnp.float32, jnp.bfloat16
    return pl.pallas_call(
        pooled_kernel,
        out_shape=(
            result((1, 1), f32),
            pltpu.HBM((n, D), f32),
            result((2 * n, 5 * D), f32, True),
            result((2 * n, 2 * D), low, True),
            result((8, D), f32, True),
        ),
        in_specs=[smem] + [hbm] * 7,
        out_specs=(smem,) + (vmem,) * 4,
        scratch_shapes=[
            pltpu.VMEM((32, n, D), low),
            pltpu.VMEM((total, total), low),
            pltpu.VMEM((total, D), f32),
            pltpu.VMEM((2 * n, 7 * D), f32),
            pltpu.VMEM((1, total), f32),
            pltpu.VMEM((8, D), f32),
            pltpu.VMEM((D, 9 * D), low),
            pltpu.SemaphoreType.DMA((36,)),
            pltpu.SemaphoreType.DMA((3,)),
        ],
        compiler_params=room(25),
    )(jnp.reshape(me, (1,)), *far(*units, w_head, *cls, valid, vecs))


def head_grad_kernel(shard, me_ref, pick_ref, *refs):
    mains, (cls, cls_low, cls_part, part_in, part_sib_in) = refs[:8], refs[8:13]
    pieces, scratch = refs[13:21], refs[21:]
    first, up, down, act, part, part_sib, stage, flat, sems, in_sems = scratch
    me = me_ref[0]
    core = me & 1
    many = mains[0].shape[0]
    n = cls.shape[0] // 2
    half = n // 2
    place = pl.multiple_of(core * n, n)
    pairs = []
    for k, whole in enumerate((first, up, down, act)):
        for side in range(2):
            pairs.append((mains[2 * k + side], whole.at[pl.ds(side * many, many)]))
    loads = bring(pairs + [(part_in, part), (part_sib_in, part_sib)], in_sems)
    top_row = lax.broadcasted_iota(jnp.int32, (16, 1), 0) == 0

    def join(whole, cols):
        for side in range(2):
            first_at = place if side == 0 else n - place
            for view in range(2):
                for slot in range(half):
                    at = pl.multiple_of(side * many + view * (many // 2) + pick_ref[side, slot], 16)
                    more = jnp.where(top_row, cls[pl.ds(first_at + view * half + slot, 1), cols], 0.0)
                    whole[pl.ds(at, 16), :] = (whole[pl.ds(at, 16), :] + more).astype(jnp.bfloat16)

    blocks, rows = stage.shape[0], stage.shape[1]
    cols = 9 * D // LANES
    pick = pick_columns(core, blocks)

    def spread(grads, first_col):
        for block in range(blocks):
            for group in range(4):
                for k in range(grads.shape[1] // LANES):
                    at = group * 8 * cols + first_col + k
                    size = 8 if group < 3 else 2
                    tile = grads[block * 32 + group * 8 : block * 32 + group * 8 + size]
                    flat[block, pl.ds(at, size, stride=cols), :] = tile[:, k * LANES : (k + 1) * LANES]

    def fill(left, right, first_col):
        chunk = 4 * LANES
        for k in range(right.shape[1] // chunk):
            spread(plain_rows(left, right[:, pl.ds(k * chunk, chunk)], NN), first_col + k * chunk // LANES)

    await_all(loads[:4])
    join(up, pl.ds(D, 4 * D))
    fill(plain_rows(pick, first[...], NT).astype(jnp.bfloat16), up, 0)
    few = plain_rows(pick, cls_low[:, :D], NT).astype(jnp.bfloat16)
    spread(plain_rows(few, cls_low[:, D:], NN), 8 * D // LANES)
    await_all(loads[4:])
    join(down, pl.ds(0, D))
    fill(plain_rows(pick, down[...], NT).astype(jnp.bfloat16), act, 4 * D // LANES)

    @pl.when(core == 1)
    def _():
        flat[blocks - 1, pl.ds(24 * cols, 48), :] = flat_of(part[...] + part_sib[...] + cls_part[...])

    outs = []
    for piece, slots in list(zip(pieces, piece_slots(me, HALVES)))[::-1]:
        for k, slot in enumerate(slots):
            chip_at = slot >> 1
            at = pl.multiple_of(slot * shard // LANES // 8 * 8 - slot * 24 * cols, 8)
            stage[chip_at] = flat[chip_at, pl.ds(at, rows), :].astype(jnp.bfloat16)
            copy = pltpu.make_async_copy(stage.at[chip_at], piece.at[k], sems.at[len(outs)])
            copy.start()
            outs.append(copy)
    for copy in outs:
        copy.wait()


def head_grads(me, shard, picks, mains, cls, cls_low, cls_part, parts):
    many = mains[0].shape[0]
    rows = block_rows(shard)
    hbm, vmem = pl.BlockSpec(memory_space=pltpu.HBM), pl.BlockSpec(memory_space=pltpu.VMEM)
    smem = pl.BlockSpec(memory_space=pltpu.SMEM)
    f32, low = jnp.float32, jnp.bfloat16
    return pl.pallas_call(
        functools.partial(head_grad_kernel, shard),
        out_shape=tuple(pltpu.HBM((2, rows, LANES), low) for _ in HALVES),
        in_specs=[smem] * 2 + [hbm] * 8 + [vmem] * 3 + [hbm] * 2,
        out_specs=(hbm,) * len(HALVES),
        scratch_shapes=[
            pltpu.VMEM((2 * many, D), low),
            pltpu.VMEM((2 * many, 4 * D), low),
            pltpu.VMEM((2 * many, D), low),
            pltpu.VMEM((2 * many, 4 * D), low),
            pltpu.VMEM((8, D), f32),
            pltpu.VMEM((8, D), f32),
            pltpu.VMEM((16, rows, LANES), low),
            pltpu.VMEM((16, 26 * 9 * D // LANES + 4, LANES), f32),
            pltpu.SemaphoreType.DMA((16,)),
            pltpu.SemaphoreType.DMA((10,)),
        ],
        compiler_params=room(44),
    )(jnp.reshape(me, (1,)), picks, *mains, cls, cls_low, cls_part, *parts)


def store_pieces(shard, layout, me, pieces, stage, flat, sems):
    rows = stage.shape[1]
    copies = []
    for piece, slots in list(zip(pieces, piece_slots(me, layout)))[::-1]:
        for k, slot in enumerate(slots):
            at = pl.multiple_of(slot * shard // LANES // 8 * 8, 8)
            stage[slot] = flat[pl.ds(at, rows), :].astype(jnp.bfloat16)
            copy = pltpu.make_async_copy(stage.at[slot], piece.at[k], sems.at[len(copies)])
            copy.start()
            copies.append(copy)
    for copy in copies:
        copy.wait()


def sum_small(value):
    for bit in (CORE, XBIT, YBIT, 8, 16):
        value = value + swap(value, bit)
    return value


def on_grid(
    embeddings,
    cotangent,
    drop_masks,
    lengths,
    buckets,
    attn_params,
    attn_moment,
    attn_second,
    attn_ema,
    head_params,
    head_moment,
    head_second,
    head_ema,
):
    tok_rows = embeddings.shape[0]
    slot_count = lengths.shape[0]
    all_rows = 2 * tok_rows
    device = lax.axis_index("sent")
    shards = (attn_params.shape[0], head_params.shape[0])
    attn_pieces, attn_first, attn_last = gather_attn(attn_params, device)
    head_zs = gather_head_line(head_params, device, attn_first)
    bucket_all = bucket_length(buckets)
    slot_ids = jnp.arange(slot_count, dtype=jnp.int32)
    valid_everything = (
        (slot_ids[None, :] < (tok_rows // bucket_all)[:, None]).astype(jnp.float32).reshape(-1)
    )
    bucket_len = bucket_all[device]

    def picks_of(length):
        count = tok_rows // length
        return jnp.concatenate([jnp.minimum(slot_ids, count - 1) * length, count[None]])

    picks = picks_of(bucket_len)
    both_picks = jnp.stack([picks, picks_of(bucket_all[device ^ CORE])])
    head_zs = after(head_zs, *attn_last)
    z_low, z_high = jnp.stack(head_zs[:2]), jnp.stack(head_zs[2:])
    y_low, x_high = swap(z_low, YBIT), swap(z_high, XBIT)
    x_low, y_high = swap(z_low, XBIT), swap(z_high, YBIT)
    head_xy = (x_low, x_high, y_low, y_high)
    (
        attn_mats,
        attn_vecs,
        emb_rows,
        attn_in_low,
        qkv_low,
        probs,
        mixed_low,
        first_res,
        first_norm,
        first_low,
    ) = attn_forward(attn_pieces, device, shards[0], bucket_len, lengths, embeddings, drop_masks)
    valid_views = jnp.broadcast_to(
        valid_everything.reshape(-1, 1, slot_count), (bucket_all.shape[0], 2, slot_count)
    ).reshape(-1)
    valid_row = valid_views[None, :]
    head_xy, first_norm, valid_row, picks, both_picks = lax.optimization_barrier(
        (head_xy, first_norm, valid_row, picks, both_picks)
    )
    head_pieces = gather_head(z_low, z_high, *head_xy)
    first_sib = swap(first_low, CORE)
    head_mats, head_vecs, unit_low, cls = make_head(
        head_pieces, device, shards[1], picks, first_norm, drop_masks
    )
    unit_zs = [unit_low] + [swap(unit_low, bit) for bit in ZBITS]
    cls_sib = swap(cls, CORE)
    active_low, slope, hidden_out, d_second_res, down_low, parts = head_forward(
        first_low, first_norm, head_mats, head_vecs, drop_masks, cotangent
    )
    active_low, down_low, unit_zs, cls_sib = lax.optimization_barrier(
        (active_low, down_low, unit_zs, cls_sib)
    )
    unit_line = jnp.stack(unit_zs)
    unit_lines = [unit_line] + [swap(unit_line, bit) for bit in (XBIT, YBIT, XBIT | YBIT)]
    active_sib, down_sib = swap(active_low, CORE), swap(down_low, CORE)
    up_low, d_first, parts = head_backward(down_low, slope, d_second_res, parts, head_mats)
    up_low, unit_lines, active_sib, down_sib = lax.optimization_barrier(
        (up_low, unit_lines, active_sib, down_sib)
    )
    units = jnp.stack(unit_lines)
    units_sib = swap(units, CORE)
    up_sib, parts_sib = swap(after(up_low, units_sib), CORE), swap(parts, CORE)
    loss_sum, d_first_cls, cls_grads, cls_low, cls_part = pooled_backward(
        device, (units, units_sib), head_mats, (cls, cls_sib), valid_row, head_vecs
    )
    head_pieces = head_grads(
        device,
        shards[1],
        both_picks,
        (first_low, first_sib, up_low, up_sib, down_low, down_sib, active_low, active_sib),
        cls_grads,
        cls_low,
        cls_part,
        (parts, parts_sib),
    )
    loss_sum = loss_sum[0, 0]
    d_first, head_pieces = lax.optimization_barrier((d_first, head_pieces))
    line_low, line_high, x_low, x_high, y_low, y_high, d_low, d_high = head_pieces
    d_low, d_high = swap(d_low, XBIT), swap(d_high, YBIT)
    d_first_res, g_out, d_mixed, norm_parts_in = norm_backward(
        picks, d_first, d_first_cls, first_res, attn_vecs, drop_masks, mixed_low, attn_mats
    )
    d_qkv, attn_parts = attn_backward(d_mixed, qkv_low, probs)
    d_qkv, d_low, d_high = lax.optimization_barrier((d_qkv, d_low, d_high))
    x_high, y_high = swap(low_sum(x_high, d_high), XBIT), swap(y_high, YBIT)
    y_low = low_sum(y_low, d_low)
    d_qkv, y_low = lax.optimization_barrier((d_qkv, y_low))
    input_grad, *attn_pieces = attn_grads(
        device,
        shards[0],
        bucket_len,
        d_qkv,
        attn_in_low,
        attn_mats,
        d_first_res,
        emb_rows,
        attn_vecs,
        drop_masks,
        g_out,
        attn_parts,
        norm_parts_in,
    )
    attn_pieces, x_low, y_low, x_high, y_high = lax.optimization_barrier(
        (attn_pieces, x_low, y_low, x_high, y_high)
    )
    line_high = low_sum(line_high, x_high, y_high)
    x_low, y_low = swap(x_low, XBIT), swap(y_low, YBIT)
    attn_sums = scatter_core(attn_pieces)
    attn_sums, x_low, y_low = lax.optimization_barrier((attn_sums, x_low, y_low))
    line_low = low_sum(line_low, x_low, y_low)
    head_sum = scatter_along(line_low[0], [line_low[1], line_high[0], line_high[1]])
    head_share = unpack_shard(head_sum, device, shards[1])
    attn_share = unpack_shard(scatter_attn(attn_sums), device, shards[0])
    squares = jnp.sum(attn_share * attn_share) + jnp.sum(head_share * head_share)
    total_squares = sum_small(squares)
    loss = loss_sum / jnp.sum(valid_everything)
    grad_norm = jnp.sqrt(total_squares)
    clip_scale = jnp.minimum(1.0, clip_bound / grad_norm)
    attn_new = adam_step(attn_share * clip_scale, attn_params, attn_moment, attn_second, attn_ema)
    head_new = adam_step(head_share * clip_scale, head_params, head_moment, head_second, head_ema)
    return (
        hidden_out,
        input_grad,
        loss,
        grad_norm,
        attn_new[0],
        attn_new[1],
        attn_new[2],
        attn_new[3],
        head_new[0],
        head_new[1],
        head_new[2],
        head_new[3],
    )


def on_any_mesh(
    embeddings,
    cotangent,
    drop_masks,
    lengths,
    buckets,
    attn_params,
    attn_moment,
    attn_second,
    attn_ema,
    head_params,
    head_moment,
    head_second,
    head_ema,
):
    tok_rows = embeddings.shape[0]
    slot_count = lengths.shape[0]
    all_rows = 2 * tok_rows
    device = lax.axis_index("sent")
    attn_full, head_full = (
        lax.all_gather(attn_params.astype(jnp.bfloat16), "sent", axis=0, tiled=True),
        lax.all_gather(head_params.astype(jnp.bfloat16), "sent", axis=0, tiled=True),
    )
    attn_mats = attn_full[: 4 * D * D].reshape(D, 4 * D)
    attn_vecs_low = attn_full[4 * D * D :].reshape(D, 8 + POS)
    attn_vecs = attn_vecs_low.astype(jnp.float32)
    head_mats = head_full[: 9 * D * D].reshape(D, 9 * D)
    head_vecs = head_full[9 * D * D :].reshape(D, 8).astype(jnp.float32)
    w_qkv = attn_mats[:, : 3 * D]
    w_out = attn_mats[:, 3 * D :]
    w_up = head_mats[:, : 4 * D]
    w_down = head_mats[:, 4 * D : 8 * D]
    w_pool = head_mats[:, 8 * D :]
    bucket_all = bucket_length(buckets)
    slot_ids = jnp.arange(slot_count, dtype=jnp.int32)
    valid_everything = (
        (slot_ids[None, :] < (tok_rows // bucket_all)[:, None]).astype(jnp.float32).reshape(-1)
    )
    bucket_len = bucket_all[device]
    sent_count = tok_rows // bucket_len
    valid_own = (slot_ids < sent_count).astype(jnp.float32)
    row_ids = jnp.arange(tok_rows, dtype=jnp.int32)
    sentence = row_ids // bucket_len
    row_place = row_ids % bucket_len
    slot_len = jnp.sum(
        jnp.where(sentence[:, None] == slot_ids[None, :], lengths[None, :], 0), axis=1
    )
    key_ok = row_place < slot_len
    block = POS
    sent_blocks = sentence.reshape(-1, block)
    ok_blocks = key_ok.reshape(-1, block)
    allowed = (sent_blocks[:, :, None] == sent_blocks[:, None, :]) & ok_blocks[:, None, :]
    allowed = jnp.concatenate([allowed, allowed], axis=0)[:, None]
    place_hot = (row_place[:, None] == jnp.arange(POS, dtype=jnp.int32)[None, :]).astype(
        jnp.bfloat16
    )
    pos_rows = plain_dot(place_hot, attn_vecs_low[:, 8:].T)
    emb_rows = embeddings.astype(jnp.float32) + pos_rows + attn_vecs[:, 7]
    normed, emb_back = jax.vjp(layer_norm, emb_rows, attn_vecs[:, 5], attn_vecs[:, 6])
    keep_masks = drop_masks.astype(jnp.float32) / keep_prob
    keep_attn = keep_masks[:, 1].reshape(all_rows, D)
    keep_ffn = keep_masks[:, 2].reshape(all_rows, D)
    attn_in = (normed[None] * keep_masks[:, 0]).reshape(all_rows, D)
    attn_in_low = attn_in.astype(jnp.bfloat16)
    qkv_bias = jnp.concatenate([attn_vecs[:, 0], jnp.zeros((D,), jnp.float32), attn_vecs[:, 1]])
    qkv_low = (plain_dot(attn_in_low, w_qkv) + qkv_bias).astype(jnp.bfloat16)
    head_split = qkv_low.reshape(-1, block, 3, H, HD)
    queries = head_split[:, :, 0]
    keys_low = head_split[:, :, 1]
    values_low = head_split[:, :, 2]
    score_scale = HD ** (-0.5)
    raw_scores = jnp.einsum(
        "bqhd,bkhd->bhqk", queries, keys_low, preferred_element_type=jnp.float32
    )
    scores = jnp.where(allowed, raw_scores * score_scale, masked_scores)
    row_top = jnp.max(scores, axis=-1, keepdims=True)
    expo_vals = jnp.exp(scores - row_top)
    row_total = jnp.sum(expo_vals, axis=-1, keepdims=True)
    attn_probs = expo_vals / row_total
    score_lse = row_top + jnp.log(row_total)
    mixed_out = jnp.einsum(
        "bhqk,bkhd->bqhd",
        attn_probs.astype(jnp.bfloat16),
        values_low,
        preferred_element_type=jnp.float32,
    )
    mixed_low = mixed_out.reshape(all_rows, D).astype(jnp.bfloat16)
    branch = plain_dot(mixed_low, w_out) + attn_vecs[:, 2]
    first_res = attn_in + keep_attn * branch
    first_norm, first_back = jax.vjp(layer_norm, first_res, attn_vecs[:, 3], attn_vecs[:, 4])
    first_low = first_norm.astype(jnp.bfloat16)
    up_bias = head_vecs[:, :4].T.reshape(4 * D)
    up_pre = plain_dot(first_low, w_up) + up_bias
    active, gelu_back = jax.vjp(gelu_exact, up_pre)
    active_low = active.astype(jnp.bfloat16)
    down_out = target_dot_terms(active_low, w_down) + head_vecs[:, 4]
    second_res = first_norm + keep_ffn * down_out
    second_norm, second_back = jax.vjp(layer_norm, second_res, head_vecs[:, 5], head_vecs[:, 6])
    hidden_out = second_norm.astype(jnp.bfloat16).reshape(2, tok_rows, D)
    cls_pick = jnp.minimum(slot_ids, sent_count - 1) * bucket_len
    cls_rows = jnp.take(second_norm.reshape(2, tok_rows, D), cls_pick, axis=1).reshape(
        2 * slot_count, D
    )
    cls_low = cls_rows.astype(jnp.bfloat16)
    pooled = jnp.tanh(plain_dot(cls_low, w_pool) + head_vecs[:, 7])
    unit_rows, unit_back = jax.vjp(unit_scale, pooled)
    unit_low = unit_rows.astype(jnp.bfloat16)
    query_embeddings = unit_low[:slot_count]
    positive_view_set = unit_low[slot_count:]
    target_sentence_set, everyone = (
        lax.all_gather(positive_view_set, "sent", axis=0, tiled=True),
        lax.all_gather(query_embeddings, "sent", axis=0, tiled=True),
    )
    own_cols = device * slot_count + slot_ids
    col_ids = jnp.arange(target_sentence_set.shape[0], dtype=jnp.int32)
    pos_hot = col_ids[None, :] == own_cols[:, None]
    cosine_logit_table = jnp.where(
        valid_everything[None, :] > 0,
        target_dot_terms(query_embeddings, target_sentence_set) / logit_divisor,
        masked_scores,
    )
    sim_top = jnp.max(cosine_logit_table, axis=-1, keepdims=True)
    row_lse = sim_top[:, 0] + jnp.log(jnp.sum(jnp.exp(cosine_logit_table - sim_top), axis=-1))
    positive = jnp.sum(jnp.where(pos_hot, cosine_logit_table, 0.0), axis=-1)
    local_loss = jnp.sum(valid_own * (row_lse - positive))
    loss_sum = lax.psum(local_loss, "sent")
    cosine_logit_cotangent = valid_own[:, None] * (
        jnp.exp(cosine_logit_table - row_lse[:, None]) - pos_hot.astype(jnp.float32)
    )
    cosine_logit_summed = (cosine_logit_cotangent / logit_divisor).astype(jnp.bfloat16)
    d_anchor = plain_dot(cosine_logit_summed, target_sentence_set)
    all_lse = lax.all_gather(row_lse, "sent", axis=0, tiled=True)
    back_sim = target_dot_terms(everyone, positive_view_set) / logit_divisor
    back_hot = (col_ids[:, None] == own_cols[None, :]).astype(jnp.float32)
    back_grad = valid_everything[:, None] * (
        jnp.exp(back_sim - all_lse[:, None]) * valid_own[None, :] - back_hot
    )
    d_partner = rows_dot((back_grad / logit_divisor).astype(jnp.bfloat16), everyone)
    d_unit = jnp.concatenate([d_anchor, d_partner], axis=0)
    d_pooled = unit_back(d_unit)[0]
    d_pool_pre = d_pooled * (1.0 - pooled * pooled)
    pool_low = d_pool_pre.astype(jnp.bfloat16)
    g_pool = rows_dot(cls_low, pool_low)
    g_pool_bias = jnp.sum(d_pool_pre, axis=0)
    d_cls = target_dot_terms(pool_low, w_pool).reshape(2, slot_count, D)
    pick_hot = ((row_ids[None, :] == cls_pick[:, None]) & (slot_ids[:, None] < sent_count)).astype(
        jnp.float32
    )
    d_second = cotangent.astype(jnp.float32) + jnp.einsum(
        "st,vsd->vtd", pick_hot, d_cls, precision=highest
    )
    d_second_res, g_gain_two, g_shift_two = second_back(d_second.reshape(all_rows, D))
    d_down = d_second_res * keep_ffn
    g_down_bias = jnp.sum(d_down, axis=0)
    down_low = d_down.astype(jnp.bfloat16)
    g_down = rows_dot(down_low, active_low)
    d_active = plain_dot(down_low, w_down)
    d_up = gelu_back(d_active)[0]
    g_up_bias = jnp.sum(d_up, axis=0)
    up_low = d_up.astype(jnp.bfloat16)
    g_up = rows_dot(first_low, up_low)
    d_first = d_second_res + target_dot_terms(up_low, w_up)
    head_vec_grad = jnp.concatenate(
        [
            g_up_bias.reshape(4, D).T,
            jnp.stack([g_down_bias, g_gain_two, g_shift_two, g_pool_bias], axis=1),
        ],
        axis=1,
    )
    head_grad = jnp.concatenate(
        [jnp.concatenate([g_up, g_down, g_pool], axis=1).reshape(-1), head_vec_grad.reshape(-1)]
    )
    d_first_res, g_gain_one, g_shift_one = first_back(d_first)
    d_branch = d_first_res * keep_attn
    g_out_bias = jnp.sum(d_branch, axis=0)
    branch_low = d_branch.astype(jnp.bfloat16)
    g_out = rows_dot(mixed_low, branch_low)
    d_mixed = target_dot_terms(branch_low, w_out).astype(jnp.bfloat16).reshape(-1, block, H, HD)
    again = jnp.where(
        allowed,
        jnp.einsum("bqhd,bkhd->bhqk", queries, keys_low, preferred_element_type=jnp.float32)
        * score_scale,
        masked_scores,
    )
    probs_again = jnp.exp(again - score_lse)
    d_values = jnp.einsum(
        "bhqk,bqhd->bkhd",
        probs_again.astype(jnp.bfloat16),
        d_mixed,
        preferred_element_type=jnp.float32,
    )
    d_probs = jnp.einsum("bqhd,bkhd->bhqk", d_mixed, values_low, preferred_element_type=jnp.float32)
    row_delta = jnp.sum(probs_again * d_probs, axis=-1, keepdims=True)
    score_low = (probs_again * (d_probs - row_delta) * score_scale).astype(jnp.bfloat16)
    d_queries = jnp.einsum(
        "bhqk,bkhd->bqhd", score_low, keys_low, preferred_element_type=jnp.float32
    )
    d_keys = jnp.einsum("bhqk,bqhd->bkhd", score_low, queries, preferred_element_type=jnp.float32)
    d_qkv = jnp.stack([d_queries, d_keys, d_values], axis=2).reshape(all_rows, 3 * D)
    g_q_bias = jnp.sum(d_queries.reshape(all_rows, D), axis=0)
    g_v_bias = jnp.sum(d_values.reshape(all_rows, D), axis=0)
    qkv_grad_low = d_qkv.astype(jnp.bfloat16)
    g_qkv = rows_dot(attn_in_low, qkv_grad_low)
    d_attn_in = d_first_res + target_dot_terms(qkv_grad_low, w_qkv)
    d_normed = jnp.sum(d_attn_in.reshape(2, tok_rows, D) * keep_masks[:, 0], axis=0)
    input_grad, g_gain_emb, g_shift_emb = emb_back(d_normed)
    g_type = jnp.sum(input_grad, axis=0)
    g_table = lax.dot_general(
        place_hot.astype(jnp.float32),
        input_grad,
        (((0,), (0,)), ((), ())),
        precision=highest,
        preferred_element_type=jnp.float32,
    )
    attn_vec_grad = jnp.concatenate(
        [
            jnp.stack(
                [
                    g_q_bias,
                    g_v_bias,
                    g_out_bias,
                    g_gain_one,
                    g_shift_one,
                    g_gain_emb,
                    g_shift_emb,
                    g_type,
                ],
                axis=1,
            ),
            g_table.T,
        ],
        axis=1,
    )
    attn_grad = jnp.concatenate(
        [jnp.concatenate([g_qkv, g_out], axis=1).reshape(-1), attn_vec_grad.reshape(-1)]
    )
    attn_share, head_share = (
        lax.psum_scatter(attn_grad, "sent", scatter_dimension=0, tiled=True),
        lax.psum_scatter(head_grad, "sent", scatter_dimension=0, tiled=True),
    )
    squares = jnp.sum(attn_share * attn_share) + jnp.sum(head_share * head_share)
    total_squares = lax.psum(squares, "sent")
    loss = loss_sum / jnp.sum(valid_everything)
    grad_norm = jnp.sqrt(total_squares)
    clip_scale = jnp.minimum(1.0, clip_bound / grad_norm)
    attn_new = adam_step(attn_share * clip_scale, attn_params, attn_moment, attn_second, attn_ema)
    head_new = adam_step(head_share * clip_scale, head_params, head_moment, head_second, head_ema)
    return (
        hidden_out,
        input_grad,
        loss,
        grad_norm,
        attn_new[0],
        attn_new[1],
        attn_new[2],
        attn_new[3],
        head_new[0],
        head_new[1],
        head_new[2],
        head_new[3],
    )


def on_device(*arrays):
    shards = (arrays[5].shape[0], arrays[9].shape[0])
    local = on_grid if is_grid(lax.axis_size("sent"), *shards) else on_any_mesh
    return local(*arrays)


def solution(mesh):
    in_specs = (
        P("sent", None),
        P(None, "sent", None),
        P(None, None, "sent", None),
        P("sent"),
        P(),
        P("sent"),
        P("sent"),
        P("sent"),
        P("sent"),
        P("sent"),
        P("sent"),
        P("sent"),
        P("sent"),
    )
    out_specs = (
        P(None, "sent", None),
        P("sent", None),
        P(),
        P(),
        P("sent"),
        P("sent"),
        P("sent"),
        P("sent"),
        P("sent"),
        P("sent"),
        P("sent"),
        P("sent"),
    )
    return jax.shard_map(
        on_device, mesh=mesh, in_specs=in_specs, out_specs=out_specs, check_vma=False
    )
```

```python
import functools

import jax
import jax.numpy as jnp
from jax import lax
from jax.experimental import pallas as pl
from jax.experimental.pallas import tpu as pltpu
from jax.sharding import PartitionSpec as P

D = 768
H = 12
HD = 64
LMIN = 32
POS = 128
STEP = 5


logit_divisor = 0.05
keep_prob = 0.9
norm_eps = 1e-06
clip_bound = 0.001
beta_first = 0.5
beta_second = 0.5
learn_rate = 0.05
decay_rate = 0.01
adam_eps = 1e-08
ema_rate = 0.8
masked_scores = -1e30
highest = lax.Precision.HIGHEST


def layer_norm(tensor, gain_vec, shift_vec):
    center = tensor - jnp.mean(tensor, axis=-1, keepdims=True)
    spread = jnp.mean(center * center, axis=-1, keepdims=True)
    return center * lax.rsqrt(spread + norm_eps) * gain_vec + shift_vec


def gelu_exact(tensor):
    return 0.5 * tensor * (1.0 + jax.scipy.special.erf(tensor * 0.7071067811865476))


def unit_scale(tensor):
    return tensor * lax.rsqrt(jnp.sum(tensor * tensor, axis=-1, keepdims=True) + norm_eps)


def bucket_length(bucket_code):
    return (LMIN * jnp.where(bucket_code == 0, 1, jnp.where(bucket_code == 1, 2, 4))).astype(
        jnp.int32
    )


def plain_dot(left_op, right_op):
    return jnp.dot(left_op, right_op, preferred_element_type=jnp.float32)


def rows_dot(left_op, right_op):
    return lax.dot_general(
        left_op, right_op, (((0,), (0,)), ((), ())), preferred_element_type=jnp.float32
    )


def target_dot_terms(left_op, right_op):
    return lax.dot_general(
        left_op, right_op, (((1,), (1,)), ((), ())), preferred_element_type=jnp.float32
    )


def adam_step(grad_flat, params, moment, second, average):
    first_new = beta_first * moment + (1.0 - beta_first) * grad_flat
    second_new = beta_second * second + (1.0 - beta_second) * grad_flat * grad_flat
    fix_first = 1.0 - beta_first**STEP
    fix_second = 1.0 - beta_second**STEP
    adam_dir = first_new / fix_first / (jnp.sqrt(second_new / fix_second) + adam_eps)
    updated = params - learn_rate * (adam_dir + decay_rate * params)
    average_new = ema_rate * average + (1.0 - ema_rate) * updated
    return (first_new, second_new, updated, average_new)


LANES = 128
VMEM_CAP = 60 * 2**20


def room(mib):
    return pltpu.CompilerParams(vmem_limit_bytes=mib * 2**20)


def far(*arrays):
    return [pltpu.with_memory_space_constraint(array, pltpu.HBM) for array in arrays]


def bring(pairs, sems, first=0):
    copies = []
    for source, target in pairs:
        copies.append(pltpu.make_async_copy(source, target, sems.at[first + len(copies)]))
        copies[-1].start()
    return copies


def await_all(copies):
    for copy in copies:
        copy.wait()


def result(shape, dtype, stays=False):
    return pltpu.VMEM(shape, dtype) if stays else jax.ShapeDtypeStruct(shape, dtype)
CORE, XBIT, YBIT, ZBITS = 1, 2, 4, (8, 16, 24)


def swap(value, bit):
    count = lax.axis_size("sent")
    return lax.ppermute(value, "sent", [(i, i ^ bit) for i in range(count)])


def is_grid(count, *shards):
    return count == 32 and all(2 * shard % LANES == 0 for shard in shards)


def block_rows(shard):
    return -(-(-(-shard // LANES) + 8) // 16) * 16


def first_row(device, shard):
    return (device * shard) // LANES


def pack_shard(values, device):
    shard = values.shape[0]
    rows = block_rows(shard)
    size = rows * LANES
    odd = (device * shard) % LANES != 0
    lead = jnp.where(
        odd,
        jnp.pad(values, (LANES // 2, size - shard - LANES // 2)),
        jnp.pad(values, (0, size - shard)),
    ).reshape(rows, LANES)
    offset = first_row(device, shard) % 8
    padded = jnp.pad(lead, ((8, 0), (0, 0)))
    return lax.dynamic_slice(padded, (8 - offset, 0), (rows, LANES)).astype(jnp.bfloat16)


def unpack_shard(block, device, shard):
    rows = -(-shard // LANES)
    offset = first_row(device, shard) % 8
    odd = (device * shard) % LANES != 0
    flat = lax.dynamic_slice(block, (offset, 0), (rows, LANES)).reshape(-1)
    longer = jnp.pad(flat, (0, LANES))
    return jnp.where(odd, longer[LANES // 2 : LANES // 2 + shard], flat[:shard])


WHOLE = ((0, 0, 4), (1, 0, 4), (2, 0, 4), (3, 0, 2), (3, 2, 2))
HALVES = tuple((across, first, 2) for across in range(4) for first in (0, 2))


def piece_slots(me, layout):
    slots = []
    for core in (0, 1):
        for across, first, n in layout:
            slots.append([me ^ (core + 2 * across + 8 * (first + k)) for k in range(n)])
    return slots


def after(value, *others):
    return lax.optimization_barrier((value, others))[0]


def with_sibling(own):
    return tuple(own) + tuple(swap(piece, CORE) for piece in own)


def gather_attn(values, device):
    block = pack_shard(values, device)
    zs = [swap(block, bit) for bit in ZBITS]
    line = jnp.stack([block] + zs)
    x, y = swap(line, XBIT), swap(line, YBIT)
    diagonal = (swap(y[:2], XBIT), swap(x[2:], YBIT))
    return with_sibling((line, x, y) + diagonal), zs[0], diagonal


def gather_head_line(values, device, first):
    block = after(pack_shard(values, device), first)
    return [block] + [swap(block, bit) for bit in ZBITS]


def gather_head(low, high, x_low, x_high, y_low, y_high):
    return with_sibling((low, high, x_low, x_high, y_low, y_high, swap(y_low, XBIT), swap(x_high, YBIT)))


def low_sum(*terms):
    total = terms[0].astype(jnp.float32)
    for term in terms[1:]:
        total = total + term.astype(jnp.float32)
    return total.astype(jnp.bfloat16)


def scatter_core(pieces):
    half = len(pieces) // 2
    got = [swap(piece, CORE) for piece in reversed(pieces[half:])][::-1]
    return [low_sum(piece, other) for piece, other in zip(pieces[:half], got)]


def scatter_attn(sums):
    line, x, y, d_low, d_high = sums
    d_low, d_high = swap(d_low, XBIT), swap(d_high, YBIT)
    x = swap(jnp.concatenate([x[:2], low_sum(x[2:], d_high)]), XBIT)
    y = swap(jnp.concatenate([low_sum(y[:2], d_low), y[2:]]), YBIT)
    line = low_sum(line, x, y)
    return scatter_along(line[0], [line[k] for k in (1, 2, 3)])


def scatter_along(own, others):
    total = own.astype(jnp.float32)
    for value, bit in zip(others, ZBITS):
        total = total + swap(value, bit).astype(jnp.float32)
    return total


def plain_rows(left, right, dims):
    return lax.dot_general(left, right, (dims, ((), ())), preferred_element_type=jnp.float32)


NN, NT, TN = ((1,), (0,)), ((1,), (1,)), ((0,), (0,))


def one_hot(shape, left, right):
    rows = lax.broadcasted_iota(jnp.int32, shape, 0)
    cols = lax.broadcasted_iota(jnp.int32, shape, 1)
    return jnp.where(left(rows, cols) == right(rows, cols), 1.0, 0.0)


def vectors_of(flat_rows):
    spread = one_hot((D, 48), lambda r, c: r >> 4, lambda r, c: c).astype(jnp.bfloat16)
    rows = plain_rows(spread, flat_rows.astype(jnp.bfloat16), NN)
    rows = rows * one_hot((D, LANES), lambda r, c: r & 15, lambda r, c: c >> 3)
    fold = one_hot((8, LANES), lambda r, c: r, lambda r, c: c & 7).astype(jnp.bfloat16)
    return plain_rows(fold, rows.astype(jnp.bfloat16), NT)


def flat_of(vectors):
    fold = one_hot((8, LANES), lambda r, c: r, lambda r, c: c & 7).astype(jnp.bfloat16)
    rows = plain_rows(vectors.astype(jnp.bfloat16), fold, TN)
    rows = rows * one_hot((D, LANES), lambda r, c: r & 15, lambda r, c: c >> 3)
    spread = one_hot((D, 48), lambda r, c: r >> 4, lambda r, c: c).astype(jnp.bfloat16)
    return plain_rows(spread, rows.astype(jnp.bfloat16), TN)


def keep_of(mask):
    return mask.astype(jnp.float32) * (1.0 / keep_prob)


def place_blocks(shard, layout, pieces, me, stage, flat, sems):
    count, rows = stage.shape[0], stage.shape[1]
    inner = shard // (8 * LANES) * 8
    for piece, slots in zip(pieces, piece_slots(me, layout)):
        for k, slot in enumerate(slots):
            pltpu.make_async_copy(piece.at[k], stage.at[slot], sems.at[slot]).start()

    def start_of(device):
        return pl.multiple_of(device * shard // LANES // 8 * 8, 8)

    def clear(device, carry):
        at = start_of(device)
        flat[pl.ds(at, 8), :] = jnp.zeros((8, LANES), jnp.float32)
        flat[pl.ds(at + inner, 16), :] = jnp.zeros((16, LANES), jnp.float32)
        return carry

    lax.fori_loop(0, count, clear, 0)

    def place(index, carry):
        device = me ^ ((index >> 4) + 2 * ((index >> 2) & 3) + 8 * (index & 3))
        pltpu.make_async_copy(pieces[0].at[0], stage.at[device], sems.at[device]).wait()
        at = start_of(device)
        flat[pl.ds(at, 8), :] += stage[device, :16].astype(jnp.float32)[:8]
        flat[pl.ds(at + 8, inner - 8), :] = stage[device].astype(jnp.float32)[8:inner]
        flat[pl.ds(at + inner, 16), :] += stage[device].astype(jnp.float32)[inner : inner + 16]
        return carry

    lax.fori_loop(0, count, place, 0)


def gather_matrix(flat, w_ref, w_out=None, out_sems=None):
    cols = w_ref.shape[1] // LANES

    def gather_rows(group, carry):
        at = pl.multiple_of(group * 16, 16)
        for col in range(cols):
            rows16 = flat[pl.ds(group * 16 * cols + col, 16, stride=cols), :]
            w_ref[pl.ds(at, 16), pl.ds(col * LANES, LANES)] = rows16.astype(jnp.bfloat16)
        return carry

    parts = 4
    span = D // parts
    copies = []
    for part in range(parts):
        lax.fori_loop(part * span // 16, (part + 1) * span // 16, gather_rows, 0)
        here = pl.ds(part * span, span)
        if w_out is not None:
            copies.append(pltpu.make_async_copy(w_ref.at[here], w_out.at[here], out_sems.at[part]))
            copies[-1].start()
    return copies


VEC = 8 + POS


def table_of(flat, base, body, tail):
    lane = lax.broadcasted_iota(jnp.int32, (D // 16, LANES), 1)
    for q in range(16):
        here = flat[pl.ds(base + q, D // 16, stride=17), :]
        later = flat[pl.ds(base + q + 1, D // 16, stride=17), :]
        both = jnp.where(lane >= 8 * q, here, later)
        shift = (LANES - 8 * q) % LANES
        body[pl.ds(q, D // 16, stride=16), :] = pltpu.roll(both, shift, 1) if shift else both
        tail[pl.ds(q, D // 16, stride=16), :] = pltpu.roll(later, shift, 1) if shift else later
    return body[...].T, tail[...].T[:8]


def flat_table(flat, base, first, last, body, tail):
    body[...] = first.T
    tail[...] = jnp.concatenate([last, jnp.zeros((LANES - 8, D), jnp.float32)]).T
    lane = lax.broadcasted_iota(jnp.int32, (D // 16, LANES), 1)
    carried = None
    for q in range(17):
        row = carried
        if q < 16:
            main = body[pl.ds(q, D // 16, stride=16), :]
            end = tail[pl.ds(q, D // 16, stride=16), :]
            if q:
                main, end = pltpu.roll(main, 8 * q, 1), pltpu.roll(end, 8 * q, 1)
            row = main if carried is None else jnp.where(lane >= 8 * q, main, carried)
            carried = jnp.where(lane < 8 * q, main, end)
        flat[pl.ds(base + q, D // 16, stride=17), :] = row


def repeat_places(table, length):
    twice = jnp.concatenate([table[:64]] * 2)
    four = jnp.concatenate([table[:32]] * 4)
    return jnp.where(length == 128, table, jnp.where(length == 64, twice, four))


def fold_places(rows, length):
    half = rows[:64] + rows[64:]
    quarter = half[:32] + half[32:]
    none = jnp.zeros_like(rows)
    twice = jnp.concatenate([half, none[:64]])
    four = jnp.concatenate([quarter, none[:96]])
    return jnp.where(length == 128, rows, jnp.where(length == 64, twice, four))


def stack_heads(pair):
    lane = lax.broadcasted_iota(jnp.int32, pair.shape, 1)
    none = jnp.zeros_like(pair)
    return jnp.concatenate([jnp.where(lane < HD, pair, none), jnp.where(lane < HD, none, pair)])


def unstack_heads(rows):
    half = rows.shape[0] // 2
    lane = lax.broadcasted_iota(jnp.int32, (half, rows.shape[1]), 1)
    return jnp.where(lane < HD, rows[:half], rows[half:])


ROWS = 64


def attn_kernel(shard, me_ref, length_ref, lens_ref, *refs):
    pieces, (emb_ref, mask_hbm) = refs[:10], refs[10:12]
    (w_out, vec_ref, rows_ref, in_low_ref, qkv_ref, prob_ref, mixed_ref, res_ref, norm_ref, low_ref) = refs[12:22]
    (stage, flat, w_ref, body, tail, mask, attn_in, bias_ref, sems, out_sems, mask_sems) = refs[22:]
    me = me_ref[0]
    tokens = emb_ref.shape[0]
    masks = []
    for view in range(2):
        for which in range(2):
            at = 2 * view + which
            masks.append(pltpu.make_async_copy(mask_hbm.at[view, which], mask.at[at], mask_sems.at[at]))
            masks[-1].start()
    place_blocks(shard, WHOLE, pieces, me, stage, flat, sems)
    copies = gather_matrix(flat, w_ref, w_out, out_sems)
    first, last = table_of(flat, D * w_ref.shape[1] // LANES, body, tail)
    vecs = first[:8]
    vec_ref[...] = vecs
    length = length_ref[0]
    places = repeat_places(jnp.concatenate([first[8:], last]), length)
    for copy in masks:
        copy.wait()
    for block in range(tokens // LANES):
        key = lax.broadcasted_iota(jnp.int32, (LANES, LANES), 1) + block * LANES
        query = lax.broadcasted_iota(jnp.int32, (LANES, LANES), 0) + block * LANES
        shift = jnp.where(length == 128, 7, jnp.where(length == 64, 6, 5))
        sent = lax.shift_right_logical(key, jnp.full_like(key, 1) * shift)
        sent_q = lax.shift_right_logical(query, jnp.full_like(key, 1) * shift)
        real = jnp.zeros_like(key)
        for slot in range(lens_ref.shape[0]):
            real = jnp.where(sent == slot, lens_ref[slot], real)
        ok = (sent == sent_q) & ((key & (length - 1)) < real)
        bias_ref[block] = jnp.where(ok, 0.0, masked_scores)
        here = pl.ds(block * LANES, LANES)
        emb = emb_ref[here, :].astype(jnp.float32) + places + vecs[7:8]
        rows_ref[here, :] = emb
        normed = layer_norm(emb, vecs[5:6], vecs[6:7])
        for view in range(2):
            at = pl.ds(view * tokens + block * LANES, LANES)
            given = normed * keep_of(mask[2 * view, here, :])
            attn_in[at, :] = given
            in_low_ref[at, :] = given.astype(jnp.bfloat16)
    for part in range(3):
        cols = pl.ds(part * D, D)
        made = plain_rows(in_low_ref[...], w_ref[:, cols], NN)
        if part != 1:
            made = made + vecs[part // 2 : part // 2 + 1]
        qkv_ref[:, cols] = made.astype(jnp.bfloat16)

    def attend(block, carry):
        here = pl.ds(pl.multiple_of(block * LANES, LANES), LANES)
        bias = bias_ref[block & 1]
        bias = jnp.concatenate([bias, bias])
        for pair in range(H // 2):
            q = stack_heads(qkv_ref[here, pl.ds(pair * LANES, LANES)])
            k = qkv_ref[here, pl.ds(D + pair * LANES, LANES)]
            v = qkv_ref[here, pl.ds(2 * D + pair * LANES, LANES)]
            scores = plain_rows(q, k, NT) * HD ** (-0.5) + bias
            expo = jnp.exp(scores - jnp.max(scores, axis=-1, keepdims=True))
            probs = expo / jnp.sum(expo, axis=-1, keepdims=True)
            prob_ref[block, pair] = probs
            mixed = unstack_heads(plain_rows(probs.astype(jnp.bfloat16), v, NN))
            mixed_ref[here, pl.ds(pair * LANES, LANES)] = mixed.astype(jnp.bfloat16)
        return carry

    lax.fori_loop(0, 2 * tokens // LANES, attend, 0)
    res_ref[...] = plain_rows(mixed_ref[...], w_ref[:, 3 * D :], NN)
    for view in range(2):
        def finish(chunk, carry, view=view):
            own = pl.ds(pl.multiple_of(chunk * ROWS, ROWS), ROWS)
            at = pl.ds(pl.multiple_of(view * tokens + chunk * ROWS, ROWS), ROWS)
            res = attn_in[at, :] + keep_of(mask[2 * view + 1, own, :]) * (res_ref[at, :] + vecs[2:3])
            res_ref[at, :] = res
            norm = layer_norm(res, vecs[3:4], vecs[4:5])
            norm_ref[at, :] = norm
            low_ref[at, :] = norm.astype(jnp.bfloat16)
            return carry

        lax.fori_loop(0, tokens // ROWS, finish, 0, unroll=True)
    for copy in copies:
        copy.wait()


def attn_forward(pieces, me, shard, length, lengths, embeddings, masks):
    rows = pieces[0].shape[1]
    whole = shard * 32 // LANES
    tokens = embeddings.shape[0]
    both = 2 * tokens
    any_space, vmem = pl.BlockSpec(memory_space=pltpu.HBM), pl.BlockSpec(memory_space=pltpu.VMEM)
    smem = pl.BlockSpec(memory_space=pltpu.SMEM)
    f32, low = jnp.float32, jnp.bfloat16
    shapes = [
        ((D, 4 * D), low),
        ((8, D), f32),
        ((tokens, D), f32),
        ((both, D), low),
        ((both, 3 * D), low),
        ((both // LANES, H // 2, 2 * LANES, LANES), f32),
        ((both, D), low),
        ((both, D), f32),
        ((both, D), f32),
        ((both, D), low),
    ]
    return pl.pallas_call(
        functools.partial(attn_kernel, shard),
        out_shape=tuple(jax.ShapeDtypeStruct(*s) for s in shapes),
        in_specs=[smem] * 3 + [any_space] * len(pieces) + [vmem, any_space],
        out_specs=(any_space,) + (vmem,) * 9,
        scratch_shapes=[
            pltpu.VMEM((32, rows, LANES), low),
            pltpu.VMEM((whole + rows, LANES), f32),
            pltpu.VMEM((D, 4 * D), low),
            pltpu.VMEM((D, LANES), f32),
            pltpu.VMEM((D, LANES), f32),
            pltpu.VMEM((4, tokens, D), jnp.int32),
            pltpu.VMEM((both, D), f32),
            pltpu.VMEM((tokens // LANES, LANES, LANES), f32),
            pltpu.SemaphoreType.DMA((32,)),
            pltpu.SemaphoreType.DMA((4,)),
            pltpu.SemaphoreType.DMA((4,)),
        ],
        compiler_params=pltpu.CompilerParams(vmem_limit_bytes=VMEM_CAP),
    )(jnp.reshape(me, (1,)), jnp.reshape(length, (1,)), lengths, *far(*pieces), embeddings, *far(masks))


def sum_rows(rows):
    return jnp.sum(rows, axis=0, keepdims=True)


def norm_back_kernel(pick_ref, d_first, d_cls_in, res_in, vec_in, mask_hbm, mixed_in, w_in,
                     d_res_ref, g_out_ref, d_mixed, part_ref,
                     mask, given, branch, d_cls, res_ref, vec_ref, mixed_ref, w_ref, sems):
    tokens = mask.shape[1]
    both = 2 * tokens
    copies = bring(
        [(d_first, given), (d_cls_in, d_cls), (res_in, res_ref), (vec_in, vec_ref)]
        + [(mask_hbm.at[view, 1], mask.at[view]) for view in range(2)]
        + [(w_in.at[:, pl.ds(3 * D, D)], w_ref), (mixed_in, mixed_ref)],
        sems,
    )
    await_all(copies[:6])
    n = d_cls.shape[0] // 2
    for slot in range(n):
        real = jnp.where(slot < pick_ref[n], 1.0, 0.0)
        for view in range(2):
            at = pl.ds(view * tokens + pick_ref[slot], 1)
            given[at, :] += real * d_cls[view * n + slot : view * n + slot + 1, :]
    gain = vec_ref[3:4, :]
    sums = tuple(jnp.zeros((1, D), jnp.float32) for _ in range(3))
    for view in range(2):
        def one_chunk(chunk, sums, view=view):
            own = pl.ds(pl.multiple_of(chunk * ROWS, ROWS), ROWS)
            at = pl.ds(pl.multiple_of(view * tokens + chunk * ROWS, ROWS), ROWS)
            grad = given[at, :]
            center, inv = norm_parts(res_ref[at, :])
            d_res, unit = norm_back(grad, center, inv, gain)
            d_branch = d_res * keep_of(mask[view, own, :])
            d_res_ref[at, :] = d_res
            branch[at, :] = d_branch.astype(jnp.bfloat16)
            return (
                sums[0] + sum_rows(d_branch),
                sums[1] + sum_rows(grad * unit),
                sums[2] + sum_rows(grad),
            )

        sums = lax.fori_loop(0, tokens // ROWS, one_chunk, sums, unroll=True)
    await_all(copies[6:])
    d_mixed[...] = plain_rows(branch[...], w_ref[...], NT).astype(jnp.bfloat16)
    g_out_ref[...] = plain_rows(mixed_ref[...], branch[...], TN).astype(jnp.bfloat16)
    for k in range(3):
        part_ref[k : k + 1, :] = sums[k]
    part_ref[3:8, :] = jnp.zeros((5, D), jnp.float32)


def norm_backward(picks, d_first, d_cls, res, vecs, masks, mixed, w_attn):
    both = res.shape[0]
    any_space, vmem = pl.BlockSpec(memory_space=pltpu.HBM), pl.BlockSpec(memory_space=pltpu.VMEM)
    f32, low = jnp.float32, jnp.bfloat16
    return pl.pallas_call(
        norm_back_kernel,
        out_shape=(
            result((both, D), f32),
            result((D, D), low),
            result((both, D), low, True),
            result((8, D), f32),
        ),
        in_specs=[pl.BlockSpec(memory_space=pltpu.SMEM)] + [any_space] * 7,
        out_specs=(vmem,) * 4,
        scratch_shapes=[
            pltpu.VMEM((2, both // 2, D), jnp.int32),
            pltpu.VMEM((both, D), f32),
            pltpu.VMEM((both, D), low),
            pltpu.VMEM(d_cls.shape, f32),
            pltpu.VMEM((both, D), f32),
            pltpu.VMEM((8, D), f32),
            pltpu.VMEM((both, D), low),
            pltpu.VMEM((D, D), low),
            pltpu.SemaphoreType.DMA((8,)),
        ],
        compiler_params=room(16),
    )(picks, *far(d_first, d_cls, res, vecs, masks, mixed, w_attn))


def attn_back_kernel(d_mixed, qkv_ref, prob_ref, d_qkv_ref, part_ref):
    part_ref[...] = jnp.zeros_like(part_ref)

    def one_block(block, carry):
        here = pl.ds(pl.multiple_of(block * LANES, LANES), LANES)
        for pair in range(H // 2):
            cols = pl.ds(pair * LANES, LANES)
            q = stack_heads(qkv_ref[here, cols])
            k = qkv_ref[here, pl.ds(D + pair * LANES, LANES)]
            v = qkv_ref[here, pl.ds(2 * D + pair * LANES, LANES)]
            d_out = stack_heads(d_mixed[here, cols])
            probs = prob_ref[block, pair]
            d_v = plain_rows(probs.astype(jnp.bfloat16), d_out, TN)
            d_probs = plain_rows(d_out, v, NT)
            delta = jnp.sum(probs * d_probs, axis=-1, keepdims=True)
            score = (probs * (d_probs - delta) * HD ** (-0.5)).astype(jnp.bfloat16)
            d_q = unstack_heads(plain_rows(score, k, NN))
            d_k = plain_rows(score, q, TN)
            d_qkv_ref[here, cols] = d_q.astype(jnp.bfloat16)
            d_qkv_ref[here, pl.ds(D + pair * LANES, LANES)] = d_k.astype(jnp.bfloat16)
            d_qkv_ref[here, pl.ds(2 * D + pair * LANES, LANES)] = d_v.astype(jnp.bfloat16)
            part_ref[0:1, cols] += sum_rows(d_q)
            part_ref[1:2, cols] += sum_rows(d_v)
        return carry

    lax.fori_loop(0, qkv_ref.shape[0] // LANES, one_block, 0)


def attn_backward(d_mixed, qkv, probs):
    vmem = pl.BlockSpec(memory_space=pltpu.VMEM)
    return pl.pallas_call(
        attn_back_kernel,
        out_shape=(result(qkv.shape, jnp.bfloat16, True), pltpu.HBM((8, D), jnp.float32)),
        in_specs=[vmem] * 3,
        out_specs=(vmem,) * 2,
        compiler_params=room(16),
    )(d_mixed, qkv, probs)


def attn_grad_kernel(shard, me_ref, length_ref, d_qkv, *refs):
    sources, input_ref, pieces, scratch = refs[:9], refs[9], refs[10:20], refs[20:]
    stage, flat, body, tail, d_in, sems, in_sems, mask = scratch[:8]
    in_low, w_ref, d_res, rows_ref, vec_ref, g_out, part_ref, norm_part_ref = scratch[8:]
    in_hbm, w_hbm, d_res_hbm, rows_hbm, vec_hbm, mask_hbm, g_hbm, part_hbm, norm_part_hbm = sources
    cols = 4 * D // LANES
    tokens = rows_ref.shape[0]
    copies = bring(
        [(in_hbm, in_low), (g_hbm, g_out), (w_hbm.at[:, pl.ds(0, 3 * D)], w_ref), (d_res_hbm, d_res)]
        + [(mask_hbm.at[view, 0], mask.at[view]) for view in range(2)]
        + [(rows_hbm, rows_ref), (vec_hbm, vec_ref), (part_hbm, part_ref), (norm_part_hbm, norm_part_ref)],
        in_sems,
    )
    await_all(copies[:2])
    span, width = 256, 3 * LANES

    def one_block(block, carry):
        left = in_low[:, pl.ds(pl.multiple_of(block * span, span), span)]
        for k in range(3 * D // width):
            grads = plain_rows(left, d_qkv[:, pl.ds(k * width, width)], TN)
            for col in range(width // LANES):
                for group in range(span // 16):
                    at = (block * span + group * 16) * cols + k * width // LANES + col
                    tile = grads[group * 16 : (group + 1) * 16, col * LANES : (col + 1) * LANES]
                    flat[pl.ds(at, 16, stride=cols), :] = tile
        return carry

    lax.fori_loop(0, D // span, one_block, 0)

    def one_group(group, carry):
        at = pl.multiple_of(group * 16, 16)
        for col in range(D // LANES):
            tile = g_out[pl.ds(at, 16), pl.ds(col * LANES, LANES)].astype(jnp.float32)
            flat[pl.ds(group * 16 * cols + 3 * D // LANES + col, 16, stride=cols), :] = tile
        return carry

    lax.fori_loop(0, D // 16, one_group, 0)
    copies[2].wait()
    d_in[...] = plain_rows(d_qkv[...], w_ref[...], NT)
    await_all(copies[3:])
    gain = vec_ref[5:6, :]

    def one_chunk(chunk, sums):
        own = pl.ds(pl.multiple_of(chunk * ROWS, ROWS), ROWS)
        other = pl.ds(pl.multiple_of(tokens + chunk * ROWS, ROWS), ROWS)
        grad = (d_in[own, :] + d_res[own, :]) * keep_of(mask[0, own, :])
        grad = grad + (d_in[other, :] + d_res[other, :]) * keep_of(mask[1, own, :])
        center, inv = norm_parts(rows_ref[own, :])
        back, unit = norm_back(grad, center, inv, gain)
        input_ref[own, :] = back
        return (sums[0] + sum_rows(grad * unit), sums[1] + sum_rows(grad), sums[2] + sum_rows(back))

    none = tuple(jnp.zeros((1, D), jnp.float32) for _ in range(3))
    sums = lax.fori_loop(0, tokens // ROWS, one_chunk, none, unroll=True)
    table = jnp.zeros((LANES, D), jnp.float32)
    for block in range(tokens // LANES):
        table = table + input_ref[block * LANES : (block + 1) * LANES, :]
    table = fold_places(table, length_ref[0])
    first = jnp.concatenate([part_ref[0:2, :], norm_part_ref[0:3, :], *sums, table[: LANES - 8]])
    base = D * cols
    flat_table(flat, base, first, table[LANES - 8 :], body, tail)
    rows = stage.shape[1]
    flat[pl.ds(base + D * VEC // LANES, rows), :] = jnp.zeros((rows, LANES), jnp.float32)
    store_pieces(shard, WHOLE, me_ref[0], pieces, stage, flat, sems)


def attn_grads(me, shard, length, d_qkv, in_low, w_attn, d_res, rows_in, vecs, masks, g_out, parts, norm_parts_in):
    rows = block_rows(shard)
    whole = shard * 32 // LANES
    tokens = rows_in.shape[0]
    counts = [len(slots) for slots in piece_slots(0, WHOLE)]
    any_space, vmem = pl.BlockSpec(memory_space=pltpu.HBM), pl.BlockSpec(memory_space=pltpu.VMEM)
    smem = pl.BlockSpec(memory_space=pltpu.SMEM)
    f32, low = jnp.float32, jnp.bfloat16
    return pl.pallas_call(
        functools.partial(attn_grad_kernel, shard),
        out_shape=(jax.ShapeDtypeStruct((tokens, D), f32),)
        + tuple(pltpu.HBM((n, rows, LANES), low) for n in counts),
        in_specs=[smem, smem, vmem] + [any_space] * 9,
        out_specs=(vmem,) + (any_space,) * len(counts),
        scratch_shapes=[
            pltpu.VMEM((32, rows, LANES), low),
            pltpu.VMEM((whole + rows, LANES), f32),
            pltpu.VMEM((D, LANES), f32),
            pltpu.VMEM((D, LANES), f32),
            pltpu.VMEM((2 * tokens, D), f32),
            pltpu.SemaphoreType.DMA((32,)),
            pltpu.SemaphoreType.DMA((10,)),
            pltpu.VMEM((2, tokens, D), jnp.int32),
            pltpu.VMEM((2 * tokens, D), low),
            pltpu.VMEM((D, 3 * D), low),
            pltpu.VMEM((2 * tokens, D), f32),
            pltpu.VMEM((tokens, D), f32),
            pltpu.VMEM((8, D), f32),
            pltpu.VMEM((D, D), low),
            pltpu.VMEM((8, D), f32),
            pltpu.VMEM((8, D), f32),
        ],
        compiler_params=room(40),
    )(
        jnp.reshape(me, (1,)),
        jnp.reshape(length, (1,)),
        d_qkv,
        *far(in_low, w_attn, d_res, rows_in, vecs, masks, g_out, parts, norm_parts_in),
    )


def head_kernel(shard, me_ref, pick_ref, *refs):
    pieces, (first_hbm, mask_hbm) = refs[:16], refs[16:18]
    w_ref, vec_ref, unit_ref, cls_ref = refs[18:22]
    stage, flat, first_all, picked, mask, sems, in_sems = refs[22:]
    cols = w_ref.shape[1] // LANES
    tokens = mask.shape[1]
    place_blocks(shard, HALVES, pieces, me_ref[0], stage, flat, sems)
    loads = [(first_hbm, first_all)] + [(mask_hbm.at[view, 2], mask.at[view]) for view in range(2)]
    loads = bring(loads, in_sems)
    gather_matrix(flat, w_ref)
    await_all(loads)
    n = unit_ref.shape[0] // 2
    for view in range(2):
        for slot in range(n):
            at, to = pick_ref[slot], view * n + slot
            picked[to : to + 1, :] = first_all[pl.ds(view * tokens + at, 1), :]
            cls_ref[to : to + 1, 2 * D : 3 * D] = keep_of(mask[view, pl.ds(at, 1), :])
    vecs = vectors_of(flat[pl.ds(D * cols, 48), :])
    vec_ref[...] = vecs
    first = picked[...]
    up_bias = jnp.concatenate([vecs[c : c + 1] for c in range(4)], axis=1)
    up_pre = plain_rows(first.astype(jnp.bfloat16), w_ref[:, : 4 * D], NN) + up_bias
    active = gelu_exact(up_pre).astype(jnp.bfloat16)
    down = plain_rows(active, w_ref[:, 4 * D : 8 * D], NT) + vecs[4:5]
    res = first + cls_ref[:, 2 * D : 3 * D] * down
    cls_low = layer_norm(res, vecs[5:6], vecs[6:7]).astype(jnp.bfloat16)
    pooled = jnp.tanh(plain_rows(cls_low, w_ref[:, 8 * D :], NN) + vecs[7:8])
    unit_ref[...] = unit_scale(pooled).astype(jnp.bfloat16)
    cls_ref[:, :D] = pooled
    cls_ref[:, D : 2 * D] = res
    cls_ref[:, 3 * D :] = up_pre


def make_head(pieces, me, shard, picks, first_norm, masks):
    rows = pieces[0].shape[1]
    whole = shard * 32 // LANES
    n = 2 * (picks.shape[0] - 1)
    any_space, vmem = pl.BlockSpec(memory_space=pltpu.HBM), pl.BlockSpec(memory_space=pltpu.VMEM)
    smem = pl.BlockSpec(memory_space=pltpu.SMEM)
    f32, low = jnp.float32, jnp.bfloat16
    return pl.pallas_call(
        functools.partial(head_kernel, shard),
        out_shape=(
            result((D, 9 * D), low, True),
            result((8, D), f32, True),
            result((n, D), low),
            result((n, 7 * D), f32),
        ),
        in_specs=[smem] * 2 + [any_space] * (len(pieces) + 2),
        out_specs=(vmem,) * 4,
        scratch_shapes=[
            pltpu.VMEM((32, rows, LANES), low),
            pltpu.VMEM((whole + rows, LANES), f32),
            pltpu.VMEM(first_norm.shape, f32),
            pltpu.VMEM((n, D), f32),
            pltpu.VMEM((2,) + masks.shape[2:], jnp.int32),
            pltpu.SemaphoreType.DMA((32,)),
            pltpu.SemaphoreType.DMA((3,)),
        ],
        compiler_params=room(42),
    )(jnp.reshape(me, (1,)), picks, *far(*pieces, first_norm, masks))


def norm_back(grad, center, inv, gain):
    unit = center * inv
    scaled = grad * gain
    mean = jnp.mean(scaled, axis=-1, keepdims=True)
    along = jnp.mean(scaled * unit, axis=-1, keepdims=True)
    return inv * (scaled - mean - unit * along), unit


def norm_parts(rows):
    center = rows - jnp.mean(rows, axis=-1, keepdims=True)
    return center, lax.rsqrt(jnp.mean(center * center, axis=-1, keepdims=True) + norm_eps)


def gelu_slope(values):
    cdf = 0.5 * (1.0 + lax.erf(values * 0.7071067811865476))
    return cdf + values * (0.3989422804014327 * jnp.exp(-0.5 * values * values))


CHUNK = 1024


def forward_kernel(first_low, first_ref, w_ref, vec_ref, mask_hbm, cot_ref,
                   act_ref, slope_ref, hidden_ref, d_res_ref, down_ref, part_ref,
                   mask, acc, made, sems):
    tokens = mask.shape[1]
    both = 2 * tokens
    copies = []
    for view in range(2):
        copies.append(pltpu.make_async_copy(mask_hbm.at[view, 2], mask.at[view], sems.at[view]))
    for copy in copies:
        copy.start()
    vecs = vec_ref[...]
    for k in range(4 * D // CHUNK):
        cols = pl.ds(k * CHUNK, CHUNK)
        bias = jnp.concatenate([vecs[c : c + 1] for c in range(4)], axis=1)[:, k * CHUNK : (k + 1) * CHUNK]
        made[...] = plain_rows(first_low[...], w_ref[:, cols], NN)

        def one_group(group, carry, bias=bias, cols=cols):
            at = pl.ds(pl.multiple_of(group * ROWS, ROWS), ROWS)
            up = made[at, :] + bias
            cdf = 0.5 * (1.0 + lax.erf(up * 0.7071067811865476))
            act_ref[at, cols] = (up * cdf).astype(jnp.bfloat16)
            slope = cdf + up * (0.3989422804014327 * jnp.exp(-0.5 * up * up))
            slope_ref[at, cols] = slope.astype(jnp.bfloat16)
            return carry

        lax.fori_loop(0, both // ROWS, one_group, 0, unroll=4)
    for copy in copies:
        copy.wait()
    acc[...] = plain_rows(act_ref[...], w_ref[:, 4 * D : 8 * D], NT)
    sums = tuple(jnp.zeros((1, D), jnp.float32) for _ in range(3))
    for view in range(2):
        def one_chunk(chunk, sums, view=view):
            own = pl.ds(pl.multiple_of(chunk * ROWS, ROWS), ROWS)
            at = pl.ds(pl.multiple_of(view * tokens + chunk * ROWS, ROWS), ROWS)
            keep = keep_of(mask[view, own, :])
            center, inv = norm_parts(first_ref[at, :] + keep * (acc[at, :] + vecs[4:5]))
            grad = cot_ref[view, own, :].astype(jnp.float32)
            hidden_ref[view, own, :] = (center * inv * vecs[5:6] + vecs[6:7]).astype(jnp.bfloat16)
            d_res, unit = norm_back(grad, center, inv, vecs[5:6])
            d_down = d_res * keep
            d_res_ref[at, :] = d_res
            down_ref[at, :] = d_down.astype(jnp.bfloat16)
            return (sums[0] + sum_rows(d_down), sums[1] + sum_rows(grad * unit), sums[2] + sum_rows(grad))

        sums = lax.fori_loop(0, tokens // ROWS, one_chunk, sums, unroll=True)
    part_ref[...] = jnp.zeros_like(part_ref)
    for k in range(3):
        part_ref[4 + k : 5 + k, :] = sums[k]


def head_forward(first_low, first_norm, w_head, vecs, masks, cotangent):
    both = first_low.shape[0]
    tokens = both // 2
    any_space, vmem = pl.BlockSpec(memory_space=pltpu.HBM), pl.BlockSpec(memory_space=pltpu.VMEM)
    f32, low = jnp.float32, jnp.bfloat16
    return pl.pallas_call(
        forward_kernel,
        out_shape=(
            result((both, 4 * D), low, True),
            result((both, 4 * D), low, True),
            result((2, tokens, D), low),
            result((both, D), f32, True),
            result((both, D), low, True),
            result((8, D), f32, True),
        ),
        in_specs=[vmem, vmem, vmem, vmem, any_space, vmem],
        out_specs=(vmem,) * 6,
        scratch_shapes=[
            pltpu.VMEM((2, tokens, D), jnp.int32),
            pltpu.VMEM((both, D), f32),
            pltpu.VMEM((both, CHUNK), f32),
            pltpu.SemaphoreType.DMA((2,)),
        ],
        compiler_params=room(14),
    )(first_low, first_norm, w_head, vecs, masks, cotangent)


def backward_kernel(down_ref, slope_ref, d_res_ref, part_in, w_ref, up_ref, first_ref, part_ref, made):
    part_ref[...] = part_in[...]
    both = down_ref.shape[0]
    sums = []
    for k in range(4 * D // CHUNK):
        cols = pl.ds(k * CHUNK, CHUNK)
        made[...] = plain_rows(down_ref[...], w_ref[:, pl.ds(4 * D + k * CHUNK, CHUNK)], NN)

        def one_group(group, total, cols=cols):
            at = pl.ds(pl.multiple_of(group * ROWS, ROWS), ROWS)
            d_up = made[at, :] * slope_ref[at, cols].astype(jnp.float32)
            up_ref[at, cols] = d_up.astype(jnp.bfloat16)
            return total + sum_rows(d_up)

        sums.append(lax.fori_loop(0, both // ROWS, one_group, jnp.zeros((1, CHUNK), jnp.float32), unroll=4))
    sums = jnp.concatenate(sums, axis=1)
    for c in range(4):
        part_ref[c : c + 1, :] = sums[:, c * D : (c + 1) * D]
    first_ref[...] = d_res_ref[...] + plain_rows(up_ref[...], w_ref[:, : 4 * D], NT)


def head_backward(down_low, slope, d_res, parts, w_head):
    both = down_low.shape[0]
    vmem = pl.BlockSpec(memory_space=pltpu.VMEM)
    f32, low = jnp.float32, jnp.bfloat16
    return pl.pallas_call(
        backward_kernel,
        out_shape=(
            result((both, 4 * D), low, True),
            pltpu.HBM((both, D), f32),
            result((8, D), f32, True),
        ),
        in_specs=[vmem] * 5,
        out_specs=(vmem,) * 3,
        scratch_shapes=[
            pltpu.VMEM((both, CHUNK), f32),
        ],
        compiler_params=room(10),
    )(down_low, slope, d_res, parts, w_head)


def pick_columns(core, blocks):
    shape = (blocks * 32, D)
    index = lax.broadcasted_iota(jnp.int32, shape, 0)
    wanted = (index >> 5) * 48 + 24 * core + (index & 31)
    return (wanted == lax.broadcasted_iota(jnp.int32, shape, 1)).astype(jnp.bfloat16)


def pooled_kernel(me_ref, own_ref, sib_ref, w_hbm, cls_own, cls_sib, valid_in, vec_in,
                  loss_ref, first_ref, out_ref, low_ref, part_ref,
                  units, sims, back, cls, valid_ref, vec_ref, w_ref, sems, w_sems):
    me = me_ref[0]
    core = me & 1
    n = units.shape[1]
    pairs = []
    for side, ref in ((0, own_ref), (1, sib_ref)):
        for across in range(4):
            for k in range(4):
                pairs.append((ref.at[across, k], units.at[me ^ (side + 2 * across + 8 * k)]))
    place = pl.multiple_of(core * n, n)
    pairs += [(cls_own, cls.at[pl.ds(place, n)]), (cls_sib, cls.at[pl.ds(n - place, n)])]
    pairs += [(valid_in, valid_ref), (vec_in, vec_ref)]
    copies = bring(pairs, sems)
    w_copies = bring(
        [
            (w_hbm.at[:, pl.ds(start, size)], w_ref.at[:, pl.ds(start, size)])
            for start, size in ((8 * D, D), (4 * D, 4 * D), (0, 4 * D))
        ],
        w_sems,
    )
    await_all(copies)
    half = n // 2
    total = units.shape[0] * n
    everyone = units[...].reshape(total, D)
    table = plain_rows(everyone, everyone, NT) * (1.0 / logit_divisor)
    row = lax.broadcasted_iota(jnp.int32, (total, total), 0)
    col = lax.broadcasted_iota(jnp.int32, (total, total), 1)
    table = jnp.where(((col & (n - 1)) >= half) & (valid_ref[...] > 0), table, masked_scores)
    top = jnp.max(table, axis=-1, keepdims=True)
    row_lse = top + jnp.log(jnp.sum(jnp.exp(table - top), axis=-1, keepdims=True))
    diagonal = col == row + half
    positive = jnp.sum(jnp.where(diagonal, table, 0.0), axis=-1, keepdims=True)
    row_one = lax.broadcasted_iota(jnp.int32, (total, 1), 0)
    anchors = ((row_one & (n - 1)) < half) & (positive > 0.5 * masked_scores)
    count = 0.5 * jnp.sum(valid_ref[...])
    loss_ref[0, 0] = jnp.sum(jnp.where(anchors, row_lse - positive, 0.0)) / count
    slope = (jnp.exp(table - row_lse) - jnp.where(diagonal, 1.0, 0.0)) * (1.0 / logit_divisor)
    sims[...] = jnp.where(anchors, slope, 0.0).astype(jnp.bfloat16)
    back[...] = plain_rows(sims[...], everyone, TN)
    chip = pl.ds(pl.multiple_of((me >> 1) * 2 * n, 2 * n), 2 * n)
    d_unit = plain_rows(sims[chip, :], everyone, NN) + back[chip, :]
    pooled = cls[:, :D]
    inv = lax.rsqrt(jnp.sum(pooled * pooled, axis=-1, keepdims=True) + norm_eps)
    along = jnp.sum(pooled * d_unit, axis=-1, keepdims=True)
    d_pooled = inv * d_unit - pooled * (inv * inv * inv * along)
    d_pre = d_pooled * (1.0 - pooled * pooled)
    pool_low = d_pre.astype(jnp.bfloat16)
    await_all(w_copies)
    d_cls = plain_rows(pool_low, w_ref[:, 8 * D :], NT)
    center, scale = norm_parts(cls[:, D : 2 * D])
    cls_low = (center * scale * vec_ref[5:6, :] + vec_ref[6:7, :]).astype(jnp.bfloat16)
    d_res, unit = norm_back(d_cls, center, scale, vec_ref[5:6, :])
    d_down = d_res * cls[:, 2 * D : 3 * D]
    down_low = d_down.astype(jnp.bfloat16)
    d_up = plain_rows(down_low, w_ref[:, 4 * D : 8 * D], NN) * gelu_slope(cls[:, 3 * D :])
    up_low = d_up.astype(jnp.bfloat16)
    cls[:, :D] = d_res + plain_rows(up_low, w_ref[:, : 4 * D], NT)
    first_ref[...] = cls[pl.ds(place, n), :D]
    out_ref[:, :D] = d_down
    out_ref[:, D:] = d_up
    low_ref[:, :D] = cls_low
    low_ref[:, D:] = pool_low
    up_sum = jnp.sum(d_up, axis=0, keepdims=True)
    rows = [up_sum[:, c * D : (c + 1) * D] for c in range(4)]
    rows += [jnp.sum(each, axis=0, keepdims=True) for each in (d_down, d_cls * unit, d_cls, d_pre)]
    for k, value in enumerate(rows):
        part_ref[k : k + 1, :] = value


def pooled_backward(me, units, w_head, cls, valid, vecs):
    n = cls[0].shape[0]
    total = valid.shape[1]
    hbm, vmem = pl.BlockSpec(memory_space=pltpu.HBM), pl.BlockSpec(memory_space=pltpu.VMEM)
    smem = pl.BlockSpec(memory_space=pltpu.SMEM)
    f32, low = jnp.float32, jnp.bfloat16
    return pl.pallas_call(
        pooled_kernel,
        out_shape=(
            result((1, 1), f32),
            pltpu.HBM((n, D), f32),
            result((2 * n, 5 * D), f32, True),
            result((2 * n, 2 * D), low, True),
            result((8, D), f32, True),
        ),
        in_specs=[smem] + [hbm] * 7,
        out_specs=(smem,) + (vmem,) * 4,
        scratch_shapes=[
            pltpu.VMEM((32, n, D), low),
            pltpu.VMEM((total, total), low),
            pltpu.VMEM((total, D), f32),
            pltpu.VMEM((2 * n, 7 * D), f32),
            pltpu.VMEM((1, total), f32),
            pltpu.VMEM((8, D), f32),
            pltpu.VMEM((D, 9 * D), low),
            pltpu.SemaphoreType.DMA((36,)),
            pltpu.SemaphoreType.DMA((3,)),
        ],
        compiler_params=room(25),
    )(jnp.reshape(me, (1,)), *far(*units, w_head, *cls, valid, vecs))


def head_grad_kernel(shard, me_ref, pick_ref, *refs):
    mains, (cls, cls_low, cls_part, part_in, part_sib_in) = refs[:8], refs[8:13]
    pieces, scratch = refs[13:21], refs[21:]
    first, up, down, act, part, part_sib, stage, flat, sems, in_sems = scratch
    me = me_ref[0]
    core = me & 1
    many = mains[0].shape[0]
    n = cls.shape[0] // 2
    half = n // 2
    place = pl.multiple_of(core * n, n)
    pairs = []
    for k, whole in enumerate((first, up, down, act)):
        for side in range(2):
            pairs.append((mains[2 * k + side], whole.at[pl.ds(side * many, many)]))
    loads = bring(pairs + [(part_in, part), (part_sib_in, part_sib)], in_sems)
    top_row = lax.broadcasted_iota(jnp.int32, (16, 1), 0) == 0

    def join(whole, cols):
        for side in range(2):
            first_at = place if side == 0 else n - place
            for view in range(2):
                for slot in range(half):
                    at = pl.multiple_of(side * many + view * (many // 2) + pick_ref[side, slot], 16)
                    more = jnp.where(top_row, cls[pl.ds(first_at + view * half + slot, 1), cols], 0.0)
                    whole[pl.ds(at, 16), :] = (whole[pl.ds(at, 16), :] + more).astype(jnp.bfloat16)

    blocks, rows = stage.shape[0], stage.shape[1]
    cols = 9 * D // LANES
    pick = pick_columns(core, blocks)

    def spread(grads, first_col):
        for block in range(blocks):
            for group in range(4):
                for k in range(grads.shape[1] // LANES):
                    at = group * 8 * cols + first_col + k
                    size = 8 if group < 3 else 2
                    tile = grads[block * 32 + group * 8 : block * 32 + group * 8 + size]
                    flat[block, pl.ds(at, size, stride=cols), :] = tile[:, k * LANES : (k + 1) * LANES]

    def fill(left, right, first_col):
        chunk = 4 * LANES
        for k in range(right.shape[1] // chunk):
            spread(plain_rows(left, right[:, pl.ds(k * chunk, chunk)], NN), first_col + k * chunk // LANES)

    await_all(loads[:4])
    join(up, pl.ds(D, 4 * D))
    fill(plain_rows(pick, first[...], NT).astype(jnp.bfloat16), up, 0)
    few = plain_rows(pick, cls_low[:, :D], NT).astype(jnp.bfloat16)
    spread(plain_rows(few, cls_low[:, D:], NN), 8 * D // LANES)
    await_all(loads[4:])
    join(down, pl.ds(0, D))
    fill(plain_rows(pick, down[...], NT).astype(jnp.bfloat16), act, 4 * D // LANES)

    @pl.when(core == 1)
    def _():
        flat[blocks - 1, pl.ds(24 * cols, 48), :] = flat_of(part[...] + part_sib[...] + cls_part[...])

    outs = []
    for piece, slots in list(zip(pieces, piece_slots(me, HALVES)))[::-1]:
        for k, slot in enumerate(slots):
            chip_at = slot >> 1
            at = pl.multiple_of(slot * shard // LANES // 8 * 8 - slot * 24 * cols, 8)
            stage[chip_at] = flat[chip_at, pl.ds(at, rows), :].astype(jnp.bfloat16)
            copy = pltpu.make_async_copy(stage.at[chip_at], piece.at[k], sems.at[len(outs)])
            copy.start()
            outs.append(copy)
    for copy in outs:
        copy.wait()


def head_grads(me, shard, picks, mains, cls, cls_low, cls_part, parts):
    many = mains[0].shape[0]
    rows = block_rows(shard)
    hbm, vmem = pl.BlockSpec(memory_space=pltpu.HBM), pl.BlockSpec(memory_space=pltpu.VMEM)
    smem = pl.BlockSpec(memory_space=pltpu.SMEM)
    f32, low = jnp.float32, jnp.bfloat16
    return pl.pallas_call(
        functools.partial(head_grad_kernel, shard),
        out_shape=tuple(pltpu.HBM((2, rows, LANES), low) for _ in HALVES),
        in_specs=[smem] * 2 + [hbm] * 8 + [vmem] * 3 + [hbm] * 2,
        out_specs=(hbm,) * len(HALVES),
        scratch_shapes=[
            pltpu.VMEM((2 * many, D), low),
            pltpu.VMEM((2 * many, 4 * D), low),
            pltpu.VMEM((2 * many, D), low),
            pltpu.VMEM((2 * many, 4 * D), low),
            pltpu.VMEM((8, D), f32),
            pltpu.VMEM((8, D), f32),
            pltpu.VMEM((16, rows, LANES), low),
            pltpu.VMEM((16, 26 * 9 * D // LANES + 4, LANES), f32),
            pltpu.SemaphoreType.DMA((16,)),
            pltpu.SemaphoreType.DMA((10,)),
        ],
        compiler_params=room(44),
    )(jnp.reshape(me, (1,)), picks, *mains, cls, cls_low, cls_part, *parts)


def store_pieces(shard, layout, me, pieces, stage, flat, sems):
    rows = stage.shape[1]
    copies = []
    for piece, slots in list(zip(pieces, piece_slots(me, layout)))[::-1]:
        for k, slot in enumerate(slots):
            at = pl.multiple_of(slot * shard // LANES // 8 * 8, 8)
            stage[slot] = flat[pl.ds(at, rows), :].astype(jnp.bfloat16)
            copy = pltpu.make_async_copy(stage.at[slot], piece.at[k], sems.at[len(copies)])
            copy.start()
            copies.append(copy)
    for copy in copies:
        copy.wait()


def sum_small(value):
    for bit in (CORE, XBIT, YBIT, 8, 16):
        value = value + swap(value, bit)
    return value


def on_grid(
    embeddings,
    cotangent,
    drop_masks,
    lengths,
    buckets,
    attn_params,
    attn_moment,
    attn_second,
    attn_ema,
    head_params,
    head_moment,
    head_second,
    head_ema,
):
    tok_rows = embeddings.shape[0]
    slot_count = lengths.shape[0]
    all_rows = 2 * tok_rows
    device = lax.axis_index("sent")
    shards = (attn_params.shape[0], head_params.shape[0])
    attn_pieces, attn_first, attn_last = gather_attn(attn_params, device)
    head_zs = gather_head_line(head_params, device, attn_first)
    bucket_all = bucket_length(buckets)
    slot_ids = jnp.arange(slot_count, dtype=jnp.int32)
    valid_everything = (
        (slot_ids[None, :] < (tok_rows // bucket_all)[:, None]).astype(jnp.float32).reshape(-1)
    )
    bucket_len = bucket_all[device]

    def picks_of(length):
        count = tok_rows // length
        return jnp.concatenate([jnp.minimum(slot_ids, count - 1) * length, count[None]])

    picks = picks_of(bucket_len)
    both_picks = jnp.stack([picks, picks_of(bucket_all[device ^ CORE])])
    head_zs = after(head_zs, *attn_last)
    z_low, z_high = jnp.stack(head_zs[:2]), jnp.stack(head_zs[2:])
    y_low, x_high = swap(z_low, YBIT), swap(z_high, XBIT)
    x_low, y_high = swap(z_low, XBIT), swap(z_high, YBIT)
    head_xy = (x_low, x_high, y_low, y_high)
    (
        attn_mats,
        attn_vecs,
        emb_rows,
        attn_in_low,
        qkv_low,
        probs,
        mixed_low,
        first_res,
        first_norm,
        first_low,
    ) = attn_forward(attn_pieces, device, shards[0], bucket_len, lengths, embeddings, drop_masks)
    valid_views = jnp.broadcast_to(
        valid_everything.reshape(-1, 1, slot_count), (bucket_all.shape[0], 2, slot_count)
    ).reshape(-1)
    valid_row = valid_views[None, :]
    head_xy, first_norm, valid_row, picks, both_picks = lax.optimization_barrier(
        (head_xy, first_norm, valid_row, picks, both_picks)
    )
    head_pieces = gather_head(z_low, z_high, *head_xy)
    first_sib = swap(first_low, CORE)
    head_mats, head_vecs, unit_low, cls = make_head(
        head_pieces, device, shards[1], picks, first_norm, drop_masks
    )
    unit_zs = [unit_low] + [swap(unit_low, bit) for bit in ZBITS]
    cls_sib = swap(cls, CORE)
    active_low, slope, hidden_out, d_second_res, down_low, parts = head_forward(
        first_low, first_norm, head_mats, head_vecs, drop_masks, cotangent
    )
    active_low, down_low, unit_zs, cls_sib = lax.optimization_barrier(
        (active_low, down_low, unit_zs, cls_sib)
    )
    unit_line = jnp.stack(unit_zs)
    unit_lines = [unit_line] + [swap(unit_line, bit) for bit in (XBIT, YBIT, XBIT | YBIT)]
    active_sib, down_sib = swap(active_low, CORE), swap(down_low, CORE)
    up_low, d_first, parts = head_backward(down_low, slope, d_second_res, parts, head_mats)
    up_low, unit_lines, active_sib, down_sib = lax.optimization_barrier(
        (up_low, unit_lines, active_sib, down_sib)
    )
    units = jnp.stack(unit_lines)
    units_sib = swap(units, CORE)
    up_sib, parts_sib = swap(after(up_low, units_sib), CORE), swap(parts, CORE)
    loss, d_first_cls, cls_grads, cls_low, cls_part = pooled_backward(
        device, (units, units_sib), head_mats, (cls, cls_sib), valid_row, head_vecs
    )
    head_pieces = head_grads(
        device,
        shards[1],
        both_picks,
        (first_low, first_sib, up_low, up_sib, down_low, down_sib, active_low, active_sib),
        cls_grads,
        cls_low,
        cls_part,
        (parts, parts_sib),
    )
    loss = loss[0, 0]
    d_first, head_pieces = lax.optimization_barrier((d_first, head_pieces))
    line_low, line_high, x_low, x_high, y_low, y_high, d_low, d_high = head_pieces
    d_low, d_high = swap(d_low, XBIT), swap(d_high, YBIT)
    d_first_res, g_out, d_mixed, norm_parts_in = norm_backward(
        picks, d_first, d_first_cls, first_res, attn_vecs, drop_masks, mixed_low, attn_mats
    )
    d_qkv, attn_parts = attn_backward(d_mixed, qkv_low, probs)
    d_qkv, d_low, d_high = lax.optimization_barrier((d_qkv, d_low, d_high))
    x_high, y_high = swap(low_sum(x_high, d_high), XBIT), swap(y_high, YBIT)
    y_low = low_sum(y_low, d_low)
    d_qkv, y_low = lax.optimization_barrier((d_qkv, y_low))
    input_grad, *attn_pieces = attn_grads(
        device,
        shards[0],
        bucket_len,
        d_qkv,
        attn_in_low,
        attn_mats,
        d_first_res,
        emb_rows,
        attn_vecs,
        drop_masks,
        g_out,
        attn_parts,
        norm_parts_in,
    )
    attn_pieces, x_low, y_low, x_high, y_high = lax.optimization_barrier(
        (attn_pieces, x_low, y_low, x_high, y_high)
    )
    line_high = low_sum(line_high, x_high, y_high)
    x_low, y_low = swap(x_low, XBIT), swap(y_low, YBIT)
    attn_sums = scatter_core(attn_pieces)
    attn_sums, x_low, y_low = lax.optimization_barrier((attn_sums, x_low, y_low))
    line_low = low_sum(line_low, x_low, y_low)
    head_sum = scatter_along(line_low[0], [line_low[1], line_high[0], line_high[1]])
    head_share = unpack_shard(head_sum, device, shards[1])
    attn_share = unpack_shard(scatter_attn(attn_sums), device, shards[0])
    squares = jnp.sum(attn_share * attn_share) + jnp.sum(head_share * head_share)
    total_squares = sum_small(squares)
    grad_norm = jnp.sqrt(total_squares)
    clip_scale = jnp.minimum(1.0, clip_bound / grad_norm)
    attn_new = adam_step(attn_share * clip_scale, attn_params, attn_moment, attn_second, attn_ema)
    head_new = adam_step(head_share * clip_scale, head_params, head_moment, head_second, head_ema)
    return (
        hidden_out,
        input_grad,
        loss,
        grad_norm,
        attn_new[0],
        attn_new[1],
        attn_new[2],
        attn_new[3],
        head_new[0],
        head_new[1],
        head_new[2],
        head_new[3],
    )


def on_any_mesh(
    embeddings,
    cotangent,
    drop_masks,
    lengths,
    buckets,
    attn_params,
    attn_moment,
    attn_second,
    attn_ema,
    head_params,
    head_moment,
    head_second,
    head_ema,
):
    tok_rows = embeddings.shape[0]
    slot_count = lengths.shape[0]
    all_rows = 2 * tok_rows
    device = lax.axis_index("sent")
    attn_full, head_full = (
        lax.all_gather(attn_params.astype(jnp.bfloat16), "sent", axis=0, tiled=True),
        lax.all_gather(head_params.astype(jnp.bfloat16), "sent", axis=0, tiled=True),
    )
    attn_mats = attn_full[: 4 * D * D].reshape(D, 4 * D)
    attn_vecs_low = attn_full[4 * D * D :].reshape(D, 8 + POS)
    attn_vecs = attn_vecs_low.astype(jnp.float32)
    head_mats = head_full[: 9 * D * D].reshape(D, 9 * D)
    head_vecs = head_full[9 * D * D :].reshape(D, 8).astype(jnp.float32)
    w_qkv = attn_mats[:, : 3 * D]
    w_out = attn_mats[:, 3 * D :]
    w_up = head_mats[:, : 4 * D]
    w_down = head_mats[:, 4 * D : 8 * D]
    w_pool = head_mats[:, 8 * D :]
    bucket_all = bucket_length(buckets)
    slot_ids = jnp.arange(slot_count, dtype=jnp.int32)
    valid_everything = (
        (slot_ids[None, :] < (tok_rows // bucket_all)[:, None]).astype(jnp.float32).reshape(-1)
    )
    bucket_len = bucket_all[device]
    sent_count = tok_rows // bucket_len
    valid_own = (slot_ids < sent_count).astype(jnp.float32)
    row_ids = jnp.arange(tok_rows, dtype=jnp.int32)
    sentence = row_ids // bucket_len
    row_place = row_ids % bucket_len
    slot_len = jnp.sum(
        jnp.where(sentence[:, None] == slot_ids[None, :], lengths[None, :], 0), axis=1
    )
    key_ok = row_place < slot_len
    block = POS
    sent_blocks = sentence.reshape(-1, block)
    ok_blocks = key_ok.reshape(-1, block)
    allowed = (sent_blocks[:, :, None] == sent_blocks[:, None, :]) & ok_blocks[:, None, :]
    allowed = jnp.concatenate([allowed, allowed], axis=0)[:, None]
    place_hot = (row_place[:, None] == jnp.arange(POS, dtype=jnp.int32)[None, :]).astype(
        jnp.bfloat16
    )
    pos_rows = plain_dot(place_hot, attn_vecs_low[:, 8:].T)
    emb_rows = embeddings.astype(jnp.float32) + pos_rows + attn_vecs[:, 7]
    normed, emb_back = jax.vjp(layer_norm, emb_rows, attn_vecs[:, 5], attn_vecs[:, 6])
    keep_masks = drop_masks.astype(jnp.float32) / keep_prob
    keep_attn = keep_masks[:, 1].reshape(all_rows, D)
    keep_ffn = keep_masks[:, 2].reshape(all_rows, D)
    attn_in = (normed[None] * keep_masks[:, 0]).reshape(all_rows, D)
    attn_in_low = attn_in.astype(jnp.bfloat16)
    qkv_bias = jnp.concatenate([attn_vecs[:, 0], jnp.zeros((D,), jnp.float32), attn_vecs[:, 1]])
    qkv_low = (plain_dot(attn_in_low, w_qkv) + qkv_bias).astype(jnp.bfloat16)
    head_split = qkv_low.reshape(-1, block, 3, H, HD)
    queries = head_split[:, :, 0]
    keys_low = head_split[:, :, 1]
    values_low = head_split[:, :, 2]
    score_scale = HD ** (-0.5)
    raw_scores = jnp.einsum(
        "bqhd,bkhd->bhqk", queries, keys_low, preferred_element_type=jnp.float32
    )
    scores = jnp.where(allowed, raw_scores * score_scale, masked_scores)
    row_top = jnp.max(scores, axis=-1, keepdims=True)
    expo_vals = jnp.exp(scores - row_top)
    row_total = jnp.sum(expo_vals, axis=-1, keepdims=True)
    attn_probs = expo_vals / row_total
    score_lse = row_top + jnp.log(row_total)
    mixed_out = jnp.einsum(
        "bhqk,bkhd->bqhd",
        attn_probs.astype(jnp.bfloat16),
        values_low,
        preferred_element_type=jnp.float32,
    )
    mixed_low = mixed_out.reshape(all_rows, D).astype(jnp.bfloat16)
    branch = plain_dot(mixed_low, w_out) + attn_vecs[:, 2]
    first_res = attn_in + keep_attn * branch
    first_norm, first_back = jax.vjp(layer_norm, first_res, attn_vecs[:, 3], attn_vecs[:, 4])
    first_low = first_norm.astype(jnp.bfloat16)
    up_bias = head_vecs[:, :4].T.reshape(4 * D)
    up_pre = plain_dot(first_low, w_up) + up_bias
    active, gelu_back = jax.vjp(gelu_exact, up_pre)
    active_low = active.astype(jnp.bfloat16)
    down_out = target_dot_terms(active_low, w_down) + head_vecs[:, 4]
    second_res = first_norm + keep_ffn * down_out
    second_norm, second_back = jax.vjp(layer_norm, second_res, head_vecs[:, 5], head_vecs[:, 6])
    hidden_out = second_norm.astype(jnp.bfloat16).reshape(2, tok_rows, D)
    cls_pick = jnp.minimum(slot_ids, sent_count - 1) * bucket_len
    cls_rows = jnp.take(second_norm.reshape(2, tok_rows, D), cls_pick, axis=1).reshape(
        2 * slot_count, D
    )
    cls_low = cls_rows.astype(jnp.bfloat16)
    pooled = jnp.tanh(plain_dot(cls_low, w_pool) + head_vecs[:, 7])
    unit_rows, unit_back = jax.vjp(unit_scale, pooled)
    unit_low = unit_rows.astype(jnp.bfloat16)
    query_embeddings = unit_low[:slot_count]
    positive_view_set = unit_low[slot_count:]
    target_sentence_set, everyone = (
        lax.all_gather(positive_view_set, "sent", axis=0, tiled=True),
        lax.all_gather(query_embeddings, "sent", axis=0, tiled=True),
    )
    own_cols = device * slot_count + slot_ids
    col_ids = jnp.arange(target_sentence_set.shape[0], dtype=jnp.int32)
    pos_hot = col_ids[None, :] == own_cols[:, None]
    cosine_logit_table = jnp.where(
        valid_everything[None, :] > 0,
        target_dot_terms(query_embeddings, target_sentence_set) / logit_divisor,
        masked_scores,
    )
    sim_top = jnp.max(cosine_logit_table, axis=-1, keepdims=True)
    row_lse = sim_top[:, 0] + jnp.log(jnp.sum(jnp.exp(cosine_logit_table - sim_top), axis=-1))
    positive = jnp.sum(jnp.where(pos_hot, cosine_logit_table, 0.0), axis=-1)
    local_loss = jnp.sum(valid_own * (row_lse - positive))
    loss_sum = lax.psum(local_loss, "sent")
    cosine_logit_cotangent = valid_own[:, None] * (
        jnp.exp(cosine_logit_table - row_lse[:, None]) - pos_hot.astype(jnp.float32)
    )
    cosine_logit_summed = (cosine_logit_cotangent / logit_divisor).astype(jnp.bfloat16)
    d_anchor = plain_dot(cosine_logit_summed, target_sentence_set)
    all_lse = lax.all_gather(row_lse, "sent", axis=0, tiled=True)
    back_sim = target_dot_terms(everyone, positive_view_set) / logit_divisor
    back_hot = (col_ids[:, None] == own_cols[None, :]).astype(jnp.float32)
    back_grad = valid_everything[:, None] * (
        jnp.exp(back_sim - all_lse[:, None]) * valid_own[None, :] - back_hot
    )
    d_partner = rows_dot((back_grad / logit_divisor).astype(jnp.bfloat16), everyone)
    d_unit = jnp.concatenate([d_anchor, d_partner], axis=0)
    d_pooled = unit_back(d_unit)[0]
    d_pool_pre = d_pooled * (1.0 - pooled * pooled)
    pool_low = d_pool_pre.astype(jnp.bfloat16)
    g_pool = rows_dot(cls_low, pool_low)
    g_pool_bias = jnp.sum(d_pool_pre, axis=0)
    d_cls = target_dot_terms(pool_low, w_pool).reshape(2, slot_count, D)
    pick_hot = ((row_ids[None, :] == cls_pick[:, None]) & (slot_ids[:, None] < sent_count)).astype(
        jnp.float32
    )
    d_second = cotangent.astype(jnp.float32) + jnp.einsum(
        "st,vsd->vtd", pick_hot, d_cls, precision=highest
    )
    d_second_res, g_gain_two, g_shift_two = second_back(d_second.reshape(all_rows, D))
    d_down = d_second_res * keep_ffn
    g_down_bias = jnp.sum(d_down, axis=0)
    down_low = d_down.astype(jnp.bfloat16)
    g_down = rows_dot(down_low, active_low)
    d_active = plain_dot(down_low, w_down)
    d_up = gelu_back(d_active)[0]
    g_up_bias = jnp.sum(d_up, axis=0)
    up_low = d_up.astype(jnp.bfloat16)
    g_up = rows_dot(first_low, up_low)
    d_first = d_second_res + target_dot_terms(up_low, w_up)
    head_vec_grad = jnp.concatenate(
        [
            g_up_bias.reshape(4, D).T,
            jnp.stack([g_down_bias, g_gain_two, g_shift_two, g_pool_bias], axis=1),
        ],
        axis=1,
    )
    head_grad = jnp.concatenate(
        [jnp.concatenate([g_up, g_down, g_pool], axis=1).reshape(-1), head_vec_grad.reshape(-1)]
    )
    d_first_res, g_gain_one, g_shift_one = first_back(d_first)
    d_branch = d_first_res * keep_attn
    g_out_bias = jnp.sum(d_branch, axis=0)
    branch_low = d_branch.astype(jnp.bfloat16)
    g_out = rows_dot(mixed_low, branch_low)
    d_mixed = target_dot_terms(branch_low, w_out).astype(jnp.bfloat16).reshape(-1, block, H, HD)
    again = jnp.where(
        allowed,
        jnp.einsum("bqhd,bkhd->bhqk", queries, keys_low, preferred_element_type=jnp.float32)
        * score_scale,
        masked_scores,
    )
    probs_again = jnp.exp(again - score_lse)
    d_values = jnp.einsum(
        "bhqk,bqhd->bkhd",
        probs_again.astype(jnp.bfloat16),
        d_mixed,
        preferred_element_type=jnp.float32,
    )
    d_probs = jnp.einsum("bqhd,bkhd->bhqk", d_mixed, values_low, preferred_element_type=jnp.float32)
    row_delta = jnp.sum(probs_again * d_probs, axis=-1, keepdims=True)
    score_low = (probs_again * (d_probs - row_delta) * score_scale).astype(jnp.bfloat16)
    d_queries = jnp.einsum(
        "bhqk,bkhd->bqhd", score_low, keys_low, preferred_element_type=jnp.float32
    )
    d_keys = jnp.einsum("bhqk,bqhd->bkhd", score_low, queries, preferred_element_type=jnp.float32)
    d_qkv = jnp.stack([d_queries, d_keys, d_values], axis=2).reshape(all_rows, 3 * D)
    g_q_bias = jnp.sum(d_queries.reshape(all_rows, D), axis=0)
    g_v_bias = jnp.sum(d_values.reshape(all_rows, D), axis=0)
    qkv_grad_low = d_qkv.astype(jnp.bfloat16)
    g_qkv = rows_dot(attn_in_low, qkv_grad_low)
    d_attn_in = d_first_res + target_dot_terms(qkv_grad_low, w_qkv)
    d_normed = jnp.sum(d_attn_in.reshape(2, tok_rows, D) * keep_masks[:, 0], axis=0)
    input_grad, g_gain_emb, g_shift_emb = emb_back(d_normed)
    g_type = jnp.sum(input_grad, axis=0)
    g_table = lax.dot_general(
        place_hot.astype(jnp.float32),
        input_grad,
        (((0,), (0,)), ((), ())),
        precision=highest,
        preferred_element_type=jnp.float32,
    )
    attn_vec_grad = jnp.concatenate(
        [
            jnp.stack(
                [
                    g_q_bias,
                    g_v_bias,
                    g_out_bias,
                    g_gain_one,
                    g_shift_one,
                    g_gain_emb,
                    g_shift_emb,
                    g_type,
                ],
                axis=1,
            ),
            g_table.T,
        ],
        axis=1,
    )
    attn_grad = jnp.concatenate(
        [jnp.concatenate([g_qkv, g_out], axis=1).reshape(-1), attn_vec_grad.reshape(-1)]
    )
    attn_share, head_share = (
        lax.psum_scatter(attn_grad, "sent", scatter_dimension=0, tiled=True),
        lax.psum_scatter(head_grad, "sent", scatter_dimension=0, tiled=True),
    )
    squares = jnp.sum(attn_share * attn_share) + jnp.sum(head_share * head_share)
    total_squares = lax.psum(squares, "sent")
    loss = loss_sum / jnp.sum(valid_everything)
    grad_norm = jnp.sqrt(total_squares)
    clip_scale = jnp.minimum(1.0, clip_bound / grad_norm)
    attn_new = adam_step(attn_share * clip_scale, attn_params, attn_moment, attn_second, attn_ema)
    head_new = adam_step(head_share * clip_scale, head_params, head_moment, head_second, head_ema)
    return (
        hidden_out,
        input_grad,
        loss,
        grad_norm,
        attn_new[0],
        attn_new[1],
        attn_new[2],
        attn_new[3],
        head_new[0],
        head_new[1],
        head_new[2],
        head_new[3],
    )


def on_device(*arrays):
    shards = (arrays[5].shape[0], arrays[9].shape[0])
    local = on_grid if is_grid(lax.axis_size("sent"), *shards) else on_any_mesh
    return local(*arrays)


def solution(mesh):
    in_specs = (
        P("sent", None),
        P(None, "sent", None),
        P(None, None, "sent", None),
        P("sent"),
        P(),
        P("sent"),
        P("sent"),
        P("sent"),
        P("sent"),
        P("sent"),
        P("sent"),
        P("sent"),
        P("sent"),
    )
    out_specs = (
        P(None, "sent", None),
        P("sent", None),
        P(),
        P(),
        P("sent"),
        P("sent"),
        P("sent"),
        P("sent"),
        P("sent"),
        P("sent"),
        P("sent"),
        P("sent"),
    )
    return jax.shard_map(
        on_device, mesh=mesh, in_specs=in_specs, out_specs=out_specs, check_vma=False
    )
```
